32 devices in a mesh: head: 4 (over x, core), seq: 8 (over z, y).
Axes of the slice: x: 2, y: 2, z: 4, core: 2. Of those that a mesh axis runs over, the one named last changes fastest.
Arguments:
- tokens: bfloat16 [8192, 1536], P(('seq', 'head')), may hold values from -6 to 6
- cotangent: bfloat16 [8192, 1536], P(('seq', 'head')), may hold values from -6 to 6
- attn_gain: float32 [1536], P(('head', 'seq')), may hold values from 0.5 to 1.5
- ffn_gain: float32 [1536], P(('head', 'seq')), may hold values from 0.5 to 1.5
- qkv_stack: float32 [256, 96, 112], P(('head', 'seq')), may hold values from -0.15625 to 0.15625
- out_stack: float32 [256, 96, 96], P(('head', 'seq')), may hold values from -1.25 to 1.25
- gateup_stack: float32 [1536, 96, 96], P(('head', 'seq')), may hold values from -0.15625 to 0.15625
- down_stack: float32 [768, 96, 96], P(('head', 'seq')), may hold values from -0.09375 to 0.09375
- qkv_left: float32 [256, 96, 96], P(('head', 'seq')), as said below
- qkv_right: float32 [256, 112, 112], P(('head', 'seq')), as said below
- out_left: float32 [256, 96, 96], P(('head', 'seq')), as said below
- out_right: float32 [256, 96, 96], P(('head', 'seq')), as said below
- gateup_left: float32 [1536, 96, 96], P(('head', 'seq')), as said below
- gateup_right: float32 [1536, 96, 96], P(('head', 'seq')), as said below
- down_left: float32 [768, 96, 96], P(('head', 'seq')), as said below
- down_right: float32 [768, 96, 96], P(('head', 'seq')), as said below
- qkv_left_root: float32 [256, 96, 96], P(('head', 'seq')), as said below
- qkv_right_root: float32 [256, 112, 112], P(('head', 'seq')), as said below
- out_left_root: float32 [256, 96, 96], P(('head', 'seq')), as said below
- out_right_root: float32 [256, 96, 96], P(('head', 'seq')), as said below
- gateup_left_root: float32 [1536, 96, 96], P(('head', 'seq')), as said below
- gateup_right_root: float32 [1536, 96, 96], P(('head', 'seq')), as said below
- down_left_root: float32 [768, 96, 96], P(('head', 'seq')), as said below
- down_right_root: float32 [768, 96, 96], P(('head', 'seq')), as said below
- sequence_ids: int32 [8192], replicated, may hold values from 0 to 2, as said below
- token_order: int32 [8192], P('seq'), may hold values from 0 to 1023, as said below
Outputs:
- block_out: bfloat16 [8192, 1536], P(('seq', 'head'))
- input_grad: float32 [8192, 1536], P(('seq', 'head'))
- attn_gain_grad: float32 [1536], P(('head', 'seq'))
- ffn_gain_grad: float32 [1536], P(('head', 'seq'))
- qkv_left_new: float32 [256, 96, 96], P(('head', 'seq'))
- qkv_right_new: float32 [256, 112, 112], P(('head', 'seq'))
- qkv_weight_new: float32 [256, 96, 112], P(('head', 'seq'))
- out_left_new: float32 [256, 96, 96], P(('head', 'seq'))
- out_right_new: float32 [256, 96, 96], P(('head', 'seq'))
- out_weight_new: float32 [256, 96, 96], P(('head', 'seq'))
- gateup_left_new: float32 [1536, 96, 96], P(('head', 'seq'))
- gateup_right_new: float32 [1536, 96, 96], P(('head', 'seq'))
- gateup_weight_new: float32 [1536, 96, 96], P(('head', 'seq'))
- down_left_new: float32 [768, 96, 96], P(('head', 'seq'))
- down_right_new: float32 [768, 96, 96], P(('head', 'seq'))
- down_weight_new: float32 [768, 96, 96], P(('head', 'seq'))
The draws below stay inside these ranges and needn't reach their ends.
Inputs may be any that keep to these rules, and one draw needn't show every extreme that they name: `token_order`: each aligned block of 1024 entries is a permutation of 0 to 1023. `sequence_ids`: never falls along the stream, starts at 0 and rises by one at each change; a value's run is at most 4096 positions long, one run exactly that long; apart from the first, no run begins at a multiple of 1024. `qkv_left`: symmetric blocks. `qkv_right`: symmetric blocks. `out_left`: symmetric blocks. `out_right`: symmetric blocks. `gateup_left`: symmetric blocks. `gateup_right`: symmetric blocks. `down_left`: symmetric blocks. `down_right`: symmetric blocks. `qkv_left_root`: symmetric blocks. `qkv_right_root`: symmetric blocks. `out_left_root`: symmetric blocks. `out_right_root`: symmetric blocks. `gateup_left_root`: symmetric blocks. `gateup_right_root`: symmetric blocks. `down_left_root`: symmetric blocks. `down_right_root`: symmetric blocks.
All inputs are finite; a program needn't handle non-finite values.
Results may differ from the reference program's by a relative error of at most 0.017.
Values may be sent and summed in bfloat16 or wider, within the bound.
A program may use at most 256 MiB of HBM per device.

```python
import jax
import jax.numpy as jnp
from jax import lax

D = 1536
HEADS = 12
HEAD_DIM = 128
FF = 4608
WINDOW = 1024
GRID = 16
QW = 1536
QKV = 1792
BLK = 96
BQ = 112
BH = 96
NU = 48
GROUP = 1024
TOKENS = 8192


def symmetric_blocks(key, count, order, lowest, highest, spread):
    diag_key, noise_key = jax.random.split(key)
    diagonal = jnp.exp(jax.random.uniform(diag_key, (count, order), jnp.float32, jnp.log(lowest), jnp.log(highest)))
    noise = jax.random.normal(noise_key, (count, order, order), jnp.float32) * (spread / order ** 0.5)
    mirrored = 0.5 * (noise + jnp.swapaxes(noise, 1, 2))
    identity = jnp.eye(order, dtype=jnp.float32)
    return mirrored * (1.0 - identity) + diagonal[:, :, None] * identity


def statistic(key, salt, count, order):
    return symmetric_blocks(jax.random.fold_in(key, salt), count, order, 0.3, 3.0, 0.3)


def inverse_root(key, salt, count, order):
    return symmetric_blocks(jax.random.fold_in(key, salt), count, order, 0.5, 2.0, 0.6)


def draw_qkv_left(key, part):
    return statistic(key, 1, GRID * GRID, BLK)


def draw_qkv_right(key, part):
    return statistic(key, 2, GRID * GRID, BQ)


def draw_out_left(key, part):
    return statistic(key, 3, GRID * GRID, BH)


def draw_out_right(key, part):
    return statistic(key, 4, GRID * GRID, BLK)


def draw_gateup_left(key, part):
    return statistic(key, 5, NU * 2 * GRID, BLK)


def draw_gateup_right(key, part):
    return statistic(key, 6, NU * 2 * GRID, BLK)


def draw_down_left(key, part):
    return statistic(key, 7, NU * GRID, BLK)


def draw_down_right(key, part):
    return statistic(key, 8, NU * GRID, BLK)


def draw_qkv_left_root(key, part):
    return inverse_root(key, 11, GRID * GRID, BLK)


def draw_qkv_right_root(key, part):
    return inverse_root(key, 12, GRID * GRID, BQ)


def draw_out_left_root(key, part):
    return inverse_root(key, 13, GRID * GRID, BH)


def draw_out_right_root(key, part):
    return inverse_root(key, 14, GRID * GRID, BLK)


def draw_gateup_left_root(key, part):
    return inverse_root(key, 15, NU * 2 * GRID, BLK)


def draw_gateup_right_root(key, part):
    return inverse_root(key, 16, NU * 2 * GRID, BLK)


def draw_down_left_root(key, part):
    return inverse_root(key, 17, NU * GRID, BLK)


def draw_down_right_root(key, part):
    return inverse_root(key, 18, NU * GRID, BLK)


def draw_sequence_ids(key, part):
    block_count = TOKENS // (2 * WINDOW)
    offsets = jax.random.randint(jax.random.fold_in(key, 31), (block_count,), 1, WINDOW).astype(jnp.int32)
    offsets = offsets.at[3].set(offsets[1])
    block_index = jnp.arange(block_count, dtype=jnp.int32)
    starts = block_index * (2 * WINDOW) + offsets
    counted = ((block_index >= 1) & (block_index != 2)).astype(jnp.int32)
    positions = jnp.arange(TOKENS, dtype=jnp.int32)
    passed = (positions[:, None] >= starts[None, :]).astype(jnp.int32) * counted[None, :]
    return jnp.sum(passed, axis=1).astype(jnp.int32)


def draw_token_order(key, part):
    group_keys = jax.random.split(jax.random.fold_in(key, 21), TOKENS // GROUP)
    orders = jax.vmap(lambda single: jax.random.permutation(single, GROUP))(group_keys)
    return orders.reshape(TOKENS).astype(jnp.int32)


def steps_of(stream_key, shape, cuts, least, high):
    def one(axis_at, blocks):
        steps = jax.random.uniform(jax.random.fold_in(jax.random.fold_in(stream_key, 6), axis_at), (blocks,), jnp.float32, least / len(cuts), high / len(cuts))
        return jnp.repeat(jnp.exp(steps), shape[axis_at] // blocks).reshape((-1,) + (1,) * (len(shape) - axis_at - 1))

    level = one(*cuts[0])
    for cut in cuts[1:]:
        level = level * one(*cut)
    return level


def bell_draw(stream_key, shape, width, reach, pieces=(), held_as=jnp.bfloat16):
    drawn = jax.random.normal(stream_key, shape, jnp.float32) * width
    if len(pieces) > 0:
        drawn = steps_of(stream_key, shape, pieces, -0.22, 0.18) * drawn
    return jnp.clip(drawn, min=-reach, max=reach).astype(held_as)


def setup_inputs(seed: int = 0) -> dict:
    splits = jax.random.split(jax.random.key(seed), 27)
    return {
        "tokens": bell_draw(splits[0], (TOKENS, D), 1.0, 6.0, ((0, 32),)),
        "cotangent": bell_draw(splits[1], (TOKENS, D), 1.0, 6.0, ((0, 32),)),
        "attn_gain": jnp.clip(1.0 + 0.1 * jax.random.normal(splits[2], (D,), jnp.float32), 0.5, 1.5),
        "ffn_gain": jnp.clip(1.0 + 0.1 * jax.random.normal(splits[3], (D,), jnp.float32), 0.5, 1.5),
        "qkv_stack": bell_draw(splits[4], (GRID * GRID, BLK, BQ), D ** -0.5, 0.15625, ((0, 32),), jnp.float32),
        "out_stack": bell_draw(splits[5], (GRID * GRID, BH, BLK), (QW // 64) ** -0.5, 1.25, ((0, 32),), jnp.float32),
        "gateup_stack": bell_draw(splits[6], (NU * 2 * GRID, BLK, BLK), D ** -0.5, 0.15625, ((0, 32),), jnp.float32),
        "down_stack": bell_draw(splits[7], (NU * GRID, BLK, BLK), FF ** -0.5, 0.09375, ((0, 32),), jnp.float32),
        "qkv_left": draw_qkv_left(jax.random.fold_in(splits[26], 71), 0),
        "qkv_right": draw_qkv_right(jax.random.fold_in(splits[26], 71), 0),
        "out_left": draw_out_left(jax.random.fold_in(splits[26], 71), 0),
        "out_right": draw_out_right(jax.random.fold_in(splits[26], 71), 0),
        "gateup_left": draw_gateup_left(jax.random.fold_in(splits[26], 71), 0),
        "gateup_right": draw_gateup_right(jax.random.fold_in(splits[26], 71), 0),
        "down_left": draw_down_left(jax.random.fold_in(splits[26], 71), 0),
        "down_right": draw_down_right(jax.random.fold_in(splits[26], 71), 0),
        "qkv_left_root": draw_qkv_left_root(jax.random.fold_in(splits[26], 71), 0),
        "qkv_right_root": draw_qkv_right_root(jax.random.fold_in(splits[26], 71), 0),
        "out_left_root": draw_out_left_root(jax.random.fold_in(splits[26], 71), 0),
        "out_right_root": draw_out_right_root(jax.random.fold_in(splits[26], 71), 0),
        "gateup_left_root": draw_gateup_left_root(jax.random.fold_in(splits[26], 71), 0),
        "gateup_right_root": draw_gateup_right_root(jax.random.fold_in(splits[26], 71), 0),
        "down_left_root": draw_down_left_root(jax.random.fold_in(splits[26], 71), 0),
        "down_right_root": draw_down_right_root(jax.random.fold_in(splits[26], 71), 0),
        "sequence_ids": draw_sequence_ids(jax.random.fold_in(splits[26], 71), 0),
        "token_order": draw_token_order(jax.random.fold_in(splits[26], 71), 0),
    }


norm_eps = 1e-06
stat_eps = 1e-06
neg_fill = -1e+30

@jax.custom_vjp
def low(v):
    return lax.optimization_barrier(v.astype(jnp.bfloat16)).astype(jnp.float32)

@jax.custom_vjp
def low_back(v):
    return v

def low_keep(v):
    return (low(v), None)

def low_pass(kept, grad):
    return (grad,)

def back_keep(v):
    return (v, None)

def back_low(kept, grad):
    return (low(grad),)
low.defvjp(low_keep, low_pass)
low_back.defvjp(back_keep, back_low)

def rms_norm(values, gain):
    return values * lax.rsqrt(lax.optimization_barrier(jnp.mean(values * values, axis=-1, keepdims=True)) + norm_eps) * gain

def gelu_product(gate, upper):
    return jax.nn.gelu(gate, approximate=True) * upper

def precondition(weight, grad, left, right, left_root, right_root, rate):
    highest = lax.Precision.HIGHEST
    mean_square = lax.optimization_barrier(jnp.mean(grad * grad, axis=(1, 2), keepdims=True)) + stat_eps
    left_new = 0.5 * left + 0.5 * jnp.einsum('bij,bkj->bik', grad, grad, precision=highest) / (grad.shape[2] * mean_square)
    right_new = 0.5 * right + 0.5 * jnp.einsum('bji,bjk->bik', grad, grad, precision=highest) / (grad.shape[1] * mean_square)
    step = jnp.einsum('bij,bjk->bik', left_root, grad, precision=highest)
    step = jnp.einsum('bij,bjk->bik', step, right_root, precision=highest)
    return (left_new, right_new, weight - rate * step * lax.rsqrt(mean_square))

def forward(tokens_float, attn_gain, ffn_gain, qkv_stack, out_stack, gateup_stack, down_stack, sequence_ids, token_order):
    highest = lax.Precision.HIGHEST
    gain_one = low(attn_gain)
    gain_two = low(ffn_gain)
    qkv_grid = low(qkv_stack).reshape(GRID, GRID, BLK, BQ)
    out_grid = low(out_stack).reshape(GRID, GRID, BH, BLK)
    gateup_grid = low(gateup_stack).reshape(NU, 2, GRID, BLK, BLK)
    down_grid = low(down_stack).reshape(NU, GRID, BLK, BLK)
    row_block = min(TOKENS, 4096)
    block_count = TOKENS // row_block
    token_blocks = tokens_float.reshape(block_count, row_block, D)

    def first_section(rows_in):
        normed = low(rms_norm(rows_in, gain_one))
        projected = jnp.einsum('tri,rcij->tcj', normed.reshape(row_block, GRID, BLK), qkv_grid, precision=highest)
        return low(low_back(projected.reshape(row_block, QKV)))
    qkv_rows = lax.map(jax.checkpoint(first_section), token_blocks).reshape(TOKENS, QKV)
    group_start = jnp.arange(TOKENS, dtype=jnp.int32) // GROUP * GROUP
    source_rows = (group_start + token_order).astype(jnp.int32)
    stream = jnp.take(qkv_rows, source_rows, axis=0)
    padded = jnp.concatenate([jnp.zeros((GROUP, QKV), jnp.float32), stream], axis=0)
    padded_ids = jnp.concatenate([jnp.full((GROUP,), -1, jnp.int32), sequence_ids.astype(jnp.int32)])
    scale = HEAD_DIM ** (-0.5)
    query_pos = jnp.arange(GROUP, dtype=jnp.int32)
    key_pos = jnp.arange(2 * GROUP, dtype=jnp.int32)
    distance = query_pos[:, None] + GROUP - key_pos[None, :]
    nearby = (distance >= 0) & (distance < WINDOW)

    def attend(index):
        start = (index * GROUP).astype(jnp.int32)
        own = lax.dynamic_slice_in_dim(padded, start + GROUP, GROUP, 0)
        both = lax.dynamic_slice_in_dim(padded, start, 2 * GROUP, 0)
        own_ids = lax.dynamic_slice_in_dim(padded_ids, start + GROUP, GROUP, 0)
        both_ids = lax.dynamic_slice_in_dim(padded_ids, start, 2 * GROUP, 0)
        allowed = nearby & (own_ids[:, None] == both_ids[None, :])
        queries = own[:, :QW].reshape(GROUP, HEADS, HEAD_DIM)
        keys = both[:, QW:QW + HEAD_DIM]
        values = both[:, QW + HEAD_DIM:]
        scores = low_back(jnp.einsum('qhd,kd->hqk', queries, keys, precision=highest) * scale)
        scores = jnp.where(allowed[None], scores, neg_fill)
        top = lax.optimization_barrier(jnp.max(scores, axis=-1, keepdims=True))
        expo = jnp.exp(scores - top)
        probs = low(expo / lax.optimization_barrier(jnp.sum(expo, axis=-1, keepdims=True)))
        mixed = jnp.einsum('hqk,kd->qhd', probs, values, precision=highest).reshape(GROUP, QW)
        return low(low_back(mixed))
    mixed_stream = lax.map(jax.checkpoint(attend), jnp.arange(TOKENS // GROUP, dtype=jnp.int32)).reshape(TOKENS, QW)
    attended = jnp.zeros((TOKENS, QW), jnp.float32).at[source_rows].set(mixed_stream)

    def second_section(pair):
        rows_in, mixed_rows = pair
        projected = jnp.einsum('tri,rcij->tcj', mixed_rows.reshape(row_block, GRID, BH), out_grid, precision=highest).reshape(row_block, D)
        resid = rows_in + low_back(projected)
        normed = low(rms_norm(resid, gain_two))
        gate_up = low_back(jnp.einsum('tri,ukrij->tukj', normed.reshape(row_block, GRID, BLK), gateup_grid, precision=highest))
        hidden = low(gelu_product(gate_up[:, :, 0], gate_up[:, :, 1]))
        down = jnp.einsum('tui,ucij->tcj', hidden, down_grid, precision=highest).reshape(row_block, D)
        return resid + down
    result = lax.map(jax.checkpoint(second_section), (token_blocks, attended.reshape(block_count, row_block, QW)))
    return result.reshape(TOKENS, D)

def reference(tokens, cotangent, attn_gain, ffn_gain, qkv_stack, out_stack, gateup_stack, down_stack, qkv_left, qkv_right, out_left, out_right, gateup_left, gateup_right, down_left, down_right, qkv_left_root, qkv_right_root, out_left_root, out_right_root, gateup_left_root, gateup_right_root, down_left_root, down_right_root, sequence_ids, token_order):

    def wrapped(tokens_float, gain_first, gain_second, qkv_master, out_master, gateup_master, down_master):
        return forward(tokens_float, gain_first, gain_second, qkv_master, out_master, gateup_master, down_master, sequence_ids, token_order)
    result, pullback = jax.vjp(wrapped, tokens.astype(jnp.float32), attn_gain, ffn_gain, qkv_stack, out_stack, gateup_stack, down_stack)
    grads = pullback(cotangent.astype(jnp.float32))
    qkv_rate = 0.5 * D ** (-0.5)
    out_rate = 0.5 * (QW // 64) ** (-0.5)
    gateup_rate = 0.5 * D ** (-0.5)
    down_rate = 0.5 * FF ** (-0.5)
    qkv_new = precondition(qkv_stack, grads[3], qkv_left, qkv_right, qkv_left_root, qkv_right_root, qkv_rate)
    out_new = precondition(out_stack, grads[4], out_left, out_right, out_left_root, out_right_root, out_rate)
    gateup_new = precondition(gateup_stack, grads[5], gateup_left, gateup_right, gateup_left_root, gateup_right_root, gateup_rate)
    down_new = precondition(down_stack, grads[6], down_left, down_right, down_left_root, down_right_root, down_rate)
    return (result.astype(jnp.bfloat16), grads[0], grads[1], grads[2], qkv_new[0], qkv_new[1], qkv_new[2], out_new[0], out_new[1], out_new[2], gateup_new[0], gateup_new[1], gateup_new[2], down_new[0], down_new[1], down_new[2])
```

```python
import functools

import jax
import jax.numpy as jnp
from jax import lax
from jax.experimental import pallas as pl
from jax.experimental.pallas import tpu as pltpu
from jax.sharding import PartitionSpec as P

D = 1536
HEAD_DIM = 128
FF = 4608
WINDOW = 1024
GRID = 16
QW = 1536
QKV = 1792
BLK = 96
BQ = 112
BH = 96
NU = 48

norm_eps = 1e-06
stat_eps = 1e-06
neg_fill = -1e30

QUERY_TILE = 256
SPAN = WINDOW + QUERY_TILE

low = jnp.bfloat16
full = jnp.float32

NT = (((1,), (1,)), ((), ()))
NN = (((1,), (0,)), ((), ()))
TN = (((0,), (0,)), ((), ()))


def mul(a, b, dims, kind=full):
    return lax.dot_general(a, b, dims, preferred_element_type=kind)


def ring_place(index, count):
    return jnp.where(index % 2 == 0, index // 2, count - 1 - index // 2)


def ring_index(place, count):
    return jnp.where(place < count // 2, 2 * place, 2 * (count - 1 - place) + 1)


def ring_routes(count):
    order = [i for i in range(0, count, 2)] + [i for i in range(count - 1, 0, -2)]
    up = [(order[i], order[(i + 1) % count]) for i in range(count)]
    return up, [(b, a) for a, b in up]


def seq_gather(shard):
    count = lax.axis_size("seq")
    rows = shard.shape[0]
    half = rows // 2
    me = lax.axis_index("seq")
    place = ring_place(me, count)
    up, down = ring_routes(count)
    out = jnp.zeros((count,) + shard.shape, shard.dtype)
    out = lax.dynamic_update_slice(out, shard[None], (me, 0, 0))
    ahead = shard
    behind = shard
    for step in range(1, count // 2):
        ahead = lax.ppermute(ahead, "seq", up)
        behind = lax.ppermute(behind, "seq", down)
        out = lax.dynamic_update_slice(
            out, ahead[None], (ring_index((place - step + count) % count, count), 0, 0)
        )
        out = lax.dynamic_update_slice(
            out, behind[None], (ring_index((place + step) % count, count), 0, 0)
        )
    ahead = lax.ppermute(ahead[:half], "seq", up)
    behind = lax.ppermute(behind[half:], "seq", down)
    far = ring_index((place + count // 2) % count, count)
    out = lax.dynamic_update_slice(out, ahead[None], (far, 0, 0))
    return lax.dynamic_update_slice(out, behind[None], (far, half, 0))


def seq_sum(parts):
    count, rows = parts.shape[:2]
    half = rows // 2
    place = ring_place(lax.axis_index("seq"), count)
    up, down = ring_routes(count)

    def part(offset):
        index = ring_index((place + offset + count) % count, count)
        return lax.dynamic_slice_in_dim(parts, index, 1, 0)[0]

    far = part(count // 2)
    ahead = lax.ppermute(far[:half], "seq", up)
    behind = lax.ppermute(far[half:], "seq", down)
    for offset in range(count // 2 - 1, 0, -1):
        local = part(offset)
        if ahead.shape[0] == rows:
            local = (local.astype(full) + ahead.astype(full)).astype(low)
        else:
            local = jnp.concatenate(
                [(local[:half].astype(full) + ahead.astype(full)).astype(low), local[half:]]
            )
        ahead = lax.ppermute(local, "seq", up)
        local = part(-offset)
        if behind.shape[0] == rows:
            local = (local.astype(full) + behind.astype(full)).astype(low)
        else:
            local = jnp.concatenate(
                [local[:half], (local[half:].astype(full) + behind.astype(full)).astype(low)]
            )
        behind = lax.ppermute(local, "seq", down)
    return part(0).astype(full) + ahead.astype(full) + behind.astype(full)


def gather_rows(stack, unit, layout):
    short = stack.astype(low)
    if stack.shape[0] % unit == 0:
        shard = layout(short)
        rows = shard.reshape(-1, shard.shape[-1])
        out = seq_gather(rows)
        return out.reshape((-1,) + shard.shape[1:])
    return layout(lax.all_gather(short, "seq", axis=0, tiled=True))


def sum_rows(rows, local, unit, back):
    count = lax.axis_size("seq")
    if local % unit == 0:
        own = seq_sum(rows.reshape(count, -1, rows.shape[-1]))
        return back(own.reshape((-1,) + rows.shape[1:]))
    return lax.psum_scatter(back(rows), "seq", scatter_dimension=0, tiled=True).astype(full)


def to_columns(stack):
    n, i, j = stack.shape
    return stack.reshape(n // 8, 8, i, j).transpose(0, 2, 1, 3).reshape(n // 8, i, 8 * j)


def from_columns(rows):
    n, i, j = rows.shape
    return rows.reshape(n, i, 8, j // 8).transpose(0, 2, 1, 3).reshape(n * 8, i, j // 8)


def to_units(stack):
    n, i, j = stack.shape
    return stack.reshape(n // 16, 16, i, j).transpose(0, 3, 1, 2).reshape(n // 16, j, 16 * i)


def from_units(rows):
    n, j, i = rows.shape
    return rows.reshape(n, j, 16, i // 16).transpose(0, 2, 3, 1).reshape(n * 16, i // 16, j)


def joined_halves(rows):
    n, i, j = rows.shape
    return rows.reshape(n // 2, 2, i, j).transpose(0, 2, 1, 3).reshape(n // 2 * i, 2 * j)


def split_halves(matrix, i):
    rows, columns = matrix.shape
    m = rows // i
    return (
        matrix.reshape(m, i, 2, columns // 2).transpose(0, 2, 1, 3).reshape(2 * m, i, columns // 2)
    )


def to_partner(value, which):
    count = lax.axis_size("head")
    return lax.ppermute(value, "head", [(i, i ^ which) for i in range(count)])


def head_gather(value):
    across = to_partner(value, 2)
    mate = to_partner(value, 1)
    return value, mate, across, to_partner(across, 1)


def head_exchange(parts):
    return (parts[0],) + tuple(to_partner(parts[j], j) for j in (2, 1, 3))


def head_sum(parts):
    across = (parts[2].astype(full) + to_partner(parts[3], 1).astype(full)).astype(low)
    across = to_partner(across, 2)
    mine = parts[0].astype(full) + to_partner(parts[1], 1).astype(full)
    return mine + across.astype(full)


def in_order(parts, axis):
    me = lax.axis_index("head")
    odd = me % 2 == 1
    lower = [jnp.where(odd, parts[1], parts[0]), jnp.where(odd, parts[0], parts[1])]
    upper = [jnp.where(odd, parts[3], parts[2]), jnp.where(odd, parts[2], parts[3])]
    second = me >= 2
    return jnp.concatenate(
        [jnp.where(second, b, a) for a, b in zip(lower, upper)]
        + [jnp.where(second, a, b) for a, b in zip(lower, upper)],
        axis=axis,
    )


def tile_bias(tile, key_ids, query_ids, bias_ref):
    start = pl.multiple_of(tile * QUERY_TILE, QUERY_TILE)
    shape = (SPAN, QUERY_TILE)
    key = lax.broadcasted_iota(jnp.int32, shape, 0)
    query = lax.broadcasted_iota(jnp.int32, shape, 1)
    same = key_ids[pl.ds(start, SPAN), :] == query_ids[...]
    allowed = same & (key > query) & (key <= query + WINDOW)
    bias_ref[...] = jnp.where(allowed, 0.0, neg_fill)


def attend_kernel(q_ref, kv_ref, kvt_ref, key_ids, query_ids, out_ref, lse_ref, bias_ref):
    tile = pl.program_id(0)
    start = pl.multiple_of(tile * QUERY_TILE, QUERY_TILE)

    @pl.when(pl.program_id(1) == 0)
    def _():
        tile_bias(tile, key_ids, query_ids, bias_ref)

    keys = kv_ref[pl.ds(start, SPAN), :HEAD_DIM]
    scores = mul(keys, q_ref[...], NT) * HEAD_DIM ** (-0.5) + bias_ref[...]
    top = jnp.max(scores, axis=0, keepdims=True)
    expo = jnp.exp(scores - top)
    total = jnp.sum(expo, axis=0, keepdims=True)
    values = kvt_ref[HEAD_DIM:, pl.ds(start, SPAN)]
    mixed = mul(values, expo.astype(low), NN) / total
    out_ref[...] = mixed.T.astype(low)
    lse_ref[0] = top + jnp.log(total)


def attend_back_kernel(
    q_ref, g_ref, kv_ref, kvt_ref, key_ids, query_ids, lse_ref, dq_ref, dkv_ref, bias_ref
):
    tile = pl.program_id(0)
    start = pl.multiple_of(tile * QUERY_TILE, QUERY_TILE)
    scale = HEAD_DIM ** (-0.5)

    @pl.when((tile == 0) & (pl.program_id(1) == 0))
    def _():
        dkv_ref[...] = jnp.zeros_like(dkv_ref)

    @pl.when(pl.program_id(1) == 0)
    def _():
        tile_bias(tile, key_ids, query_ids, bias_ref)

    here = pl.ds(start, SPAN)
    queries = q_ref[...]
    grads = g_ref[...]
    scores = mul(kv_ref[here, :HEAD_DIM], queries, NT) * scale + bias_ref[...]
    probs = jnp.exp(scores - lse_ref[0])
    prob_grad = mul(kv_ref[here, HEAD_DIM:], grads, NT)
    delta = jnp.sum(probs * prob_grad, axis=0, keepdims=True)
    score_grad = (probs * (prob_grad - delta)).astype(low)
    dq = mul(kvt_ref[:HEAD_DIM, here], score_grad, NN) * scale
    dq_ref[...] = dq.T.astype(low)
    dkv_ref[here, :HEAD_DIM] += mul(score_grad, queries, NN) * scale
    dkv_ref[here, HEAD_DIM:] += mul(probs.astype(low), grads, NN)


def attention_specs(group):
    whole = lambda *shape: pl.BlockSpec(shape, lambda t, h: (0,) * len(shape))
    head_rows = pl.BlockSpec((QUERY_TILE, HEAD_DIM), lambda t, h: (t, h))
    keys = whole(2 * group, 2 * HEAD_DIM)
    keys_turned = whole(2 * HEAD_DIM, 2 * group)
    key_ids = whole(2 * group, 1)
    query_ids = pl.BlockSpec((1, QUERY_TILE), lambda t, h: (0, t))
    lse = pl.BlockSpec((1, 1, QUERY_TILE), lambda t, h: (h, 0, t))
    return head_rows, keys, keys_turned, key_ids, query_ids, lse


attention_params = pltpu.CompilerParams(
    dimension_semantics=("arbitrary", "arbitrary"), vmem_limit_bytes=40 * 1024 * 1024
)


def attend(queries, kv, kv_turned, key_ids, query_ids):
    group, width = queries.shape
    heads = width // HEAD_DIM
    rows, keys, turned, kids, qids, lse = attention_specs(group)
    work = heads * (group // QUERY_TILE) * SPAN * QUERY_TILE
    return pl.pallas_call(
        attend_kernel,
        grid=(group // QUERY_TILE, heads),
        in_specs=[rows, keys, turned, kids, qids],
        out_specs=[rows, lse],
        out_shape=[
            jax.ShapeDtypeStruct((group, width), low),
            jax.ShapeDtypeStruct((heads, 1, group), full),
        ],
        scratch_shapes=[pltpu.VMEM((SPAN, QUERY_TILE), full)],
        compiler_params=attention_params,
        cost_estimate=pl.CostEstimate(
            flops=8 * work * HEAD_DIM, bytes_accessed=6 << 20, transcendentals=work
        ),
        name="attend",
    )(queries, kv, kv_turned, key_ids, query_ids)


def attend_back(queries, grads, kv, kv_turned, key_ids, query_ids, lse_rows):
    group, width = queries.shape
    heads = width // HEAD_DIM
    rows, keys, turned, kids, qids, lse = attention_specs(group)
    work = heads * (group // QUERY_TILE) * SPAN * QUERY_TILE
    return pl.pallas_call(
        attend_back_kernel,
        grid=(group // QUERY_TILE, heads),
        in_specs=[rows, rows, keys, turned, kids, qids, lse],
        out_specs=[rows, keys],
        out_shape=[
            jax.ShapeDtypeStruct((group, width), low),
            jax.ShapeDtypeStruct((2 * group, 2 * HEAD_DIM), full),
        ],
        scratch_shapes=[pltpu.VMEM((SPAN, QUERY_TILE), full)],
        compiler_params=attention_params,
        cost_estimate=pl.CostEstimate(
            flops=20 * work * HEAD_DIM, bytes_accessed=8 << 20, transcendentals=work
        ),
        name="attend_back",
    )(queries, grads, kv, kv_turned, key_ids, query_ids, lse_rows)


def update_kernel(rate, w_ref, g_ref, l_ref, r_ref, lr_ref, rr_ref, ln_ref, rn_ref, wn_ref):
    count, rows, columns = g_ref.shape

    def block(b, carry):
        grad = g_ref[b]
        square = jnp.sum(jnp.sum(grad * grad, axis=1, keepdims=True), axis=0, keepdims=True)
        square = square * (1.0 / (rows * columns)) + stat_eps
        short = grad.astype(low)
        turned = grad.T.astype(low)
        ln_ref[b] = 0.5 * l_ref[b] + mul(short, turned, NN) * (0.5 / (columns * square))
        rn_ref[b] = 0.5 * r_ref[b] + mul(turned, short, NN) * (0.5 / (rows * square))
        step = mul(lr_ref[b].astype(low), short, NN).astype(low)
        step = mul(step, rr_ref[b].astype(low), NN)
        wn_ref[b] = w_ref[b] - step * (rate * lax.rsqrt(square))
        return carry

    lax.fori_loop(0, count, block, 0, unroll=2 if count % 2 == 0 else 1)


def update(weight, grad, left, right, left_root, right_root, rate):
    count, rows, columns = weight.shape
    batch = next(b for b in (8, 6, 4, 3, 2, 1) if count % b == 0)
    spec = lambda i, j: pl.BlockSpec((batch, i, j), lambda b: (b, 0, 0))
    return pl.pallas_call(
        functools.partial(update_kernel, rate),
        grid=(count // batch,),
        in_specs=[
            spec(rows, columns),
            spec(rows, columns),
            spec(rows, rows),
            spec(columns, columns),
            spec(rows, rows),
            spec(columns, columns),
        ],
        out_specs=[spec(rows, rows), spec(columns, columns), spec(rows, columns)],
        out_shape=[
            jax.ShapeDtypeStruct(left.shape, full),
            jax.ShapeDtypeStruct(right.shape, full),
            jax.ShapeDtypeStruct(weight.shape, full),
        ],
        compiler_params=pltpu.CompilerParams(vmem_limit_bytes=24 * 1024 * 1024),
        cost_estimate=pl.CostEstimate(
            flops=16 * count * 256 * 256 * 128,
            bytes_accessed=36 * count * rows * 128,
            transcendentals=0,
        ),
        name="update",
    )(weight, grad, left, right, left_root, right_root)


def norm_back(values, inverse, gain, grad):
    scaled = gain * grad
    mean = jnp.mean(values * scaled, axis=-1, keepdims=True)
    return inverse * scaled - values * (inverse * inverse * inverse * mean)


def inverse_norm(values):
    return lax.rsqrt(jnp.mean(values * values, axis=-1, keepdims=True) + norm_eps)


def on_device(
    tokens,
    cotangent,
    attn_gain,
    ffn_gain,
    qkv_stack,
    out_stack,
    gateup_stack,
    down_stack,
    qkv_left,
    qkv_right,
    out_left,
    out_right,
    gateup_left,
    gateup_right,
    down_left,
    down_right,
    qkv_left_root,
    qkv_right_root,
    out_left_root,
    out_right_root,
    gateup_left_root,
    gateup_right_root,
    down_left_root,
    down_right_root,
    sequence_ids,
    token_order,
):
    row_count = tokens.shape[0]
    head_count = lax.axis_size("head")
    seq_count = lax.axis_size("seq")
    device_count = head_count * seq_count
    group = row_count * head_count
    seq_index = lax.axis_index("seq")
    head_index = lax.axis_index("head")
    chip = head_index // 2
    core = head_index % 2
    local_width = QW // head_count

    gains = jnp.concatenate([attn_gain, ffn_gain]).astype(low).astype(full)[None]
    gains = lax.all_to_all(
        jnp.broadcast_to(gains, (device_count, gains.shape[1])),
        ("head", "seq"),
        split_axis=0,
        concat_axis=0,
        tiled=True,
    )
    own_gains = attn_gain.shape[0]
    gain_one = gains[:, :own_gains].reshape(1, D)
    gain_two = gains[:, own_gains:].reshape(1, D)

    qkv_rows = joined_halves(gather_rows(qkv_stack, 8, to_columns))
    out_rows = joined_halves(gather_rows(out_stack, 8, to_columns))
    gateup_shard, down_shard, qkv_rows, out_rows = lax.optimization_barrier(
        (gateup_stack, down_stack, qkv_rows, out_rows)
    )
    gateup = gather_rows(gateup_shard, 16, to_units)
    down = gather_rows(down_shard, 8, to_columns)
    unit_count = gateup.shape[0] // 2
    gateup = gateup.reshape(2 * unit_count * BLK, D)
    down = joined_halves(down)

    tokens_float = tokens.astype(full)
    inverse_one = inverse_norm(tokens_float)
    normed_one = (tokens_float * inverse_one * gain_one).astype(low)
    normed_one_group = jnp.concatenate(head_gather(normed_one))

    def chip_columns(which):
        return jnp.concatenate(
            [
                lax.dynamic_slice_in_dim(qkv_rows, which * 2 * local_width, 2 * local_width, 1),
                qkv_rows[:, QW:],
            ],
            axis=1,
        )

    def core_columns(block, which):
        return jnp.concatenate(
            [
                lax.dynamic_slice_in_dim(block, which * local_width, local_width, 1),
                block[:, 2 * local_width :],
            ],
            axis=1,
        )

    own_block = chip_columns(chip)
    across_block = to_partner(chip_columns(1 - chip), 2)
    qkv_own = in_order(
        [
            core_columns(own_block, core),
            to_partner(core_columns(own_block, 1 - core), 1),
            core_columns(across_block, core),
            to_partner(core_columns(across_block, 1 - core), 1),
        ],
        0,
    )
    projected = mul(normed_one_group, qkv_own, NN, low)

    buffer_rows = ((token_order // row_count) ^ head_index) * row_count + token_order % row_count
    shuffle = (
        buffer_rows[:, None] == lax.broadcasted_iota(jnp.int32, (group, group), 1)
    ).astype(low)
    stream = mul(shuffle, projected, NN, low)
    query_stream = stream[:, :local_width]
    kv_stream = stream[:, local_width:]
    kv_before = lax.ppermute(kv_stream, "seq", [(i, i + 1) for i in range(seq_count - 1)])
    kv_both = jnp.concatenate([kv_before, kv_stream], axis=0)
    kv_turned = kv_both.T
    ids_own = lax.dynamic_slice_in_dim(sequence_ids, seq_index * group, group, 0)
    ids_before = lax.dynamic_slice_in_dim(
        sequence_ids, jnp.maximum(seq_index - 1, 0) * group, group, 0
    )
    ids_before = jnp.where(seq_index > 0, ids_before, -1)
    key_ids = jnp.concatenate([ids_before, ids_own])[:, None]
    query_ids = ids_own[None, :]
    mixed_stream, lse = attend(query_stream, kv_both, kv_turned, key_ids, query_ids)
    mixed_group = mul(shuffle, mixed_stream, TN, low)

    mixed_parts = head_exchange([mixed_group[i * row_count :][:row_count] for i in range(4)])
    order = (0, 2, 1, 3)
    mixed_parts = [mixed_parts[order.index(j)] for j in range(4)]
    attended = jnp.concatenate(mixed_parts, axis=1)
    out_all = jnp.concatenate(head_gather(out_rows))
    resid = tokens_float + mul(attended, out_all, NN)
    inverse_two = inverse_norm(resid)
    normed_two = (resid * inverse_two * gain_two).astype(low)
    normed_group = jnp.concatenate(head_gather(normed_two))
    grad_group = jnp.concatenate(head_gather(cotangent))

    gate_up = mul(gateup, normed_group, NT).reshape(unit_count, 2, BLK, group)
    hidden, act_pull = jax.vjp(
        lambda g, u: jax.nn.gelu(g, approximate=True) * u, gate_up[:, 0], gate_up[:, 1]
    )
    hidden = hidden.astype(low).reshape(unit_count * BLK, group)
    hidden_grad = mul(down, grad_group, NT).reshape(unit_count, BLK, group)
    gate_grad, up_grad = act_pull(hidden_grad)
    gate_up_grad = (
        jnp.stack([gate_grad, up_grad], axis=1).astype(low).reshape(2 * unit_count * BLK, group)
    )
    normed_part = mul(gate_up_grad, gateup, TN, low)
    normed_two_grad = head_sum([normed_part[i * row_count :][:row_count] for i in range(4)])
    gateup_wgrad = mul(gate_up_grad, normed_group, NN, low).reshape(2 * unit_count, BLK, D)
    down_wgrad = split_halves(mul(hidden, grad_group, NN, low), BLK)
    gateup_grad_own = sum_rows(gateup_wgrad, gateup_stack.shape[0], 16, from_units)
    down_grad_own = sum_rows(down_wgrad, down_stack.shape[0], 8, from_columns)
    ffn_part = mul(hidden, down, TN, low)
    ffn_out = head_sum([ffn_part[i * row_count :][:row_count] for i in range(4)])
    block_out = (resid + ffn_out).astype(low)

    resid_grad = cotangent.astype(full) + norm_back(resid, inverse_two, gain_two, normed_two_grad)
    gain_two_grad = jnp.sum(normed_two_grad * resid * inverse_two, axis=0)
    proj_grad = resid_grad.astype(low)
    attended_grad = mul(proj_grad, out_all, NT, low)
    grad_parts = head_exchange(
        [attended_grad[:, i * local_width : (i + 1) * local_width] for i in range(4)]
    )
    mixed_grad_group = jnp.concatenate([grad_parts[order.index(j)] for j in range(4)])
    mixed_grad_stream = mul(shuffle, mixed_grad_group, NN, low)
    proj_grad_group = jnp.concatenate(head_gather(proj_grad))
    out_wgrad = split_halves(mul(mixed_group, proj_grad_group, TN, low), BLK)
    out_grad_own = sum_rows(out_wgrad, out_stack.shape[0], 8, from_columns)

    query_grad, kv_grad = attend_back(
        query_stream, mixed_grad_stream, kv_both, kv_turned, key_ids, query_ids, lse
    )
    kv_later = lax.ppermute(
        kv_grad[:group].astype(low), "seq", [(i, i - 1) for i in range(1, seq_count)]
    )
    kv_grad = (kv_grad[group:] + kv_later.astype(full)).astype(low)
    grad_local = mul(shuffle, jnp.concatenate([query_grad, kv_grad], axis=1), TN, low)
    gathered = head_gather(grad_local)

    def own_order(value, j):
        quarters = [value[i * row_count :][:row_count] for i in range(4)]
        return jnp.concatenate([quarters[i ^ j] for i in range(4)])

    gathered = [own_order(value, j) for j, value in enumerate(gathered)]
    kv_total = sum(value[:, local_width:].astype(full) for value in gathered).astype(low)
    qkv_grad = jnp.concatenate(
        [in_order([value[:, :local_width] for value in gathered], 1), kv_total], axis=1
    )
    feature_start = head_index * local_width
    features = lax.dynamic_slice_in_dim(normed_one_group, feature_start, local_width, 1)
    qkv_wgrad = split_halves(mul(features, qkv_grad, TN, low), BLK)
    qkv_grad_own = sum_rows(qkv_wgrad, qkv_stack.shape[0], 8, from_columns)
    feature_grad = mul(qkv_grad, qkv_rows, NT, low)
    feature_parts = head_exchange([feature_grad[i * row_count :][:row_count] for i in range(4)])
    normed_one_grad = in_order([feature_parts[order.index(j)] for j in range(4)], 1).astype(full)
    input_grad = resid_grad + norm_back(tokens_float, inverse_one, gain_one, normed_one_grad)
    gain_one_grad = jnp.sum(normed_one_grad * tokens_float * inverse_one, axis=0)
    gain_grads = jnp.concatenate(
        [gain_one_grad.reshape(device_count, -1), gain_two_grad.reshape(device_count, -1)], axis=1
    )
    gain_grads = lax.all_to_all(
        gain_grads, ("head", "seq"), split_axis=0, concat_axis=0, tiled=True
    )
    gain_grads = jnp.sum(gain_grads, axis=0)

    gateup_new = update(
        gateup_stack,
        gateup_grad_own,
        gateup_left,
        gateup_right,
        gateup_left_root,
        gateup_right_root,
        0.5 * D ** (-0.5),
    )
    down_new = update(
        down_stack,
        down_grad_own,
        down_left,
        down_right,
        down_left_root,
        down_right_root,
        0.5 * FF ** (-0.5),
    )
    out_new = update(
        out_stack,
        out_grad_own,
        out_left,
        out_right,
        out_left_root,
        out_right_root,
        0.5 * (QW // 64) ** (-0.5),
    )
    qkv_new = update(
        qkv_stack,
        qkv_grad_own,
        qkv_left,
        qkv_right,
        qkv_left_root,
        qkv_right_root,
        0.5 * D ** (-0.5),
    )
    return (
        (block_out, input_grad, gain_grads[:own_gains], gain_grads[own_gains:])
        + tuple(qkv_new)
        + tuple(out_new)
        + tuple(gateup_new)
        + tuple(down_new)
    )


def solution(mesh):
    rows = P(("seq", "head"), None)
    gain = P(("head", "seq"))
    blocks = P(("head", "seq"), None, None)
    return jax.shard_map(
        on_device,
        mesh=mesh,
        in_specs=(rows, rows, gain, gain) + (blocks,) * 20 + (P(), P("seq")),
        out_specs=(rows, rows, gain, gain) + (blocks,) * 12,
        check_vma=False,
    )
```

```python
import functools

import jax
import jax.numpy as jnp
from jax import lax
from jax.experimental import pallas as pl
from jax.experimental.pallas import tpu as pltpu
from jax.sharding import PartitionSpec as P

D = 1536
HEAD_DIM = 128
FF = 4608
WINDOW = 1024
GRID = 16
QW = 1536
QKV = 1792
BLK = 96
BQ = 112
BH = 96
NU = 48

norm_eps = 1e-06
stat_eps = 1e-06
neg_fill = -1e30

QUERY_TILE = 256
SPAN = WINDOW + QUERY_TILE

low = jnp.bfloat16
full = jnp.float32

NT = (((1,), (1,)), ((), ()))
NN = (((1,), (0,)), ((), ()))
TN = (((0,), (0,)), ((), ()))


def mul(a, b, dims, kind=full):
    return lax.dot_general(a, b, dims, preferred_element_type=kind)


def ring_place(index, count):
    return jnp.where(index % 2 == 0, index // 2, count - 1 - index // 2)


def ring_index(place, count):
    return jnp.where(place < count // 2, 2 * place, 2 * (count - 1 - place) + 1)


def ring_routes(count):
    order = [i for i in range(0, count, 2)] + [i for i in range(count - 1, 0, -2)]
    up = [(order[i], order[(i + 1) % count]) for i in range(count)]
    return up, [(b, a) for a, b in up]


def seq_gather(shard):
    count = lax.axis_size("seq")
    rows = shard.shape[0]
    half = rows // 2
    me = lax.axis_index("seq")
    place = ring_place(me, count)
    up, down = ring_routes(count)
    out = jnp.zeros((count,) + shard.shape, shard.dtype)
    out = lax.dynamic_update_slice(out, shard[None], (me, 0, 0))
    ahead = shard
    behind = shard
    for step in range(1, count // 2):
        ahead = lax.ppermute(ahead, "seq", up)
        behind = lax.ppermute(behind, "seq", down)
        out = lax.dynamic_update_slice(
            out, ahead[None], (ring_index((place - step + count) % count, count), 0, 0)
        )
        out = lax.dynamic_update_slice(
            out, behind[None], (ring_index((place + step) % count, count), 0, 0)
        )
    ahead = lax.ppermute(ahead[:half], "seq", up)
    behind = lax.ppermute(behind[half:], "seq", down)
    far = ring_index((place + count // 2) % count, count)
    out = lax.dynamic_update_slice(out, ahead[None], (far, 0, 0))
    return lax.dynamic_update_slice(out, behind[None], (far, half, 0))


def seq_sum(parts):
    count, rows = parts.shape[:2]
    half = rows // 2
    place = ring_place(lax.axis_index("seq"), count)
    up, down = ring_routes(count)

    def part(offset):
        index = ring_index((place + offset + count) % count, count)
        return lax.dynamic_slice_in_dim(parts, index, 1, 0)[0]

    far = part(count // 2)
    ahead = lax.ppermute(far[:half], "seq", up)
    behind = lax.ppermute(far[half:], "seq", down)
    for offset in range(count // 2 - 1, 0, -1):
        local = part(offset)
        if ahead.shape[0] == rows:
            local = (local.astype(full) + ahead.astype(full)).astype(low)
        else:
            local = jnp.concatenate(
                [(local[:half].astype(full) + ahead.astype(full)).astype(low), local[half:]]
            )
        ahead = lax.ppermute(local, "seq", up)
        local = part(-offset)
        if behind.shape[0] == rows:
            local = (local.astype(full) + behind.astype(full)).astype(low)
        else:
            local = jnp.concatenate(
                [local[:half], (local[half:].astype(full) + behind.astype(full)).astype(low)]
            )
        behind = lax.ppermute(local, "seq", down)
    return part(0).astype(full) + ahead.astype(full) + behind.astype(full)


def gather_rows(stack, unit, layout):
    short = stack.astype(low)
    if stack.shape[0] % unit == 0:
        shard = layout(short)
        rows = shard.reshape(-1, shard.shape[-1])
        out = seq_gather(rows)
        return out.reshape((-1,) + shard.shape[1:])
    return layout(lax.all_gather(short, "seq", axis=0, tiled=True))


def sum_rows(rows, local, unit, back):
    count = lax.axis_size("seq")
    if local % unit == 0:
        own = seq_sum(rows.reshape(count, -1, rows.shape[-1]))
        return back(own.reshape((-1,) + rows.shape[1:]))
    return lax.psum_scatter(back(rows), "seq", scatter_dimension=0, tiled=True).astype(full)


def to_columns(stack):
    n, i, j = stack.shape
    return stack.reshape(n // 8, 8, i, j).transpose(0, 2, 1, 3).reshape(n // 8, i, 8 * j)


def from_columns(rows):
    n, i, j = rows.shape
    return rows.reshape(n, i, 8, j // 8).transpose(0, 2, 1, 3).reshape(n * 8, i, j // 8)


def to_units(stack):
    n, i, j = stack.shape
    return stack.reshape(n // 16, 16, i, j).transpose(0, 3, 1, 2).reshape(n // 16, j, 16 * i)


def from_units(rows):
    n, j, i = rows.shape
    return rows.reshape(n, j, 16, i // 16).transpose(0, 2, 3, 1).reshape(n * 16, i // 16, j)


def joined_halves(rows):
    n, i, j = rows.shape
    return rows.reshape(n // 2, 2, i, j).transpose(0, 2, 1, 3).reshape(n // 2 * i, 2 * j)


def split_halves(matrix, i):
    rows, columns = matrix.shape
    m = rows // i
    return (
        matrix.reshape(m, i, 2, columns // 2).transpose(0, 2, 1, 3).reshape(2 * m, i, columns // 2)
    )


def to_partner(value, which):
    count = lax.axis_size("head")
    return lax.ppermute(value, "head", [(i, i ^ which) for i in range(count)])


def head_gather(value):
    across = to_partner(value, 2)
    mate = to_partner(value, 1)
    return value, mate, across, to_partner(across, 1)


def head_exchange(parts):
    return (parts[0],) + tuple(to_partner(parts[j], j) for j in (2, 1, 3))


def head_sum(parts):
    across = (parts[2].astype(full) + to_partner(parts[3], 1).astype(full)).astype(low)
    across = to_partner(across, 2)
    mine = parts[0].astype(full) + to_partner(parts[1], 1).astype(full)
    return mine + across.astype(full)


def in_order(parts, axis):
    me = lax.axis_index("head")
    odd = me % 2 == 1
    lower = [jnp.where(odd, parts[1], parts[0]), jnp.where(odd, parts[0], parts[1])]
    upper = [jnp.where(odd, parts[3], parts[2]), jnp.where(odd, parts[2], parts[3])]
    second = me >= 2
    return jnp.concatenate(
        [jnp.where(second, b, a) for a, b in zip(lower, upper)]
        + [jnp.where(second, a, b) for a, b in zip(lower, upper)],
        axis=axis,
    )


def tile_bias(tile, key_ids, query_ids, bias_ref):
    start = pl.multiple_of(tile * QUERY_TILE, QUERY_TILE)
    shape = (SPAN, QUERY_TILE)
    key = lax.broadcasted_iota(jnp.int32, shape, 0)
    query = lax.broadcasted_iota(jnp.int32, shape, 1)
    same = key_ids[pl.ds(start, SPAN), :] == query_ids[...]
    allowed = same & (key > query) & (key <= query + WINDOW)
    bias_ref[...] = jnp.where(allowed, 0.0, neg_fill)


def attend_kernel(q_ref, kv_ref, kvt_ref, key_ids, query_ids, out_ref, lse_ref, bias_ref):
    tile = pl.program_id(0)
    start = pl.multiple_of(tile * QUERY_TILE, QUERY_TILE)

    @pl.when(pl.program_id(1) == 0)
    def _():
        tile_bias(tile, key_ids, query_ids, bias_ref)

    keys = kv_ref[pl.ds(start, SPAN), :HEAD_DIM]
    scores = mul(keys, q_ref[...], NT) * HEAD_DIM ** (-0.5) + bias_ref[...]
    top = jnp.max(scores, axis=0, keepdims=True)
    expo = jnp.exp(scores - top)
    total = jnp.sum(expo, axis=0, keepdims=True)
    values = kvt_ref[HEAD_DIM:, pl.ds(start, SPAN)]
    mixed = mul(values, expo.astype(low), NN) / total
    out_ref[...] = mixed.T.astype(low)
    lse_ref[0] = top + jnp.log(total)


def attend_back_kernel(
    q_ref, g_ref, kv_ref, kvt_ref, key_ids, query_ids, lse_ref, dq_ref, dkv_ref, bias_ref
):
    tile = pl.program_id(0)
    start = pl.multiple_of(tile * QUERY_TILE, QUERY_TILE)
    scale = HEAD_DIM ** (-0.5)

    @pl.when((tile == 0) & (pl.program_id(1) == 0))
    def _():
        dkv_ref[...] = jnp.zeros_like(dkv_ref)

    @pl.when(pl.program_id(1) == 0)
    def _():
        tile_bias(tile, key_ids, query_ids, bias_ref)

    here = pl.ds(start, SPAN)
    queries = q_ref[...]
    grads = g_ref[...]
    scores = mul(kv_ref[here, :HEAD_DIM], queries, NT) * scale + bias_ref[...]
    probs = jnp.exp(scores - lse_ref[0])
    prob_grad = mul(kv_ref[here, HEAD_DIM:], grads, NT)
    delta = jnp.sum(probs * prob_grad, axis=0, keepdims=True)
    score_grad = (probs * (prob_grad - delta)).astype(low)
    dq = mul(kvt_ref[:HEAD_DIM, here], score_grad, NN) * scale
    dq_ref[...] = dq.T.astype(low)
    dkv_ref[here, :HEAD_DIM] += mul(score_grad, queries, NN) * scale
    dkv_ref[here, HEAD_DIM:] += mul(probs.astype(low), grads, NN)


def attention_specs(group):
    whole = lambda *shape: pl.BlockSpec(shape, lambda t, h: (0,) * len(shape))
    head_rows = pl.BlockSpec((QUERY_TILE, HEAD_DIM), lambda t, h: (t, h))
    keys = whole(2 * group, 2 * HEAD_DIM)
    keys_turned = whole(2 * HEAD_DIM, 2 * group)
    key_ids = whole(2 * group, 1)
    query_ids = pl.BlockSpec((1, QUERY_TILE), lambda t, h: (0, t))
    lse = pl.BlockSpec((1, 1, QUERY_TILE), lambda t, h: (h, 0, t))
    return head_rows, keys, keys_turned, key_ids, query_ids, lse


attention_params = pltpu.CompilerParams(
    dimension_semantics=("arbitrary", "arbitrary"), vmem_limit_bytes=40 * 1024 * 1024
)


def attend(queries, kv, kv_turned, key_ids, query_ids):
    group, width = queries.shape
    heads = width // HEAD_DIM
    rows, keys, turned, kids, qids, lse = attention_specs(group)
    work = heads * (group // QUERY_TILE) * SPAN * QUERY_TILE
    return pl.pallas_call(
        attend_kernel,
        grid=(group // QUERY_TILE, heads),
        in_specs=[rows, keys, turned, kids, qids],
        out_specs=[rows, lse],
        out_shape=[
            jax.ShapeDtypeStruct((group, width), low),
            jax.ShapeDtypeStruct((heads, 1, group), full),
        ],
        scratch_shapes=[pltpu.VMEM((SPAN, QUERY_TILE), full)],
        compiler_params=attention_params,
        cost_estimate=pl.CostEstimate(
            flops=8 * work * HEAD_DIM, bytes_accessed=6 << 20, transcendentals=work
        ),
        name="attend",
    )(queries, kv, kv_turned, key_ids, query_ids)


def attend_back(queries, grads, kv, kv_turned, key_ids, query_ids, lse_rows):
    group, width = queries.shape
    heads = width // HEAD_DIM
    rows, keys, turned, kids, qids, lse = attention_specs(group)
    work = heads * (group // QUERY_TILE) * SPAN * QUERY_TILE
    return pl.pallas_call(
        attend_back_kernel,
        grid=(group // QUERY_TILE, heads),
        in_specs=[rows, rows, keys, turned, kids, qids, lse],
        out_specs=[rows, keys],
        out_shape=[
            jax.ShapeDtypeStruct((group, width), low),
            jax.ShapeDtypeStruct((2 * group, 2 * HEAD_DIM), full),
        ],
        scratch_shapes=[pltpu.VMEM((SPAN, QUERY_TILE), full)],
        compiler_params=attention_params,
        cost_estimate=pl.CostEstimate(
            flops=20 * work * HEAD_DIM, bytes_accessed=8 << 20, transcendentals=work
        ),
        name="attend_back",
    )(queries, grads, kv, kv_turned, key_ids, query_ids, lse_rows)


def remote(source, target, send, recv, where):
    return pltpu.make_async_remote_copy(
        src_ref=source,
        dst_ref=target,
        send_sem=send,
        recv_sem=recv,
        device_id=where,
        device_id_type=pl.DeviceIdType.MESH,
    )


class Ring:
    def __init__(self, count, view, send, recv):
        me = lax.axis_index("seq")
        odd = lax.rem(me, 2)
        self.count = count
        self.view = view
        self.send = send
        self.recv = recv
        self.place = (1 - odd) * (me // 2) + odd * (count - 1 - me // 2)
        self.ahead = {"seq": self.shard(1)}
        self.behind = {"seq": self.shard(-1)}
        self.copies = []

    def shard(self, offset):
        place = lax.rem(self.place + offset + self.count, self.count)
        upper = place // (self.count // 2)
        return (1 - upper) * 2 * place + upper * (2 * (self.count - 1 - place) + 1)

    def pair(self, offset, step):
        last = step == self.count // 2
        views = [
            self.view(self.shard(-offset), 0 if last else None),
            self.view(self.shard(offset), 1 if last else None),
        ]
        return [
            remote(view, view, self.send.at[i, step - 1], self.recv.at[i, step - 1], where)
            for i, (view, where) in enumerate(zip(views, (self.ahead, self.behind)))
        ]

    def start(self, step):
        for copy in self.pair(step - 1, step):
            copy.start()
            self.copies.append(copy)

    def arrive(self, step):
        for copy in self.pair(step, step):
            copy.wait_recv()

    def finish(self):
        for copy in self.copies:
            copy.wait_send()


def forward_kernel(
    count,
    tokens,
    cotangent,
    gains,
    qkv_shard,
    out_shard,
    gateup_shard,
    down_shard,
    order,
    key_ids,
    query_ids,
    resid,
    normed_group,
    grad_group,
    gateup,
    down,
    features,
    qkv_rows,
    out_rows,
    stream,
    kv_both,
    kv_turned,
    lse,
    mixed_group,
    shuffle,
    tokens_group,
    normed,
    weights,
    projected,
    mixed,
    bias,
    part_out,
    part_in,
    own_sem,
    ring_send,
    ring_recv,
    head_send,
    head_recv,
    kv_send,
    kv_recv,
):
    rows = tokens.shape[0]
    group = 4 * rows
    width = features.shape[1]
    heads = width // HEAD_DIM
    head = lax.axis_index("head")
    me = lax.axis_index("seq")
    mate = {"head": head + 1 - 2 * lax.rem(head, 2)}
    across = {"head": lax.rem(head + 2, 4)}
    band = pl.multiple_of(head * width, 128)

    def quarter(ref, i):
        return ref.at[pl.ds(i * rows, rows)]

    copies = []

    def send(index, source, target, where):
        copy = remote(source, target, head_send.at[index], head_recv.at[index], where)
        copy.start()
        copies.append(copy)

    def arrived(index, target, where):
        remote(target, target, head_send.at[index], head_recv.at[index], where).wait_recv()

    def qkv_view(shard, part):
        first = pl.multiple_of(band + (shard // 2) * BLK, 32)
        columns = pl.ds(pl.multiple_of(lax.rem(shard, 2) * (QKV // 2), 128), QKV // 2)
        if part is None:
            return weights.at[pl.ds(first, BLK), columns]
        return weights.at[pl.ds(pl.multiple_of(first + part * (BLK // 2), 16), BLK // 2), columns]

    def out_view(shard, part):
        first = pl.multiple_of((shard // 2) * BLK, 32)
        columns = pl.ds(pl.multiple_of(lax.rem(shard, 2) * (D // 2), 128), D // 2)
        if part is None:
            return out_rows.at[pl.ds(first, BLK), columns]
        return out_rows.at[pl.ds(pl.multiple_of(first + part * (BLK // 2), 16), BLK // 2), columns]

    def gateup_view(shard, part):
        size = gateup.shape[1]
        if part is None:
            return gateup.at[shard]
        return gateup.at[shard, pl.ds(part * (size // 2), size // 2)]

    def down_view(shard, part):
        if part is None:
            return down.at[shard]
        return down.at[shard, :, pl.ds(part * (BLK // 2), BLK // 2)]

    rings = [
        Ring(count, view, ring_send.at[i], ring_recv.at[i])
        for i, view in enumerate((qkv_view, out_view, gateup_view, down_view))
    ]
    qkv_ring, out_ring, gateup_ring, down_ring = rings

    barrier = pltpu.get_barrier_semaphore()
    for where in (qkv_ring.ahead, qkv_ring.behind, mate, across):
        pl.semaphore_signal(barrier, inc=1, device_id=where, device_id_type=pl.DeviceIdType.MESH)

    @pl.when(me > 0)
    def _():
        pl.semaphore_signal(
            barrier, inc=1, device_id={"seq": me - 1}, device_id_type=pl.DeviceIdType.MESH
        )

    pl.semaphore_wait(barrier, 5 - me // (count - 1))

    own = [
        pltpu.make_async_copy(gateup_shard, gateup.at[me], own_sem.at[0]),
        pltpu.make_async_copy(down_shard, down.at[me], own_sem.at[1]),
        pltpu.make_async_copy(cotangent, quarter(grad_group, 0), own_sem.at[2]),
        pltpu.make_async_copy(qkv_shard, qkv_view(me, None), own_sem.at[3]),
        pltpu.make_async_copy(out_shard, out_view(me, None), own_sem.at[4]),
    ]
    for copy in own:
        copy.start()
    own[3].wait()
    qkv_ring.start(1)
    own[0].wait()
    own[1].wait()
    gateup_ring.start(1)
    down_ring.start(1)

    def band_view(which, offset):
        shard = qkv_ring.shard(offset)
        first = pl.multiple_of(which * width + (shard // 2) * BLK, 32)
        columns = pl.ds(pl.multiple_of(lax.rem(shard, 2) * (QKV // 2), 128), QKV // 2)
        return weights.at[pl.ds(first, BLK), columns]

    across_head = lax.rem(head + 2, 4)
    offsets = [[0]] + [[-i, i] for i in range(1, count // 2)] + [[count // 2]]

    def pass_across(step):
        for offset in offsets[step]:
            part = band_view(head, offset)
            send(17 + offset % count, part, part, across)

    def pass_on(step):
        for offset in offsets[step]:
            part = band_view(across_head, offset)
            arrived(17 + offset % count, part, across)
            send(17 + count + offset % count, part, part, mate)

    pass_across(0)
    send(0, tokens, quarter(tokens_group, 2), across)
    send(1, tokens, quarter(tokens_group, 1), mate)

    def norm_rows(source, i):
        values = source[...].astype(full)
        normed[pl.ds(i * rows, rows), :] = (
            values * inverse_norm(values) * gains[0:1, :]
        ).astype(low)

    norm_rows(tokens, 0)
    qkv_ring.arrive(1)
    qkv_ring.start(2)
    pass_across(1)
    at = order[...]
    owner = at // rows
    flip = head - 2 * (owner // 2) * (head // 2) * 2 - 2 * lax.rem(owner, 2) * lax.rem(head, 2)
    place = (owner + flip) * rows + lax.rem(at, rows)
    for i in range(4):
        shuffle[pl.ds(i * rows, rows), :] = jnp.where(
            place[i * rows : (i + 1) * rows]
            == lax.broadcasted_iota(jnp.int32, (rows, group), 1),
            1.0,
            0.0,
        ).astype(low)
    arrived(1, quarter(tokens_group, 1), mate)
    norm_rows(quarter(tokens_group, 1), 1)
    for step in range(2, count // 2):
        qkv_ring.arrive(step)
        qkv_ring.start(step + 1)
        pass_across(step)
        pass_on(step - 2)
    arrived(0, quarter(tokens_group, 2), across)
    send(2, quarter(tokens_group, 2), quarter(tokens_group, 3), mate)
    norm_rows(quarter(tokens_group, 2), 2)
    qkv_ring.arrive(count // 2)
    pass_across(count // 2)
    part = weights.at[pl.ds(band, width)]
    send(5, part, part, mate)
    own[4].wait()
    out_ring.start(1)
    own[2].wait()
    send(8, quarter(grad_group, 0), quarter(grad_group, 2), across)
    send(9, quarter(grad_group, 0), quarter(grad_group, 1), mate)
    pass_on(count // 2 - 2)
    arrived(2, quarter(tokens_group, 3), mate)
    norm_rows(quarter(tokens_group, 3), 3)
    features[...] = normed[:, pl.ds(band, width)]
    qkv_rows[...] = weights[pl.ds(band, width), :]
    pass_on(count // 2 - 1)
    gateup_ring.arrive(1)
    gateup_ring.start(2)
    down_ring.arrive(1)
    down_ring.start(2)
    out_ring.arrive(1)
    out_ring.start(2)
    pass_on(count // 2)
    mate_head = head + 1 - 2 * lax.rem(head, 2)
    mate_band = pl.multiple_of(mate_head * width, 128)
    arrived(5, weights.at[pl.ds(mate_band, width)], mate)
    for offset in range(count):
        arrived(17 + count + offset, band_view(3 - head, offset), mate)

    key_values = pl.ds(width, 2 * HEAD_DIM)

    def project(columns, target):
        def step(i, carry):
            here = pl.ds(pl.multiple_of(i * rows, rows), rows)
            projected[here, target] = mul(normed[here, :], weights[:, columns], NN).astype(low)
            return carry

        lax.fori_loop(0, 4, step, 0)

        def turn(i, carry):
            here = pl.ds(pl.multiple_of(i * rows, rows), rows)
            stream[here, target] = mul(shuffle[here, :], projected[:, target], NN).astype(low)
            return carry

        lax.fori_loop(0, 4, turn, 0)

    project(pl.ds(QW, 2 * HEAD_DIM), key_values)
    kv_both[pl.ds(group, group), :] = stream[:, key_values]
    kv_copy = remote(
        kv_both.at[pl.ds(group, group)],
        kv_both.at[pl.ds(0, group)],
        kv_send,
        kv_recv,
        {"seq": lax.rem(me + 1, count)},
    )

    @pl.when(me < count - 1)
    def _():
        kv_copy.start()

    @pl.when(me == 0)
    def _():
        kv_both[pl.ds(0, group), :] = jnp.zeros((group, 2 * HEAD_DIM), low)

    out_ring.arrive(2)
    out_ring.start(3)
    project(pl.ds(band, width), pl.ds(0, width))
    for i in range(4, 8):
        kv_turned[:, i * rows : (i + 1) * rows] = kv_both[i * rows : (i + 1) * rows, :].T

    @pl.when(me > 0)
    def _():
        kv_copy.wait_recv()

    for i in range(4):
        kv_turned[:, i * rows : (i + 1) * rows] = kv_both[i * rows : (i + 1) * rows, :].T
    out_ring.arrive(3)
    out_ring.start(4)

    def attend_tile(tile, carry):
        start = pl.multiple_of(tile * QUERY_TILE, QUERY_TILE)
        here = pl.ds(start, QUERY_TILE)
        span = pl.ds(start, SPAN)
        shape = (SPAN, QUERY_TILE)
        key = lax.broadcasted_iota(jnp.int32, shape, 0)
        query = lax.broadcasted_iota(jnp.int32, shape, 1)
        same = key_ids[span, :] == query_ids[:, here]
        allowed = same & (key > query) & (key <= query + WINDOW)
        bias[...] = jnp.where(allowed, 0.0, neg_fill)

        def attend_head(j, carry):
            lanes = pl.ds(pl.multiple_of(j * HEAD_DIM, HEAD_DIM), HEAD_DIM)
            scores = mul(kv_both[span, :HEAD_DIM], stream[here, lanes], NT)
            scores = scores * HEAD_DIM ** (-0.5) + bias[...]
            top = jnp.max(scores, axis=0, keepdims=True)
            expo = jnp.exp(scores - top)
            total = jnp.sum(expo, axis=0, keepdims=True)
            out = mul(kv_turned[HEAD_DIM:, span], expo.astype(low), NN) / total
            mixed[here, lanes] = out.T.astype(low)
            lse[j, :, here] = top + jnp.log(total)
            return carry

        return lax.fori_loop(0, heads, attend_head, carry)

    lax.fori_loop(0, group // QUERY_TILE, attend_tile, 0)

    gateup_ring.arrive(2)
    gateup_ring.start(3)
    down_ring.arrive(2)
    down_ring.start(3)

    def turn_back(i, carry):
        here = pl.ds(pl.multiple_of(i * rows, rows), rows)
        mixed_group[here, :] = mul(shuffle[:, here], mixed[...], TN).astype(low)
        return carry

    lax.fori_loop(0, 4, turn_back, 0)
    out_ring.arrive(4)

    def projection(i):
        return mul(mixed_group[i * rows : (i + 1) * rows, :], out_rows[...], NN)

    part_out[0] = projection(3).astype(low)
    send(10, part_out.at[0], part_in.at[0], mate)
    part_out[1] = projection(1).astype(low)
    send(11, part_out.at[1], part_in.at[1], mate)
    resid[...] = projection(2)
    arrived(10, part_in.at[0], mate)
    part_out[2] = (resid[...] + part_in[0].astype(full)).astype(low)
    send(12, part_out.at[2], part_in.at[2], across)
    resid[...] = projection(0) + tokens[...].astype(full)
    arrived(11, part_in.at[1], mate)
    resid[...] += part_in[1].astype(full)
    arrived(8, quarter(grad_group, 2), across)
    send(13, quarter(grad_group, 2), quarter(grad_group, 3), mate)
    arrived(12, part_in.at[2], across)
    resid[...] += part_in[2].astype(full)
    values = resid[...]
    normed_group[pl.ds(0, rows), :] = (values * inverse_norm(values) * gains[1:2, :]).astype(low)
    send(14, quarter(normed_group, 0), quarter(normed_group, 2), across)
    send(15, quarter(normed_group, 0), quarter(normed_group, 1), mate)
    gateup_ring.arrive(3)
    gateup_ring.start(4)
    down_ring.arrive(3)
    down_ring.start(4)
    arrived(14, quarter(normed_group, 2), across)
    send(16, quarter(normed_group, 2), quarter(normed_group, 3), mate)
    arrived(9, quarter(grad_group, 1), mate)
    arrived(13, quarter(grad_group, 3), mate)
    arrived(15, quarter(normed_group, 1), mate)
    arrived(16, quarter(normed_group, 3), mate)
    gateup_ring.arrive(4)
    down_ring.arrive(4)
    for ring in rings:
        ring.finish()
    for copy in copies:
        copy.wait_send()

    @pl.when(me < count - 1)
    def _():
        kv_copy.wait_send()


def forward_section(tokens, cotangent, gains, shards, order, key_ids, query_ids, count):
    rows = tokens.shape[0]
    group = 4 * rows
    width = QW // 4
    steps = count // 2
    qkv_shard, out_shard, gateup_shard, down_shard = shards
    vmem = pl.BlockSpec(memory_space=pltpu.VMEM)
    hbm = pl.BlockSpec(memory_space=pl.ANY)
    outs = [
        ((rows, D), full, vmem),
        ((group, D), low, vmem),
        ((group, D), low, hbm),
        ((count,) + gateup_shard.shape, low, hbm),
        ((count,) + down_shard.shape, low, hbm),
        ((group, width), low, vmem),
        ((width, QKV), low, vmem),
        ((width, D), low, vmem),
        ((group, width + 2 * HEAD_DIM), low, vmem),
        ((2 * group, 2 * HEAD_DIM), low, vmem),
        ((2 * HEAD_DIM, 2 * group), low, vmem),
        ((width // HEAD_DIM, 1, group), full, vmem),
        ((group, width), low, vmem),
        ((group, group), low, vmem),
    ]
    dma = pltpu.SemaphoreType.DMA
    return pl.pallas_call(
        functools.partial(forward_kernel, count),
        in_specs=[vmem, hbm, vmem, hbm, hbm, hbm, hbm, vmem, vmem, vmem],
        out_specs=[spec for _, _, spec in outs],
        out_shape=[jax.ShapeDtypeStruct(shape, kind) for shape, kind, _ in outs],
        scratch_shapes=[
            pltpu.VMEM((group, D), low),
            pltpu.VMEM((group, D), low),
            pltpu.VMEM((D, QKV), low),
            pltpu.VMEM((group, width + 2 * HEAD_DIM), low),
            pltpu.VMEM((group, width), low),
            pltpu.VMEM((SPAN, QUERY_TILE), full),
            pltpu.VMEM((3, rows, D), low),
            pltpu.VMEM((3, rows, D), low),
            dma((5,)),
            dma((4, 2, steps)),
            dma((4, 2, steps)),
            dma((17 + 2 * count,)),
            dma((17 + 2 * count,)),
            dma,
            dma,
        ],
        compiler_params=pltpu.CompilerParams(
            collective_id=0, has_side_effects=True, vmem_limit_bytes=58 * 1024 * 1024
        ),
        name="forward_section",
    )(
        tokens,
        cotangent,
        gains,
        qkv_shard,
        out_shard,
        gateup_shard,
        down_shard,
        order,
        key_ids,
        query_ids,
    )


class SumRing:
    def __init__(self, count, view, first, buffers, send, recv):
        self.ring = Ring(count, None, None, None)
        self.steps = count // 2
        self.view = view
        self.first = first
        self.buffers = buffers
        self.rows = buffers.shape[2]
        self.send = send
        self.recv = recv
        self.copies = []

    def where(self, way):
        return self.ring.behind if way else self.ring.ahead

    def half(self, way):
        return self.buffers.at[way, 0, pl.ds(way * (self.rows // 2), self.rows // 2)]

    def copy(self, way, step, source, target):
        return remote(source, target, self.send.at[way, step], self.recv.at[way, step], self.where(way))

    def start(self):
        shard = self.ring.shard(self.steps)
        for way in range(2):
            copy = self.copy(way, 0, self.first(shard, way), self.half(way))
            copy.start()
            self.copies.append(copy)

    def arrived(self, way, step):
        target = self.buffers.at[way, step] if step else self.half(way)
        self.copy(way, step, target, target).wait_recv()

    def step(self, step):
        block = 48
        for way in range(2):
            self.arrived(way, step - 1)
            offset = self.steps - step
            local = self.view(self.ring.shard(-offset if way else offset))
            buffer = self.buffers.at[way, step - 1]

            def add(i, carry):
                here = pl.ds(pl.multiple_of(i * block, 16), block)
                buffer[here, :] = (local[here, :].astype(full) + buffer[here, :].astype(full)).astype(low)
                return carry

            def keep(i, carry):
                here = pl.ds(pl.multiple_of(i * block, 16), block)
                buffer[here, :] = local[here, :]
                return carry

            blocks = self.rows // block
            if step > 1:
                lax.fori_loop(0, blocks, add, 0)
            else:
                lax.fori_loop(way * (blocks // 2), (way + 1) * (blocks // 2), add, 0)
                lax.fori_loop((1 - way) * (blocks // 2), (2 - way) * (blocks // 2), keep, 0)
            copy = self.copy(way, step, buffer, self.buffers.at[way, step])
            copy.start()
            self.copies.append(copy)

    def finish(self, out):
        block = 48
        last = self.steps - 1
        for way in range(2):
            self.arrived(way, last)
        local = self.view(self.ring.shard(0))

        def add(i, carry):
            here = pl.ds(pl.multiple_of(i * block, 16), block)
            out[here, :] = (
                local[here, :].astype(full)
                + self.buffers[0, last, here, :].astype(full)
                + self.buffers[1, last, here, :].astype(full)
            )
            return carry

        lax.fori_loop(0, self.rows // block, add, 0)
        for copy in self.copies:
            copy.wait_send()


class StagedSumRing(SumRing):
    def __init__(self, count, parts, buffers, held, terms, load, send, recv):
        size = parts.shape[1] // 2
        first = lambda shard, part: parts.at[shard, pl.ds(part * size, size)]
        super().__init__(count, None, first, buffers, send, recv)
        self.parts = parts
        self.held = held
        self.terms = terms
        self.load = load
        self.last = [None, None]

    def fetch(self, way, offset):
        shard = self.ring.shard(-offset if way else offset)
        copy = pltpu.make_async_copy(
            self.parts.at[shard], self.terms.at[way], self.load.at[1, way]
        )
        copy.start()
        return copy

    def start(self):
        super().start()
        self.fetched = [self.fetch(way, self.steps - 1) for way in range(2)]

    def take(self, way, step):
        self.arrived(way, step)
        if self.last[way] is not None:
            self.last[way].wait_send()
        source, target = self.buffers.at[way, step], self.held.at[way]
        if step == 0:
            half = pl.ds(way * (self.rows // 2), self.rows // 2)
            source, target = self.half(way), self.held.at[way, half]
        copy = pltpu.make_async_copy(source, target, self.load.at[0, way])
        copy.start()
        return copy

    def step(self, step):
        block = 48
        taken = [self.take(way, step - 1) for way in range(2)]
        for way in range(2):
            taken[way].wait()
            self.fetched[way].wait()
            held, terms = self.held.at[way], self.terms.at[way]

            def add(i, carry):
                here = pl.ds(pl.multiple_of(i * block, 16), block)
                held[here, :] = (terms[here, :].astype(full) + held[here, :].astype(full)).astype(low)
                return carry

            def keep(i, carry):
                here = pl.ds(pl.multiple_of(i * block, 16), block)
                held[here, :] = terms[here, :]
                return carry

            blocks = self.rows // block
            if step > 1:
                lax.fori_loop(0, blocks, add, 0)
            else:
                lax.fori_loop(way * (blocks // 2), (way + 1) * (blocks // 2), add, 0)
                lax.fori_loop((1 - way) * (blocks // 2), (2 - way) * (blocks // 2), keep, 0)
            self.last[way] = self.copy(way, step, held, self.buffers.at[way, step])
            self.last[way].start()
            if step < self.steps - 1 or way == 0:
                self.fetched[way] = self.fetch(way, self.steps - 1 - step)

    def finish(self, out):
        block = 48
        taken = [self.take(way, self.steps - 1) for way in range(2)]
        for copy in taken:
            copy.wait()
        self.fetched[0].wait()

        def add(i, carry):
            here = pl.ds(pl.multiple_of(i * block, 16), block)
            out[here, :] = (
                self.terms[0, here, :].astype(full)
                + self.held[0, here, :].astype(full)
                + self.held[1, here, :].astype(full)
            )
            return carry

        lax.fori_loop(0, self.rows // block, add, 0)
        for copy in self.copies:
            copy.wait_send()


def backward_kernel(
    count,
    tokens,
    cotangent,
    gains,
    resid,
    normed_part,
    ffn_part,
    gateup_parts,
    down_parts,
    features,
    qkv_rows,
    out_rows,
    stream,
    kv_both,
    kv_turned,
    lse,
    mixed_group,
    shuffle,
    key_ids,
    query_ids,
    block_out,
    input_grad,
    gain_grads,
    gateup_grad,
    down_grad,
    qkv_grad,
    out_grad,
    gateup_sums,
    down_sums,
    gateup_held,
    gateup_terms,
    down_held,
    down_terms,
    part_quarter,
    qkv_local,
    out_local,
    qkv_sums,
    out_sums,
    sum_out,
    sum_in,
    proj_group,
    turned_grad,
    grad_stream,
    kv_total,
    kv_out,
    kv_in,
    stream_grad,
    kv_mate,
    all_grad,
    normed_grad,
    bias,
    load_sem,
    part_sem,
    ring_send,
    ring_recv,
    head_send,
    head_recv,
    kv_send,
    kv_recv,
):
    rows = tokens.shape[0]
    group = 4 * rows
    width = features.shape[1]
    heads = width // HEAD_DIM
    scale = HEAD_DIM ** (-0.5)
    query_grad = turned_grad
    feature_grad = grad_stream
    head = lax.axis_index("head")
    me = lax.axis_index("seq")
    mate_head = head + 1 - 2 * lax.rem(head, 2)
    across_head = lax.rem(head + 2, 4)
    mate = {"head": mate_head}
    across = {"head": across_head}
    corner = {"head": 3 - head}

    def lanes(of):
        return pl.ds(pl.multiple_of(of * width, 128), width)

    def quarter(i):
        return pl.ds(i * rows, rows)

    copies = []

    def send(index, source, target, where):
        copy = remote(source, target, head_send.at[index], head_recv.at[index], where)
        copy.start()
        copies.append(copy)

    def arrived(index, target, where):
        remote(target, target, head_send.at[index], head_recv.at[index], where).wait_recv()

    def shard_view(ref, columns):
        def view(shard, part=None):
            first = pl.multiple_of((shard // 2) * BLK, 32)
            at = pl.ds(pl.multiple_of(lax.rem(shard, 2) * columns, 128), columns)
            if part is None:
                return ref.at[pl.ds(first, BLK), at]
            return ref.at[pl.ds(pl.multiple_of(first + part * (BLK // 2), 16), BLK // 2), at]

        return view

    qkv_view = shard_view(qkv_local, QKV // 2)
    out_view = shard_view(out_local, D // 2)
    gateup_ring = StagedSumRing(
        count,
        gateup_parts,
        gateup_sums,
        gateup_held,
        gateup_terms,
        load_sem.at[0],
        ring_send.at[0],
        ring_recv.at[0],
    )
    down_ring = StagedSumRing(
        count,
        down_parts,
        down_sums,
        down_held,
        down_terms,
        load_sem.at[1],
        ring_send.at[1],
        ring_recv.at[1],
    )
    qkv_ring = SumRing(count, qkv_view, qkv_view, qkv_sums, ring_send.at[2], ring_recv.at[2])
    out_ring = SumRing(count, out_view, out_view, out_sums, ring_send.at[3], ring_recv.at[3])

    barrier = pltpu.get_barrier_semaphore()
    for where in (gateup_ring.where(0), gateup_ring.where(1), mate, across, corner):
        pl.semaphore_signal(barrier, inc=1, device_id=where, device_id_type=pl.DeviceIdType.MESH)

    @pl.when(me < count - 1)
    def _():
        pl.semaphore_signal(
            barrier, inc=1, device_id={"seq": me + 1}, device_id_type=pl.DeviceIdType.MESH
        )

    pl.semaphore_wait(barrier, 5 + (me + count - 1) // count)

    def fetch(value, i):
        copy = pltpu.make_async_copy(value.at[quarter(i)], part_quarter, part_sem)
        copy.start()
        copy.wait()
        return part_quarter[...].astype(full)

    def sum_first(base, slot, value):
        send(base, value.at[quarter(3)], sum_in.at[slot], mate)
        send(base + 1, value.at[quarter(1)], sum_in.at[slot + 1], mate)

    def sum_across(base, slot, value):
        own = fetch(value, 2)
        arrived(base, sum_in.at[slot], mate)
        sum_out[slot // 3] = (own + sum_in[slot].astype(full)).astype(low)
        send(base + 2, sum_out.at[slot // 3], sum_in.at[slot + 2], across)

    def sum_last(base, slot, value):
        own = fetch(value, 0)
        arrived(base + 1, sum_in.at[slot + 1], mate)
        own = own + sum_in[slot + 1].astype(full)
        arrived(base + 2, sum_in.at[slot + 2], across)
        return own + sum_in[slot + 2].astype(full)

    sum_first(0, 0, normed_part)
    gateup_ring.start()
    down_ring.start()
    sum_across(0, 0, normed_part)
    sum_first(3, 3, ffn_part)

    normed_two_grad = sum_last(0, 0, normed_part)
    values = resid[...]
    inverse = inverse_norm(values)
    gain_grads[1:2, :] = jnp.sum(normed_two_grad * values * inverse, axis=0, keepdims=True)
    input_grad[...] = cotangent[...].astype(full) + norm_back(
        values, inverse, gains[1:2, :], normed_two_grad
    )
    proj_group[quarter(0), :] = input_grad[...].astype(low)
    send(6, proj_group.at[quarter(0)], proj_group.at[quarter(2)], across)
    send(7, proj_group.at[quarter(0)], proj_group.at[quarter(1)], mate)
    gateup_ring.step(1)
    down_ring.step(1)
    sum_across(3, 3, ffn_part)

    def back_projection(i):
        turned_grad[quarter(i), :] = mul(proj_group[quarter(i), :], out_rows[...], NT).astype(low)

    back_projection(0)
    arrived(7, proj_group.at[quarter(1)], mate)
    back_projection(1)
    arrived(6, proj_group.at[quarter(2)], across)
    send(8, proj_group.at[quarter(2)], proj_group.at[quarter(3)], mate)
    back_projection(2)
    arrived(8, proj_group.at[quarter(3)], mate)
    back_projection(3)

    def turn(i, carry):
        here = pl.ds(pl.multiple_of(i * rows, rows), rows)
        grad_stream[here, :] = mul(shuffle[here, :], turned_grad[...], NN).astype(low)
        return carry

    lax.fori_loop(0, 4, turn, 0)
    for i in range(3):
        at = slice(i * (D // 3), (i + 1) * (D // 3))
        out_local[:, at] = mul(mixed_group[...], proj_group[:, at], TN).astype(low)
    out_ring.start()
    gateup_ring.step(2)
    down_ring.step(2)

    kv_total[...] = jnp.zeros_like(kv_total)

    def back_tile(tile, carry):
        start = pl.multiple_of(tile * QUERY_TILE, QUERY_TILE)
        here = pl.ds(start, QUERY_TILE)
        span = pl.ds(start, SPAN)
        shape = (SPAN, QUERY_TILE)
        key = lax.broadcasted_iota(jnp.int32, shape, 0)
        query = lax.broadcasted_iota(jnp.int32, shape, 1)
        same = key_ids[span, :] == query_ids[:, here]
        allowed = same & (key > query) & (key <= query + WINDOW)
        bias[...] = jnp.where(allowed, 0.0, neg_fill)

        def back_head(j, carry):
            at = pl.ds(pl.multiple_of(j * HEAD_DIM, HEAD_DIM), HEAD_DIM)
            queries = stream[here, at]
            grads = grad_stream[here, at]
            scores = mul(kv_both[span, :HEAD_DIM], queries, NT) * scale + bias[...]
            probs = jnp.exp(scores - lse[j, :, here])
            prob_grad = mul(kv_both[span, HEAD_DIM:], grads, NT)
            delta = jnp.sum(probs * prob_grad, axis=0, keepdims=True)
            score_grad = (probs * (prob_grad - delta)).astype(low)
            turned = mul(kv_turned[:HEAD_DIM, span], score_grad, NN) * scale
            query_grad[here, at] = turned.T.astype(low)
            kv_total[span, :HEAD_DIM] += mul(score_grad, queries, NN) * scale
            kv_total[span, HEAD_DIM:] += mul(probs.astype(low), grads, NN)
            return carry

        return lax.fori_loop(0, heads, back_head, carry)

    lax.fori_loop(0, group // QUERY_TILE, back_tile, 0)
    kv_out[...] = kv_total[:group, :].astype(low)
    kv_copy = remote(kv_out, kv_in, kv_send, kv_recv, {"seq": lax.rem(me + count - 1, count)})

    @pl.when(me > 0)
    def _():
        kv_copy.start()

    def turn_back(i, carry):
        here = pl.ds(pl.multiple_of(i * rows, rows), rows)
        all_grad[here, lanes(head)] = mul(shuffle[:, here], query_grad[...], TN).astype(low)
        return carry

    lax.fori_loop(0, 4, turn_back, 0)

    def swapped(index, ref, columns, distance, where):
        for i in range(4):
            send(
                index + i,
                ref.at[quarter(i), columns],
                ref.at[quarter(i ^ distance), columns],
                where,
            )

    def swapped_arrived(index, ref, columns, distance, where):
        for i in range(4):
            arrived(index + i, ref.at[quarter(i ^ distance), columns], where)

    swapped(9, all_grad, lanes(head), 2, across)
    swapped(13, all_grad, lanes(head), 1, mate)
    gateup_ring.step(3)
    down_ring.step(3)
    out_ring.step(1)

    @pl.when(me < count - 1)
    def _():
        kv_copy.wait_recv()
        kv_total[pl.ds(group, group), :] += kv_in[...].astype(full)

    stream_grad[...] = kv_total[pl.ds(group, group), :].astype(low)

    def turn_keys(i, carry):
        here = pl.ds(pl.multiple_of(i * rows, rows), rows)
        kv_mate[0, here, :] = mul(shuffle[:, here], stream_grad[...], TN).astype(low)
        return carry

    lax.fori_loop(0, 4, turn_keys, 0)
    for i in range(4):
        send(17 + i, kv_mate.at[0, quarter(i)], kv_mate.at[1, quarter(i ^ 1)], mate)
    for i in range(4):
        arrived(17 + i, kv_mate.at[1, quarter(i ^ 1)], mate)
    kv_total[pl.ds(0, group), :] = kv_mate[0].astype(full) + kv_mate[1].astype(full)
    kv_mate[2] = kv_total[pl.ds(0, group), :].astype(low)
    for i in range(4):
        send(21 + i, kv_mate.at[2, quarter(i)], kv_mate.at[3, quarter(i ^ 2)], across)
    swapped_arrived(9, all_grad, lanes(across_head), 2, across)
    swapped(25, all_grad, lanes(across_head), 1, mate)
    out_ring.step(2)
    swapped_arrived(13, all_grad, lanes(mate_head), 1, mate)
    for i in range(4):
        arrived(21 + i, kv_mate.at[3, quarter(i ^ 2)], across)
    all_grad[:, QW:] = (kv_total[pl.ds(0, group), :] + kv_mate[3].astype(full)).astype(low)
    swapped_arrived(25, all_grad, lanes(3 - head), 1, mate)

    for i in range(2):
        at = slice(i * (QKV // 2), (i + 1) * (QKV // 2))
        qkv_local[:, at] = mul(features[...], all_grad[:, at], TN).astype(low)
    qkv_ring.start()
    out_ring.step(3)
    for i, where in ((2, across), (3, corner), (1, mate)):
        feature_grad[quarter(i), :] = mul(all_grad[quarter(i), :], qkv_rows[...], NT).astype(low)
        send(28 + i, feature_grad.at[quarter(i)], normed_grad.at[:, lanes(head)], where)
    normed_grad[:, lanes(head)] = mul(all_grad[quarter(0), :], qkv_rows[...], NT).astype(low)
    block_out[...] = (resid[...] + sum_last(3, 3, ffn_part)).astype(low)
    gateup_ring.finish(gateup_grad)
    down_ring.finish(down_grad)
    qkv_ring.step(1)
    for i, where, of in ((2, across, across_head), (3, corner, 3 - head), (1, mate, mate_head)):
        arrived(28 + i, normed_grad.at[:, lanes(of)], where)
    qkv_ring.step(2)
    normed_one_grad = normed_grad[...].astype(full)
    values = tokens[...].astype(full)
    inverse = inverse_norm(values)
    gain_grads[0:1, :] = jnp.sum(normed_one_grad * values * inverse, axis=0, keepdims=True)
    input_grad[...] += norm_back(values, inverse, gains[0:1, :], normed_one_grad)
    qkv_ring.step(3)
    out_ring.finish(out_grad)
    qkv_ring.finish(qkv_grad)
    for copy in copies:
        copy.wait_send()

    @pl.when(me > 0)
    def _():
        kv_copy.wait_send()


def backward_section(count, *values):
    (tokens, cotangent, gains, resid, normed_part, ffn_part, gateup_parts, down_parts) = values[:8]
    rows = tokens.shape[0]
    group = 4 * rows
    width = QW // 4
    steps = count // 2
    vmem = pl.BlockSpec(memory_space=pltpu.VMEM)
    hbm = pl.BlockSpec(memory_space=pl.ANY)
    shard = gateup_parts.shape[1:]
    down_shard = down_parts.shape[1:]
    outs = [
        ((rows, D), low),
        ((rows, D), full),
        ((2, D), full),
        (shard, full),
        (down_shard, full),
        ((BLK, QKV // 2), full),
        ((BLK, D // 2), full),
        ((2, steps) + shard, low),
        ((2, steps) + down_shard, low),
    ]
    dma = pltpu.SemaphoreType.DMA
    return pl.pallas_call(
        functools.partial(backward_kernel, count),
        in_specs=[vmem] * 4 + [hbm] * 4 + [vmem] * 11,
        out_specs=[vmem] * 7 + [hbm] * 2,
        out_shape=[jax.ShapeDtypeStruct(shape, kind) for shape, kind in outs],
        scratch_shapes=[
            pltpu.VMEM((2,) + shard, low),
            pltpu.VMEM((2,) + shard, low),
            pltpu.VMEM((2,) + down_shard, low),
            pltpu.VMEM((2,) + down_shard, low),
            pltpu.VMEM((rows, D), low),
            pltpu.VMEM((width, QKV), low),
            pltpu.VMEM((width, D), low),
            pltpu.VMEM((2, steps, BLK, QKV // 2), low),
            pltpu.VMEM((2, steps, BLK, D // 2), low),
            pltpu.VMEM((2, rows, D), low),
            pltpu.VMEM((6, rows, D), low),
            pltpu.VMEM((group, D), low),
            pltpu.VMEM((group, width), low),
            pltpu.VMEM((group, width), low),
            pltpu.VMEM((2 * group, 2 * HEAD_DIM), full),
            pltpu.VMEM((group, 2 * HEAD_DIM), low),
            pltpu.VMEM((group, 2 * HEAD_DIM), low),
            pltpu.VMEM((group, 2 * HEAD_DIM), low),
            pltpu.VMEM((4, group, 2 * HEAD_DIM), low),
            pltpu.VMEM((group, QKV), low),
            pltpu.VMEM((rows, D), low),
            pltpu.VMEM((SPAN, QUERY_TILE), full),
            dma((2, 2, 2)),
            dma,
            dma((4, 2, steps)),
            dma((4, 2, steps)),
            dma((32,)),
            dma((32,)),
            dma,
            dma,
        ],
        compiler_params=pltpu.CompilerParams(
            collective_id=1, has_side_effects=True, vmem_limit_bytes=60 * 1024 * 1024
        ),
        name="backward_section",
    )(*values)


def update_kernel(rate, w_ref, g_ref, l_ref, r_ref, lr_ref, rr_ref, ln_ref, rn_ref, wn_ref):
    count, rows, columns = g_ref.shape

    def block(b, carry):
        grad = g_ref[b]
        square = jnp.sum(jnp.sum(grad * grad, axis=1, keepdims=True), axis=0, keepdims=True)
        square = square * (1.0 / (rows * columns)) + stat_eps
        short = grad.astype(low)
        turned = grad.T.astype(low)
        ln_ref[b] = 0.5 * l_ref[b] + mul(short, turned, NN) * (0.5 / (columns * square))
        rn_ref[b] = 0.5 * r_ref[b] + mul(turned, short, NN) * (0.5 / (rows * square))
        step = mul(lr_ref[b].astype(low), short, NN).astype(low)
        step = mul(step, rr_ref[b].astype(low), NN)
        wn_ref[b] = w_ref[b] - step * (rate * lax.rsqrt(square))
        return carry

    lax.fori_loop(0, count, block, 0, unroll=2 if count % 2 == 0 else 1)


def update(weight, grad, left, right, left_root, right_root, rate):
    count, rows, columns = weight.shape
    batch = next(b for b in (8, 6, 4, 3, 2, 1) if count % b == 0)
    spec = lambda i, j: pl.BlockSpec((batch, i, j), lambda b: (b, 0, 0))
    return pl.pallas_call(
        functools.partial(update_kernel, rate),
        grid=(count // batch,),
        in_specs=[
            spec(rows, columns),
            spec(rows, columns),
            spec(rows, rows),
            spec(columns, columns),
            spec(rows, rows),
            spec(columns, columns),
        ],
        out_specs=[spec(rows, rows), spec(columns, columns), spec(rows, columns)],
        out_shape=[
            jax.ShapeDtypeStruct(left.shape, full),
            jax.ShapeDtypeStruct(right.shape, full),
            jax.ShapeDtypeStruct(weight.shape, full),
        ],
        compiler_params=pltpu.CompilerParams(vmem_limit_bytes=24 * 1024 * 1024),
        cost_estimate=pl.CostEstimate(
            flops=16 * count * 256 * 256 * 128,
            bytes_accessed=36 * count * rows * 128,
            transcendentals=0,
        ),
        name="update",
    )(weight, grad, left, right, left_root, right_root)


def norm_back(values, inverse, gain, grad):
    scaled = gain * grad
    mean = jnp.mean(values * scaled, axis=-1, keepdims=True)
    return inverse * scaled - values * (inverse * inverse * inverse * mean)


def inverse_norm(values):
    return lax.rsqrt(jnp.mean(values * values, axis=-1, keepdims=True) + norm_eps)


def forward_steps(tokens, cotangent, gain_one, gain_two, stacks, token_order, key_ids, query_ids):
    qkv_stack, out_stack, gateup_stack, down_stack = stacks
    row_count = tokens.shape[0]
    head_count = lax.axis_size("head")
    seq_count = lax.axis_size("seq")
    group = row_count * head_count
    head_index = lax.axis_index("head")
    local_width = QW // head_count
    qkv_rows = joined_halves(gather_rows(qkv_stack, 8, to_columns))
    out_rows = joined_halves(gather_rows(out_stack, 8, to_columns))
    gateup = gather_rows(gateup_stack, 16, to_units)
    down = gather_rows(down_stack, 8, to_columns)
    tokens_float = tokens.astype(full)
    normed_one = (tokens_float * inverse_norm(tokens_float) * gain_one).astype(low)
    normed_one_group = jnp.concatenate(head_gather(normed_one))
    feature_start = head_index * local_width
    features = lax.dynamic_slice_in_dim(normed_one_group, feature_start, local_width, 1)
    weights = in_order(head_gather(qkv_rows), 0)
    weights = jnp.concatenate(
        [lax.dynamic_slice_in_dim(weights, feature_start, local_width, 1), weights[:, QW:]], axis=1
    )
    projected = mul(normed_one_group, weights, NN, low)
    buffer_rows = ((token_order // row_count) ^ head_index) * row_count + token_order % row_count
    shuffle = (
        buffer_rows[:, None] == lax.broadcasted_iota(jnp.int32, (group, group), 1)
    ).astype(low)
    stream = mul(shuffle, projected, NN, low)
    kv_stream = stream[:, local_width:]
    kv_before = lax.ppermute(kv_stream, "seq", [(i, i + 1) for i in range(seq_count - 1)])
    kv_both = jnp.concatenate([kv_before, kv_stream], axis=0)
    kv_turned = kv_both.T
    mixed_stream, lse = attend(stream[:, :local_width], kv_both, kv_turned, key_ids, query_ids)
    mixed_group = mul(shuffle, mixed_stream, TN, low)
    part = mul(mixed_group, out_rows, NN, low)
    resid = tokens_float + head_sum([part[i * row_count :][:row_count] for i in range(4)])
    normed_two = (resid * inverse_norm(resid) * gain_two).astype(low)
    normed_group = jnp.concatenate(head_gather(normed_two))
    grad_group = jnp.concatenate(head_gather(cotangent))
    return (
        resid,
        normed_group,
        grad_group,
        gateup,
        down,
        features,
        qkv_rows,
        out_rows,
        stream,
        kv_both,
        kv_turned,
        lse,
        mixed_group,
        shuffle,
    )


def backward_steps(
    tokens,
    cotangent,
    gains,
    resid,
    normed_part,
    ffn_part,
    gateup_wgrad,
    down_wgrad,
    features,
    qkv_rows,
    out_rows,
    stream,
    kv_both,
    kv_turned,
    lse,
    mixed_group,
    shuffle,
    key_ids,
    query_ids,
    counts,
):
    row_count = tokens.shape[0]
    group = row_count * lax.axis_size("head")
    seq_count = lax.axis_size("seq")
    local_width = features.shape[1]
    query_stream = stream[:, :local_width]
    gain_one, gain_two = gains[0], gains[1]
    tokens_float = tokens.astype(full)
    inverse_one = inverse_norm(tokens_float)
    inverse_two = inverse_norm(resid)
    normed_two_grad = head_sum([normed_part[i * row_count :][:row_count] for i in range(4)])
    gateup_grad_own = sum_rows(gateup_wgrad, counts[2], 16, from_units)
    down_grad_own = sum_rows(down_wgrad, counts[3], 8, from_columns)
    ffn_out = head_sum([ffn_part[i * row_count :][:row_count] for i in range(4)])
    block_out = (resid + ffn_out).astype(low)

    resid_grad = cotangent.astype(full) + norm_back(resid, inverse_two, gain_two, normed_two_grad)
    gain_two_grad = jnp.sum(normed_two_grad * resid * inverse_two, axis=0)
    proj_grad = resid_grad.astype(low)
    proj_grad_group = jnp.concatenate(head_gather(proj_grad))
    mixed_grad_group = mul(proj_grad_group, out_rows, NT, low)
    mixed_grad_stream = mul(shuffle, mixed_grad_group, NN, low)
    out_wgrad = split_halves(mul(mixed_group, proj_grad_group, TN, low), BLK)
    out_grad_own = sum_rows(out_wgrad, counts[1], 8, from_columns)

    query_grad, kv_grad = attend_back(
        query_stream, mixed_grad_stream, kv_both, kv_turned, key_ids, query_ids, lse
    )
    kv_later = lax.ppermute(
        kv_grad[:group].astype(low), "seq", [(i, i - 1) for i in range(1, seq_count)]
    )
    kv_grad = (kv_grad[group:] + kv_later.astype(full)).astype(low)
    grad_local = mul(shuffle, jnp.concatenate([query_grad, kv_grad], axis=1), TN, low)
    gathered = head_gather(grad_local)

    def own_order(value, j):
        quarters = [value[i * row_count :][:row_count] for i in range(4)]
        return jnp.concatenate([quarters[i ^ j] for i in range(4)])

    gathered = [own_order(value, j) for j, value in enumerate(gathered)]
    kv_total = sum(value[:, local_width:].astype(full) for value in gathered).astype(low)
    qkv_grad = jnp.concatenate(
        [in_order([value[:, :local_width] for value in gathered], 1), kv_total], axis=1
    )
    qkv_wgrad = split_halves(mul(features, qkv_grad, TN, low), BLK)
    qkv_grad_own = sum_rows(qkv_wgrad, counts[0], 8, from_columns)
    feature_grad = mul(qkv_grad, qkv_rows, NT, low)
    order = (0, 2, 1, 3)
    feature_parts = head_exchange([feature_grad[i * row_count :][:row_count] for i in range(4)])
    normed_one_grad = in_order([feature_parts[order.index(j)] for j in range(4)], 1).astype(full)
    input_grad = resid_grad + norm_back(tokens_float, inverse_one, gain_one, normed_one_grad)
    gain_one_grad = jnp.sum(normed_one_grad * tokens_float * inverse_one, axis=0)
    return (
        block_out,
        input_grad,
        jnp.stack([gain_one_grad, gain_two_grad]),
        gateup_grad_own,
        down_grad_own,
        qkv_grad_own,
        out_grad_own,
    )


def on_device(
    tokens,
    cotangent,
    attn_gain,
    ffn_gain,
    qkv_stack,
    out_stack,
    gateup_stack,
    down_stack,
    qkv_left,
    qkv_right,
    out_left,
    out_right,
    gateup_left,
    gateup_right,
    down_left,
    down_right,
    qkv_left_root,
    qkv_right_root,
    out_left_root,
    out_right_root,
    gateup_left_root,
    gateup_right_root,
    down_left_root,
    down_right_root,
    sequence_ids,
    token_order,
):
    row_count = tokens.shape[0]
    head_count = lax.axis_size("head")
    seq_count = lax.axis_size("seq")
    device_count = head_count * seq_count
    group = row_count * head_count
    seq_index = lax.axis_index("seq")
    local_width = QW // head_count

    gains = jnp.concatenate([attn_gain, ffn_gain]).astype(low).astype(full)[None]
    gains = lax.all_to_all(
        jnp.broadcast_to(gains, (device_count, gains.shape[1])),
        ("head", "seq"),
        split_axis=0,
        concat_axis=0,
        tiled=True,
    )
    own_gains = attn_gain.shape[0]
    gain_one = gains[:, :own_gains].reshape(1, D)
    gain_two = gains[:, own_gains:].reshape(1, D)

    ids_own = lax.dynamic_slice_in_dim(sequence_ids, seq_index * group, group, 0)
    ids_before = lax.dynamic_slice_in_dim(
        sequence_ids, jnp.maximum(seq_index - 1, 0) * group, group, 0
    )
    ids_before = jnp.where(seq_index > 0, ids_before, -1)
    key_ids = jnp.concatenate([ids_before, ids_own])[:, None]
    query_ids = ids_own[None, :]
    stacks = (qkv_stack, out_stack, gateup_stack, down_stack)
    whole_rows = all(s.shape[0] % u == 0 for s, u in zip(stacks, (8, 8, 16, 8)))
    if whole_rows:
        layouts = (to_columns, to_columns, to_units, to_columns)
        shards = [turn(s.astype(low)) for s, turn in zip(stacks, layouts)]
        shards = (shards[0][0], shards[1][0], shards[2].reshape(-1, D), shards[3])
        section = forward_section(
            tokens,
            cotangent,
            jnp.concatenate([gain_one, gain_two]),
            shards,
            token_order[:, None],
            key_ids,
            query_ids,
            seq_count,
        )
    else:
        section = forward_steps(
            tokens, cotangent, gain_one, gain_two, stacks, token_order, key_ids, query_ids
        )
    (
        resid,
        normed_group,
        grad_group,
        gateup,
        down,
        features,
        qkv_rows,
        out_rows,
        stream,
        kv_both,
        kv_turned,
        lse,
        mixed_group,
        shuffle,
    ) = section
    gateup = gateup.reshape(-1, D)
    down = joined_halves(down.reshape(-1, BLK, D // 2))
    unit_count = down.shape[0] // BLK

    gate_up = mul(gateup, normed_group, NT).reshape(unit_count, 2, BLK, group)
    hidden, act_pull = jax.vjp(
        lambda g, u: jax.nn.gelu(g, approximate=True) * u, gate_up[:, 0], gate_up[:, 1]
    )
    hidden = hidden.astype(low).reshape(unit_count * BLK, group)
    hidden_grad = mul(down, grad_group, NT).reshape(unit_count, BLK, group)
    gate_grad, up_grad = act_pull(hidden_grad)
    gate_up_grad = (
        jnp.stack([gate_grad, up_grad], axis=1).astype(low).reshape(2 * unit_count * BLK, group)
    )
    normed_part = mul(gate_up_grad, gateup, TN, low)
    gateup_wgrad = mul(gate_up_grad, normed_group, NN, low).reshape(2 * unit_count, BLK, D)
    down_wgrad = split_halves(mul(hidden, grad_group, NN, low), BLK)
    ffn_part = mul(hidden, down, TN, low)
    gains_both = jnp.concatenate([gain_one, gain_two])
    kept = (features, qkv_rows, out_rows, stream, kv_both, kv_turned, lse, mixed_group, shuffle)
    counts = [s.shape[0] for s in stacks]
    if whole_rows:
        (block_out, input_grad, gain_grads, gateup_own, down_own, qkv_own, out_own, *_) = (
            backward_section(
                seq_count,
                tokens,
                cotangent,
                gains_both,
                resid,
                normed_part,
                ffn_part,
                gateup_wgrad.reshape(seq_count, -1, D),
                down_wgrad.reshape(seq_count, -1, D // 2),
                *kept,
                key_ids,
                query_ids,
            )
        )
        gateup_grad_own = from_units(gateup_own.reshape(-1, BLK, D))
        down_grad_own = from_columns(down_own.reshape(-1, BLK, D // 2))
        qkv_grad_own = from_columns(qkv_own[None])
        out_grad_own = from_columns(out_own[None])
    else:
        section = backward_steps(
            tokens, cotangent, gains_both, resid, normed_part, ffn_part, gateup_wgrad, down_wgrad, *kept,
            key_ids, query_ids, counts,
        )
        (block_out, input_grad, gain_grads, gateup_grad_own, down_grad_own, qkv_grad_own, out_grad_own) = section
    gain_one_grad, gain_two_grad = gain_grads[0], gain_grads[1]
    gain_grads = jnp.concatenate(
        [gain_one_grad.reshape(device_count, -1), gain_two_grad.reshape(device_count, -1)], axis=1
    )
    gain_grads = lax.all_to_all(
        gain_grads, ("head", "seq"), split_axis=0, concat_axis=0, tiled=True
    )
    gain_grads = jnp.sum(gain_grads, axis=0)

    gateup_new = update(
        gateup_stack,
        gateup_grad_own,
        gateup_left,
        gateup_right,
        gateup_left_root,
        gateup_right_root,
        0.5 * D ** (-0.5),
    )
    down_new = update(
        down_stack,
        down_grad_own,
        down_left,
        down_right,
        down_left_root,
        down_right_root,
        0.5 * FF ** (-0.5),
    )
    out_new = update(
        out_stack,
        out_grad_own,
        out_left,
        out_right,
        out_left_root,
        out_right_root,
        0.5 * (QW // 64) ** (-0.5),
    )
    qkv_new = update(
        qkv_stack,
        qkv_grad_own,
        qkv_left,
        qkv_right,
        qkv_left_root,
        qkv_right_root,
        0.5 * D ** (-0.5),
    )
    return (
        (block_out, input_grad, gain_grads[:own_gains], gain_grads[own_gains:])
        + tuple(qkv_new)
        + tuple(out_new)
        + tuple(gateup_new)
        + tuple(down_new)
    )


def solution(mesh):
    rows = P(("seq", "head"), None)
    gain = P(("head", "seq"))
    blocks = P(("head", "seq"), None, None)
    return jax.shard_map(
        on_device,
        mesh=mesh,
        in_specs=(rows, rows, gain, gain) + (blocks,) * 20 + (P(), P("seq")),
        out_specs=(rows, rows, gain, gain) + (blocks,) * 12,
        check_vma=False,
    )
```

```python
import functools

import jax
import jax.numpy as jnp
from jax import lax
from jax.experimental import pallas as pl
from jax.experimental.pallas import tpu as pltpu
from jax.sharding import PartitionSpec as P

D = 1536
HEAD_DIM = 128
FF = 4608
WINDOW = 1024
GRID = 16
QW = 1536
QKV = 1792
BLK = 96
BQ = 112
BH = 96
NU = 48

norm_eps = 1e-06
stat_eps = 1e-06
neg_fill = -1e30

QUERY_TILE = 256
SPAN = WINDOW + QUERY_TILE

low = jnp.bfloat16
full = jnp.float32

NT = (((1,), (1,)), ((), ()))
NN = (((1,), (0,)), ((), ()))
TN = (((0,), (0,)), ((), ()))


def mul(a, b, dims, kind=full):
    return lax.dot_general(a, b, dims, preferred_element_type=kind)


def ring_place(index, count):
    return jnp.where(index % 2 == 0, index // 2, count - 1 - index // 2)


def ring_index(place, count):
    return jnp.where(place < count // 2, 2 * place, 2 * (count - 1 - place) + 1)


def ring_routes(count):
    order = [i for i in range(0, count, 2)] + [i for i in range(count - 1, 0, -2)]
    up = [(order[i], order[(i + 1) % count]) for i in range(count)]
    return up, [(b, a) for a, b in up]


def seq_gather(shard):
    count = lax.axis_size("seq")
    rows = shard.shape[0]
    half = rows // 2
    me = lax.axis_index("seq")
    place = ring_place(me, count)
    up, down = ring_routes(count)
    out = jnp.zeros((count,) + shard.shape, shard.dtype)
    out = lax.dynamic_update_slice(out, shard[None], (me, 0, 0))
    ahead = shard
    behind = shard
    for step in range(1, count // 2):
        ahead = lax.ppermute(ahead, "seq", up)
        behind = lax.ppermute(behind, "seq", down)
        out = lax.dynamic_update_slice(
            out, ahead[None], (ring_index((place - step + count) % count, count), 0, 0)
        )
        out = lax.dynamic_update_slice(
            out, behind[None], (ring_index((place + step) % count, count), 0, 0)
        )
    ahead = lax.ppermute(ahead[:half], "seq", up)
    behind = lax.ppermute(behind[half:], "seq", down)
    far = ring_index((place + count // 2) % count, count)
    out = lax.dynamic_update_slice(out, ahead[None], (far, 0, 0))
    return lax.dynamic_update_slice(out, behind[None], (far, half, 0))


def seq_sum(parts):
    count, rows = parts.shape[:2]
    half = rows // 2
    place = ring_place(lax.axis_index("seq"), count)
    up, down = ring_routes(count)

    def part(offset):
        index = ring_index((place + offset + count) % count, count)
        return lax.dynamic_slice_in_dim(parts, index, 1, 0)[0]

    far = part(count // 2)
    ahead = lax.ppermute(far[:half], "seq", up)
    behind = lax.ppermute(far[half:], "seq", down)
    for offset in range(count // 2 - 1, 0, -1):
        local = part(offset)
        if ahead.shape[0] == rows:
            local = (local.astype(full) + ahead.astype(full)).astype(low)
        else:
            local = jnp.concatenate(
                [(local[:half].astype(full) + ahead.astype(full)).astype(low), local[half:]]
            )
        ahead = lax.ppermute(local, "seq", up)
        local = part(-offset)
        if behind.shape[0] == rows:
            local = (local.astype(full) + behind.astype(full)).astype(low)
        else:
            local = jnp.concatenate(
                [local[:half], (local[half:].astype(full) + behind.astype(full)).astype(low)]
            )
        behind = lax.ppermute(local, "seq", down)
    return part(0).astype(full) + ahead.astype(full) + behind.astype(full)


def gather_rows(stack, unit, layout):
    short = stack.astype(low)
    if stack.shape[0] % unit == 0:
        shard = layout(short)
        rows = shard.reshape(-1, shard.shape[-1])
        out = seq_gather(rows)
        return out.reshape((-1,) + shard.shape[1:])
    return layout(lax.all_gather(short, "seq", axis=0, tiled=True))


def sum_rows(rows, local, unit, back):
    count = lax.axis_size("seq")
    if local % unit == 0:
        own = seq_sum(rows.reshape(count, -1, rows.shape[-1]))
        return back(own.reshape((-1,) + rows.shape[1:]))
    return lax.psum_scatter(back(rows), "seq", scatter_dimension=0, tiled=True).astype(full)


def to_columns(stack):
    n, i, j = stack.shape
    return stack.reshape(n // 8, 8, i, j).transpose(0, 2, 1, 3).reshape(n // 8, i, 8 * j)


def from_columns(rows):
    n, i, j = rows.shape
    return rows.reshape(n, i, 8, j // 8).transpose(0, 2, 1, 3).reshape(n * 8, i, j // 8)


def to_units(stack):
    n, i, j = stack.shape
    return stack.reshape(n // 16, 16, i, j).transpose(0, 3, 1, 2).reshape(n // 16, j, 16 * i)


def from_units(rows):
    n, j, i = rows.shape
    return rows.reshape(n, j, 16, i // 16).transpose(0, 2, 3, 1).reshape(n * 16, i // 16, j)


def joined_halves(rows):
    n, i, j = rows.shape
    return rows.reshape(n // 2, 2, i, j).transpose(0, 2, 1, 3).reshape(n // 2 * i, 2 * j)


def split_halves(matrix, i):
    rows, columns = matrix.shape
    m = rows // i
    return (
        matrix.reshape(m, i, 2, columns // 2).transpose(0, 2, 1, 3).reshape(2 * m, i, columns // 2)
    )


def to_partner(value, which):
    count = lax.axis_size("head")
    return lax.ppermute(value, "head", [(i, i ^ which) for i in range(count)])


def head_gather(value):
    across = to_partner(value, 2)
    mate = to_partner(value, 1)
    return value, mate, across, to_partner(across, 1)


def head_exchange(parts):
    return (parts[0],) + tuple(to_partner(parts[j], j) for j in (2, 1, 3))


def head_sum(parts):
    across = (parts[2].astype(full) + to_partner(parts[3], 1).astype(full)).astype(low)
    across = to_partner(across, 2)
    mine = parts[0].astype(full) + to_partner(parts[1], 1).astype(full)
    return mine + across.astype(full)


def in_order(parts, axis):
    me = lax.axis_index("head")
    odd = me % 2 == 1
    lower = [jnp.where(odd, parts[1], parts[0]), jnp.where(odd, parts[0], parts[1])]
    upper = [jnp.where(odd, parts[3], parts[2]), jnp.where(odd, parts[2], parts[3])]
    second = me >= 2
    return jnp.concatenate(
        [jnp.where(second, b, a) for a, b in zip(lower, upper)]
        + [jnp.where(second, a, b) for a, b in zip(lower, upper)],
        axis=axis,
    )


def tile_bias(tile, key_ids, query_ids, bias_ref):
    start = pl.multiple_of(tile * QUERY_TILE, QUERY_TILE)
    shape = (SPAN, QUERY_TILE)
    key = lax.broadcasted_iota(jnp.int32, shape, 0)
    query = lax.broadcasted_iota(jnp.int32, shape, 1)
    same = key_ids[pl.ds(start, SPAN), :] == query_ids[...]
    allowed = same & (key > query) & (key <= query + WINDOW)
    bias_ref[...] = jnp.where(allowed, 0.0, neg_fill)


def attend_kernel(q_ref, kv_ref, kvt_ref, key_ids, query_ids, out_ref, lse_ref, bias_ref):
    tile = pl.program_id(0)
    start = pl.multiple_of(tile * QUERY_TILE, QUERY_TILE)

    @pl.when(pl.program_id(1) == 0)
    def _():
        tile_bias(tile, key_ids, query_ids, bias_ref)

    keys = kv_ref[pl.ds(start, SPAN), :HEAD_DIM]
    scores = mul(keys, q_ref[...], NT) * HEAD_DIM ** (-0.5) + bias_ref[...]
    top = jnp.max(scores, axis=0, keepdims=True)
    expo = jnp.exp(scores - top)
    total = jnp.sum(expo, axis=0, keepdims=True)
    values = kvt_ref[HEAD_DIM:, pl.ds(start, SPAN)]
    mixed = mul(values, expo.astype(low), NN) / total
    out_ref[...] = mixed.T.astype(low)
    lse_ref[0] = top + jnp.log(total)


def attend_back_kernel(
    q_ref, g_ref, kv_ref, kvt_ref, key_ids, query_ids, lse_ref, dq_ref, dkv_ref, bias_ref
):
    tile = pl.program_id(0)
    start = pl.multiple_of(tile * QUERY_TILE, QUERY_TILE)
    scale = HEAD_DIM ** (-0.5)

    @pl.when((tile == 0) & (pl.program_id(1) == 0))
    def _():
        dkv_ref[...] = jnp.zeros_like(dkv_ref)

    @pl.when(pl.program_id(1) == 0)
    def _():
        tile_bias(tile, key_ids, query_ids, bias_ref)

    here = pl.ds(start, SPAN)
    queries = q_ref[...]
    grads = g_ref[...]
    scores = mul(kv_ref[here, :HEAD_DIM], queries, NT) * scale + bias_ref[...]
    probs = jnp.exp(scores - lse_ref[0])
    prob_grad = mul(kv_ref[here, HEAD_DIM:], grads, NT)
    delta = jnp.sum(probs * prob_grad, axis=0, keepdims=True)
    score_grad = (probs * (prob_grad - delta)).astype(low)
    dq = mul(kvt_ref[:HEAD_DIM, here], score_grad, NN) * scale
    dq_ref[...] = dq.T.astype(low)
    dkv_ref[here, :HEAD_DIM] += mul(score_grad, queries, NN) * scale
    dkv_ref[here, HEAD_DIM:] += mul(probs.astype(low), grads, NN)


def attention_specs(group):
    whole = lambda *shape: pl.BlockSpec(shape, lambda t, h: (0,) * len(shape))
    head_rows = pl.BlockSpec((QUERY_TILE, HEAD_DIM), lambda t, h: (t, h))
    keys = whole(2 * group, 2 * HEAD_DIM)
    keys_turned = whole(2 * HEAD_DIM, 2 * group)
    key_ids = whole(2 * group, 1)
    query_ids = pl.BlockSpec((1, QUERY_TILE), lambda t, h: (0, t))
    lse = pl.BlockSpec((1, 1, QUERY_TILE), lambda t, h: (h, 0, t))
    return head_rows, keys, keys_turned, key_ids, query_ids, lse


attention_params = pltpu.CompilerParams(
    dimension_semantics=("arbitrary", "arbitrary"), vmem_limit_bytes=40 * 1024 * 1024
)


def attend(queries, kv, kv_turned, key_ids, query_ids):
    group, width = queries.shape
    heads = width // HEAD_DIM
    rows, keys, turned, kids, qids, lse = attention_specs(group)
    work = heads * (group // QUERY_TILE) * SPAN * QUERY_TILE
    return pl.pallas_call(
        attend_kernel,
        grid=(group // QUERY_TILE, heads),
        in_specs=[rows, keys, turned, kids, qids],
        out_specs=[rows, lse],
        out_shape=[
            jax.ShapeDtypeStruct((group, width), low),
            jax.ShapeDtypeStruct((heads, 1, group), full),
        ],
        scratch_shapes=[pltpu.VMEM((SPAN, QUERY_TILE), full)],
        compiler_params=attention_params,
        cost_estimate=pl.CostEstimate(
            flops=8 * work * HEAD_DIM, bytes_accessed=6 << 20, transcendentals=work
        ),
        name="attend",
    )(queries, kv, kv_turned, key_ids, query_ids)


def attend_back(queries, grads, kv, kv_turned, key_ids, query_ids, lse_rows):
    group, width = queries.shape
    heads = width // HEAD_DIM
    rows, keys, turned, kids, qids, lse = attention_specs(group)
    work = heads * (group // QUERY_TILE) * SPAN * QUERY_TILE
    return pl.pallas_call(
        attend_back_kernel,
        grid=(group // QUERY_TILE, heads),
        in_specs=[rows, rows, keys, turned, kids, qids, lse],
        out_specs=[rows, keys],
        out_shape=[
            jax.ShapeDtypeStruct((group, width), low),
            jax.ShapeDtypeStruct((2 * group, 2 * HEAD_DIM), full),
        ],
        scratch_shapes=[pltpu.VMEM((SPAN, QUERY_TILE), full)],
        compiler_params=attention_params,
        cost_estimate=pl.CostEstimate(
            flops=20 * work * HEAD_DIM, bytes_accessed=8 << 20, transcendentals=work
        ),
        name="attend_back",
    )(queries, grads, kv, kv_turned, key_ids, query_ids, lse_rows)


def remote(source, target, send, recv, where):
    return pltpu.make_async_remote_copy(
        src_ref=source,
        dst_ref=target,
        send_sem=send,
        recv_sem=recv,
        device_id=where,
        device_id_type=pl.DeviceIdType.MESH,
    )


class Ring:
    def __init__(self, count, view, send, recv, split=True):
        me = lax.axis_index("seq")
        self.split = split
        odd = lax.rem(me, 2)
        self.count = count
        self.view = view
        self.send = send
        self.recv = recv
        self.place = (1 - odd) * (me // 2) + odd * (count - 1 - me // 2)
        self.ahead = {"seq": self.shard(1)}
        self.behind = {"seq": self.shard(-1)}
        self.copies = []

    def shard(self, offset):
        place = lax.rem(self.place + offset + self.count, self.count)
        upper = place // (self.count // 2)
        return (1 - upper) * 2 * place + upper * (2 * (self.count - 1 - place) + 1)

    def pair(self, offset, step):
        last = step == self.count // 2
        halved = last and self.split
        views = [
            self.view(self.shard(-offset), 0 if halved else None),
            self.view(self.shard(offset), 1 if halved else None),
        ]
        if last and not self.split:
            views = views[:1]
        return [
            remote(view, view, self.send.at[i, step - 1], self.recv.at[i, step - 1], where)
            for i, (view, where) in enumerate(zip(views, (self.ahead, self.behind)))
        ]

    def start(self, step):
        for copy in self.pair(step - 1, step):
            copy.start()
            self.copies.append(copy)

    def arrive(self, step):
        for copy in self.pair(step, step):
            copy.wait_recv()

    def finish(self):
        for copy in self.copies:
            copy.wait_send()


def turned_row(row):
    size = row.shape[1]
    return jnp.broadcast_to(row.astype(full), (128, size)).T[:, :1]


def forward_kernel(
    count,
    tokens,
    own_gains,
    qkv_stack,
    out_stack,
    gateup_stack,
    down_stack,
    order,
    ids,
    gains,
    resid,
    normed_group,
    gateup,
    down,
    features,
    qkv_rows,
    out_all,
    stream,
    kv_both,
    kv_turned,
    lse,
    mixed_group,
    shuffle,
    key_ids,
    query_ids,
    tokens_group,
    normed,
    weights,
    projected,
    mixed,
    mixed_all,
    bias,
    wide,
    gateup_own,
    down_own,
    gain_tiles,
    own_sem,
    ring_send,
    ring_recv,
    head_send,
    head_recv,
    kv_send,
    kv_recv,
):
    rows = tokens.shape[0]
    group = 4 * rows
    width = features.shape[1]
    heads = width // HEAD_DIM
    head = lax.axis_index("head")
    me = lax.axis_index("seq")
    mate_head = head + 1 - 2 * lax.rem(head, 2)
    across_head = lax.rem(head + 2, 4)
    mate = {"head": mate_head}
    across = {"head": across_head}

    def band(of):
        return pl.ds(pl.multiple_of(of * width, 128), width)

    def chip_columns(of):
        return pl.ds(pl.multiple_of((of // 2) * 2 * width, 128), 2 * width)

    def quarter(ref, i):
        return ref.at[pl.ds(i * rows, rows)]

    copies = []

    def send(index, source, target, where):
        copy = remote(source, target, head_send.at[index], head_recv.at[index], where)
        copy.start()
        copies.append(copy)

    def arrived(index, target, where):
        remote(target, target, head_send.at[index], head_recv.at[index], where).wait_recv()

    def stack_view(ref, columns):
        def view(shard, part):
            first = pl.multiple_of(head * width + (shard // 2) * BLK, 32)
            at = pl.ds(pl.multiple_of(lax.rem(shard, 2) * columns, 128), columns)
            if part is None:
                return ref.at[pl.ds(first, BLK), at]
            return ref.at[pl.ds(pl.multiple_of(first + part * (BLK // 2), 16), BLK // 2), at]

        return view

    def gateup_view(shard, part):
        size = gateup.shape[1]
        if part is None:
            return gateup.at[shard]
        return gateup.at[shard, pl.ds(part * (size // 2), size // 2)]

    def down_view(shard, part):
        if part is None:
            return down.at[shard]
        return down.at[shard, :, pl.ds(part * (BLK // 2), BLK // 2)]

    qkv_view = stack_view(weights, QKV // 2)
    out_view = stack_view(out_all, D // 2)
    gain_view = lambda shard, part: gain_tiles.at[head, shard]
    qkv_ring, out_ring, gateup_ring, down_ring, gain_ring = rings = [
        Ring(count, view, ring_send.at[i], ring_recv.at[i], view is not gain_view)
        for i, view in enumerate((qkv_view, out_view, gateup_view, down_view, gain_view))
    ]

    barrier = pltpu.get_barrier_semaphore()
    for where in (qkv_ring.ahead, qkv_ring.behind, mate, across):
        pl.semaphore_signal(barrier, inc=1, device_id=where, device_id_type=pl.DeviceIdType.MESH)

    @pl.when(me > 0)
    def _():
        pl.semaphore_signal(
            barrier, inc=1, device_id={"seq": me - 1}, device_id_type=pl.DeviceIdType.MESH
        )

    def side_by_side(stack, first):
        size = stack.shape[2]
        blocks = 8
        for c in range(blocks):
            wide[:, c * size : (c + 1) * size] = stack[first + c]
        return wide[:, : blocks * size].astype(low)

    qkv_view(me, None)[...] = side_by_side(qkv_stack, 0)
    gain_tiles[head, me] = own_gains[...]
    pl.semaphore_wait(barrier, 5 - me // (count - 1))
    send(0, tokens, quarter(tokens_group, 2), across)
    send(1, tokens, quarter(tokens_group, 1), mate)
    qkv_ring.start(1)
    gain_ring.start(1)
    for q in range(gateup_own.shape[0] // BLK):
        for r in range(GRID):
            wide[:, r * BLK : (r + 1) * BLK] = gateup_stack[q * GRID + r].T
        gateup_own[q * BLK : (q + 1) * BLK, :] = wide[:, :D].astype(low)
    for m in range(down_own.shape[0]):
        down_own[m] = side_by_side(down_stack, 8 * m)
    own = [
        pltpu.make_async_copy(gateup_own, gateup.at[me], own_sem.at[0]),
        pltpu.make_async_copy(down_own, down.at[me], own_sem.at[1]),
    ]
    for copy in own:
        copy.start()
    out_view(me, None)[...] = side_by_side(out_stack, 0)
    for copy in own:
        copy.wait()

    def pump(step):
        if step > 1:
            gateup_ring.arrive(step - 1)
            down_ring.arrive(step - 1)
        if step <= count // 2:
            gateup_ring.start(step)
            down_ring.start(step)

    pump(1)
    tokens_group[:rows, :] = tokens[...]
    qkv_ring.arrive(1)
    qkv_ring.start(2)
    gain_ring.arrive(1)
    gain_ring.start(2)

    for i in range(4):
        at = turned_row(order[:, i * rows : (i + 1) * rows]).astype(jnp.int32)
        owner = at // rows
        flip = head - 4 * (owner // 2) * (head // 2) - 2 * lax.rem(owner, 2) * lax.rem(head, 2)
        place = (owner + flip) * rows + lax.rem(at, rows)
        shuffle[i * rows : (i + 1) * rows, :] = jnp.where(
            place == lax.broadcasted_iota(jnp.int32, (rows, group), 1), 1.0, 0.0
        ).astype(low)
    query_ids[...] = ids[:, pl.ds(pl.multiple_of(me * group, 128), group)].astype(full)
    before = (me - (me + count - 1) // count) * group
    for i in range(4):
        here = slice(i * rows, (i + 1) * rows)
        at = pl.multiple_of(before + i * rows, 128)
        key_ids[here, :] = jnp.where(me > 0, turned_row(ids[:, pl.ds(at, rows)]), -1.0)
        there = slice(group + i * rows, group + (i + 1) * rows)
        key_ids[there, :] = turned_row(query_ids[:, here])
    for step in range(2, count // 2):
        qkv_ring.arrive(step)
        qkv_ring.start(step + 1)
        gain_ring.arrive(step)
        gain_ring.start(step + 1)
    qkv_ring.arrive(count // 2)

    key_columns = pl.ds(QW, 2 * HEAD_DIM)

    def weight_parts(of, chip_of):
        return [weights.at[band(of), columns] for columns in (chip_columns(chip_of), key_columns)]

    for i, part in enumerate(weight_parts(head, across_head)):
        send(3 + i, part, part, across)
    for i, part in enumerate(weight_parts(head, head)):
        send(7 + i, part, part, mate)
    gain_ring.arrive(count // 2)
    send(9, gain_tiles.at[head], gain_tiles.at[head], across)
    send(10, gain_tiles.at[head], gain_tiles.at[head], mate)
    out_ring.start(1)
    arrived(0, quarter(tokens_group, 2), across)
    send(2, quarter(tokens_group, 2), quarter(tokens_group, 3), mate)
    qkv_rows[...] = weights[band(head), :]
    arrived(9, gain_tiles.at[across_head], across)
    send(11, gain_tiles.at[across_head], gain_tiles.at[across_head], mate)
    arrived(10, gain_tiles.at[mate_head], mate)
    arrived(11, gain_tiles.at[3 - head], mate)
    size = D // (4 * count)
    for h in range(4):
        for i in range(count):
            at = (h * count + i) * size
            wide[:8, at : at + size] = gain_tiles[h, i][:, :size]
    gains[...] = wide[:2, :D].astype(low).astype(full)

    def norm_rows(i):
        here = pl.ds(i * rows, rows)
        values = tokens_group[here, :].astype(full)
        normed[here, :] = (values * inverse_norm(values) * gains[0:1, :]).astype(low)

    norm_rows(0)
    arrived(1, quarter(tokens_group, 1), mate)
    norm_rows(1)
    out_ring.arrive(1)
    out_ring.start(2)
    norm_rows(2)
    arrived(2, quarter(tokens_group, 3), mate)
    norm_rows(3)
    features[...] = normed[:, band(head)]
    for i, part in enumerate(weight_parts(across_head, head)):
        arrived(3 + i, part, across)
        send(5 + i, part, part, mate)
    out_ring.arrive(2)
    out_ring.start(3)
    for i, part in enumerate(weight_parts(mate_head, head)):
        arrived(7 + i, part, mate)
    for i, part in enumerate(weight_parts(3 - head, head)):
        arrived(5 + i, part, mate)

    key_values = pl.ds(width, 2 * HEAD_DIM)

    def project(columns, target):
        def step(i, carry):
            here = pl.ds(pl.multiple_of(i * rows, rows), rows)
            projected[here, target] = mul(normed[here, :], weights[:, columns], NN).astype(low)
            return carry

        lax.fori_loop(0, 4, step, 0)

        def turn(i, carry):
            here = pl.ds(pl.multiple_of(i * rows, rows), rows)
            stream[here, target] = mul(shuffle[here, :], projected[:, target], NN).astype(low)
            return carry

        lax.fori_loop(0, 4, turn, 0)

    project(key_columns, key_values)
    kv_both[pl.ds(group, group), :] = stream[:, key_values]
    kv_copy = remote(
        kv_both.at[pl.ds(group, group)],
        kv_both.at[pl.ds(0, group)],
        kv_send,
        kv_recv,
        {"seq": lax.rem(me + 1, count)},
    )

    @pl.when(me < count - 1)
    def _():
        kv_copy.start()

    @pl.when(me == 0)
    def _():
        kv_both[pl.ds(0, group), :] = jnp.zeros((group, 2 * HEAD_DIM), low)

    out_ring.arrive(3)
    out_ring.start(4)
    pump(2)
    project(band(head), pl.ds(0, width))
    for i in range(4, 8):
        kv_turned[:, i * rows : (i + 1) * rows] = kv_both[i * rows : (i + 1) * rows, :].T
    out_ring.arrive(4)
    half = width // 2

    def out_part(of, i):
        return out_all.at[pl.ds(pl.multiple_of(of * width + i * half, 64), half)]

    for i in range(2):
        send(12 + i, out_part(head, i), out_part(head, i), across)
    send(16, out_all.at[band(head)], out_all.at[band(head)], mate)

    @pl.when(me > 0)
    def _():
        kv_copy.wait_recv()

    for i in range(4):
        kv_turned[:, i * rows : (i + 1) * rows] = kv_both[i * rows : (i + 1) * rows, :].T

    def attend_tile(tile, carry):
        start = pl.multiple_of(tile * QUERY_TILE, QUERY_TILE)
        here = pl.ds(start, QUERY_TILE)
        span = pl.ds(start, SPAN)
        shape = (SPAN, QUERY_TILE)
        key = lax.broadcasted_iota(jnp.int32, shape, 0)
        query = lax.broadcasted_iota(jnp.int32, shape, 1)
        same = key_ids[span, :] == query_ids[:, here]
        allowed = same & (key > query) & (key <= query + WINDOW)
        bias[...] = jnp.where(allowed, 0.0, neg_fill)

        def attend_head(j, carry):
            lanes = pl.ds(pl.multiple_of(j * HEAD_DIM, HEAD_DIM), HEAD_DIM)
            scores = mul(kv_both[span, :HEAD_DIM], stream[here, lanes], NT)
            scores = scores * HEAD_DIM ** (-0.5) + bias[...]
            top = jnp.max(scores, axis=0, keepdims=True)
            expo = jnp.exp(scores - top)
            total = jnp.sum(expo, axis=0, keepdims=True)
            out = mul(kv_turned[HEAD_DIM:, span], expo.astype(low), NN) / total
            mixed[here, lanes] = out.T.astype(low)
            lse[j, :, here] = top + jnp.log(total)
            return carry

        return lax.fori_loop(0, heads, attend_head, carry)

    lax.fori_loop(0, group // QUERY_TILE, attend_tile, 0)

    def turn_back(i, carry):
        here = pl.ds(pl.multiple_of(i * rows, rows), rows)
        mixed_group[here, :] = mul(shuffle[:, here], mixed[...], TN).astype(low)
        return carry

    lax.fori_loop(0, 4, turn_back, 0)

    def mixed_part(of, i, size):
        return mixed_all.at[pl.ds(i * size, size), band(of)]

    for i in range(2):
        source = mixed_group.at[pl.ds(i * 2 * rows, 2 * rows)]
        send(17 + i, source, mixed_part(head, 1 - i, 2 * rows), across)
    for i in range(4):
        send(19 + i, quarter(mixed_group, i), mixed_part(head, i ^ 1, rows), mate)
    mixed_all[:, band(head)] = mixed_group[...]
    for i in range(2):
        arrived(12 + i, out_part(across_head, i), across)
        send(14 + i, out_part(across_head, i), out_part(across_head, i), mate)
    pump(3)
    arrived(16, out_all.at[band(mate_head)], mate)
    for i in range(2):
        arrived(14 + i, out_part(3 - head, i), mate)
    for i in range(4):
        arrived(19 + i, mixed_part(mate_head, i ^ 1, rows), mate)
    for i in range(2):
        arrived(17 + i, mixed_part(across_head, 1 - i, 2 * rows), across)
        for j in (2 - 2 * i, 3 - 2 * i):
            part = mixed_part(across_head, j, rows)
            send(23 + j, part, mixed_part(across_head, j ^ 1, rows), mate)
    for j in range(4):
        arrived(23 + j, mixed_part(3 - head, j ^ 1, rows), mate)

    def second(i, carry):
        here = pl.ds(pl.multiple_of((3 - i) * rows, rows), rows)
        resid[...] = tokens_group[here, :].astype(full) + mul(mixed_all[here, :], out_all[...], NN)
        values = resid[...]
        normed_group[here, :] = (values * inverse_norm(values) * gains[1:2, :]).astype(low)
        return carry

    lax.fori_loop(0, 4, second, 0)
    pump(4)
    pump(5)
    for ring in rings:
        ring.finish()
    for copy in copies:
        copy.wait_send()

    @pl.when(me < count - 1)
    def _():
        kv_copy.wait_send()


def forward_section(tokens, gains, stacks, order, ids, count):
    rows = tokens.shape[0]
    group = 4 * rows
    width = QW // 4
    steps = count // 2
    gateup_rows = stacks[2].shape[0] // GRID * BLK
    down_parts = stacks[3].shape[0] // 8
    vmem = pl.BlockSpec(memory_space=pltpu.VMEM)
    hbm = pl.BlockSpec(memory_space=pl.ANY)
    outs = [
        ((2, D), full, vmem),
        ((rows, D), full, vmem),
        ((group, D), low, vmem),
        ((count, gateup_rows, D), low, hbm),
        ((count, down_parts, BLK, D // 2), low, hbm),
        ((group, width), low, vmem),
        ((width, QKV), low, vmem),
        ((D, D), low, vmem),
        ((group, width + 2 * HEAD_DIM), low, vmem),
        ((2 * group, 2 * HEAD_DIM), low, vmem),
        ((2 * HEAD_DIM, 2 * group), low, vmem),
        ((width // HEAD_DIM, 1, group), full, vmem),
        ((group, width), low, vmem),
        ((group, group), low, vmem),
        ((2 * group, 1), full, vmem),
        ((1, group), full, vmem),
    ]
    dma = pltpu.SemaphoreType.DMA
    return pl.pallas_call(
        functools.partial(forward_kernel, count),
        in_specs=[vmem] * 8,
        out_specs=[spec for _, _, spec in outs],
        out_shape=[jax.ShapeDtypeStruct(shape, kind) for shape, kind, _ in outs],
        scratch_shapes=[
            pltpu.VMEM((group, D), low),
            pltpu.VMEM((group, D), low),
            pltpu.VMEM((D, QKV), low),
            pltpu.VMEM((group, width + 2 * HEAD_DIM), low),
            pltpu.VMEM((group, width), low),
            pltpu.VMEM((group, D), low),
            pltpu.VMEM((SPAN, QUERY_TILE), full),
            pltpu.VMEM((BLK, D), full),
            pltpu.VMEM((gateup_rows, D), low),
            pltpu.VMEM((down_parts, BLK, D // 2), low),
            pltpu.VMEM((4, count, 8, 128), full),
            dma((2,)),
            dma((5, 2, steps)),
            dma((5, 2, steps)),
            dma((27,)),
            dma((27,)),
            dma,
            dma,
        ],
        compiler_params=pltpu.CompilerParams(
            collective_id=0, has_side_effects=True, vmem_limit_bytes=58 * 1024 * 1024
        ),
        name="forward_section",
    )(tokens, gains, *stacks, order, ids)


class SumRing:
    def __init__(self, count, view, first, buffers, send, recv):
        self.ring = Ring(count, None, None, None)
        self.steps = count // 2
        self.view = view
        self.first = first
        self.buffers = buffers
        self.rows = buffers.shape[2]
        self.send = send
        self.recv = recv
        self.copies = []

    def where(self, way):
        return self.ring.behind if way else self.ring.ahead

    def half(self, way):
        return self.buffers.at[way, 0, pl.ds(way * (self.rows // 2), self.rows // 2)]

    def copy(self, way, step, source, target):
        return remote(source, target, self.send.at[way, step], self.recv.at[way, step], self.where(way))

    def start(self):
        shard = self.ring.shard(self.steps)
        for way in range(2):
            copy = self.copy(way, 0, self.first(shard, way), self.half(way))
            copy.start()
            self.copies.append(copy)

    def arrived(self, way, step):
        target = self.buffers.at[way, step] if step else self.half(way)
        self.copy(way, step, target, target).wait_recv()

    def step(self, step):
        block = 48
        for way in range(2):
            self.arrived(way, step - 1)
            offset = self.steps - step
            local = self.view(self.ring.shard(-offset if way else offset))
            buffer = self.buffers.at[way, step - 1]

            def add(i, carry):
                here = pl.ds(pl.multiple_of(i * block, 16), block)
                buffer[here, :] = (local[here, :].astype(full) + buffer[here, :].astype(full)).astype(low)
                return carry

            def keep(i, carry):
                here = pl.ds(pl.multiple_of(i * block, 16), block)
                buffer[here, :] = local[here, :]
                return carry

            blocks = self.rows // block
            if step > 1:
                lax.fori_loop(0, blocks, add, 0)
            else:
                lax.fori_loop(way * (blocks // 2), (way + 1) * (blocks // 2), add, 0)
                lax.fori_loop((1 - way) * (blocks // 2), (2 - way) * (blocks // 2), keep, 0)
            copy = self.copy(way, step, buffer, self.buffers.at[way, step])
            copy.start()
            self.copies.append(copy)

    def finish(self, out):
        block = 48
        last = self.steps - 1
        for way in range(2):
            self.arrived(way, last)
        local = self.view(self.ring.shard(0))

        def add(i, carry):
            here = pl.ds(pl.multiple_of(i * block, 16), block)
            out[here, :] = (
                local[here, :].astype(full)
                + self.buffers[0, last, here, :].astype(full)
                + self.buffers[1, last, here, :].astype(full)
            )
            return carry

        lax.fori_loop(0, self.rows // block, add, 0)
        for copy in self.copies:
            copy.wait_send()


class StagedSumRing(SumRing):
    def __init__(self, count, parts, buffers, held, terms, load, send, recv):
        size = parts.shape[1] // 2
        first = lambda shard, part: parts.at[shard, pl.ds(part * size, size)]
        super().__init__(count, None, first, buffers, send, recv)
        self.parts = parts
        self.held = held
        self.terms = terms
        self.load = load
        self.last = [None, None]

    def fetch(self, way, offset):
        shard = self.ring.shard(-offset if way else offset)
        copy = pltpu.make_async_copy(
            self.parts.at[shard], self.terms.at[way], self.load.at[1, way]
        )
        copy.start()
        return copy

    def start(self):
        super().start()
        self.fetched = [self.fetch(way, self.steps - 1) for way in range(2)]

    def take(self, way, step):
        self.arrived(way, step)
        if self.last[way] is not None:
            self.last[way].wait_send()
        source, target = self.buffers.at[way, step], self.held.at[way]
        if step == 0:
            half = pl.ds(way * (self.rows // 2), self.rows // 2)
            source, target = self.half(way), self.held.at[way, half]
        copy = pltpu.make_async_copy(source, target, self.load.at[0, way])
        copy.start()
        return copy

    def step(self, step):
        block = 48
        taken = [self.take(way, step - 1) for way in range(2)]
        for way in range(2):
            taken[way].wait()
            self.fetched[way].wait()
            held, terms = self.held.at[way], self.terms.at[way]

            def add(i, carry):
                here = pl.ds(pl.multiple_of(i * block, 16), block)
                held[here, :] = (terms[here, :].astype(full) + held[here, :].astype(full)).astype(low)
                return carry

            def keep(i, carry):
                here = pl.ds(pl.multiple_of(i * block, 16), block)
                held[here, :] = terms[here, :]
                return carry

            blocks = self.rows // block
            if step > 1:
                lax.fori_loop(0, blocks, add, 0)
            else:
                lax.fori_loop(way * (blocks // 2), (way + 1) * (blocks // 2), add, 0)
                lax.fori_loop((1 - way) * (blocks // 2), (2 - way) * (blocks // 2), keep, 0)
            self.last[way] = self.copy(way, step, held, self.buffers.at[way, step])
            self.last[way].start()
            if step < self.steps - 1 or way == 0:
                self.fetched[way] = self.fetch(way, self.steps - 1 - step)

    def finish(self, out):
        block = 48
        taken = [self.take(way, self.steps - 1) for way in range(2)]
        for copy in taken:
            copy.wait()
        self.fetched[0].wait()

        def add(i, carry):
            here = pl.ds(pl.multiple_of(i * block, 16), block)
            out[here, :] = (
                self.terms[0, here, :].astype(full)
                + self.held[0, here, :].astype(full)
                + self.held[1, here, :].astype(full)
            )
            return carry

        lax.fori_loop(0, self.rows // block, add, 0)
        for copy in self.copies:
            copy.wait_send()


def backward_kernel(
    count,
    tokens,
    cotangent,
    gains,
    resid,
    normed_part,
    ffn_part,
    gateup_parts,
    down_parts,
    features,
    qkv_rows,
    out_rows,
    stream,
    kv_both,
    kv_turned,
    lse,
    mixed_group,
    shuffle,
    key_ids,
    query_ids,
    block_out,
    input_grad,
    gain_grads,
    gateup_grad,
    down_grad,
    qkv_grad,
    out_grad,
    gateup_sums,
    down_sums,
    gateup_held,
    gateup_terms,
    down_held,
    down_terms,
    part_quarter,
    qkv_local,
    out_local,
    qkv_sums,
    out_sums,
    sum_out,
    sum_in,
    proj_group,
    turned_grad,
    grad_stream,
    kv_total,
    kv_out,
    kv_in,
    stream_grad,
    kv_mate,
    all_grad,
    normed_grad,
    bias,
    load_sem,
    part_sem,
    ring_send,
    ring_recv,
    head_send,
    head_recv,
    kv_send,
    kv_recv,
):
    rows = tokens.shape[0]
    group = 4 * rows
    width = features.shape[1]
    heads = width // HEAD_DIM
    scale = HEAD_DIM ** (-0.5)
    query_grad = turned_grad
    feature_grad = grad_stream
    head = lax.axis_index("head")
    me = lax.axis_index("seq")
    mate_head = head + 1 - 2 * lax.rem(head, 2)
    across_head = lax.rem(head + 2, 4)
    mate = {"head": mate_head}
    across = {"head": across_head}
    corner = {"head": 3 - head}

    def lanes(of):
        return pl.ds(pl.multiple_of(of * width, 128), width)

    def quarter(i):
        return pl.ds(i * rows, rows)

    copies = []

    def send(index, source, target, where):
        copy = remote(source, target, head_send.at[index], head_recv.at[index], where)
        copy.start()
        copies.append(copy)

    def arrived(index, target, where):
        remote(target, target, head_send.at[index], head_recv.at[index], where).wait_recv()

    def shard_view(ref, columns):
        def view(shard, part=None):
            first = pl.multiple_of((shard // 2) * BLK, 32)
            at = pl.ds(pl.multiple_of(lax.rem(shard, 2) * columns, 128), columns)
            if part is None:
                return ref.at[pl.ds(first, BLK), at]
            return ref.at[pl.ds(pl.multiple_of(first + part * (BLK // 2), 16), BLK // 2), at]

        return view

    qkv_view = shard_view(qkv_local, QKV // 2)
    out_view = shard_view(out_local, D // 2)
    gateup_ring = StagedSumRing(
        count,
        gateup_parts,
        gateup_sums,
        gateup_held,
        gateup_terms,
        load_sem.at[0],
        ring_send.at[0],
        ring_recv.at[0],
    )
    down_ring = StagedSumRing(
        count,
        down_parts,
        down_sums,
        down_held,
        down_terms,
        load_sem.at[1],
        ring_send.at[1],
        ring_recv.at[1],
    )
    qkv_ring = SumRing(count, qkv_view, qkv_view, qkv_sums, ring_send.at[2], ring_recv.at[2])
    out_ring = SumRing(count, out_view, out_view, out_sums, ring_send.at[3], ring_recv.at[3])

    barrier = pltpu.get_barrier_semaphore()
    for where in (gateup_ring.where(0), gateup_ring.where(1), mate, across, corner):
        pl.semaphore_signal(barrier, inc=1, device_id=where, device_id_type=pl.DeviceIdType.MESH)

    @pl.when(me < count - 1)
    def _():
        pl.semaphore_signal(
            barrier, inc=1, device_id={"seq": me + 1}, device_id_type=pl.DeviceIdType.MESH
        )

    pl.semaphore_wait(barrier, 5 + (me + count - 1) // count)

    def fetch(value, i):
        copy = pltpu.make_async_copy(value.at[quarter(i)], part_quarter, part_sem)
        copy.start()
        copy.wait()
        return part_quarter[...].astype(full)

    def sum_first(base, slot, value):
        send(base, value.at[quarter(3)], sum_in.at[slot], mate)
        send(base + 1, value.at[quarter(1)], sum_in.at[slot + 1], mate)

    def sum_across(base, slot, value):
        own = fetch(value, 2)
        arrived(base, sum_in.at[slot], mate)
        sum_out[slot // 3] = (own + sum_in[slot].astype(full)).astype(low)
        send(base + 2, sum_out.at[slot // 3], sum_in.at[slot + 2], across)

    def sum_last(base, slot, value):
        own = fetch(value, 0)
        arrived(base + 1, sum_in.at[slot + 1], mate)
        own = own + sum_in[slot + 1].astype(full)
        arrived(base + 2, sum_in.at[slot + 2], across)
        return own + sum_in[slot + 2].astype(full)

    sum_first(0, 0, normed_part)
    gateup_ring.start()
    down_ring.start()
    sum_across(0, 0, normed_part)
    sum_first(3, 3, ffn_part)

    normed_two_grad = sum_last(0, 0, normed_part)
    values = resid[...]
    inverse = inverse_norm(values)
    gain_grads[1:2, :] = jnp.sum(normed_two_grad * values * inverse, axis=0, keepdims=True)
    input_grad[...] = cotangent[...].astype(full) + norm_back(
        values, inverse, gains[1:2, :], normed_two_grad
    )
    proj_group[quarter(0), :] = input_grad[...].astype(low)
    send(6, proj_group.at[quarter(0)], proj_group.at[quarter(2)], across)
    send(7, proj_group.at[quarter(0)], proj_group.at[quarter(1)], mate)
    gateup_ring.step(1)
    down_ring.step(1)
    sum_across(3, 3, ffn_part)

    def back_projection(i):
        turned_grad[quarter(i), :] = mul(proj_group[quarter(i), :], out_rows[...], NT).astype(low)

    back_projection(0)
    arrived(7, proj_group.at[quarter(1)], mate)
    back_projection(1)
    arrived(6, proj_group.at[quarter(2)], across)
    send(8, proj_group.at[quarter(2)], proj_group.at[quarter(3)], mate)
    back_projection(2)
    arrived(8, proj_group.at[quarter(3)], mate)
    back_projection(3)

    def turn(i, carry):
        here = pl.ds(pl.multiple_of(i * rows, rows), rows)
        grad_stream[here, :] = mul(shuffle[here, :], turned_grad[...], NN).astype(low)
        return carry

    lax.fori_loop(0, 4, turn, 0)
    for i in range(3):
        at = slice(i * (D // 3), (i + 1) * (D // 3))
        out_local[:, at] = mul(mixed_group[...], proj_group[:, at], TN).astype(low)
    out_ring.start()
    gateup_ring.step(2)
    down_ring.step(2)

    kv_total[...] = jnp.zeros_like(kv_total)

    def back_tile(tile, carry):
        start = pl.multiple_of(tile * QUERY_TILE, QUERY_TILE)
        here = pl.ds(start, QUERY_TILE)
        span = pl.ds(start, SPAN)
        shape = (SPAN, QUERY_TILE)
        key = lax.broadcasted_iota(jnp.int32, shape, 0)
        query = lax.broadcasted_iota(jnp.int32, shape, 1)
        same = key_ids[span, :] == query_ids[:, here]
        allowed = same & (key > query) & (key <= query + WINDOW)
        bias[...] = jnp.where(allowed, 0.0, neg_fill)

        def back_head(j, carry):
            at = pl.ds(pl.multiple_of(j * HEAD_DIM, HEAD_DIM), HEAD_DIM)
            queries = stream[here, at]
            grads = grad_stream[here, at]
            scores = mul(kv_both[span, :HEAD_DIM], queries, NT) * scale + bias[...]
            probs = jnp.exp(scores - lse[j, :, here])
            prob_grad = mul(kv_both[span, HEAD_DIM:], grads, NT)
            delta = jnp.sum(probs * prob_grad, axis=0, keepdims=True)
            score_grad = (probs * (prob_grad - delta)).astype(low)
            turned = mul(kv_turned[:HEAD_DIM, span], score_grad, NN) * scale
            query_grad[here, at] = turned.T.astype(low)
            kv_total[span, :HEAD_DIM] += mul(score_grad, queries, NN) * scale
            kv_total[span, HEAD_DIM:] += mul(probs.astype(low), grads, NN)
            return carry

        return lax.fori_loop(0, heads, back_head, carry)

    lax.fori_loop(0, group // QUERY_TILE, back_tile, 0)
    kv_out[...] = kv_total[:group, :].astype(low)
    kv_copy = remote(kv_out, kv_in, kv_send, kv_recv, {"seq": lax.rem(me + count - 1, count)})

    @pl.when(me > 0)
    def _():
        kv_copy.start()

    def turn_back(i, carry):
        here = pl.ds(pl.multiple_of(i * rows, rows), rows)
        all_grad[here, lanes(head)] = mul(shuffle[:, here], query_grad[...], TN).astype(low)
        return carry

    lax.fori_loop(0, 4, turn_back, 0)

    def swapped(index, ref, columns, distance, where):
        for i in range(4):
            send(
                index + i,
                ref.at[quarter(i), columns],
                ref.at[quarter(i ^ distance), columns],
                where,
            )

    def swapped_arrived(index, ref, columns, distance, where):
        for i in range(4):
            arrived(index + i, ref.at[quarter(i ^ distance), columns], where)

    swapped(9, all_grad, lanes(head), 2, across)
    swapped(13, all_grad, lanes(head), 1, mate)
    gateup_ring.step(3)
    down_ring.step(3)
    out_ring.step(1)

    @pl.when(me < count - 1)
    def _():
        kv_copy.wait_recv()
        kv_total[pl.ds(group, group), :] += kv_in[...].astype(full)

    stream_grad[...] = kv_total[pl.ds(group, group), :].astype(low)

    def turn_keys(i, carry):
        here = pl.ds(pl.multiple_of(i * rows, rows), rows)
        kv_mate[0, here, :] = mul(shuffle[:, here], stream_grad[...], TN).astype(low)
        return carry

    lax.fori_loop(0, 4, turn_keys, 0)
    for i in range(4):
        send(17 + i, kv_mate.at[0, quarter(i)], kv_mate.at[1, quarter(i ^ 1)], mate)
    for i in range(4):
        arrived(17 + i, kv_mate.at[1, quarter(i ^ 1)], mate)
    kv_total[pl.ds(0, group), :] = kv_mate[0].astype(full) + kv_mate[1].astype(full)
    kv_mate[2] = kv_total[pl.ds(0, group), :].astype(low)
    for i in range(4):
        send(21 + i, kv_mate.at[2, quarter(i)], kv_mate.at[3, quarter(i ^ 2)], across)
    swapped_arrived(9, all_grad, lanes(across_head), 2, across)
    swapped(25, all_grad, lanes(across_head), 1, mate)
    out_ring.step(2)
    swapped_arrived(13, all_grad, lanes(mate_head), 1, mate)
    for i in range(4):
        arrived(21 + i, kv_mate.at[3, quarter(i ^ 2)], across)
    all_grad[:, QW:] = (kv_total[pl.ds(0, group), :] + kv_mate[3].astype(full)).astype(low)
    swapped_arrived(25, all_grad, lanes(3 - head), 1, mate)

    for i in range(2):
        at = slice(i * (QKV // 2), (i + 1) * (QKV // 2))
        qkv_local[:, at] = mul(features[...], all_grad[:, at], TN).astype(low)
    qkv_ring.start()
    out_ring.step(3)
    for i, where in ((2, across), (3, corner), (1, mate)):
        feature_grad[quarter(i), :] = mul(all_grad[quarter(i), :], qkv_rows[...], NT).astype(low)
        send(28 + i, feature_grad.at[quarter(i)], normed_grad.at[:, lanes(head)], where)
    normed_grad[:, lanes(head)] = mul(all_grad[quarter(0), :], qkv_rows[...], NT).astype(low)
    block_out[...] = (resid[...] + sum_last(3, 3, ffn_part)).astype(low)
    gateup_ring.finish(gateup_grad)
    down_ring.finish(down_grad)
    qkv_ring.step(1)
    for i, where, of in ((2, across, across_head), (3, corner, 3 - head), (1, mate, mate_head)):
        arrived(28 + i, normed_grad.at[:, lanes(of)], where)
    qkv_ring.step(2)
    normed_one_grad = normed_grad[...].astype(full)
    values = tokens[...].astype(full)
    inverse = inverse_norm(values)
    gain_grads[0:1, :] = jnp.sum(normed_one_grad * values * inverse, axis=0, keepdims=True)
    input_grad[...] += norm_back(values, inverse, gains[0:1, :], normed_one_grad)
    qkv_ring.step(3)
    out_ring.finish(out_grad)
    qkv_ring.finish(qkv_grad)
    for copy in copies:
        copy.wait_send()

    @pl.when(me > 0)
    def _():
        kv_copy.wait_send()


def backward_section(count, *values):
    (tokens, cotangent, gains, resid, normed_part, ffn_part, gateup_parts, down_parts) = values[:8]
    rows = tokens.shape[0]
    group = 4 * rows
    width = QW // 4
    steps = count // 2
    vmem = pl.BlockSpec(memory_space=pltpu.VMEM)
    hbm = pl.BlockSpec(memory_space=pl.ANY)
    shard = gateup_parts.shape[1:]
    down_shard = down_parts.shape[1:]
    outs = [
        ((rows, D), low),
        ((rows, D), full),
        ((2, D), full),
        (shard, full),
        (down_shard, full),
        ((BLK, QKV // 2), full),
        ((BLK, D // 2), full),
        ((2, steps) + shard, low),
        ((2, steps) + down_shard, low),
    ]
    dma = pltpu.SemaphoreType.DMA
    return pl.pallas_call(
        functools.partial(backward_kernel, count),
        in_specs=[vmem] * 4 + [hbm] * 4 + [vmem] * 11,
        out_specs=[vmem] * 7 + [hbm] * 2,
        out_shape=[jax.ShapeDtypeStruct(shape, kind) for shape, kind in outs],
        scratch_shapes=[
            pltpu.VMEM((2,) + shard, low),
            pltpu.VMEM((2,) + shard, low),
            pltpu.VMEM((2,) + down_shard, low),
            pltpu.VMEM((2,) + down_shard, low),
            pltpu.VMEM((rows, D), low),
            pltpu.VMEM((width, QKV), low),
            pltpu.VMEM((width, D), low),
            pltpu.VMEM((2, steps, BLK, QKV // 2), low),
            pltpu.VMEM((2, steps, BLK, D // 2), low),
            pltpu.VMEM((2, rows, D), low),
            pltpu.VMEM((6, rows, D), low),
            pltpu.VMEM((group, D), low),
            pltpu.VMEM((group, width), low),
            pltpu.VMEM((group, width), low),
            pltpu.VMEM((2 * group, 2 * HEAD_DIM), full),
            pltpu.VMEM((group, 2 * HEAD_DIM), low),
            pltpu.VMEM((group, 2 * HEAD_DIM), low),
            pltpu.VMEM((group, 2 * HEAD_DIM), low),
            pltpu.VMEM((4, group, 2 * HEAD_DIM), low),
            pltpu.VMEM((group, QKV), low),
            pltpu.VMEM((rows, D), low),
            pltpu.VMEM((SPAN, QUERY_TILE), full),
            dma((2, 2, 2)),
            dma,
            dma((4, 2, steps)),
            dma((4, 2, steps)),
            dma((32,)),
            dma((32,)),
            dma,
            dma,
        ],
        compiler_params=pltpu.CompilerParams(
            collective_id=1, has_side_effects=True, vmem_limit_bytes=60 * 1024 * 1024
        ),
        name="backward_section",
    )(*values)


def update_kernel(
    rate, turned, w_ref, g_ref, l_ref, r_ref, lr_ref, rr_ref, ln_ref, rn_ref, wn_ref
):
    count, rows, columns = w_ref.shape
    size = g_ref.shape[1] // count
    for b in range(count):
        grad = g_ref[:, b * size : (b + 1) * size]
        other = grad.T
        if turned:
            grad, other = other, grad
        square = jnp.sum(jnp.sum(grad * grad, axis=1, keepdims=True), axis=0, keepdims=True)
        square = square * (1.0 / (rows * columns)) + stat_eps
        grad = grad.astype(low)
        other = other.astype(low)
        ln_ref[b] = 0.5 * l_ref[b] + mul(grad, other, NN) * (0.5 / (columns * square))
        rn_ref[b] = 0.5 * r_ref[b] + mul(other, grad, NN) * (0.5 / (rows * square))
        step = mul(lr_ref[b].astype(low), grad, NN).astype(low)
        step = mul(step, rr_ref[b].astype(low), NN)
        wn_ref[b] = w_ref[b] - step * (rate * lax.rsqrt(square))


def update(weight, grad, left, right, left_root, right_root, rate, turned=False):
    count, rows, columns = weight.shape
    if grad.ndim == 3:
        grad = grad.transpose(1, 0, 2).reshape(rows, count * columns)
    height = columns if turned else rows
    batch = count // (grad.shape[0] // height)
    spec = lambda i, j: pl.BlockSpec((batch, i, j), lambda b: (b, 0, 0))
    return pl.pallas_call(
        functools.partial(update_kernel, rate, turned),
        grid=(count // batch,),
        in_specs=[
            spec(rows, columns),
            pl.BlockSpec((height, grad.shape[1]), lambda b: (b, 0)),
            spec(rows, rows),
            spec(columns, columns),
            spec(rows, rows),
            spec(columns, columns),
        ],
        out_specs=[spec(rows, rows), spec(columns, columns), spec(rows, columns)],
        out_shape=[
            jax.ShapeDtypeStruct(left.shape, full),
            jax.ShapeDtypeStruct(right.shape, full),
            jax.ShapeDtypeStruct(weight.shape, full),
        ],
        compiler_params=pltpu.CompilerParams(vmem_limit_bytes=58 * 1024 * 1024),
        cost_estimate=pl.CostEstimate(
            flops=16 * count * 256 * 256 * 128,
            bytes_accessed=36 * count * rows * 128,
            transcendentals=0,
        ),
        name="update",
    )(weight, grad, left, right, left_root, right_root)


def norm_back(values, inverse, gain, grad):
    scaled = gain * grad
    mean = jnp.mean(values * scaled, axis=-1, keepdims=True)
    return inverse * scaled - values * (inverse * inverse * inverse * mean)


def inverse_norm(values):
    return lax.rsqrt(jnp.mean(values * values, axis=-1, keepdims=True) + norm_eps)


def forward_steps(tokens, cotangent, attn_gain, ffn_gain, stacks, token_order, sequence_ids):
    qkv_stack, out_stack, gateup_stack, down_stack = stacks
    row_count = tokens.shape[0]
    head_count = lax.axis_size("head")
    seq_count = lax.axis_size("seq")
    group = row_count * head_count
    head_index = lax.axis_index("head")
    local_width = QW // head_count
    seq_index = lax.axis_index("seq")
    gains = jnp.concatenate([attn_gain, ffn_gain]).astype(low).astype(full)[None]
    gains = lax.all_to_all(
        jnp.broadcast_to(gains, (head_count * seq_count, gains.shape[1])),
        ("head", "seq"),
        split_axis=0,
        concat_axis=0,
        tiled=True,
    )
    own_gains = attn_gain.shape[0]
    gain_one = gains[:, :own_gains].reshape(1, D)
    gain_two = gains[:, own_gains:].reshape(1, D)


    ids_own = lax.dynamic_slice_in_dim(sequence_ids, seq_index * group, group, 0)
    ids_before = lax.dynamic_slice_in_dim(
        sequence_ids, jnp.maximum(seq_index - 1, 0) * group, group, 0
    )
    ids_before = jnp.where(seq_index > 0, ids_before, -1)
    key_ids = jnp.concatenate([ids_before, ids_own])[:, None]
    query_ids = ids_own[None, :]
    qkv_rows = joined_halves(gather_rows(qkv_stack, 8, to_columns))
    out_rows = joined_halves(gather_rows(out_stack, 8, to_columns))
    gateup = gather_rows(gateup_stack, 16, to_units)
    down = gather_rows(down_stack, 8, to_columns)
    tokens_float = tokens.astype(full)
    normed_one = (tokens_float * inverse_norm(tokens_float) * gain_one).astype(low)
    normed_one_group = jnp.concatenate(head_gather(normed_one))
    feature_start = head_index * local_width
    features = lax.dynamic_slice_in_dim(normed_one_group, feature_start, local_width, 1)
    weights = in_order(head_gather(qkv_rows), 0)
    weights = jnp.concatenate(
        [lax.dynamic_slice_in_dim(weights, feature_start, local_width, 1), weights[:, QW:]], axis=1
    )
    projected = mul(normed_one_group, weights, NN, low)
    buffer_rows = ((token_order // row_count) ^ head_index) * row_count + token_order % row_count
    shuffle = (
        buffer_rows[:, None] == lax.broadcasted_iota(jnp.int32, (group, group), 1)
    ).astype(low)
    stream = mul(shuffle, projected, NN, low)
    kv_stream = stream[:, local_width:]
    kv_before = lax.ppermute(kv_stream, "seq", [(i, i + 1) for i in range(seq_count - 1)])
    kv_both = jnp.concatenate([kv_before, kv_stream], axis=0)
    kv_turned = kv_both.T
    mixed_stream, lse = attend(stream[:, :local_width], kv_both, kv_turned, key_ids, query_ids)
    mixed_group = mul(shuffle, mixed_stream, TN, low)
    part = mul(mixed_group, out_rows, NN, low)
    resid = tokens_float + head_sum([part[i * row_count :][:row_count] for i in range(4)])
    normed_two = (resid * inverse_norm(resid) * gain_two).astype(low)
    normed_group = jnp.concatenate(head_gather(normed_two))
    grad_group = jnp.concatenate(head_gather(cotangent))
    section = (
        jnp.concatenate([gain_one, gain_two]),
        resid,
        normed_group,
        gateup,
        down,
        features,
        qkv_rows,
        out_rows,
        stream,
        kv_both,
        kv_turned,
        lse,
        mixed_group,
        shuffle,
        key_ids,
        query_ids,
    )
    return grad_group, section


def backward_steps(
    tokens,
    cotangent,
    gains,
    resid,
    normed_part,
    ffn_part,
    gateup_wgrad,
    down_wgrad,
    features,
    qkv_rows,
    out_rows,
    stream,
    kv_both,
    kv_turned,
    lse,
    mixed_group,
    shuffle,
    key_ids,
    query_ids,
    counts,
):
    row_count = tokens.shape[0]
    group = row_count * lax.axis_size("head")
    seq_count = lax.axis_size("seq")
    local_width = features.shape[1]
    query_stream = stream[:, :local_width]
    gain_one, gain_two = gains[0], gains[1]
    tokens_float = tokens.astype(full)
    inverse_one = inverse_norm(tokens_float)
    inverse_two = inverse_norm(resid)
    normed_two_grad = head_sum([normed_part[i * row_count :][:row_count] for i in range(4)])
    gateup_grad_own = sum_rows(gateup_wgrad, counts[2], 16, from_units)
    down_grad_own = sum_rows(down_wgrad, counts[3], 8, from_columns)
    ffn_out = head_sum([ffn_part[i * row_count :][:row_count] for i in range(4)])
    block_out = (resid + ffn_out).astype(low)

    resid_grad = cotangent.astype(full) + norm_back(resid, inverse_two, gain_two, normed_two_grad)
    gain_two_grad = jnp.sum(normed_two_grad * resid * inverse_two, axis=0)
    proj_grad = resid_grad.astype(low)
    proj_grad_group = jnp.concatenate(head_gather(proj_grad))
    mixed_grad_group = mul(proj_grad_group, out_rows, NT, low)
    mixed_grad_stream = mul(shuffle, mixed_grad_group, NN, low)
    out_wgrad = split_halves(mul(mixed_group, proj_grad_group, TN, low), BLK)
    out_grad_own = sum_rows(out_wgrad, counts[1], 8, from_columns)

    query_grad, kv_grad = attend_back(
        query_stream, mixed_grad_stream, kv_both, kv_turned, key_ids, query_ids, lse
    )
    kv_later = lax.ppermute(
        kv_grad[:group].astype(low), "seq", [(i, i - 1) for i in range(1, seq_count)]
    )
    kv_grad = (kv_grad[group:] + kv_later.astype(full)).astype(low)
    grad_local = mul(shuffle, jnp.concatenate([query_grad, kv_grad], axis=1), TN, low)
    gathered = head_gather(grad_local)

    def own_order(value, j):
        quarters = [value[i * row_count :][:row_count] for i in range(4)]
        return jnp.concatenate([quarters[i ^ j] for i in range(4)])

    gathered = [own_order(value, j) for j, value in enumerate(gathered)]
    kv_total = sum(value[:, local_width:].astype(full) for value in gathered).astype(low)
    qkv_grad = jnp.concatenate(
        [in_order([value[:, :local_width] for value in gathered], 1), kv_total], axis=1
    )
    qkv_wgrad = split_halves(mul(features, qkv_grad, TN, low), BLK)
    qkv_grad_own = sum_rows(qkv_wgrad, counts[0], 8, from_columns)
    feature_grad = mul(qkv_grad, qkv_rows, NT, low)
    order = (0, 2, 1, 3)
    feature_parts = head_exchange([feature_grad[i * row_count :][:row_count] for i in range(4)])
    normed_one_grad = in_order([feature_parts[order.index(j)] for j in range(4)], 1).astype(full)
    input_grad = resid_grad + norm_back(tokens_float, inverse_one, gain_one, normed_one_grad)
    gain_one_grad = jnp.sum(normed_one_grad * tokens_float * inverse_one, axis=0)
    return (
        block_out,
        input_grad,
        jnp.stack([gain_one_grad, gain_two_grad]),
        gateup_grad_own,
        down_grad_own,
        qkv_grad_own,
        out_grad_own,
    )


def on_device(
    tokens,
    cotangent,
    attn_gain,
    ffn_gain,
    qkv_stack,
    out_stack,
    gateup_stack,
    down_stack,
    qkv_left,
    qkv_right,
    out_left,
    out_right,
    gateup_left,
    gateup_right,
    down_left,
    down_right,
    qkv_left_root,
    qkv_right_root,
    out_left_root,
    out_right_root,
    gateup_left_root,
    gateup_right_root,
    down_left_root,
    down_right_root,
    sequence_ids,
    token_order,
):
    row_count = tokens.shape[0]
    head_count = lax.axis_size("head")
    seq_count = lax.axis_size("seq")
    device_count = head_count * seq_count
    group = row_count * head_count
    seq_index = lax.axis_index("seq")
    local_width = QW // head_count

    own_gains = attn_gain.shape[0]
    stacks = (qkv_stack, out_stack, gateup_stack, down_stack)
    whole_rows = all(s.shape[0] % u == 0 for s, u in zip(stacks, (8, 8, 16, 8)))
    if whole_rows:
        tile = jnp.concatenate([attn_gain[None], ffn_gain[None]])
        section = forward_section(
            tokens,
            jnp.pad(tile, ((0, 6), (0, 128 - own_gains))),
            stacks,
            token_order[None, :],
            sequence_ids[None, :],
            seq_count,
        )
        cotangent_late, section = lax.optimization_barrier((cotangent, section))
        grad_group = jnp.concatenate(head_gather(cotangent_late))
    else:
        grad_group, section = forward_steps(
            tokens, cotangent, attn_gain, ffn_gain, stacks, token_order, sequence_ids
        )
    (
        gains_both,
        resid,
        normed_group,
        gateup,
        down,
        features,
        qkv_rows,
        out_all,
        stream,
        kv_both,
        kv_turned,
        lse,
        mixed_group,
        shuffle,
        key_ids,
        query_ids,
    ) = section
    gateup = gateup.reshape(-1, D)
    down = joined_halves(down.reshape(-1, BLK, D // 2))
    unit_count = down.shape[0] // BLK

    gate_up = mul(gateup, normed_group, NT).reshape(unit_count, 2, BLK, group)
    hidden, act_pull = jax.vjp(
        lambda g, u: jax.nn.gelu(g, approximate=True) * u, gate_up[:, 0], gate_up[:, 1]
    )
    hidden = hidden.astype(low).reshape(unit_count * BLK, group)
    hidden_grad = mul(down, grad_group, NT).reshape(unit_count, BLK, group)
    gate_grad, up_grad = act_pull(hidden_grad)
    gate_up_grad = (
        jnp.stack([gate_grad, up_grad], axis=1).astype(low).reshape(2 * unit_count * BLK, group)
    )
    normed_part = mul(gate_up_grad, gateup, TN, low)
    gateup_wgrad = mul(gate_up_grad, normed_group, NN, low).reshape(2 * unit_count, BLK, D)
    down_wgrad = split_halves(mul(hidden, grad_group, NN, low), BLK)
    ffn_part = mul(hidden, down, TN, low)
    out_rows = out_all
    if whole_rows:
        start = lax.axis_index("head") * local_width
        out_rows = lax.dynamic_slice_in_dim(out_all, start, local_width, 0)
    kept = (features, qkv_rows, out_rows, stream, kv_both, kv_turned, lse, mixed_group, shuffle)
    counts = [s.shape[0] for s in stacks]
    if whole_rows:
        (block_out, input_grad, gain_grads, gateup_own, down_own, qkv_own, out_own, *_) = (
            backward_section(
                seq_count,
                tokens,
                cotangent,
                gains_both,
                resid,
                normed_part,
                ffn_part,
                gateup_wgrad.reshape(seq_count, -1, D),
                down_wgrad.reshape(seq_count, -1, D // 2),
                *kept,
                key_ids,
                query_ids,
            )
        )
        gateup_grad_own, down_grad_own = gateup_own, down_own
        qkv_grad_own, out_grad_own = qkv_own, out_own
    else:
        section = backward_steps(
            tokens, cotangent, gains_both, resid, normed_part, ffn_part, gateup_wgrad, down_wgrad, *kept,
            key_ids, query_ids, counts,
        )
        (block_out, input_grad, gain_grads, gateup_grad_own, down_grad_own, qkv_grad_own, out_grad_own) = section
    gain_one_grad, gain_two_grad = gain_grads[0], gain_grads[1]
    gain_grads = jnp.concatenate(
        [gain_one_grad.reshape(device_count, -1), gain_two_grad.reshape(device_count, -1)], axis=1
    )
    gain_grads = lax.all_to_all(
        gain_grads, ("head", "seq"), split_axis=0, concat_axis=0, tiled=True
    )
    gain_grads = jnp.sum(gain_grads, axis=0)

    gateup_new = update(
        gateup_stack,
        gateup_grad_own,
        gateup_left,
        gateup_right,
        gateup_left_root,
        gateup_right_root,
        0.5 * D ** (-0.5),
        whole_rows,
    )
    down_new = update(
        down_stack,
        down_grad_own,
        down_left,
        down_right,
        down_left_root,
        down_right_root,
        0.5 * FF ** (-0.5),
    )
    out_new = update(
        out_stack,
        out_grad_own,
        out_left,
        out_right,
        out_left_root,
        out_right_root,
        0.5 * (QW // 64) ** (-0.5),
    )
    qkv_new = update(
        qkv_stack,
        qkv_grad_own,
        qkv_left,
        qkv_right,
        qkv_left_root,
        qkv_right_root,
        0.5 * D ** (-0.5),
    )
    return (
        (block_out, input_grad, gain_grads[:own_gains], gain_grads[own_gains:])
        + tuple(qkv_new)
        + tuple(out_new)
        + tuple(gateup_new)
        + tuple(down_new)
    )


def solution(mesh):
    rows = P(("seq", "head"), None)
    gain = P(("head", "seq"))
    blocks = P(("head", "seq"), None, None)
    return jax.shard_map(
        on_device,
        mesh=mesh,
        in_specs=(rows, rows, gain, gain) + (blocks,) * 20 + (P(), P("seq")),
        out_specs=(rows, rows, gain, gain) + (blocks,) * 12,
        check_vma=False,
    )
```

```python
import functools

import jax
import jax.numpy as jnp
from jax import lax
from jax.experimental import pallas as pl
from jax.experimental.pallas import tpu as pltpu
from jax.sharding import PartitionSpec as P

D = 1536
HEAD_DIM = 128
FF = 4608
WINDOW = 1024
GRID = 16
QW = 1536
QKV = 1792
BLK = 96
BQ = 112
BH = 96
NU = 48

norm_eps = 1e-06
stat_eps = 1e-06
neg_fill = -1e30

QUERY_TILE = 256
SPAN = WINDOW + QUERY_TILE

low = jnp.bfloat16
full = jnp.float32

NT = (((1,), (1,)), ((), ()))
NN = (((1,), (0,)), ((), ()))
TN = (((0,), (0,)), ((), ()))


def mul(a, b, dims, kind=full):
    return lax.dot_general(a, b, dims, preferred_element_type=kind)


def ring_place(index, count):
    return jnp.where(index % 2 == 0, index // 2, count - 1 - index // 2)


def ring_index(place, count):
    return jnp.where(place < count // 2, 2 * place, 2 * (count - 1 - place) + 1)


def ring_routes(count):
    order = [i for i in range(0, count, 2)] + [i for i in range(count - 1, 0, -2)]
    up = [(order[i], order[(i + 1) % count]) for i in range(count)]
    return up, [(b, a) for a, b in up]


def seq_gather(shard):
    count = lax.axis_size("seq")
    rows = shard.shape[0]
    half = rows // 2
    me = lax.axis_index("seq")
    place = ring_place(me, count)
    up, down = ring_routes(count)
    out = jnp.zeros((count,) + shard.shape, shard.dtype)
    out = lax.dynamic_update_slice(out, shard[None], (me, 0, 0))
    ahead = shard
    behind = shard
    for step in range(1, count // 2):
        ahead = lax.ppermute(ahead, "seq", up)
        behind = lax.ppermute(behind, "seq", down)
        out = lax.dynamic_update_slice(
            out, ahead[None], (ring_index((place - step + count) % count, count), 0, 0)
        )
        out = lax.dynamic_update_slice(
            out, behind[None], (ring_index((place + step) % count, count), 0, 0)
        )
    ahead = lax.ppermute(ahead[:half], "seq", up)
    behind = lax.ppermute(behind[half:], "seq", down)
    far = ring_index((place + count // 2) % count, count)
    out = lax.dynamic_update_slice(out, ahead[None], (far, 0, 0))
    return lax.dynamic_update_slice(out, behind[None], (far, half, 0))


def seq_sum(parts):
    count, rows = parts.shape[:2]
    half = rows // 2
    place = ring_place(lax.axis_index("seq"), count)
    up, down = ring_routes(count)

    def part(offset):
        index = ring_index((place + offset + count) % count, count)
        return lax.dynamic_slice_in_dim(parts, index, 1, 0)[0]

    far = part(count // 2)
    ahead = lax.ppermute(far[:half], "seq", up)
    behind = lax.ppermute(far[half:], "seq", down)
    for offset in range(count // 2 - 1, 0, -1):
        local = part(offset)
        if ahead.shape[0] == rows:
            local = (local.astype(full) + ahead.astype(full)).astype(low)
        else:
            local = jnp.concatenate(
                [(local[:half].astype(full) + ahead.astype(full)).astype(low), local[half:]]
            )
        ahead = lax.ppermute(local, "seq", up)
        local = part(-offset)
        if behind.shape[0] == rows:
            local = (local.astype(full) + behind.astype(full)).astype(low)
        else:
            local = jnp.concatenate(
                [local[:half], (local[half:].astype(full) + behind.astype(full)).astype(low)]
            )
        behind = lax.ppermute(local, "seq", down)
    return part(0).astype(full) + ahead.astype(full) + behind.astype(full)


def gather_rows(stack, unit, layout):
    short = stack.astype(low)
    if stack.shape[0] % unit == 0:
        shard = layout(short)
        rows = shard.reshape(-1, shard.shape[-1])
        out = seq_gather(rows)
        return out.reshape((-1,) + shard.shape[1:])
    return layout(lax.all_gather(short, "seq", axis=0, tiled=True))


def sum_rows(rows, local, unit, back):
    count = lax.axis_size("seq")
    if local % unit == 0:
        own = seq_sum(rows.reshape(count, -1, rows.shape[-1]))
        return back(own.reshape((-1,) + rows.shape[1:]))
    return lax.psum_scatter(back(rows), "seq", scatter_dimension=0, tiled=True).astype(full)


def to_columns(stack):
    n, i, j = stack.shape
    return stack.reshape(n // 8, 8, i, j).transpose(0, 2, 1, 3).reshape(n // 8, i, 8 * j)


def from_columns(rows):
    n, i, j = rows.shape
    return rows.reshape(n, i, 8, j // 8).transpose(0, 2, 1, 3).reshape(n * 8, i, j // 8)


def to_units(stack):
    n, i, j = stack.shape
    return stack.reshape(n // 16, 16, i, j).transpose(0, 3, 1, 2).reshape(n // 16, j, 16 * i)


def from_units(rows):
    n, j, i = rows.shape
    return rows.reshape(n, j, 16, i // 16).transpose(0, 2, 3, 1).reshape(n * 16, i // 16, j)


def joined_halves(rows):
    n, i, j = rows.shape
    return rows.reshape(n // 2, 2, i, j).transpose(0, 2, 1, 3).reshape(n // 2 * i, 2 * j)


def split_halves(matrix, i):
    rows, columns = matrix.shape
    half = columns // 2
    parts = [matrix[:, at : at + half].reshape(rows // i, i, half) for at in (0, half)]
    return jnp.stack(parts, axis=1).reshape(2 * rows // i, i, half)


def to_partner(value, which):
    count = lax.axis_size("head")
    return lax.ppermute(value, "head", [(i, i ^ which) for i in range(count)])


def head_gather(value):
    across = to_partner(value, 2)
    mate = to_partner(value, 1)
    return value, mate, across, to_partner(across, 1)


def head_exchange(parts):
    return (parts[0],) + tuple(to_partner(parts[j], j) for j in (2, 1, 3))


def head_sum(parts):
    across = (parts[2].astype(full) + to_partner(parts[3], 1).astype(full)).astype(low)
    across = to_partner(across, 2)
    mine = parts[0].astype(full) + to_partner(parts[1], 1).astype(full)
    return mine + across.astype(full)


def in_order(parts, axis):
    me = lax.axis_index("head")
    odd = me % 2 == 1
    lower = [jnp.where(odd, parts[1], parts[0]), jnp.where(odd, parts[0], parts[1])]
    upper = [jnp.where(odd, parts[3], parts[2]), jnp.where(odd, parts[2], parts[3])]
    second = me >= 2
    return jnp.concatenate(
        [jnp.where(second, b, a) for a, b in zip(lower, upper)]
        + [jnp.where(second, a, b) for a, b in zip(lower, upper)],
        axis=axis,
    )


def tile_bias(tile, key_ids, query_ids, bias_ref):
    start = pl.multiple_of(tile * QUERY_TILE, QUERY_TILE)
    shape = (SPAN, QUERY_TILE)
    key = lax.broadcasted_iota(jnp.int32, shape, 0)
    query = lax.broadcasted_iota(jnp.int32, shape, 1)
    same = key_ids[pl.ds(start, SPAN), :] == query_ids[...]
    allowed = same & (key > query) & (key <= query + WINDOW)
    bias_ref[...] = jnp.where(allowed, 0.0, neg_fill)


def attend_kernel(q_ref, kv_ref, kvt_ref, key_ids, query_ids, out_ref, lse_ref, bias_ref):
    tile = pl.program_id(0)
    start = pl.multiple_of(tile * QUERY_TILE, QUERY_TILE)

    @pl.when(pl.program_id(1) == 0)
    def _():
        tile_bias(tile, key_ids, query_ids, bias_ref)

    keys = kv_ref[pl.ds(start, SPAN), :HEAD_DIM]
    scores = mul(keys, q_ref[...], NT) * HEAD_DIM ** (-0.5) + bias_ref[...]
    top = jnp.max(scores, axis=0, keepdims=True)
    expo = jnp.exp(scores - top)
    total = jnp.sum(expo, axis=0, keepdims=True)
    values = kvt_ref[HEAD_DIM:, pl.ds(start, SPAN)]
    mixed = mul(values, expo.astype(low), NN) / total
    out_ref[...] = mixed.T.astype(low)
    lse_ref[0] = top + jnp.log(total)


def attend_back_kernel(
    q_ref, g_ref, kv_ref, kvt_ref, key_ids, query_ids, lse_ref, dq_ref, dkv_ref, bias_ref
):
    tile = pl.program_id(0)
    start = pl.multiple_of(tile * QUERY_TILE, QUERY_TILE)
    scale = HEAD_DIM ** (-0.5)

    @pl.when((tile == 0) & (pl.program_id(1) == 0))
    def _():
        dkv_ref[...] = jnp.zeros_like(dkv_ref)

    @pl.when(pl.program_id(1) == 0)
    def _():
        tile_bias(tile, key_ids, query_ids, bias_ref)

    here = pl.ds(start, SPAN)
    queries = q_ref[...]
    grads = g_ref[...]
    scores = mul(kv_ref[here, :HEAD_DIM], queries, NT) * scale + bias_ref[...]
    probs = jnp.exp(scores - lse_ref[0])
    prob_grad = mul(kv_ref[here, HEAD_DIM:], grads, NT)
    delta = jnp.sum(probs * prob_grad, axis=0, keepdims=True)
    score_grad = (probs * (prob_grad - delta)).astype(low)
    dq = mul(kvt_ref[:HEAD_DIM, here], score_grad, NN) * scale
    dq_ref[...] = dq.T.astype(low)
    dkv_ref[here, :HEAD_DIM] += mul(score_grad, queries, NN) * scale
    dkv_ref[here, HEAD_DIM:] += mul(probs.astype(low), grads, NN)


def attention_specs(group):
    whole = lambda *shape: pl.BlockSpec(shape, lambda t, h: (0,) * len(shape))
    head_rows = pl.BlockSpec((QUERY_TILE, HEAD_DIM), lambda t, h: (t, h))
    keys = whole(2 * group, 2 * HEAD_DIM)
    keys_turned = whole(2 * HEAD_DIM, 2 * group)
    key_ids = whole(2 * group, 1)
    query_ids = pl.BlockSpec((1, QUERY_TILE), lambda t, h: (0, t))
    lse = pl.BlockSpec((1, 1, QUERY_TILE), lambda t, h: (h, 0, t))
    return head_rows, keys, keys_turned, key_ids, query_ids, lse


attention_params = pltpu.CompilerParams(
    dimension_semantics=("arbitrary", "arbitrary"), vmem_limit_bytes=40 * 1024 * 1024
)


def attend(queries, kv, kv_turned, key_ids, query_ids):
    group, width = queries.shape
    heads = width // HEAD_DIM
    rows, keys, turned, kids, qids, lse = attention_specs(group)
    work = heads * (group // QUERY_TILE) * SPAN * QUERY_TILE
    return pl.pallas_call(
        attend_kernel,
        grid=(group // QUERY_TILE, heads),
        in_specs=[rows, keys, turned, kids, qids],
        out_specs=[rows, lse],
        out_shape=[
            jax.ShapeDtypeStruct((group, width), low),
            jax.ShapeDtypeStruct((heads, 1, group), full),
        ],
        scratch_shapes=[pltpu.VMEM((SPAN, QUERY_TILE), full)],
        compiler_params=attention_params,
        cost_estimate=pl.CostEstimate(
            flops=8 * work * HEAD_DIM, bytes_accessed=6 << 20, transcendentals=work
        ),
        name="attend",
    )(queries, kv, kv_turned, key_ids, query_ids)


def attend_back(queries, grads, kv, kv_turned, key_ids, query_ids, lse_rows):
    group, width = queries.shape
    heads = width // HEAD_DIM
    rows, keys, turned, kids, qids, lse = attention_specs(group)
    work = heads * (group // QUERY_TILE) * SPAN * QUERY_TILE
    return pl.pallas_call(
        attend_back_kernel,
        grid=(group // QUERY_TILE, heads),
        in_specs=[rows, rows, keys, turned, kids, qids, lse],
        out_specs=[rows, keys],
        out_shape=[
            jax.ShapeDtypeStruct((group, width), low),
            jax.ShapeDtypeStruct((2 * group, 2 * HEAD_DIM), full),
        ],
        scratch_shapes=[pltpu.VMEM((SPAN, QUERY_TILE), full)],
        compiler_params=attention_params,
        cost_estimate=pl.CostEstimate(
            flops=20 * work * HEAD_DIM, bytes_accessed=8 << 20, transcendentals=work
        ),
        name="attend_back",
    )(queries, grads, kv, kv_turned, key_ids, query_ids, lse_rows)


def remote(source, target, send, recv, where):
    return pltpu.make_async_remote_copy(
        src_ref=source,
        dst_ref=target,
        send_sem=send,
        recv_sem=recv,
        device_id=where,
        device_id_type=pl.DeviceIdType.MESH,
    )


class Ring:
    def __init__(self, count, view, send, recv, split=True):
        me = lax.axis_index("seq")
        self.split = split
        odd = lax.rem(me, 2)
        self.count = count
        self.view = view
        self.send = send
        self.recv = recv
        self.place = (1 - odd) * (me // 2) + odd * (count - 1 - me // 2)
        self.ahead = {"seq": self.shard(1)}
        self.behind = {"seq": self.shard(-1)}
        self.copies = []

    def shard(self, offset):
        place = lax.rem(self.place + offset + self.count, self.count)
        upper = place // (self.count // 2)
        return (1 - upper) * 2 * place + upper * (2 * (self.count - 1 - place) + 1)

    def pair(self, offset, step):
        last = step == self.count // 2
        halved = last and self.split
        views = [
            self.view(self.shard(-offset), 0 if halved else None),
            self.view(self.shard(offset), 1 if halved else None),
        ]
        if last and not self.split:
            views = views[:1]
        return [
            remote(view, view, self.send.at[i, step - 1], self.recv.at[i, step - 1], where)
            for i, (view, where) in enumerate(zip(views, (self.ahead, self.behind)))
        ]

    def start(self, step):
        for copy in self.pair(step - 1, step):
            copy.start()
            self.copies.append(copy)

    def arrive(self, step):
        for copy in self.pair(step, step):
            copy.wait_recv()

    def finish(self):
        for copy in self.copies:
            copy.wait_send()


def turned_row(row):
    size = row.shape[1]
    return jnp.broadcast_to(row.astype(full), (128, size)).T[:, :1]


def forward_kernel(
    count,
    tokens,
    cotangent,
    own_gains,
    qkv_stack,
    out_stack,
    gateup_stack,
    down_stack,
    order,
    ids,
    gains,
    resid,
    normed_group,
    grad_group,
    gateup,
    down,
    features,
    qkv_rows,
    out_all,
    stream,
    kv_both,
    kv_turned,
    lse,
    mixed_group,
    shuffle,
    key_ids,
    query_ids,
    tokens_group,
    normed,
    weights,
    projected,
    mixed,
    mixed_all,
    bias,
    wide,
    tall,
    gateup_own,
    down_own,
    gain_tiles,
    own_sem,
    ring_send,
    ring_recv,
    head_send,
    head_recv,
    kv_send,
    kv_recv,
):
    rows = tokens.shape[0]
    group = 4 * rows
    width = features.shape[1]
    heads = width // HEAD_DIM
    head = lax.axis_index("head")
    me = lax.axis_index("seq")
    mate_head = head + 1 - 2 * lax.rem(head, 2)
    across_head = lax.rem(head + 2, 4)
    mate = {"head": mate_head}
    across = {"head": across_head}

    def band(of):
        return pl.ds(pl.multiple_of(of * width, 128), width)

    def chip_columns(of):
        return pl.ds(pl.multiple_of((of // 2) * 2 * width, 128), 2 * width)

    def quarter(ref, i):
        return ref.at[pl.ds(i * rows, rows)]

    copies = []

    def send(index, source, target, where):
        copy = remote(source, target, head_send.at[index], head_recv.at[index], where)
        copy.start()
        copies.append(copy)

    def arrived(index, target, where):
        remote(target, target, head_send.at[index], head_recv.at[index], where).wait_recv()

    def stack_view(ref, columns):
        def view(shard, part):
            first = pl.multiple_of(head * width + (shard // 2) * BLK, 32)
            at = pl.ds(pl.multiple_of(lax.rem(shard, 2) * columns, 128), columns)
            if part is None:
                return ref.at[pl.ds(first, BLK), at]
            return ref.at[pl.ds(pl.multiple_of(first + part * (BLK // 2), 16), BLK // 2), at]

        return view

    def gateup_view(shard, part):
        size = gateup.shape[1]
        if part is None:
            return gateup.at[shard]
        return gateup.at[shard, pl.ds(part * (size // 2), size // 2)]

    def down_view(shard, part):
        if part is None:
            return down.at[shard]
        return down.at[shard, :, pl.ds(part * (BLK // 2), BLK // 2)]

    qkv_view = stack_view(weights, QKV // 2)
    out_view = stack_view(out_all, D // 2)
    gain_view = lambda shard, part: gain_tiles.at[head, shard]
    qkv_ring, out_ring, gateup_ring, down_ring, gain_ring = rings = [
        Ring(count, view, ring_send.at[i], ring_recv.at[i], view is not gain_view)
        for i, view in enumerate((qkv_view, out_view, gateup_view, down_view, gain_view))
    ]

    barrier = pltpu.get_barrier_semaphore()
    for where in (qkv_ring.ahead, qkv_ring.behind, mate, across):
        pl.semaphore_signal(barrier, inc=1, device_id=where, device_id_type=pl.DeviceIdType.MESH)

    @pl.when(me > 0)
    def _():
        pl.semaphore_signal(
            barrier, inc=1, device_id={"seq": me - 1}, device_id_type=pl.DeviceIdType.MESH
        )

    def side_by_side(stack, first):
        size = stack.shape[2]
        blocks = 8
        for c in range(blocks):
            tall[c * size : (c + 1) * size, :] = stack[first + c].T
        return tall[: blocks * size, :].T.astype(low)

    qkv_view(me, None)[...] = side_by_side(qkv_stack, 0)
    gain_tiles[head, me] = own_gains[...]
    pl.semaphore_wait(barrier, 5 - me // (count - 1))
    send(0, tokens, quarter(tokens_group, 2), across)
    send(1, tokens, quarter(tokens_group, 1), mate)
    qkv_ring.start(1)
    gain_ring.start(1)
    for q in range(gateup_own.shape[0] // BLK):
        column = gateup_stack[q * GRID : (q + 1) * GRID].reshape(D, BLK)
        gateup_own[q * BLK : (q + 1) * BLK, :] = column.T.astype(low)
    for m in range(down_own.shape[0]):
        down_own[m] = side_by_side(down_stack, 8 * m)
    own = [
        pltpu.make_async_copy(gateup_own, gateup.at[me], own_sem.at[0]),
        pltpu.make_async_copy(down_own, down.at[me], own_sem.at[1]),
        pltpu.make_async_copy(cotangent, quarter(grad_group, 0), own_sem.at[2]),
    ]
    for copy in own:
        copy.start()
    out_view(me, None)[...] = side_by_side(out_stack, 0)
    for copy in own[:2]:
        copy.wait()

    def pump(step):
        if step > 1:
            gateup_ring.arrive(step - 1)
            down_ring.arrive(step - 1)
        if step <= count // 2:
            gateup_ring.start(step)
            down_ring.start(step)

    pump(1)
    tokens_group[:rows, :] = tokens[...]
    qkv_ring.arrive(1)
    qkv_ring.start(2)
    gain_ring.arrive(1)
    gain_ring.start(2)

    for i in range(4):
        at = turned_row(order[:, i * rows : (i + 1) * rows]).astype(jnp.int32)
        owner = at // rows
        flip = head - 4 * (owner // 2) * (head // 2) - 2 * lax.rem(owner, 2) * lax.rem(head, 2)
        place = (owner + flip) * rows + lax.rem(at, rows)
        shuffle[i * rows : (i + 1) * rows, :] = jnp.where(
            place == lax.broadcasted_iota(jnp.int32, (rows, group), 1), 1.0, 0.0
        ).astype(low)
    query_ids[...] = ids[:, pl.ds(pl.multiple_of(me * group, 128), group)].astype(full)
    before = (me - (me + count - 1) // count) * group
    for i in range(4):
        here = slice(i * rows, (i + 1) * rows)
        at = pl.multiple_of(before + i * rows, 128)
        key_ids[here, :] = jnp.where(me > 0, turned_row(ids[:, pl.ds(at, rows)]), -1.0)
        there = slice(group + i * rows, group + (i + 1) * rows)
        key_ids[there, :] = turned_row(query_ids[:, here])
    for step in range(2, count // 2):
        qkv_ring.arrive(step)
        qkv_ring.start(step + 1)
        gain_ring.arrive(step)
        gain_ring.start(step + 1)
    qkv_ring.arrive(count // 2)

    key_columns = pl.ds(QW, 2 * HEAD_DIM)

    def weight_parts(of, chip_of):
        return [weights.at[band(of), columns] for columns in (chip_columns(chip_of), key_columns)]

    gain_ring.arrive(count // 2)
    send(9, gain_tiles.at[head], gain_tiles.at[head], across)
    send(10, gain_tiles.at[head], gain_tiles.at[head], mate)
    for i, part in enumerate(weight_parts(head, across_head)):
        send(3 + i, part, part, across)
    for i, part in enumerate(weight_parts(head, head)):
        send(7 + i, part, part, mate)
    out_ring.start(1)
    pump(2)
    arrived(0, quarter(tokens_group, 2), across)
    send(2, quarter(tokens_group, 2), quarter(tokens_group, 3), mate)
    qkv_rows[...] = weights[band(head), :]
    arrived(9, gain_tiles.at[across_head], across)
    send(11, gain_tiles.at[across_head], gain_tiles.at[across_head], mate)
    arrived(10, gain_tiles.at[mate_head], mate)
    arrived(11, gain_tiles.at[3 - head], mate)
    size = D // (4 * count)
    for h in range(4):
        for i in range(count):
            at = (h * count + i) * size
            wide[:8, at : at + size] = gain_tiles[h, i][:, :size]
    gains[...] = wide[:2, :D].astype(low).astype(full)

    def norm_rows(i):
        here = pl.ds(i * rows, rows)
        values = tokens_group[here, :].astype(full)
        normed[here, :] = (values * inverse_norm(values) * gains[0:1, :]).astype(low)

    norm_rows(0)
    arrived(1, quarter(tokens_group, 1), mate)
    norm_rows(1)
    out_ring.arrive(1)
    out_ring.start(2)
    norm_rows(2)
    arrived(2, quarter(tokens_group, 3), mate)
    norm_rows(3)
    features[...] = normed[:, band(head)]
    for i, part in enumerate(weight_parts(across_head, head)):
        arrived(3 + i, part, across)
        send(5 + i, part, part, mate)
    out_ring.arrive(2)
    out_ring.start(3)
    for i, part in enumerate(weight_parts(mate_head, head)):
        arrived(7 + i, part, mate)
    send(27, cotangent, quarter(grad_group, 2), across)
    send(28, cotangent, quarter(grad_group, 1), mate)
    for i, part in enumerate(weight_parts(3 - head, head)):
        arrived(5 + i, part, mate)

    key_values = pl.ds(width, 2 * HEAD_DIM)

    def project(columns, target):
        def step(i, carry):
            here = pl.ds(pl.multiple_of(i * rows, rows), rows)
            projected[here, target] = mul(normed[here, :], weights[:, columns], NN).astype(low)
            return carry

        lax.fori_loop(0, 4, step, 0)

        def turn(i, carry):
            here = pl.ds(pl.multiple_of(i * rows, rows), rows)
            stream[here, target] = mul(shuffle[here, :], projected[:, target], NN).astype(low)
            return carry

        lax.fori_loop(0, 4, turn, 0)

    project(key_columns, key_values)
    kv_both[pl.ds(group, group), :] = stream[:, key_values]
    kv_copy = remote(
        kv_both.at[pl.ds(group, group)],
        kv_both.at[pl.ds(0, group)],
        kv_send,
        kv_recv,
        {"seq": lax.rem(me + 1, count)},
    )

    @pl.when(me < count - 1)
    def _():
        kv_copy.start()

    @pl.when(me == 0)
    def _():
        kv_both[pl.ds(0, group), :] = jnp.zeros((group, 2 * HEAD_DIM), low)

    out_ring.arrive(3)
    out_ring.start(4)
    project(band(head), pl.ds(0, width))
    pump(3)
    for i in range(4, 8):
        kv_turned[:, i * rows : (i + 1) * rows] = kv_both[i * rows : (i + 1) * rows, :].T
    out_ring.arrive(4)
    half = width // 2

    def out_part(of, i):
        return out_all.at[pl.ds(pl.multiple_of(of * width + i * half, 64), half)]

    for i in range(2):
        send(12 + i, out_part(head, i), out_part(head, i), across)
    send(16, out_all.at[band(head)], out_all.at[band(head)], mate)

    @pl.when(me > 0)
    def _():
        kv_copy.wait_recv()

    for i in range(4):
        kv_turned[:, i * rows : (i + 1) * rows] = kv_both[i * rows : (i + 1) * rows, :].T
    arrived(27, quarter(grad_group, 2), across)
    send(29, quarter(grad_group, 2), quarter(grad_group, 3), mate)

    def attend_tile(tile, carry):
        start = pl.multiple_of(tile * QUERY_TILE, QUERY_TILE)
        here = pl.ds(start, QUERY_TILE)
        span = pl.ds(start, SPAN)
        shape = (SPAN, QUERY_TILE)
        key = lax.broadcasted_iota(jnp.int32, shape, 0)
        query = lax.broadcasted_iota(jnp.int32, shape, 1)
        same = key_ids[span, :] == query_ids[:, here]
        allowed = same & (key > query) & (key <= query + WINDOW)
        bias[...] = jnp.where(allowed, 0.0, neg_fill)

        def attend_head(j, carry):
            lanes = pl.ds(pl.multiple_of(j * HEAD_DIM, HEAD_DIM), HEAD_DIM)
            scores = mul(kv_both[span, :HEAD_DIM], stream[here, lanes], NT)
            scores = scores * HEAD_DIM ** (-0.5) + bias[...]
            top = jnp.max(scores, axis=0, keepdims=True)
            expo = jnp.exp(scores - top)
            total = jnp.sum(expo, axis=0, keepdims=True)
            out = mul(kv_turned[HEAD_DIM:, span], expo.astype(low), NN) / total
            mixed[here, lanes] = out.T.astype(low)
            lse[j, :, here] = top + jnp.log(total)
            return carry

        return lax.fori_loop(0, heads, attend_head, carry)

    lax.fori_loop(0, group // QUERY_TILE, attend_tile, 0)

    def turn_back(i, carry):
        here = pl.ds(pl.multiple_of(i * rows, rows), rows)
        mixed_group[here, :] = mul(shuffle[:, here], mixed[...], TN).astype(low)
        return carry

    lax.fori_loop(0, 4, turn_back, 0)

    def mixed_part(of, i, size):
        return mixed_all.at[pl.ds(i * size, size), band(of)]

    for i in range(2):
        source = mixed_group.at[pl.ds(i * 2 * rows, 2 * rows)]
        send(17 + i, source, mixed_part(head, 1 - i, 2 * rows), across)
    for i in range(4):
        send(19 + i, quarter(mixed_group, i), mixed_part(head, i ^ 1, rows), mate)
    mixed_all[:, band(head)] = mixed_group[...]
    for i in range(2):
        arrived(12 + i, out_part(across_head, i), across)
        send(14 + i, out_part(across_head, i), out_part(across_head, i), mate)
    pump(4)
    arrived(16, out_all.at[band(mate_head)], mate)
    for i in range(2):
        arrived(14 + i, out_part(3 - head, i), mate)
    for i in range(4):
        arrived(19 + i, mixed_part(mate_head, i ^ 1, rows), mate)
    for i in range(2):
        arrived(17 + i, mixed_part(across_head, 1 - i, 2 * rows), across)
        for j in (2 - 2 * i, 3 - 2 * i):
            part = mixed_part(across_head, j, rows)
            send(23 + j, part, mixed_part(across_head, j ^ 1, rows), mate)
    for j in range(4):
        arrived(23 + j, mixed_part(3 - head, j ^ 1, rows), mate)

    def second(i, carry):
        here = pl.ds(pl.multiple_of((3 - i) * rows, rows), rows)
        resid[...] = tokens_group[here, :].astype(full) + mul(mixed_all[here, :], out_all[...], NN)
        values = resid[...]
        normed_group[here, :] = (values * inverse_norm(values) * gains[1:2, :]).astype(low)
        return carry

    lax.fori_loop(0, 4, second, 0)
    arrived(28, quarter(grad_group, 1), mate)
    arrived(29, quarter(grad_group, 3), mate)
    pump(5)
    own[2].wait()
    for ring in rings:
        ring.finish()
    for copy in copies:
        copy.wait_send()

    @pl.when(me < count - 1)
    def _():
        kv_copy.wait_send()


def forward_section(tokens, cotangent, gains, stacks, order, ids, count):
    rows = tokens.shape[0]
    group = 4 * rows
    width = QW // 4
    steps = count // 2
    gateup_rows = stacks[2].shape[0] // GRID * BLK
    down_parts = stacks[3].shape[0] // 8
    vmem = pl.BlockSpec(memory_space=pltpu.VMEM)
    hbm = pl.BlockSpec(memory_space=pl.ANY)
    outs = [
        ((2, D), full, vmem),
        ((rows, D), full, vmem),
        ((group, D), low, vmem),
        ((group, D), low, hbm),
        ((count, gateup_rows, D), low, hbm),
        ((count, down_parts, BLK, D // 2), low, hbm),
        ((group, width), low, vmem),
        ((width, QKV), low, vmem),
        ((D, D), low, vmem),
        ((group, width + 2 * HEAD_DIM), low, vmem),
        ((2 * group, 2 * HEAD_DIM), low, vmem),
        ((2 * HEAD_DIM, 2 * group), low, vmem),
        ((width // HEAD_DIM, 1, group), full, vmem),
        ((group, width), low, vmem),
        ((group, group), low, vmem),
        ((2 * group, 1), full, vmem),
        ((1, group), full, vmem),
    ]
    dma = pltpu.SemaphoreType.DMA
    return pl.pallas_call(
        functools.partial(forward_kernel, count),
        in_specs=[vmem] * 9,
        out_specs=[spec for _, _, spec in outs],
        out_shape=[jax.ShapeDtypeStruct(shape, kind) for shape, kind, _ in outs],
        scratch_shapes=[
            pltpu.VMEM((group, D), low),
            pltpu.VMEM((group, D), low),
            pltpu.VMEM((D, QKV), low),
            pltpu.VMEM((group, width + 2 * HEAD_DIM), low),
            pltpu.VMEM((group, width), low),
            pltpu.VMEM((group, D), low),
            pltpu.VMEM((SPAN, QUERY_TILE), full),
            pltpu.VMEM((8, D), full),
            pltpu.VMEM((QKV // 2, BLK), full),
            pltpu.VMEM((gateup_rows, D), low),
            pltpu.VMEM((down_parts, BLK, D // 2), low),
            pltpu.VMEM((4, count, 8, 128), full),
            dma((3,)),
            dma((5, 2, steps)),
            dma((5, 2, steps)),
            dma((30,)),
            dma((30,)),
            dma,
            dma,
        ],
        compiler_params=pltpu.CompilerParams(
            collective_id=0, has_side_effects=True, vmem_limit_bytes=58 * 1024 * 1024
        ),
        name="forward_section",
    )(tokens, cotangent, gains, *stacks, order, ids)


class SumRing:
    def __init__(self, count, view, first, buffers, send, recv):
        self.ring = Ring(count, None, None, None)
        self.steps = count // 2
        self.view = view
        self.first = first
        self.buffers = buffers
        self.rows = buffers.shape[2]
        self.send = send
        self.recv = recv
        self.copies = []

    def where(self, way):
        return self.ring.behind if way else self.ring.ahead

    def half(self, way):
        return self.buffers.at[way, 0, pl.ds(way * (self.rows // 2), self.rows // 2)]

    def copy(self, way, step, source, target):
        return remote(source, target, self.send.at[way, step], self.recv.at[way, step], self.where(way))

    def start(self):
        shard = self.ring.shard(self.steps)
        for way in range(2):
            copy = self.copy(way, 0, self.first(shard, way), self.half(way))
            copy.start()
            self.copies.append(copy)

    def arrived(self, way, step):
        target = self.buffers.at[way, step] if step else self.half(way)
        self.copy(way, step, target, target).wait_recv()

    def step(self, step):
        block = 48
        for way in range(2):
            self.arrived(way, step - 1)
            offset = self.steps - step
            local = self.view(self.ring.shard(-offset if way else offset))
            buffer = self.buffers.at[way, step - 1]

            def add(i, carry):
                here = pl.ds(pl.multiple_of(i * block, 16), block)
                buffer[here, :] = (local[here, :].astype(full) + buffer[here, :].astype(full)).astype(low)
                return carry

            def keep(i, carry):
                here = pl.ds(pl.multiple_of(i * block, 16), block)
                buffer[here, :] = local[here, :]
                return carry

            blocks = self.rows // block
            if step > 1:
                lax.fori_loop(0, blocks, add, 0)
            else:
                lax.fori_loop(way * (blocks // 2), (way + 1) * (blocks // 2), add, 0)
                lax.fori_loop((1 - way) * (blocks // 2), (2 - way) * (blocks // 2), keep, 0)
            copy = self.copy(way, step, buffer, self.buffers.at[way, step])
            copy.start()
            self.copies.append(copy)

    def finish(self, out):
        block = 48
        last = self.steps - 1
        for way in range(2):
            self.arrived(way, last)
        local = self.view(self.ring.shard(0))

        def add(i, carry):
            here = pl.ds(pl.multiple_of(i * block, 16), block)
            out[here, :] = (
                local[here, :].astype(full)
                + self.buffers[0, last, here, :].astype(full)
                + self.buffers[1, last, here, :].astype(full)
            )
            return carry

        lax.fori_loop(0, self.rows // block, add, 0)
        for copy in self.copies:
            copy.wait_send()


class StagedSumRing(SumRing):
    def __init__(self, count, parts, buffers, held, terms, load, send, recv):
        size = parts.shape[1] // 2
        first = lambda shard, part: parts.at[shard, pl.ds(part * size, size)]
        super().__init__(count, None, first, buffers, send, recv)
        self.parts = parts
        self.held = held
        self.terms = terms
        self.load = load
        self.last = [None, None]

    def fetch(self, way, offset):
        shard = self.ring.shard(-offset if way else offset)
        copy = pltpu.make_async_copy(
            self.parts.at[shard], self.terms.at[way], self.load.at[1, way]
        )
        copy.start()
        return copy

    def start(self):
        super().start()
        self.fetched = [self.fetch(way, self.steps - 1) for way in range(2)]

    def take(self, way, step):
        self.arrived(way, step)
        if self.last[way] is not None:
            self.last[way].wait_send()
        source, target = self.buffers.at[way, step], self.held.at[way]
        if step == 0:
            half = pl.ds(way * (self.rows // 2), self.rows // 2)
            source, target = self.half(way), self.held.at[way, half]
        copy = pltpu.make_async_copy(source, target, self.load.at[0, way])
        copy.start()
        return copy

    def step(self, step):
        block = 48
        taken = [self.take(way, step - 1) for way in range(2)]
        for way in range(2):
            taken[way].wait()
            self.fetched[way].wait()
            held, terms = self.held.at[way], self.terms.at[way]

            def add(i, carry):
                here = pl.ds(pl.multiple_of(i * block, 16), block)
                held[here, :] = (terms[here, :].astype(full) + held[here, :].astype(full)).astype(low)
                return carry

            def keep(i, carry):
                here = pl.ds(pl.multiple_of(i * block, 16), block)
                held[here, :] = terms[here, :]
                return carry

            blocks = self.rows // block
            if step > 1:
                lax.fori_loop(0, blocks, add, 0)
            else:
                lax.fori_loop(way * (blocks // 2), (way + 1) * (blocks // 2), add, 0)
                lax.fori_loop((1 - way) * (blocks // 2), (2 - way) * (blocks // 2), keep, 0)
            self.last[way] = self.copy(way, step, held, self.buffers.at[way, step])
            self.last[way].start()
            if step < self.steps - 1 or way == 0:
                self.fetched[way] = self.fetch(way, self.steps - 1 - step)

    def finish(self, out):
        block = 48
        taken = [self.take(way, self.steps - 1) for way in range(2)]
        for copy in taken:
            copy.wait()
        self.fetched[0].wait()

        def add(i, carry):
            here = pl.ds(pl.multiple_of(i * block, 16), block)
            out[here, :] = (
                self.terms[0, here, :].astype(full)
                + self.held[0, here, :].astype(full)
                + self.held[1, here, :].astype(full)
            )
            return carry

        lax.fori_loop(0, self.rows // block, add, 0)
        for copy in self.copies:
            copy.wait_send()


def backward_kernel(
    count,
    tokens,
    cotangent,
    gains,
    resid,
    normed_part,
    ffn_part,
    gateup_parts,
    down_parts,
    features,
    qkv_rows,
    out_rows,
    stream,
    kv_both,
    kv_turned,
    lse,
    mixed_group,
    shuffle,
    key_ids,
    query_ids,
    block_out,
    input_grad,
    gain_grads,
    gateup_grad,
    down_grad,
    qkv_grad,
    out_grad,
    gateup_sums,
    down_sums,
    gateup_held,
    gateup_terms,
    down_held,
    down_terms,
    part_quarter,
    qkv_local,
    out_local,
    qkv_sums,
    out_sums,
    sum_out,
    sum_in,
    proj_group,
    turned_grad,
    grad_stream,
    kv_total,
    kv_out,
    kv_in,
    stream_grad,
    kv_mate,
    all_grad,
    normed_grad,
    bias,
    load_sem,
    part_sem,
    ring_send,
    ring_recv,
    head_send,
    head_recv,
    kv_send,
    kv_recv,
):
    rows = tokens.shape[0]
    group = 4 * rows
    width = features.shape[1]
    heads = width // HEAD_DIM
    scale = HEAD_DIM ** (-0.5)
    query_grad = turned_grad
    feature_grad = grad_stream
    head = lax.axis_index("head")
    me = lax.axis_index("seq")
    mate_head = head + 1 - 2 * lax.rem(head, 2)
    across_head = lax.rem(head + 2, 4)
    mate = {"head": mate_head}
    across = {"head": across_head}
    corner = {"head": 3 - head}

    def lanes(of):
        return pl.ds(pl.multiple_of(of * width, 128), width)

    def quarter(i):
        return pl.ds(i * rows, rows)

    copies = []

    def send(index, source, target, where):
        copy = remote(source, target, head_send.at[index], head_recv.at[index], where)
        copy.start()
        copies.append(copy)

    def arrived(index, target, where):
        remote(target, target, head_send.at[index], head_recv.at[index], where).wait_recv()

    def shard_view(ref, columns):
        def view(shard, part=None):
            first = pl.multiple_of((shard // 2) * BLK, 32)
            at = pl.ds(pl.multiple_of(lax.rem(shard, 2) * columns, 128), columns)
            if part is None:
                return ref.at[pl.ds(first, BLK), at]
            return ref.at[pl.ds(pl.multiple_of(first + part * (BLK // 2), 16), BLK // 2), at]

        return view

    qkv_view = shard_view(qkv_local, QKV // 2)
    out_view = shard_view(out_local, D // 2)
    gateup_ring = StagedSumRing(
        count,
        gateup_parts,
        gateup_sums,
        gateup_held,
        gateup_terms,
        load_sem.at[0],
        ring_send.at[0],
        ring_recv.at[0],
    )
    down_ring = StagedSumRing(
        count,
        down_parts,
        down_sums,
        down_held,
        down_terms,
        load_sem.at[1],
        ring_send.at[1],
        ring_recv.at[1],
    )
    qkv_ring = SumRing(count, qkv_view, qkv_view, qkv_sums, ring_send.at[2], ring_recv.at[2])
    out_ring = SumRing(count, out_view, out_view, out_sums, ring_send.at[3], ring_recv.at[3])

    barrier = pltpu.get_barrier_semaphore()
    for where in (gateup_ring.where(0), gateup_ring.where(1), mate, across, corner):
        pl.semaphore_signal(barrier, inc=1, device_id=where, device_id_type=pl.DeviceIdType.MESH)

    @pl.when(me < count - 1)
    def _():
        pl.semaphore_signal(
            barrier, inc=1, device_id={"seq": me + 1}, device_id_type=pl.DeviceIdType.MESH
        )

    pl.semaphore_wait(barrier, 5 + (me + count - 1) // count)

    def fetch(value, i):
        copy = pltpu.make_async_copy(value.at[quarter(i)], part_quarter, part_sem)
        copy.start()
        copy.wait()
        return part_quarter[...].astype(full)

    def sum_first(base, slot, value):
        send(base, value.at[quarter(3)], sum_in.at[slot], mate)
        send(base + 1, value.at[quarter(1)], sum_in.at[slot + 1], mate)

    def sum_across(base, slot, value):
        own = fetch(value, 2)
        arrived(base, sum_in.at[slot], mate)
        sum_out[slot // 3] = (own + sum_in[slot].astype(full)).astype(low)
        send(base + 2, sum_out.at[slot // 3], sum_in.at[slot + 2], across)

    def sum_last(base, slot, value):
        own = fetch(value, 0)
        arrived(base + 1, sum_in.at[slot + 1], mate)
        own = own + sum_in[slot + 1].astype(full)
        arrived(base + 2, sum_in.at[slot + 2], across)
        return own + sum_in[slot + 2].astype(full)

    sum_first(0, 0, normed_part)
    gateup_ring.start()
    down_ring.start()
    sum_across(0, 0, normed_part)
    sum_first(3, 3, ffn_part)

    normed_two_grad = sum_last(0, 0, normed_part)
    values = resid[...]
    inverse = inverse_norm(values)
    gain_grads[1:2, :] = jnp.sum(normed_two_grad * values * inverse, axis=0, keepdims=True)
    input_grad[...] = cotangent[...].astype(full) + norm_back(
        values, inverse, gains[1:2, :], normed_two_grad
    )
    proj_group[quarter(0), :] = input_grad[...].astype(low)
    send(6, proj_group.at[quarter(0)], proj_group.at[quarter(2)], across)
    send(7, proj_group.at[quarter(0)], proj_group.at[quarter(1)], mate)
    gateup_ring.step(1)
    down_ring.step(1)
    sum_across(3, 3, ffn_part)

    def back_projection(i):
        turned_grad[quarter(i), :] = mul(proj_group[quarter(i), :], out_rows[...], NT).astype(low)

    back_projection(0)
    arrived(7, proj_group.at[quarter(1)], mate)
    back_projection(1)
    arrived(6, proj_group.at[quarter(2)], across)
    send(8, proj_group.at[quarter(2)], proj_group.at[quarter(3)], mate)
    back_projection(2)
    arrived(8, proj_group.at[quarter(3)], mate)
    back_projection(3)

    def turn(i, carry):
        here = pl.ds(pl.multiple_of(i * rows, rows), rows)
        grad_stream[here, :] = mul(shuffle[here, :], turned_grad[...], NN).astype(low)
        return carry

    lax.fori_loop(0, 4, turn, 0)
    for i in range(3):
        at = slice(i * (D // 3), (i + 1) * (D // 3))
        out_local[:, at] = mul(mixed_group[...], proj_group[:, at], TN).astype(low)
    out_ring.start()
    gateup_ring.step(2)
    down_ring.step(2)

    kv_total[...] = jnp.zeros_like(kv_total)

    def back_tile(tile, carry):
        start = pl.multiple_of(tile * QUERY_TILE, QUERY_TILE)
        here = pl.ds(start, QUERY_TILE)
        span = pl.ds(start, SPAN)
        shape = (SPAN, QUERY_TILE)
        key = lax.broadcasted_iota(jnp.int32, shape, 0)
        query = lax.broadcasted_iota(jnp.int32, shape, 1)
        same = key_ids[span, :] == query_ids[:, here]
        allowed = same & (key > query) & (key <= query + WINDOW)
        bias[...] = jnp.where(allowed, 0.0, neg_fill)

        def back_head(j, carry):
            at = pl.ds(pl.multiple_of(j * HEAD_DIM, HEAD_DIM), HEAD_DIM)
            queries = stream[here, at]
            grads = grad_stream[here, at]
            scores = mul(kv_both[span, :HEAD_DIM], queries, NT) * scale + bias[...]
            probs = jnp.exp(scores - lse[j, :, here])
            prob_grad = mul(kv_both[span, HEAD_DIM:], grads, NT)
            delta = jnp.sum(probs * prob_grad, axis=0, keepdims=True)
            score_grad = (probs * (prob_grad - delta)).astype(low)
            turned = mul(kv_turned[:HEAD_DIM, span], score_grad, NN) * scale
            query_grad[here, at] = turned.T.astype(low)
            kv_total[span, :HEAD_DIM] += mul(score_grad, queries, NN) * scale
            kv_total[span, HEAD_DIM:] += mul(probs.astype(low), grads, NN)
            return carry

        return lax.fori_loop(0, heads, back_head, carry)

    lax.fori_loop(0, group // QUERY_TILE, back_tile, 0)
    kv_out[...] = kv_total[:group, :].astype(low)
    kv_copy = remote(kv_out, kv_in, kv_send, kv_recv, {"seq": lax.rem(me + count - 1, count)})

    @pl.when(me > 0)
    def _():
        kv_copy.start()

    def turn_back(i, carry):
        here = pl.ds(pl.multiple_of(i * rows, rows), rows)
        all_grad[here, lanes(head)] = mul(shuffle[:, here], query_grad[...], TN).astype(low)
        return carry

    lax.fori_loop(0, 4, turn_back, 0)

    def swapped(index, ref, columns, distance, where):
        for i in range(4):
            send(
                index + i,
                ref.at[quarter(i), columns],
                ref.at[quarter(i ^ distance), columns],
                where,
            )

    def swapped_arrived(index, ref, columns, distance, where):
        for i in range(4):
            arrived(index + i, ref.at[quarter(i ^ distance), columns], where)

    swapped(9, all_grad, lanes(head), 2, across)
    swapped(13, all_grad, lanes(head), 1, mate)
    gateup_ring.step(3)
    down_ring.step(3)
    out_ring.step(1)

    @pl.when(me < count - 1)
    def _():
        kv_copy.wait_recv()
        kv_total[pl.ds(group, group), :] += kv_in[...].astype(full)

    stream_grad[...] = kv_total[pl.ds(group, group), :].astype(low)

    def turn_keys(i, carry):
        here = pl.ds(pl.multiple_of(i * rows, rows), rows)
        kv_mate[0, here, :] = mul(shuffle[:, here], stream_grad[...], TN).astype(low)
        return carry

    lax.fori_loop(0, 4, turn_keys, 0)
    for i in range(4):
        send(17 + i, kv_mate.at[0, quarter(i)], kv_mate.at[1, quarter(i ^ 1)], mate)
    for i in range(4):
        arrived(17 + i, kv_mate.at[1, quarter(i ^ 1)], mate)
    kv_total[pl.ds(0, group), :] = kv_mate[0].astype(full) + kv_mate[1].astype(full)
    kv_mate[2] = kv_total[pl.ds(0, group), :].astype(low)
    for i in range(4):
        send(21 + i, kv_mate.at[2, quarter(i)], kv_mate.at[3, quarter(i ^ 2)], across)
    swapped_arrived(9, all_grad, lanes(across_head), 2, across)
    swapped(25, all_grad, lanes(across_head), 1, mate)
    out_ring.step(2)
    swapped_arrived(13, all_grad, lanes(mate_head), 1, mate)
    for i in range(4):
        arrived(21 + i, kv_mate.at[3, quarter(i ^ 2)], across)
    all_grad[:, QW:] = (kv_total[pl.ds(0, group), :] + kv_mate[3].astype(full)).astype(low)
    swapped_arrived(25, all_grad, lanes(3 - head), 1, mate)

    for i in range(2):
        at = slice(i * (QKV // 2), (i + 1) * (QKV // 2))
        qkv_local[:, at] = mul(features[...], all_grad[:, at], TN).astype(low)
    qkv_ring.start()
    out_ring.step(3)
    for i, where in ((2, across), (3, corner), (1, mate)):
        feature_grad[quarter(i), :] = mul(all_grad[quarter(i), :], qkv_rows[...], NT).astype(low)
        send(28 + i, feature_grad.at[quarter(i)], normed_grad.at[:, lanes(head)], where)
    normed_grad[:, lanes(head)] = mul(all_grad[quarter(0), :], qkv_rows[...], NT).astype(low)
    block_out[...] = (resid[...] + sum_last(3, 3, ffn_part)).astype(low)
    gateup_ring.finish(gateup_grad)
    down_ring.finish(down_grad)
    qkv_ring.step(1)
    for i, where, of in ((2, across, across_head), (3, corner, 3 - head), (1, mate, mate_head)):
        arrived(28 + i, normed_grad.at[:, lanes(of)], where)
    qkv_ring.step(2)
    normed_one_grad = normed_grad[...].astype(full)
    values = tokens[...].astype(full)
    inverse = inverse_norm(values)
    gain_grads[0:1, :] = jnp.sum(normed_one_grad * values * inverse, axis=0, keepdims=True)
    input_grad[...] += norm_back(values, inverse, gains[0:1, :], normed_one_grad)
    qkv_ring.step(3)
    out_ring.finish(out_grad)
    qkv_ring.finish(qkv_grad)
    for copy in copies:
        copy.wait_send()

    @pl.when(me > 0)
    def _():
        kv_copy.wait_send()


def backward_section(count, *values):
    (tokens, cotangent, gains, resid, normed_part, ffn_part, gateup_parts, down_parts) = values[:8]
    rows = tokens.shape[0]
    group = 4 * rows
    width = QW // 4
    steps = count // 2
    vmem = pl.BlockSpec(memory_space=pltpu.VMEM)
    hbm = pl.BlockSpec(memory_space=pl.ANY)
    shard = gateup_parts.shape[1:]
    down_shard = down_parts.shape[1:]
    outs = [
        ((rows, D), low),
        ((rows, D), full),
        ((2, D), full),
        (shard, full),
        (down_shard, full),
        ((BLK, QKV // 2), full),
        ((BLK, D // 2), full),
        ((2, steps) + shard, low),
        ((2, steps) + down_shard, low),
    ]
    dma = pltpu.SemaphoreType.DMA
    return pl.pallas_call(
        functools.partial(backward_kernel, count),
        in_specs=[vmem] * 4 + [hbm] * 4 + [vmem] * 11,
        out_specs=[vmem] * 7 + [hbm] * 2,
        out_shape=[jax.ShapeDtypeStruct(shape, kind) for shape, kind in outs],
        scratch_shapes=[
            pltpu.VMEM((2,) + shard, low),
            pltpu.VMEM((2,) + shard, low),
            pltpu.VMEM((2,) + down_shard, low),
            pltpu.VMEM((2,) + down_shard, low),
            pltpu.VMEM((rows, D), low),
            pltpu.VMEM((width, QKV), low),
            pltpu.VMEM((width, D), low),
            pltpu.VMEM((2, steps, BLK, QKV // 2), low),
            pltpu.VMEM((2, steps, BLK, D // 2), low),
            pltpu.VMEM((2, rows, D), low),
            pltpu.VMEM((6, rows, D), low),
            pltpu.VMEM((group, D), low),
            pltpu.VMEM((group, width), low),
            pltpu.VMEM((group, width), low),
            pltpu.VMEM((2 * group, 2 * HEAD_DIM), full),
            pltpu.VMEM((group, 2 * HEAD_DIM), low),
            pltpu.VMEM((group, 2 * HEAD_DIM), low),
            pltpu.VMEM((group, 2 * HEAD_DIM), low),
            pltpu.VMEM((4, group, 2 * HEAD_DIM), low),
            pltpu.VMEM((group, QKV), low),
            pltpu.VMEM((rows, D), low),
            pltpu.VMEM((SPAN, QUERY_TILE), full),
            dma((2, 2, 2)),
            dma,
            dma((4, 2, steps)),
            dma((4, 2, steps)),
            dma((32,)),
            dma((32,)),
            dma,
            dma,
        ],
        compiler_params=pltpu.CompilerParams(
            collective_id=1, has_side_effects=True, vmem_limit_bytes=60 * 1024 * 1024
        ),
        name="backward_section",
    )(*values)


def ffn_kernel(
    normed, cotangent, gateup, down, hidden, gate_up_grad, normed_part, ffn_part, normed_sum, ffn_sum
):
    units = down.shape[0]
    tile = next(u for u in (4, 3, 2, 1) if units % u == 0)
    size = normed.shape[0]
    half = D // 2
    root = (2.0 / 3.141592653589793) ** 0.5

    def step(c, carry):
        here = pl.ds(pl.multiple_of(c * tile * BLK, 32), tile * BLK)
        pair = pl.ds(pl.multiple_of(c * tile * 2 * BLK, 64), 2 * tile * BLK)
        weights = gateup[pair, :]
        parts = [down[pl.ds(c * tile, tile), i].reshape(tile * BLK, half) for i in range(2)]
        both = mul(weights, normed[...], NT).reshape(tile, 2, BLK, size)
        gate = both[:, 0].reshape(tile * BLK, size)
        upper = both[:, 1].reshape(tile * BLK, size)
        grad = mul(parts[0], cotangent[:, :half], NT) + mul(parts[1], cotangent[:, half:], NT)
        square = gate * gate
        bent = jnp.tanh(root * gate * (1.0 + 0.044715 * square))
        share = 0.5 * (1.0 + bent)
        active = gate * share
        slope = share + 0.5 * gate * (1.0 - bent * bent) * (root * (1.0 + 0.134145 * square))
        units_out = (active * upper).astype(low)
        grads = [(grad * upper * slope).astype(low), (grad * active).astype(low)]
        grads = [g.reshape(tile, 1, BLK, size) for g in grads]
        grads = jnp.concatenate(grads, axis=1).reshape(2 * tile * BLK, size)
        hidden[here, :] = units_out
        gate_up_grad[pair, :] = grads
        first = c == 0
        term = mul(grads, weights, TN)
        terms = [mul(units_out, part, TN) for part in parts]

        @pl.when(first)
        def _():
            normed_sum[...] = term
            ffn_sum[:, :half] = terms[0]
            ffn_sum[:, half:] = terms[1]

        @pl.when(jnp.logical_not(first))
        def _():
            normed_sum[...] += term
            ffn_sum[:, :half] += terms[0]
            ffn_sum[:, half:] += terms[1]

        return carry

    lax.fori_loop(0, units // tile, step, 0)
    normed_part[...] = normed_sum[...].astype(low)
    ffn_part[...] = ffn_sum[...].astype(low)


def feed_forward(normed, cotangent, gateup, down):
    group = normed.shape[0]
    units = down.shape[0]
    size = min(512, group)
    rows = pl.BlockSpec((size, D), lambda t: (t, 0))
    once = pl.Buffered(1)
    return pl.pallas_call(
        ffn_kernel,
        grid=(group // size,),
        in_specs=[
            rows,
            rows,
            pl.BlockSpec(gateup.shape, lambda t: (0, 0), pipeline_mode=once),
            pl.BlockSpec(down.shape, lambda t: (0, 0, 0, 0), pipeline_mode=once),
        ],
        out_specs=[
            pl.BlockSpec((units * BLK, size), lambda t: (0, t)),
            pl.BlockSpec((2 * units * BLK, size), lambda t: (0, t)),
            rows,
            rows,
        ],
        out_shape=[
            jax.ShapeDtypeStruct((units * BLK, group), low),
            jax.ShapeDtypeStruct((2 * units * BLK, group), low),
            jax.ShapeDtypeStruct((group, D), low),
            jax.ShapeDtypeStruct((group, D), low),
        ],
        scratch_shapes=[pltpu.VMEM((size, D), full), pltpu.VMEM((size, D), full)],
        compiler_params=pltpu.CompilerParams(vmem_limit_bytes=58 * 1024 * 1024),
        cost_estimate=pl.CostEstimate(
            flops=12 * units * BLK * group * D,
            bytes_accessed=40 << 20,
            transcendentals=units * BLK * group,
        ),
        name="feed_forward",
    )(normed, cotangent, gateup, down)


def update_kernel(
    rate, turned, w_ref, g_ref, l_ref, r_ref, lr_ref, rr_ref, ln_ref, rn_ref, wn_ref
):
    count, rows, columns = w_ref.shape
    blocks = g_ref[...].T.reshape(count, g_ref.shape[1] // count, g_ref.shape[0])
    for b in range(count):
        grad = blocks[b]
        other = grad.T
        if not turned:
            grad, other = other, grad
        square = jnp.sum(jnp.sum(grad * grad, axis=1, keepdims=True), axis=0, keepdims=True)
        square = square * (1.0 / (rows * columns)) + stat_eps
        grad = grad.astype(low)
        other = other.astype(low)
        ln_ref[b] = 0.5 * l_ref[b] + mul(grad, other, NN) * (0.5 / (columns * square))
        rn_ref[b] = 0.5 * r_ref[b] + mul(other, grad, NN) * (0.5 / (rows * square))
        step = mul(lr_ref[b].astype(low), grad, NN).astype(low)
        step = mul(step, rr_ref[b].astype(low), NN)
        wn_ref[b] = w_ref[b] - step * (rate * lax.rsqrt(square))


def update(weight, grad, left, right, left_root, right_root, rate, turned=False):
    count, rows, columns = weight.shape
    if grad.ndim == 3:
        grad = grad.transpose(1, 0, 2).reshape(rows, count * columns)
    height = columns if turned else rows
    batch = count // (grad.shape[0] // height)
    spec = lambda i, j: pl.BlockSpec((batch, i, j), lambda b: (b, 0, 0))
    return pl.pallas_call(
        functools.partial(update_kernel, rate, turned),
        grid=(count // batch,),
        in_specs=[
            spec(rows, columns),
            pl.BlockSpec((height, grad.shape[1]), lambda b: (b, 0)),
            spec(rows, rows),
            spec(columns, columns),
            spec(rows, rows),
            spec(columns, columns),
        ],
        out_specs=[spec(rows, rows), spec(columns, columns), spec(rows, columns)],
        out_shape=[
            jax.ShapeDtypeStruct(left.shape, full),
            jax.ShapeDtypeStruct(right.shape, full),
            jax.ShapeDtypeStruct(weight.shape, full),
        ],
        compiler_params=pltpu.CompilerParams(vmem_limit_bytes=58 * 1024 * 1024),
        cost_estimate=pl.CostEstimate(
            flops=16 * count * 256 * 256 * 128,
            bytes_accessed=36 * count * rows * 128,
            transcendentals=0,
        ),
        name="update",
    )(weight, grad, left, right, left_root, right_root)


def norm_back(values, inverse, gain, grad):
    scaled = gain * grad
    mean = jnp.mean(values * scaled, axis=-1, keepdims=True)
    return inverse * scaled - values * (inverse * inverse * inverse * mean)


def inverse_norm(values):
    return lax.rsqrt(jnp.mean(values * values, axis=-1, keepdims=True) + norm_eps)


def forward_steps(tokens, cotangent, attn_gain, ffn_gain, stacks, token_order, sequence_ids):
    qkv_stack, out_stack, gateup_stack, down_stack = stacks
    row_count = tokens.shape[0]
    head_count = lax.axis_size("head")
    seq_count = lax.axis_size("seq")
    group = row_count * head_count
    head_index = lax.axis_index("head")
    local_width = QW // head_count
    seq_index = lax.axis_index("seq")
    gains = jnp.concatenate([attn_gain, ffn_gain]).astype(low).astype(full)[None]
    gains = lax.all_to_all(
        jnp.broadcast_to(gains, (head_count * seq_count, gains.shape[1])),
        ("head", "seq"),
        split_axis=0,
        concat_axis=0,
        tiled=True,
    )
    own_gains = attn_gain.shape[0]
    gain_one = gains[:, :own_gains].reshape(1, D)
    gain_two = gains[:, own_gains:].reshape(1, D)


    ids_own = lax.dynamic_slice_in_dim(sequence_ids, seq_index * group, group, 0)
    ids_before = lax.dynamic_slice_in_dim(
        sequence_ids, jnp.maximum(seq_index - 1, 0) * group, group, 0
    )
    ids_before = jnp.where(seq_index > 0, ids_before, -1)
    key_ids = jnp.concatenate([ids_before, ids_own])[:, None]
    query_ids = ids_own[None, :]
    qkv_rows = joined_halves(gather_rows(qkv_stack, 8, to_columns))
    out_rows = joined_halves(gather_rows(out_stack, 8, to_columns))
    gateup = gather_rows(gateup_stack, 16, to_units)
    down = gather_rows(down_stack, 8, to_columns)
    tokens_float = tokens.astype(full)
    normed_one = (tokens_float * inverse_norm(tokens_float) * gain_one).astype(low)
    normed_one_group = jnp.concatenate(head_gather(normed_one))
    feature_start = head_index * local_width
    features = lax.dynamic_slice_in_dim(normed_one_group, feature_start, local_width, 1)
    weights = in_order(head_gather(qkv_rows), 0)
    weights = jnp.concatenate(
        [lax.dynamic_slice_in_dim(weights, feature_start, local_width, 1), weights[:, QW:]], axis=1
    )
    projected = mul(normed_one_group, weights, NN, low)
    buffer_rows = ((token_order // row_count) ^ head_index) * row_count + token_order % row_count
    shuffle = (
        buffer_rows[:, None] == lax.broadcasted_iota(jnp.int32, (group, group), 1)
    ).astype(low)
    stream = mul(shuffle, projected, NN, low)
    kv_stream = stream[:, local_width:]
    kv_before = lax.ppermute(kv_stream, "seq", [(i, i + 1) for i in range(seq_count - 1)])
    kv_both = jnp.concatenate([kv_before, kv_stream], axis=0)
    kv_turned = kv_both.T
    mixed_stream, lse = attend(stream[:, :local_width], kv_both, kv_turned, key_ids, query_ids)
    mixed_group = mul(shuffle, mixed_stream, TN, low)
    part = mul(mixed_group, out_rows, NN, low)
    resid = tokens_float + head_sum([part[i * row_count :][:row_count] for i in range(4)])
    normed_two = (resid * inverse_norm(resid) * gain_two).astype(low)
    normed_group = jnp.concatenate(head_gather(normed_two))
    grad_group = jnp.concatenate(head_gather(cotangent))
    section = (
        jnp.concatenate([gain_one, gain_two]),
        resid,
        normed_group,
        grad_group,
        gateup,
        down,
        features,
        qkv_rows,
        out_rows,
        stream,
        kv_both,
        kv_turned,
        lse,
        mixed_group,
        shuffle,
        key_ids,
        query_ids,
    )
    return section


def backward_steps(
    tokens,
    cotangent,
    gains,
    resid,
    normed_part,
    ffn_part,
    gateup_wgrad,
    down_wgrad,
    features,
    qkv_rows,
    out_rows,
    stream,
    kv_both,
    kv_turned,
    lse,
    mixed_group,
    shuffle,
    key_ids,
    query_ids,
    counts,
):
    row_count = tokens.shape[0]
    group = row_count * lax.axis_size("head")
    seq_count = lax.axis_size("seq")
    local_width = features.shape[1]
    query_stream = stream[:, :local_width]
    gain_one, gain_two = gains[0], gains[1]
    tokens_float = tokens.astype(full)
    inverse_one = inverse_norm(tokens_float)
    inverse_two = inverse_norm(resid)
    normed_two_grad = head_sum([normed_part[i * row_count :][:row_count] for i in range(4)])
    gateup_grad_own = sum_rows(gateup_wgrad, counts[2], 16, from_units)
    down_grad_own = sum_rows(down_wgrad, counts[3], 8, from_columns)
    ffn_out = head_sum([ffn_part[i * row_count :][:row_count] for i in range(4)])
    block_out = (resid + ffn_out).astype(low)

    resid_grad = cotangent.astype(full) + norm_back(resid, inverse_two, gain_two, normed_two_grad)
    gain_two_grad = jnp.sum(normed_two_grad * resid * inverse_two, axis=0)
    proj_grad = resid_grad.astype(low)
    proj_grad_group = jnp.concatenate(head_gather(proj_grad))
    mixed_grad_group = mul(proj_grad_group, out_rows, NT, low)
    mixed_grad_stream = mul(shuffle, mixed_grad_group, NN, low)
    out_wgrad = split_halves(mul(mixed_group, proj_grad_group, TN, low), BLK)
    out_grad_own = sum_rows(out_wgrad, counts[1], 8, from_columns)

    query_grad, kv_grad = attend_back(
        query_stream, mixed_grad_stream, kv_both, kv_turned, key_ids, query_ids, lse
    )
    kv_later = lax.ppermute(
        kv_grad[:group].astype(low), "seq", [(i, i - 1) for i in range(1, seq_count)]
    )
    kv_grad = (kv_grad[group:] + kv_later.astype(full)).astype(low)
    grad_local = mul(shuffle, jnp.concatenate([query_grad, kv_grad], axis=1), TN, low)
    gathered = head_gather(grad_local)

    def own_order(value, j):
        quarters = [value[i * row_count :][:row_count] for i in range(4)]
        return jnp.concatenate([quarters[i ^ j] for i in range(4)])

    gathered = [own_order(value, j) for j, value in enumerate(gathered)]
    kv_total = sum(value[:, local_width:].astype(full) for value in gathered).astype(low)
    qkv_grad = jnp.concatenate(
        [in_order([value[:, :local_width] for value in gathered], 1), kv_total], axis=1
    )
    qkv_wgrad = split_halves(mul(features, qkv_grad, TN, low), BLK)
    qkv_grad_own = sum_rows(qkv_wgrad, counts[0], 8, from_columns)
    feature_grad = mul(qkv_grad, qkv_rows, NT, low)
    order = (0, 2, 1, 3)
    feature_parts = head_exchange([feature_grad[i * row_count :][:row_count] for i in range(4)])
    normed_one_grad = in_order([feature_parts[order.index(j)] for j in range(4)], 1).astype(full)
    input_grad = resid_grad + norm_back(tokens_float, inverse_one, gain_one, normed_one_grad)
    gain_one_grad = jnp.sum(normed_one_grad * tokens_float * inverse_one, axis=0)
    return (
        block_out,
        input_grad,
        jnp.stack([gain_one_grad, gain_two_grad]),
        gateup_grad_own,
        down_grad_own,
        qkv_grad_own,
        out_grad_own,
    )


def on_device(
    tokens,
    cotangent,
    attn_gain,
    ffn_gain,
    qkv_stack,
    out_stack,
    gateup_stack,
    down_stack,
    qkv_left,
    qkv_right,
    out_left,
    out_right,
    gateup_left,
    gateup_right,
    down_left,
    down_right,
    qkv_left_root,
    qkv_right_root,
    out_left_root,
    out_right_root,
    gateup_left_root,
    gateup_right_root,
    down_left_root,
    down_right_root,
    sequence_ids,
    token_order,
):
    row_count = tokens.shape[0]
    head_count = lax.axis_size("head")
    seq_count = lax.axis_size("seq")
    device_count = head_count * seq_count
    group = row_count * head_count
    seq_index = lax.axis_index("seq")
    local_width = QW // head_count

    own_gains = attn_gain.shape[0]
    stacks = (qkv_stack, out_stack, gateup_stack, down_stack)
    whole_rows = all(s.shape[0] % u == 0 for s, u in zip(stacks, (8, 8, 16, 8)))
    if whole_rows:
        tile = jnp.concatenate([attn_gain[None], ffn_gain[None]])
        section = forward_section(
            tokens,
            cotangent,
            jnp.pad(tile, ((0, 6), (0, 128 - own_gains))),
            stacks,
            token_order[None, :],
            sequence_ids[None, :],
            seq_count,
        )
    else:
        section = forward_steps(
            tokens, cotangent, attn_gain, ffn_gain, stacks, token_order, sequence_ids
        )
    (
        gains_both,
        resid,
        normed_group,
        grad_group,
        gateup,
        down,
        features,
        qkv_rows,
        out_all,
        stream,
        kv_both,
        kv_turned,
        lse,
        mixed_group,
        shuffle,
        key_ids,
        query_ids,
    ) = section
    gateup = gateup.reshape(-1, D)
    down = down.reshape(-1, 2, BLK, D // 2)
    unit_count = down.shape[0]
    hidden, gate_up_grad, normed_part, ffn_part = feed_forward(
        normed_group, grad_group, gateup, down
    )
    gateup_wgrad = mul(gate_up_grad, normed_group, NN, low)
    down_wgrad = split_halves(mul(hidden, grad_group, NN, low), BLK)
    out_rows = out_all
    if whole_rows:
        start = lax.axis_index("head") * local_width
        out_rows = lax.dynamic_slice_in_dim(out_all, start, local_width, 0)
    kept = (features, qkv_rows, out_rows, stream, kv_both, kv_turned, lse, mixed_group, shuffle)
    counts = [s.shape[0] for s in stacks]
    if not whole_rows:
        gateup_wgrad = gateup_wgrad.reshape(2 * unit_count, BLK, D)
    if whole_rows:
        (block_out, input_grad, gain_grads, gateup_own, down_own, qkv_own, out_own, *_) = (
            backward_section(
                seq_count,
                tokens,
                cotangent,
                gains_both,
                resid,
                normed_part,
                ffn_part,
                gateup_wgrad.reshape(seq_count, -1, D),
                down_wgrad.reshape(seq_count, -1, D // 2),
                *kept,
                key_ids,
                query_ids,
            )
        )
        gateup_grad_own, down_grad_own = gateup_own, down_own
        qkv_grad_own, out_grad_own = qkv_own, out_own
    else:
        section = backward_steps(
            tokens, cotangent, gains_both, resid, normed_part, ffn_part, gateup_wgrad, down_wgrad, *kept,
            key_ids, query_ids, counts,
        )
        (block_out, input_grad, gain_grads, gateup_grad_own, down_grad_own, qkv_grad_own, out_grad_own) = section
    gain_one_grad, gain_two_grad = gain_grads[0], gain_grads[1]
    gain_grads = jnp.concatenate(
        [gain_one_grad.reshape(device_count, -1), gain_two_grad.reshape(device_count, -1)], axis=1
    )
    gain_grads = lax.all_to_all(
        gain_grads, ("head", "seq"), split_axis=0, concat_axis=0, tiled=True
    )
    gain_grads = jnp.sum(gain_grads, axis=0)

    gateup_new = update(
        gateup_stack,
        gateup_grad_own,
        gateup_left,
        gateup_right,
        gateup_left_root,
        gateup_right_root,
        0.5 * D ** (-0.5),
        whole_rows,
    )
    down_new = update(
        down_stack,
        down_grad_own,
        down_left,
        down_right,
        down_left_root,
        down_right_root,
        0.5 * FF ** (-0.5),
    )
    out_new = update(
        out_stack,
        out_grad_own,
        out_left,
        out_right,
        out_left_root,
        out_right_root,
        0.5 * (QW // 64) ** (-0.5),
    )
    qkv_new = update(
        qkv_stack,
        qkv_grad_own,
        qkv_left,
        qkv_right,
        qkv_left_root,
        qkv_right_root,
        0.5 * D ** (-0.5),
    )
    return (
        (block_out, input_grad, gain_grads[:own_gains], gain_grads[own_gains:])
        + tuple(qkv_new)
        + tuple(out_new)
        + tuple(gateup_new)
        + tuple(down_new)
    )


def solution(mesh):
    rows = P(("seq", "head"), None)
    gain = P(("head", "seq"))
    blocks = P(("head", "seq"), None, None)
    return jax.shard_map(
        on_device,
        mesh=mesh,
        in_specs=(rows, rows, gain, gain) + (blocks,) * 20 + (P(), P("seq")),
        out_specs=(rows, rows, gain, gain) + (blocks,) * 12,
        check_vma=False,
    )
```

```python
import functools

import jax
import jax.numpy as jnp
from jax import lax
from jax.experimental import pallas as pl
from jax.experimental.pallas import tpu as pltpu
from jax.sharding import PartitionSpec as P

D = 1536
HEAD_DIM = 128
FF = 4608
WINDOW = 1024
GRID = 16
QW = 1536
QKV = 1792
BLK = 96
BQ = 112
BH = 96
NU = 48

norm_eps = 1e-06
stat_eps = 1e-06
neg_fill = -1e30

QUERY_TILE = 256
SPAN = WINDOW + QUERY_TILE

low = jnp.bfloat16
full = jnp.float32

NT = (((1,), (1,)), ((), ()))
NN = (((1,), (0,)), ((), ()))
TN = (((0,), (0,)), ((), ()))


def mul(a, b, dims, kind=full):
    return lax.dot_general(a, b, dims, preferred_element_type=kind)


def ring_place(index, count):
    return jnp.where(index % 2 == 0, index // 2, count - 1 - index // 2)


def ring_index(place, count):
    return jnp.where(place < count // 2, 2 * place, 2 * (count - 1 - place) + 1)


def ring_routes(count):
    order = [i for i in range(0, count, 2)] + [i for i in range(count - 1, 0, -2)]
    up = [(order[i], order[(i + 1) % count]) for i in range(count)]
    return up, [(b, a) for a, b in up]


def seq_gather(shard):
    count = lax.axis_size("seq")
    rows = shard.shape[0]
    half = rows // 2
    me = lax.axis_index("seq")
    place = ring_place(me, count)
    up, down = ring_routes(count)
    out = jnp.zeros((count,) + shard.shape, shard.dtype)
    out = lax.dynamic_update_slice(out, shard[None], (me, 0, 0))
    ahead = shard
    behind = shard
    for step in range(1, count // 2):
        ahead = lax.ppermute(ahead, "seq", up)
        behind = lax.ppermute(behind, "seq", down)
        out = lax.dynamic_update_slice(
            out, ahead[None], (ring_index((place - step + count) % count, count), 0, 0)
        )
        out = lax.dynamic_update_slice(
            out, behind[None], (ring_index((place + step) % count, count), 0, 0)
        )
    ahead = lax.ppermute(ahead[:half], "seq", up)
    behind = lax.ppermute(behind[half:], "seq", down)
    far = ring_index((place + count // 2) % count, count)
    out = lax.dynamic_update_slice(out, ahead[None], (far, 0, 0))
    return lax.dynamic_update_slice(out, behind[None], (far, half, 0))


def seq_sum(parts):
    count, rows = parts.shape[:2]
    half = rows // 2
    place = ring_place(lax.axis_index("seq"), count)
    up, down = ring_routes(count)

    def part(offset):
        index = ring_index((place + offset + count) % count, count)
        return lax.dynamic_slice_in_dim(parts, index, 1, 0)[0]

    far = part(count // 2)
    ahead = lax.ppermute(far[:half], "seq", up)
    behind = lax.ppermute(far[half:], "seq", down)
    for offset in range(count // 2 - 1, 0, -1):
        local = part(offset)
        if ahead.shape[0] == rows:
            local = (local.astype(full) + ahead.astype(full)).astype(low)
        else:
            local = jnp.concatenate(
                [(local[:half].astype(full) + ahead.astype(full)).astype(low), local[half:]]
            )
        ahead = lax.ppermute(local, "seq", up)
        local = part(-offset)
        if behind.shape[0] == rows:
            local = (local.astype(full) + behind.astype(full)).astype(low)
        else:
            local = jnp.concatenate(
                [local[:half], (local[half:].astype(full) + behind.astype(full)).astype(low)]
            )
        behind = lax.ppermute(local, "seq", down)
    return part(0).astype(full) + ahead.astype(full) + behind.astype(full)


def gather_rows(stack, unit, layout):
    short = stack.astype(low)
    if stack.shape[0] % unit == 0:
        shard = layout(short)
        rows = shard.reshape(-1, shard.shape[-1])
        out = seq_gather(rows)
        return out.reshape((-1,) + shard.shape[1:])
    return layout(lax.all_gather(short, "seq", axis=0, tiled=True))


def sum_rows(rows, local, unit, back):
    count = lax.axis_size("seq")
    if local % unit == 0:
        own = seq_sum(rows.reshape(count, -1, rows.shape[-1]))
        return back(own.reshape((-1,) + rows.shape[1:]))
    return lax.psum_scatter(back(rows), "seq", scatter_dimension=0, tiled=True).astype(full)


def to_columns(stack):
    n, i, j = stack.shape
    return stack.reshape(n // 8, 8, i, j).transpose(0, 2, 1, 3).reshape(n // 8, i, 8 * j)


def from_columns(rows):
    n, i, j = rows.shape
    return rows.reshape(n, i, 8, j // 8).transpose(0, 2, 1, 3).reshape(n * 8, i, j // 8)


def to_units(stack):
    n, i, j = stack.shape
    return stack.reshape(n // 16, 16, i, j).transpose(0, 3, 1, 2).reshape(n // 16, j, 16 * i)


def from_units(rows):
    n, j, i = rows.shape
    return rows.reshape(n, j, 16, i // 16).transpose(0, 2, 3, 1).reshape(n * 16, i // 16, j)


def joined_halves(rows):
    n, i, j = rows.shape
    return rows.reshape(n // 2, 2, i, j).transpose(0, 2, 1, 3).reshape(n // 2 * i, 2 * j)


def split_halves(matrix, i):
    rows, columns = matrix.shape
    half = columns // 2
    parts = [matrix[:, at : at + half].reshape(rows // i, i, half) for at in (0, half)]
    return jnp.stack(parts, axis=1).reshape(2 * rows // i, i, half)


def to_partner(value, which):
    count = lax.axis_size("head")
    return lax.ppermute(value, "head", [(i, i ^ which) for i in range(count)])


def head_gather(value):
    across = to_partner(value, 2)
    mate = to_partner(value, 1)
    return value, mate, across, to_partner(across, 1)


def head_exchange(parts):
    return (parts[0],) + tuple(to_partner(parts[j], j) for j in (2, 1, 3))


def head_sum(parts):
    across = (parts[2].astype(full) + to_partner(parts[3], 1).astype(full)).astype(low)
    across = to_partner(across, 2)
    mine = parts[0].astype(full) + to_partner(parts[1], 1).astype(full)
    return mine + across.astype(full)


def in_order(parts, axis):
    me = lax.axis_index("head")
    odd = me % 2 == 1
    lower = [jnp.where(odd, parts[1], parts[0]), jnp.where(odd, parts[0], parts[1])]
    upper = [jnp.where(odd, parts[3], parts[2]), jnp.where(odd, parts[2], parts[3])]
    second = me >= 2
    return jnp.concatenate(
        [jnp.where(second, b, a) for a, b in zip(lower, upper)]
        + [jnp.where(second, a, b) for a, b in zip(lower, upper)],
        axis=axis,
    )


def tile_bias(tile, key_ids, query_ids, bias_ref):
    start = pl.multiple_of(tile * QUERY_TILE, QUERY_TILE)
    shape = (SPAN, QUERY_TILE)
    key = lax.broadcasted_iota(jnp.int32, shape, 0)
    query = lax.broadcasted_iota(jnp.int32, shape, 1)
    same = key_ids[pl.ds(start, SPAN), :] == query_ids[...]
    allowed = same & (key > query) & (key <= query + WINDOW)
    bias_ref[...] = jnp.where(allowed, 0.0, neg_fill)


def attend_kernel(q_ref, kv_ref, kvt_ref, key_ids, query_ids, out_ref, lse_ref, bias_ref):
    tile = pl.program_id(0)
    start = pl.multiple_of(tile * QUERY_TILE, QUERY_TILE)

    @pl.when(pl.program_id(1) == 0)
    def _():
        tile_bias(tile, key_ids, query_ids, bias_ref)

    keys = kv_ref[pl.ds(start, SPAN), :HEAD_DIM]
    scores = mul(keys, q_ref[...], NT) * HEAD_DIM ** (-0.5) + bias_ref[...]
    top = jnp.max(scores, axis=0, keepdims=True)
    expo = jnp.exp(scores - top)
    total = jnp.sum(expo, axis=0, keepdims=True)
    values = kvt_ref[HEAD_DIM:, pl.ds(start, SPAN)]
    mixed = mul(values, expo.astype(low), NN) / total
    out_ref[...] = mixed.T.astype(low)
    lse_ref[0] = top + jnp.log(total)


def attend_back_kernel(
    q_ref, g_ref, kv_ref, kvt_ref, key_ids, query_ids, lse_ref, dq_ref, dkv_ref, bias_ref
):
    tile = pl.program_id(0)
    start = pl.multiple_of(tile * QUERY_TILE, QUERY_TILE)
    scale = HEAD_DIM ** (-0.5)

    @pl.when((tile == 0) & (pl.program_id(1) == 0))
    def _():
        dkv_ref[...] = jnp.zeros_like(dkv_ref)

    @pl.when(pl.program_id(1) == 0)
    def _():
        tile_bias(tile, key_ids, query_ids, bias_ref)

    here = pl.ds(start, SPAN)
    queries = q_ref[...]
    grads = g_ref[...]
    scores = mul(kv_ref[here, :HEAD_DIM], queries, NT) * scale + bias_ref[...]
    probs = jnp.exp(scores - lse_ref[0])
    prob_grad = mul(kv_ref[here, HEAD_DIM:], grads, NT)
    delta = jnp.sum(probs * prob_grad, axis=0, keepdims=True)
    score_grad = (probs * (prob_grad - delta)).astype(low)
    dq = mul(kvt_ref[:HEAD_DIM, here], score_grad, NN) * scale
    dq_ref[...] = dq.T.astype(low)
    dkv_ref[here, :HEAD_DIM] += mul(score_grad, queries, NN) * scale
    dkv_ref[here, HEAD_DIM:] += mul(probs.astype(low), grads, NN)


def attention_specs(group):
    whole = lambda *shape: pl.BlockSpec(shape, lambda t, h: (0,) * len(shape))
    head_rows = pl.BlockSpec((QUERY_TILE, HEAD_DIM), lambda t, h: (t, h))
    keys = whole(2 * group, 2 * HEAD_DIM)
    keys_turned = whole(2 * HEAD_DIM, 2 * group)
    key_ids = whole(2 * group, 1)
    query_ids = pl.BlockSpec((1, QUERY_TILE), lambda t, h: (0, t))
    lse = pl.BlockSpec((1, 1, QUERY_TILE), lambda t, h: (h, 0, t))
    return head_rows, keys, keys_turned, key_ids, query_ids, lse


attention_params = pltpu.CompilerParams(
    dimension_semantics=("arbitrary", "arbitrary"), vmem_limit_bytes=40 * 1024 * 1024
)


def attend(queries, kv, kv_turned, key_ids, query_ids):
    group, width = queries.shape
    heads = width // HEAD_DIM
    rows, keys, turned, kids, qids, lse = attention_specs(group)
    work = heads * (group // QUERY_TILE) * SPAN * QUERY_TILE
    return pl.pallas_call(
        attend_kernel,
        grid=(group // QUERY_TILE, heads),
        in_specs=[rows, keys, turned, kids, qids],
        out_specs=[rows, lse],
        out_shape=[
            jax.ShapeDtypeStruct((group, width), low),
            jax.ShapeDtypeStruct((heads, 1, group), full),
        ],
        scratch_shapes=[pltpu.VMEM((SPAN, QUERY_TILE), full)],
        compiler_params=attention_params,
        cost_estimate=pl.CostEstimate(
            flops=8 * work * HEAD_DIM, bytes_accessed=6 << 20, transcendentals=work
        ),
        name="attend",
    )(queries, kv, kv_turned, key_ids, query_ids)


def attend_back(queries, grads, kv, kv_turned, key_ids, query_ids, lse_rows):
    group, width = queries.shape
    heads = width // HEAD_DIM
    rows, keys, turned, kids, qids, lse = attention_specs(group)
    work = heads * (group // QUERY_TILE) * SPAN * QUERY_TILE
    return pl.pallas_call(
        attend_back_kernel,
        grid=(group // QUERY_TILE, heads),
        in_specs=[rows, rows, keys, turned, kids, qids, lse],
        out_specs=[rows, keys],
        out_shape=[
            jax.ShapeDtypeStruct((group, width), low),
            jax.ShapeDtypeStruct((2 * group, 2 * HEAD_DIM), full),
        ],
        scratch_shapes=[pltpu.VMEM((SPAN, QUERY_TILE), full)],
        compiler_params=attention_params,
        cost_estimate=pl.CostEstimate(
            flops=20 * work * HEAD_DIM, bytes_accessed=8 << 20, transcendentals=work
        ),
        name="attend_back",
    )(queries, grads, kv, kv_turned, key_ids, query_ids, lse_rows)


def remote(source, target, send, recv, where):
    return pltpu.make_async_remote_copy(
        src_ref=source,
        dst_ref=target,
        send_sem=send,
        recv_sem=recv,
        device_id=where,
        device_id_type=pl.DeviceIdType.MESH,
    )


class Ring:
    def __init__(self, count, view, send, recv, split=True):
        me = lax.axis_index("seq")
        self.split = split
        odd = lax.rem(me, 2)
        self.count = count
        self.view = view
        self.send = send
        self.recv = recv
        self.place = (1 - odd) * (me // 2) + odd * (count - 1 - me // 2)
        self.ahead = {"seq": self.shard(1)}
        self.behind = {"seq": self.shard(-1)}
        self.copies = []

    def shard(self, offset):
        place = lax.rem(self.place + offset + self.count, self.count)
        upper = place // (self.count // 2)
        return (1 - upper) * 2 * place + upper * (2 * (self.count - 1 - place) + 1)

    def pair(self, offset, step):
        last = step == self.count // 2
        halved = last and self.split
        views = [
            self.view(self.shard(-offset), 0 if halved else None),
            self.view(self.shard(offset), 1 if halved else None),
        ]
        if last and not self.split:
            views = views[:1]
        return [
            remote(view, view, self.send.at[i, step - 1], self.recv.at[i, step - 1], where)
            for i, (view, where) in enumerate(zip(views, (self.ahead, self.behind)))
        ]

    def start(self, step):
        for copy in self.pair(step - 1, step):
            copy.start()
            self.copies.append(copy)

    def arrive(self, step):
        for copy in self.pair(step, step):
            copy.wait_recv()

    def finish(self):
        for copy in self.copies:
            copy.wait_send()


def turned_row(row):
    size = row.shape[1]
    return jnp.broadcast_to(row.astype(full), (128, size)).T[:, :1]


def forward_kernel(
    count,
    tokens,
    cotangent,
    own_gains,
    qkv_stack,
    out_stack,
    gateup_stack,
    down_stack,
    order,
    ids,
    gains,
    resid,
    normed_group,
    grad_group,
    gateup,
    down,
    features,
    qkv_rows,
    out_all,
    stream,
    kv_both,
    kv_turned,
    lse,
    mixed_group,
    shuffle,
    key_ids,
    query_ids,
    tokens_group,
    normed,
    weights,
    projected,
    mixed,
    mixed_all,
    bias,
    wide,
    tall,
    gateup_own,
    down_own,
    gain_tiles,
    own_sem,
    ring_send,
    ring_recv,
    head_send,
    head_recv,
    kv_send,
    kv_recv,
):
    rows = tokens.shape[0]
    group = 4 * rows
    width = features.shape[1]
    heads = width // HEAD_DIM
    head = lax.axis_index("head")
    me = lax.axis_index("seq")
    mate_head = head + 1 - 2 * lax.rem(head, 2)
    across_head = lax.rem(head + 2, 4)
    mate = {"head": mate_head}
    across = {"head": across_head}

    def band(of):
        return pl.ds(pl.multiple_of(of * width, 128), width)

    def chip_columns(of):
        return pl.ds(pl.multiple_of((of // 2) * 2 * width, 128), 2 * width)

    def quarter(ref, i):
        return ref.at[pl.ds(i * rows, rows)]

    copies = []

    def send(index, source, target, where):
        copy = remote(source, target, head_send.at[index], head_recv.at[index], where)
        copy.start()
        copies.append(copy)

    def arrived(index, target, where):
        remote(target, target, head_send.at[index], head_recv.at[index], where).wait_recv()

    def stack_view(ref, columns):
        def view(shard, part):
            first = pl.multiple_of(head * width + (shard // 2) * BLK, 32)
            at = pl.ds(pl.multiple_of(lax.rem(shard, 2) * columns, 128), columns)
            if part is None:
                return ref.at[pl.ds(first, BLK), at]
            return ref.at[pl.ds(pl.multiple_of(first + part * (BLK // 2), 16), BLK // 2), at]

        return view

    def gateup_view(shard, part):
        size = gateup.shape[1]
        if part is None:
            return gateup.at[shard]
        return gateup.at[shard, pl.ds(part * (size // 2), size // 2)]

    def down_view(shard, part):
        if part is None:
            return down.at[shard]
        return down.at[shard, :, pl.ds(part * (BLK // 2), BLK // 2)]

    qkv_view = stack_view(weights, QKV // 2)
    out_view = stack_view(out_all, D // 2)
    gain_view = lambda shard, part: gain_tiles.at[head, shard]
    qkv_ring, out_ring, gateup_ring, down_ring, gain_ring = rings = [
        Ring(count, view, ring_send.at[i], ring_recv.at[i], view is not gain_view)
        for i, view in enumerate((qkv_view, out_view, gateup_view, down_view, gain_view))
    ]

    barrier = pltpu.get_barrier_semaphore()
    for where in (qkv_ring.ahead, qkv_ring.behind, mate, across):
        pl.semaphore_signal(barrier, inc=1, device_id=where, device_id_type=pl.DeviceIdType.MESH)

    @pl.when(me > 0)
    def _():
        pl.semaphore_signal(
            barrier, inc=1, device_id={"seq": me - 1}, device_id_type=pl.DeviceIdType.MESH
        )

    def side_by_side(stack, first):
        size = stack.shape[2]
        blocks = 8
        for c in range(blocks):
            tall[c * size : (c + 1) * size, :] = stack[first + c].T
        return tall[: blocks * size, :].T.astype(low)

    qkv_view(me, None)[...] = side_by_side(qkv_stack, 0)
    gain_tiles[head, me] = own_gains[...]
    pl.semaphore_wait(barrier, 5 - me // (count - 1))
    send(0, tokens, quarter(tokens_group, 2), across)
    send(1, tokens, quarter(tokens_group, 1), mate)
    qkv_ring.start(1)
    gain_ring.start(1)
    for q in range(gateup_own.shape[0] // BLK):
        column = gateup_stack[q * GRID : (q + 1) * GRID].reshape(D, BLK)
        gateup_own[q * BLK : (q + 1) * BLK, :] = column.T.astype(low)
    for m in range(down_own.shape[0]):
        down_own[m] = side_by_side(down_stack, 8 * m)
    own = [
        pltpu.make_async_copy(gateup_own, gateup.at[me], own_sem.at[0]),
        pltpu.make_async_copy(down_own, down.at[me], own_sem.at[1]),
        pltpu.make_async_copy(cotangent, quarter(grad_group, 0), own_sem.at[2]),
    ]
    for copy in own:
        copy.start()
    out_view(me, None)[...] = side_by_side(out_stack, 0)
    for copy in own[:2]:
        copy.wait()

    def pump(step):
        if step > 1:
            gateup_ring.arrive(step - 1)
            down_ring.arrive(step - 1)
        if step <= count // 2:
            gateup_ring.start(step)
            down_ring.start(step)

    pump(1)
    tokens_group[:rows, :] = tokens[...]
    qkv_ring.arrive(1)
    qkv_ring.start(2)
    gain_ring.arrive(1)
    gain_ring.start(2)

    for i in range(4):
        at = turned_row(order[:, i * rows : (i + 1) * rows]).astype(jnp.int32)
        owner = at // rows
        flip = head - 4 * (owner // 2) * (head // 2) - 2 * lax.rem(owner, 2) * lax.rem(head, 2)
        place = (owner + flip) * rows + lax.rem(at, rows)
        shuffle[i * rows : (i + 1) * rows, :] = jnp.where(
            place == lax.broadcasted_iota(jnp.int32, (rows, group), 1), 1.0, 0.0
        ).astype(low)
    query_ids[...] = ids[:, pl.ds(pl.multiple_of(me * group, 128), group)].astype(full)
    before = (me - (me + count - 1) // count) * group
    for i in range(4):
        here = slice(i * rows, (i + 1) * rows)
        at = pl.multiple_of(before + i * rows, 128)
        key_ids[here, :] = jnp.where(me > 0, turned_row(ids[:, pl.ds(at, rows)]), -1.0)
        there = slice(group + i * rows, group + (i + 1) * rows)
        key_ids[there, :] = turned_row(query_ids[:, here])
    for step in range(2, count // 2):
        qkv_ring.arrive(step)
        qkv_ring.start(step + 1)
        gain_ring.arrive(step)
        gain_ring.start(step + 1)
    qkv_ring.arrive(count // 2)

    key_columns = pl.ds(QW, 2 * HEAD_DIM)

    def weight_parts(of, chip_of):
        return [weights.at[band(of), columns] for columns in (chip_columns(chip_of), key_columns)]

    gain_ring.arrive(count // 2)
    send(9, gain_tiles.at[head], gain_tiles.at[head], across)
    send(10, gain_tiles.at[head], gain_tiles.at[head], mate)
    for i, part in enumerate(weight_parts(head, across_head)):
        send(3 + i, part, part, across)
    for i, part in enumerate(weight_parts(head, head)):
        send(7 + i, part, part, mate)
    out_ring.start(1)
    pump(2)
    arrived(0, quarter(tokens_group, 2), across)
    send(2, quarter(tokens_group, 2), quarter(tokens_group, 3), mate)
    qkv_rows[...] = weights[band(head), :]
    arrived(9, gain_tiles.at[across_head], across)
    send(11, gain_tiles.at[across_head], gain_tiles.at[across_head], mate)
    arrived(10, gain_tiles.at[mate_head], mate)
    arrived(11, gain_tiles.at[3 - head], mate)
    size = D // (4 * count)
    for h in range(4):
        for i in range(count):
            at = (h * count + i) * size
            wide[:8, at : at + size] = gain_tiles[h, i][:, :size]
    gains[...] = wide[:2, :D].astype(low).astype(full)

    def norm_rows(i):
        here = pl.ds(i * rows, rows)
        values = tokens_group[here, :].astype(full)
        normed[here, :] = (values * inverse_norm(values) * gains[0:1, :]).astype(low)

    norm_rows(0)
    arrived(1, quarter(tokens_group, 1), mate)
    norm_rows(1)
    out_ring.arrive(1)
    out_ring.start(2)
    norm_rows(2)
    arrived(2, quarter(tokens_group, 3), mate)
    norm_rows(3)
    features[...] = normed[:, band(head)]
    for i, part in enumerate(weight_parts(across_head, head)):
        arrived(3 + i, part, across)
        send(5 + i, part, part, mate)
    out_ring.arrive(2)
    out_ring.start(3)
    for i, part in enumerate(weight_parts(mate_head, head)):
        arrived(7 + i, part, mate)
    send(27, cotangent, quarter(grad_group, 2), across)
    send(28, cotangent, quarter(grad_group, 1), mate)
    for i, part in enumerate(weight_parts(3 - head, head)):
        arrived(5 + i, part, mate)

    key_values = pl.ds(width, 2 * HEAD_DIM)

    def project(columns, target):
        def step(i, carry):
            here = pl.ds(pl.multiple_of(i * rows, rows), rows)
            projected[here, target] = mul(normed[here, :], weights[:, columns], NN).astype(low)
            return carry

        lax.fori_loop(0, 4, step, 0)

        def turn(i, carry):
            here = pl.ds(pl.multiple_of(i * rows, rows), rows)
            stream[here, target] = mul(shuffle[here, :], projected[:, target], NN).astype(low)
            return carry

        lax.fori_loop(0, 4, turn, 0)

    project(key_columns, key_values)
    kv_both[pl.ds(group, group), :] = stream[:, key_values]
    kv_copy = remote(
        kv_both.at[pl.ds(group, group)],
        kv_both.at[pl.ds(0, group)],
        kv_send,
        kv_recv,
        {"seq": lax.rem(me + 1, count)},
    )

    @pl.when(me < count - 1)
    def _():
        kv_copy.start()

    @pl.when(me == 0)
    def _():
        kv_both[pl.ds(0, group), :] = jnp.zeros((group, 2 * HEAD_DIM), low)

    out_ring.arrive(3)
    out_ring.start(4)
    project(band(head), pl.ds(0, width))
    pump(3)
    for i in range(4, 8):
        kv_turned[:, i * rows : (i + 1) * rows] = kv_both[i * rows : (i + 1) * rows, :].T
    out_ring.arrive(4)
    half = width // 2

    def out_part(of, i):
        return out_all.at[pl.ds(pl.multiple_of(of * width + i * half, 64), half)]

    for i in range(2):
        send(12 + i, out_part(head, i), out_part(head, i), across)
    send(16, out_all.at[band(head)], out_all.at[band(head)], mate)

    @pl.when(me > 0)
    def _():
        kv_copy.wait_recv()

    for i in range(4):
        kv_turned[:, i * rows : (i + 1) * rows] = kv_both[i * rows : (i + 1) * rows, :].T
    arrived(27, quarter(grad_group, 2), across)
    send(29, quarter(grad_group, 2), quarter(grad_group, 3), mate)

    def attend_tile(tile, carry):
        start = pl.multiple_of(tile * QUERY_TILE, QUERY_TILE)
        here = pl.ds(start, QUERY_TILE)
        span = pl.ds(start, SPAN)
        shape = (SPAN, QUERY_TILE)
        key = lax.broadcasted_iota(jnp.int32, shape, 0)
        query = lax.broadcasted_iota(jnp.int32, shape, 1)
        same = key_ids[span, :] == query_ids[:, here]
        allowed = same & (key > query) & (key <= query + WINDOW)
        bias[...] = jnp.where(allowed, 0.0, neg_fill)

        def attend_head(j, carry):
            lanes = pl.ds(pl.multiple_of(j * HEAD_DIM, HEAD_DIM), HEAD_DIM)
            scores = mul(kv_both[span, :HEAD_DIM], stream[here, lanes], NT)
            scores = scores * HEAD_DIM ** (-0.5) + bias[...]
            top = jnp.max(scores, axis=0, keepdims=True)
            expo = jnp.exp(scores - top)
            total = jnp.sum(expo, axis=0, keepdims=True)
            out = mul(kv_turned[HEAD_DIM:, span], expo.astype(low), NN) / total
            mixed[here, lanes] = out.T.astype(low)
            lse[j, :, here] = top + jnp.log(total)
            return carry

        return lax.fori_loop(0, heads, attend_head, carry)

    lax.fori_loop(0, group // QUERY_TILE, attend_tile, 0)

    def turn_back(i, carry):
        here = pl.ds(pl.multiple_of(i * rows, rows), rows)
        mixed_group[here, :] = mul(shuffle[:, here], mixed[...], TN).astype(low)
        return carry

    lax.fori_loop(0, 4, turn_back, 0)

    def mixed_part(of, i, size):
        return mixed_all.at[pl.ds(i * size, size), band(of)]

    for i in range(2):
        source = mixed_group.at[pl.ds(i * 2 * rows, 2 * rows)]
        send(17 + i, source, mixed_part(head, 1 - i, 2 * rows), across)
    for i in range(4):
        send(19 + i, quarter(mixed_group, i), mixed_part(head, i ^ 1, rows), mate)
    mixed_all[:, band(head)] = mixed_group[...]
    for i in range(2):
        arrived(12 + i, out_part(across_head, i), across)
        send(14 + i, out_part(across_head, i), out_part(across_head, i), mate)
    pump(4)
    arrived(16, out_all.at[band(mate_head)], mate)
    for i in range(2):
        arrived(14 + i, out_part(3 - head, i), mate)
    for i in range(4):
        arrived(19 + i, mixed_part(mate_head, i ^ 1, rows), mate)
    for i in range(2):
        arrived(17 + i, mixed_part(across_head, 1 - i, 2 * rows), across)
        for j in (2 - 2 * i, 3 - 2 * i):
            part = mixed_part(across_head, j, rows)
            send(23 + j, part, mixed_part(across_head, j ^ 1, rows), mate)
    for j in range(4):
        arrived(23 + j, mixed_part(3 - head, j ^ 1, rows), mate)

    def second(i, carry):
        here = pl.ds(pl.multiple_of((3 - i) * rows, rows), rows)
        resid[...] = tokens_group[here, :].astype(full) + mul(mixed_all[here, :], out_all[...], NN)
        values = resid[...]
        normed_group[here, :] = (values * inverse_norm(values) * gains[1:2, :]).astype(low)
        return carry

    lax.fori_loop(0, 4, second, 0)
    arrived(28, quarter(grad_group, 1), mate)
    arrived(29, quarter(grad_group, 3), mate)
    pump(5)
    own[2].wait()
    for ring in rings:
        ring.finish()
    for copy in copies:
        copy.wait_send()

    @pl.when(me < count - 1)
    def _():
        kv_copy.wait_send()


def forward_section(tokens, cotangent, gains, stacks, order, ids, count):
    rows = tokens.shape[0]
    group = 4 * rows
    width = QW // 4
    steps = count // 2
    gateup_rows = stacks[2].shape[0] // GRID * BLK
    down_parts = stacks[3].shape[0] // 8
    vmem = pl.BlockSpec(memory_space=pltpu.VMEM)
    hbm = pl.BlockSpec(memory_space=pl.ANY)
    outs = [
        ((2, D), full, vmem),
        ((rows, D), full, vmem),
        ((group, D), low, vmem),
        ((group, D), low, hbm),
        ((count, gateup_rows, D), low, hbm),
        ((count, down_parts, BLK, D // 2), low, hbm),
        ((group, width), low, vmem),
        ((width, QKV), low, vmem),
        ((D, D), low, vmem),
        ((group, width + 2 * HEAD_DIM), low, vmem),
        ((2 * group, 2 * HEAD_DIM), low, vmem),
        ((2 * HEAD_DIM, 2 * group), low, vmem),
        ((width // HEAD_DIM, 1, group), full, vmem),
        ((group, width), low, vmem),
        ((group, group), low, vmem),
        ((2 * group, 1), full, vmem),
        ((1, group), full, vmem),
    ]
    dma = pltpu.SemaphoreType.DMA
    return pl.pallas_call(
        functools.partial(forward_kernel, count),
        in_specs=[vmem] * 9,
        out_specs=[spec for _, _, spec in outs],
        out_shape=[jax.ShapeDtypeStruct(shape, kind) for shape, kind, _ in outs],
        scratch_shapes=[
            pltpu.VMEM((group, D), low),
            pltpu.VMEM((group, D), low),
            pltpu.VMEM((D, QKV), low),
            pltpu.VMEM((group, width + 2 * HEAD_DIM), low),
            pltpu.VMEM((group, width), low),
            pltpu.VMEM((group, D), low),
            pltpu.VMEM((SPAN, QUERY_TILE), full),
            pltpu.VMEM((8, D), full),
            pltpu.VMEM((QKV // 2, BLK), full),
            pltpu.VMEM((gateup_rows, D), low),
            pltpu.VMEM((down_parts, BLK, D // 2), low),
            pltpu.VMEM((4, count, 8, 128), full),
            dma((3,)),
            dma((5, 2, steps)),
            dma((5, 2, steps)),
            dma((30,)),
            dma((30,)),
            dma,
            dma,
        ],
        compiler_params=pltpu.CompilerParams(
            collective_id=0, has_side_effects=True, vmem_limit_bytes=58 * 1024 * 1024
        ),
        name="forward_section",
    )(tokens, cotangent, gains, *stacks, order, ids)


class SumRing:
    def __init__(self, count, view, first, buffers, send, recv):
        self.ring = Ring(count, None, None, None)
        self.steps = count // 2
        self.view = view
        self.first = first
        self.buffers = buffers
        self.rows = buffers.shape[2]
        self.send = send
        self.recv = recv
        self.copies = []

    def where(self, way):
        return self.ring.behind if way else self.ring.ahead

    def half(self, way):
        return self.buffers.at[way, 0, pl.ds(way * (self.rows // 2), self.rows // 2)]

    def copy(self, way, step, source, target):
        return remote(source, target, self.send.at[way, step], self.recv.at[way, step], self.where(way))

    def start(self):
        shard = self.ring.shard(self.steps)
        for way in range(2):
            copy = self.copy(way, 0, self.first(shard, way), self.half(way))
            copy.start()
            self.copies.append(copy)

    def arrived(self, way, step):
        target = self.buffers.at[way, step] if step else self.half(way)
        self.copy(way, step, target, target).wait_recv()

    def step(self, step):
        block = 48
        for way in range(2):
            self.arrived(way, step - 1)
            offset = self.steps - step
            local = self.view(self.ring.shard(-offset if way else offset))
            buffer = self.buffers.at[way, step - 1]

            def add(i, carry):
                here = pl.ds(pl.multiple_of(i * block, 16), block)
                buffer[here, :] = (local[here, :].astype(full) + buffer[here, :].astype(full)).astype(low)
                return carry

            def keep(i, carry):
                here = pl.ds(pl.multiple_of(i * block, 16), block)
                buffer[here, :] = local[here, :]
                return carry

            blocks = self.rows // block
            if step > 1:
                lax.fori_loop(0, blocks, add, 0)
            else:
                lax.fori_loop(way * (blocks // 2), (way + 1) * (blocks // 2), add, 0)
                lax.fori_loop((1 - way) * (blocks // 2), (2 - way) * (blocks // 2), keep, 0)
            copy = self.copy(way, step, buffer, self.buffers.at[way, step])
            copy.start()
            self.copies.append(copy)

    def finish(self, out):
        block = 48
        last = self.steps - 1
        for way in range(2):
            self.arrived(way, last)
        local = self.view(self.ring.shard(0))

        def add(i, carry):
            here = pl.ds(pl.multiple_of(i * block, 16), block)
            out[here, :] = (
                local[here, :].astype(full)
                + self.buffers[0, last, here, :].astype(full)
                + self.buffers[1, last, here, :].astype(full)
            )
            return carry

        lax.fori_loop(0, self.rows // block, add, 0)
        for copy in self.copies:
            copy.wait_send()


class StagedSumRing(SumRing):
    def __init__(self, count, parts, buffers, held, terms, load, send, recv):
        size = parts.shape[1] // 2
        first = lambda shard, part: parts.at[shard, pl.ds(part * size, size)]
        super().__init__(count, None, first, buffers, send, recv)
        self.parts = parts
        self.held = held
        self.terms = terms
        self.load = load
        self.last = [None, None]

    def fetch(self, way, offset):
        shard = self.ring.shard(-offset if way else offset)
        copy = pltpu.make_async_copy(
            self.parts.at[shard], self.terms.at[way], self.load.at[1, way]
        )
        copy.start()
        return copy

    def start(self):
        super().start()
        self.fetched = [self.fetch(way, self.steps - 1) for way in range(2)]

    def take(self, way, step):
        self.arrived(way, step)
        if self.last[way] is not None:
            self.last[way].wait_send()
        source, target = self.buffers.at[way, step], self.held.at[way]
        if step == 0:
            half = pl.ds(way * (self.rows // 2), self.rows // 2)
            source, target = self.half(way), self.held.at[way, half]
        copy = pltpu.make_async_copy(source, target, self.load.at[0, way])
        copy.start()
        return copy

    def step(self, step):
        block = 48
        taken = [self.take(way, step - 1) for way in range(2)]
        for way in range(2):
            taken[way].wait()
            self.fetched[way].wait()
            held, terms = self.held.at[way], self.terms.at[way]

            def add(i, carry):
                here = pl.ds(pl.multiple_of(i * block, 16), block)
                held[here, :] = (terms[here, :].astype(full) + held[here, :].astype(full)).astype(low)
                return carry

            def keep(i, carry):
                here = pl.ds(pl.multiple_of(i * block, 16), block)
                held[here, :] = terms[here, :]
                return carry

            blocks = self.rows // block
            if step > 1:
                lax.fori_loop(0, blocks, add, 0)
            else:
                lax.fori_loop(way * (blocks // 2), (way + 1) * (blocks // 2), add, 0)
                lax.fori_loop((1 - way) * (blocks // 2), (2 - way) * (blocks // 2), keep, 0)
            self.last[way] = self.copy(way, step, held, self.buffers.at[way, step])
            self.last[way].start()
            if step < self.steps - 1 or way == 0:
                self.fetched[way] = self.fetch(way, self.steps - 1 - step)

    def finish(self, out):
        block = 48
        taken = [self.take(way, self.steps - 1) for way in range(2)]
        for copy in taken:
            copy.wait()
        self.fetched[0].wait()

        def add(i, carry):
            here = pl.ds(pl.multiple_of(i * block, 16), block)
            out[here, :] = (
                self.terms[0, here, :].astype(full)
                + self.held[0, here, :].astype(full)
                + self.held[1, here, :].astype(full)
            )
            return carry

        lax.fori_loop(0, self.rows // block, add, 0)
        for copy in self.copies:
            copy.wait_send()


def backward_kernel(
    count,
    tokens,
    cotangent,
    gains,
    resid,
    normed_part,
    ffn_part,
    gateup_parts,
    down_parts,
    features,
    qkv_rows,
    out_all,
    stream,
    kv_both,
    kv_turned,
    lse,
    mixed_group,
    shuffle,
    key_ids,
    query_ids,
    block_out,
    input_grad,
    gain_grads,
    gateup_grad,
    down_grad,
    qkv_grad,
    out_grad,
    gateup_sums,
    down_sums,
    gateup_held,
    gateup_terms,
    down_held,
    down_terms,
    part_quarter,
    qkv_local,
    out_local,
    qkv_sums,
    out_sums,
    sum_out,
    sum_in,
    proj_group,
    turned_out,
    turned_grad,
    grad_stream,
    kv_total,
    kv_out,
    kv_in,
    stream_grad,
    kv_mate,
    all_grad,
    normed_grad,
    bias,
    load_sem,
    part_sem,
    ring_send,
    ring_recv,
    head_send,
    head_recv,
    kv_send,
    kv_recv,
):
    rows = tokens.shape[0]
    group = 4 * rows
    width = features.shape[1]
    heads = width // HEAD_DIM
    scale = HEAD_DIM ** (-0.5)
    query_grad = turned_grad
    feature_grad = grad_stream
    head = lax.axis_index("head")
    me = lax.axis_index("seq")
    mate_head = head + 1 - 2 * lax.rem(head, 2)
    across_head = lax.rem(head + 2, 4)
    mate = {"head": mate_head}
    across = {"head": across_head}
    corner = {"head": 3 - head}

    def lanes(of):
        return pl.ds(pl.multiple_of(of * width, 128), width)

    def quarter(i):
        return pl.ds(i * rows, rows)

    copies = []

    def send(index, source, target, where):
        copy = remote(source, target, head_send.at[index], head_recv.at[index], where)
        copy.start()
        copies.append(copy)

    def arrived(index, target, where):
        remote(target, target, head_send.at[index], head_recv.at[index], where).wait_recv()

    def shard_view(ref, columns):
        def view(shard, part=None):
            first = pl.multiple_of((shard // 2) * BLK, 32)
            at = pl.ds(pl.multiple_of(lax.rem(shard, 2) * columns, 128), columns)
            if part is None:
                return ref.at[pl.ds(first, BLK), at]
            return ref.at[pl.ds(pl.multiple_of(first + part * (BLK // 2), 16), BLK // 2), at]

        return view

    qkv_view = shard_view(qkv_local, QKV // 2)
    out_view = shard_view(out_local, D // 2)
    gateup_ring = StagedSumRing(
        count,
        gateup_parts,
        gateup_sums,
        gateup_held,
        gateup_terms,
        load_sem.at[0],
        ring_send.at[0],
        ring_recv.at[0],
    )
    down_ring = StagedSumRing(
        count,
        down_parts,
        down_sums,
        down_held,
        down_terms,
        load_sem.at[1],
        ring_send.at[1],
        ring_recv.at[1],
    )
    qkv_ring = SumRing(count, qkv_view, qkv_view, qkv_sums, ring_send.at[2], ring_recv.at[2])
    out_ring = SumRing(count, out_view, out_view, out_sums, ring_send.at[3], ring_recv.at[3])

    barrier = pltpu.get_barrier_semaphore()
    for where in (gateup_ring.where(0), gateup_ring.where(1), mate, across, corner):
        pl.semaphore_signal(barrier, inc=1, device_id=where, device_id_type=pl.DeviceIdType.MESH)

    @pl.when(me < count - 1)
    def _():
        pl.semaphore_signal(
            barrier, inc=1, device_id={"seq": me + 1}, device_id_type=pl.DeviceIdType.MESH
        )

    pl.semaphore_wait(barrier, 5 + (me + count - 1) // count)

    def fetch(value, i):
        copy = pltpu.make_async_copy(value.at[quarter(i)], part_quarter, part_sem)
        copy.start()
        copy.wait()
        return part_quarter[...].astype(full)

    def sum_first(base, slot, value):
        send(base, value.at[quarter(3)], sum_in.at[slot], mate)
        send(base + 1, value.at[quarter(1)], sum_in.at[slot + 1], mate)

    def sum_across(base, slot, value):
        own = fetch(value, 2)
        arrived(base, sum_in.at[slot], mate)
        sum_out[slot // 3] = (own + sum_in[slot].astype(full)).astype(low)
        send(base + 2, sum_out.at[slot // 3], sum_in.at[slot + 2], across)

    def sum_last(base, slot, value):
        own = fetch(value, 0)
        arrived(base + 1, sum_in.at[slot + 1], mate)
        own = own + sum_in[slot + 1].astype(full)
        arrived(base + 2, sum_in.at[slot + 2], across)
        return own + sum_in[slot + 2].astype(full)

    sum_first(0, 0, normed_part)
    gateup_ring.start()
    down_ring.start()
    sum_across(0, 0, normed_part)
    sum_first(3, 3, ffn_part)

    normed_two_grad = sum_last(0, 0, normed_part)
    values = resid[...]
    inverse = inverse_norm(values)
    gain_grads[1:2, :] = jnp.sum(normed_two_grad * values * inverse, axis=0, keepdims=True)
    input_grad[...] = cotangent[...].astype(full) + norm_back(
        values, inverse, gains[1:2, :], normed_two_grad
    )
    proj_group[quarter(0), :] = input_grad[...].astype(low)

    def back_projection(of):
        weights = out_all[pl.ds(pl.multiple_of(of * width, 128), width), :]
        return mul(proj_group[quarter(0), :], weights, NT).astype(low)

    for j, of, where in ((2, across_head, across), (3, 3 - head, corner), (1, mate_head, mate)):
        turned_out[j - 1] = back_projection(of)
        send(31 + j, turned_out.at[j - 1], turned_grad.at[quarter(j)], where)
    send(6, proj_group.at[quarter(0)], proj_group.at[quarter(2)], across)
    send(7, proj_group.at[quarter(0)], proj_group.at[quarter(1)], mate)
    turned_grad[quarter(0), :] = back_projection(head)
    gateup_ring.step(1)
    down_ring.step(1)
    for j, where in ((1, mate), (2, across), (3, corner)):
        arrived(31 + j, turned_grad.at[quarter(j)], where)

    def turn(i, carry):
        here = pl.ds(pl.multiple_of(i * rows, rows), rows)
        grad_stream[here, :] = mul(shuffle[here, :], turned_grad[...], NN).astype(low)
        return carry

    lax.fori_loop(0, 4, turn, 0)

    kv_total[...] = jnp.zeros_like(kv_total)

    def back_tile(tile, carry):
        start = pl.multiple_of(tile * QUERY_TILE, QUERY_TILE)
        here = pl.ds(start, QUERY_TILE)
        span = pl.ds(start, SPAN)
        shape = (SPAN, QUERY_TILE)
        key = lax.broadcasted_iota(jnp.int32, shape, 0)
        query = lax.broadcasted_iota(jnp.int32, shape, 1)
        same = key_ids[span, :] == query_ids[:, here]
        allowed = same & (key > query) & (key <= query + WINDOW)
        bias[...] = jnp.where(allowed, 0.0, neg_fill)

        def back_head(j, carry):
            at = pl.ds(pl.multiple_of(j * HEAD_DIM, HEAD_DIM), HEAD_DIM)
            queries = stream[here, at]
            grads = grad_stream[here, at]
            scores = mul(kv_both[span, :HEAD_DIM], queries, NT) * scale + bias[...]
            probs = jnp.exp(scores - lse[j, :, here])
            prob_grad = mul(kv_both[span, HEAD_DIM:], grads, NT)
            delta = jnp.sum(probs * prob_grad, axis=0, keepdims=True)
            score_grad = (probs * (prob_grad - delta)).astype(low)
            turned = mul(kv_turned[:HEAD_DIM, span], score_grad, NN) * scale
            query_grad[here, at] = turned.T.astype(low)
            kv_total[span, :HEAD_DIM] += mul(score_grad, queries, NN) * scale
            kv_total[span, HEAD_DIM:] += mul(probs.astype(low), grads, NN)
            return carry

        return lax.fori_loop(0, heads, back_head, carry)

    tiles = group // QUERY_TILE
    lax.fori_loop(0, tiles // 2, back_tile, 0)
    arrived(6, proj_group.at[quarter(2)], across)
    send(8, proj_group.at[quarter(2)], proj_group.at[quarter(3)], mate)
    sum_across(3, 3, ffn_part)
    gateup_ring.step(2)
    down_ring.step(2)
    lax.fori_loop(tiles // 2, tiles, back_tile, 0)
    kv_out[...] = kv_total[:group, :].astype(low)
    kv_copy = remote(kv_out, kv_in, kv_send, kv_recv, {"seq": lax.rem(me + count - 1, count)})

    @pl.when(me > 0)
    def _():
        kv_copy.start()

    def turn_back(i, carry):
        here = pl.ds(pl.multiple_of(i * rows, rows), rows)
        all_grad[here, lanes(head)] = mul(shuffle[:, here], query_grad[...], TN).astype(low)
        return carry

    lax.fori_loop(0, 4, turn_back, 0)

    def swapped(index, ref, columns, distance, where):
        for i in range(4):
            send(
                index + i,
                ref.at[quarter(i), columns],
                ref.at[quarter(i ^ distance), columns],
                where,
            )

    def swapped_arrived(index, ref, columns, distance, where):
        for i in range(4):
            arrived(index + i, ref.at[quarter(i ^ distance), columns], where)

    swapped(9, all_grad, lanes(head), 2, across)
    swapped(13, all_grad, lanes(head), 1, mate)
    gateup_ring.step(3)
    down_ring.step(3)
    arrived(7, proj_group.at[quarter(1)], mate)
    arrived(8, proj_group.at[quarter(3)], mate)
    for i in range(3):
        at = slice(i * (D // 3), (i + 1) * (D // 3))
        out_local[:, at] = mul(mixed_group[...], proj_group[:, at], TN).astype(low)
    out_ring.start()

    @pl.when(me < count - 1)
    def _():
        kv_copy.wait_recv()
        kv_total[pl.ds(group, group), :] += kv_in[...].astype(full)

    stream_grad[...] = kv_total[pl.ds(group, group), :].astype(low)

    def turn_keys(i, carry):
        here = pl.ds(pl.multiple_of(i * rows, rows), rows)
        kv_mate[0, here, :] = mul(shuffle[:, here], stream_grad[...], TN).astype(low)
        return carry

    lax.fori_loop(0, 4, turn_keys, 0)
    for i in range(4):
        send(17 + i, kv_mate.at[0, quarter(i)], kv_mate.at[1, quarter(i ^ 1)], mate)
    for i in range(4):
        arrived(17 + i, kv_mate.at[1, quarter(i ^ 1)], mate)
    kv_total[pl.ds(0, group), :] = kv_mate[0].astype(full) + kv_mate[1].astype(full)
    kv_mate[2] = kv_total[pl.ds(0, group), :].astype(low)
    mine = pl.ds(pl.multiple_of(lax.rem(head, 2) * HEAD_DIM, HEAD_DIM), HEAD_DIM)
    of_mine = pl.ds(pl.multiple_of(QW + lax.rem(head, 2) * HEAD_DIM, HEAD_DIM), HEAD_DIM)
    of_mate = pl.ds(pl.multiple_of(QW + lax.rem(mate_head, 2) * HEAD_DIM, HEAD_DIM), HEAD_DIM)
    for i in range(4):
        send(21 + i, kv_mate.at[2, quarter(i), mine], kv_mate.at[3, quarter(i ^ 2), mine], across)
    out_ring.step(1)
    swapped_arrived(9, all_grad, lanes(across_head), 2, across)
    swapped(25, all_grad, lanes(across_head), 1, mate)
    out_ring.step(2)
    swapped_arrived(13, all_grad, lanes(mate_head), 1, mate)
    for i in range(4):
        arrived(21 + i, kv_mate.at[3, quarter(i ^ 2), mine], across)
    all_grad[:, of_mine] = (
        kv_total[pl.ds(0, group), mine] + kv_mate[3, :, mine].astype(full)
    ).astype(low)
    swapped(35, all_grad, of_mine, 1, mate)
    swapped_arrived(35, all_grad, of_mate, 1, mate)
    swapped_arrived(25, all_grad, lanes(3 - head), 1, mate)

    for i in range(2):
        at = slice(i * (QKV // 2), (i + 1) * (QKV // 2))
        qkv_local[:, at] = mul(features[...], all_grad[:, at], TN).astype(low)
    qkv_ring.start()
    out_ring.step(3)
    for i, where in ((2, across), (3, corner), (1, mate)):
        feature_grad[quarter(i), :] = mul(all_grad[quarter(i), :], qkv_rows[...], NT).astype(low)
        send(28 + i, feature_grad.at[quarter(i)], normed_grad.at[:, lanes(head)], where)
    normed_grad[:, lanes(head)] = mul(all_grad[quarter(0), :], qkv_rows[...], NT).astype(low)
    qkv_ring.step(1)
    block_out[...] = (resid[...] + sum_last(3, 3, ffn_part)).astype(low)
    for i, where, of in ((2, across, across_head), (3, corner, 3 - head), (1, mate, mate_head)):
        arrived(28 + i, normed_grad.at[:, lanes(of)], where)
    qkv_ring.step(2)
    normed_one_grad = normed_grad[...].astype(full)
    values = tokens[...].astype(full)
    inverse = inverse_norm(values)
    gain_grads[0:1, :] = jnp.sum(normed_one_grad * values * inverse, axis=0, keepdims=True)
    input_grad[...] += norm_back(values, inverse, gains[0:1, :], normed_one_grad)
    qkv_ring.step(3)
    gateup_ring.finish(gateup_grad)
    down_ring.finish(down_grad)
    out_ring.finish(out_grad)
    qkv_ring.finish(qkv_grad)
    for copy in copies:
        copy.wait_send()

    @pl.when(me > 0)
    def _():
        kv_copy.wait_send()


def backward_section(count, *values):
    (tokens, cotangent, gains, resid, normed_part, ffn_part, gateup_parts, down_parts) = values[:8]
    rows = tokens.shape[0]
    group = 4 * rows
    width = QW // 4
    steps = count // 2
    vmem = pl.BlockSpec(memory_space=pltpu.VMEM)
    hbm = pl.BlockSpec(memory_space=pl.ANY)
    shard = gateup_parts.shape[1:]
    down_shard = down_parts.shape[1:]
    outs = [
        ((rows, D), low),
        ((rows, D), full),
        ((2, D), full),
        (shard, full),
        (down_shard, full),
        ((BLK, QKV // 2), full),
        ((BLK, D // 2), full),
        ((2, steps) + shard, low),
        ((2, steps) + down_shard, low),
    ]
    dma = pltpu.SemaphoreType.DMA
    return pl.pallas_call(
        functools.partial(backward_kernel, count),
        in_specs=[vmem] * 4 + [hbm] * 4 + [vmem] * 11,
        out_specs=[vmem] * 7 + [hbm] * 2,
        out_shape=[jax.ShapeDtypeStruct(shape, kind) for shape, kind in outs],
        scratch_shapes=[
            pltpu.VMEM((2,) + shard, low),
            pltpu.VMEM((2,) + shard, low),
            pltpu.VMEM((2,) + down_shard, low),
            pltpu.VMEM((2,) + down_shard, low),
            pltpu.VMEM((rows, D), low),
            pltpu.VMEM((width, QKV), low),
            pltpu.VMEM((width, D), low),
            pltpu.VMEM((2, steps, BLK, QKV // 2), low),
            pltpu.VMEM((2, steps, BLK, D // 2), low),
            pltpu.VMEM((2, rows, D), low),
            pltpu.VMEM((6, rows, D), low),
            pltpu.VMEM((group, D), low),
            pltpu.VMEM((3, rows, width), low),
            pltpu.VMEM((group, width), low),
            pltpu.VMEM((group, width), low),
            pltpu.VMEM((2 * group, 2 * HEAD_DIM), full),
            pltpu.VMEM((group, 2 * HEAD_DIM), low),
            pltpu.VMEM((group, 2 * HEAD_DIM), low),
            pltpu.VMEM((group, 2 * HEAD_DIM), low),
            pltpu.VMEM((4, group, 2 * HEAD_DIM), low),
            pltpu.VMEM((group, QKV), low),
            pltpu.VMEM((rows, D), low),
            pltpu.VMEM((SPAN, QUERY_TILE), full),
            dma((2, 2, 2)),
            dma,
            dma((4, 2, steps)),
            dma((4, 2, steps)),
            dma((39,)),
            dma((39,)),
            dma,
            dma,
        ],
        compiler_params=pltpu.CompilerParams(
            collective_id=1, has_side_effects=True, vmem_limit_bytes=63 * 1024 * 1024
        ),
        name="backward_section",
    )(*values)


def ffn_kernel(
    normed, cotangent, gateup, down, hidden, gate_up_grad, normed_part, ffn_part, normed_sum, ffn_sum
):
    units = down.shape[0]
    tile = next(u for u in (6, 4, 3, 2, 1) if units % u == 0)
    size = normed.shape[0]
    half = D // 2
    root = (2.0 / 3.141592653589793) ** 0.5

    def step(c, carry):
        here = pl.ds(pl.multiple_of(c * tile * BLK, 32), tile * BLK)
        pair = pl.ds(pl.multiple_of(c * tile * 2 * BLK, 64), 2 * tile * BLK)
        weights = gateup[pair, :]
        parts = [down[pl.ds(c * tile, tile), i].reshape(tile * BLK, half) for i in range(2)]
        both = mul(weights, normed[...], NT).reshape(tile, 2, BLK, size)
        gate = both[:, 0].reshape(tile * BLK, size)
        upper = both[:, 1].reshape(tile * BLK, size)
        grad = mul(parts[0], cotangent[:, :half], NT) + mul(parts[1], cotangent[:, half:], NT)
        square = gate * gate
        bent = jnp.tanh(root * gate * (1.0 + 0.044715 * square))
        share = 0.5 * (1.0 + bent)
        active = gate * share
        slope = share + 0.5 * gate * (1.0 - bent * bent) * (root * (1.0 + 0.134145 * square))
        units_out = (active * upper).astype(low)
        grads = [(grad * upper * slope).astype(low), (grad * active).astype(low)]
        grads = [g.reshape(tile, 1, BLK, size) for g in grads]
        grads = jnp.concatenate(grads, axis=1).reshape(2 * tile * BLK, size)
        hidden[here, :] = units_out
        gate_up_grad[pair, :] = grads
        first = c == 0
        term = mul(grads, weights, TN)
        terms = [mul(units_out, part, TN) for part in parts]

        @pl.when(first)
        def _():
            normed_sum[...] = term
            ffn_sum[:, :half] = terms[0]
            ffn_sum[:, half:] = terms[1]

        @pl.when(jnp.logical_not(first))
        def _():
            normed_sum[...] += term
            ffn_sum[:, :half] += terms[0]
            ffn_sum[:, half:] += terms[1]

        return carry

    lax.fori_loop(0, units // tile, step, 0)
    normed_part[...] = normed_sum[...].astype(low)
    ffn_part[...] = ffn_sum[...].astype(low)


def feed_forward(normed, cotangent, gateup, down):
    group = normed.shape[0]
    units = down.shape[0]
    size = min(512, group)
    rows = pl.BlockSpec((size, D), lambda t: (t, 0))
    once = pl.Buffered(1)
    return pl.pallas_call(
        ffn_kernel,
        grid=(group // size,),
        in_specs=[
            rows,
            rows,
            pl.BlockSpec(gateup.shape, lambda t: (0, 0), pipeline_mode=once),
            pl.BlockSpec(down.shape, lambda t: (0, 0, 0, 0), pipeline_mode=once),
        ],
        out_specs=[
            pl.BlockSpec((units * BLK, size), lambda t: (0, t)),
            pl.BlockSpec((2 * units * BLK, size), lambda t: (0, t)),
            rows,
            rows,
        ],
        out_shape=[
            jax.ShapeDtypeStruct((units * BLK, group), low),
            jax.ShapeDtypeStruct((2 * units * BLK, group), low),
            jax.ShapeDtypeStruct((group, D), low),
            jax.ShapeDtypeStruct((group, D), low),
        ],
        scratch_shapes=[pltpu.VMEM((size, D), full), pltpu.VMEM((size, D), full)],
        compiler_params=pltpu.CompilerParams(vmem_limit_bytes=58 * 1024 * 1024),
        cost_estimate=pl.CostEstimate(
            flops=12 * units * BLK * group * D,
            bytes_accessed=40 << 20,
            transcendentals=units * BLK * group,
        ),
        name="feed_forward",
    )(normed, cotangent, gateup, down)


def update_kernel(
    rate, turned, w_ref, g_ref, l_ref, r_ref, lr_ref, rr_ref, ln_ref, rn_ref, wn_ref
):
    count, rows, columns = w_ref.shape
    blocks = g_ref[...].T.reshape(count, g_ref.shape[1] // count, g_ref.shape[0])
    for b in range(count):
        grad = blocks[b]
        other = grad.T
        if not turned:
            grad, other = other, grad
        square = jnp.sum(jnp.sum(grad * grad, axis=1, keepdims=True), axis=0, keepdims=True)
        square = square * (1.0 / (rows * columns)) + stat_eps
        grad = grad.astype(low)
        other = other.astype(low)
        ln_ref[b] = 0.5 * l_ref[b] + mul(grad, other, NN) * (0.5 / (columns * square))
        rn_ref[b] = 0.5 * r_ref[b] + mul(other, grad, NN) * (0.5 / (rows * square))
        step = mul(lr_ref[b].astype(low), grad, NN).astype(low)
        step = mul(step, rr_ref[b].astype(low), NN)
        wn_ref[b] = w_ref[b] - step * (rate * lax.rsqrt(square))


def update(weight, grad, left, right, left_root, right_root, rate, turned=False):
    count, rows, columns = weight.shape
    if grad.ndim == 3:
        grad = grad.transpose(1, 0, 2).reshape(rows, count * columns)
    height = columns if turned else rows
    batch = count // (grad.shape[0] // height)
    spec = lambda i, j: pl.BlockSpec((batch, i, j), lambda b: (b, 0, 0))
    return pl.pallas_call(
        functools.partial(update_kernel, rate, turned),
        grid=(count // batch,),
        in_specs=[
            spec(rows, columns),
            pl.BlockSpec((height, grad.shape[1]), lambda b: (b, 0)),
            spec(rows, rows),
            spec(columns, columns),
            spec(rows, rows),
            spec(columns, columns),
        ],
        out_specs=[spec(rows, rows), spec(columns, columns), spec(rows, columns)],
        out_shape=[
            jax.ShapeDtypeStruct(left.shape, full),
            jax.ShapeDtypeStruct(right.shape, full),
            jax.ShapeDtypeStruct(weight.shape, full),
        ],
        compiler_params=pltpu.CompilerParams(vmem_limit_bytes=58 * 1024 * 1024),
        cost_estimate=pl.CostEstimate(
            flops=16 * count * 256 * 256 * 128,
            bytes_accessed=36 * count * rows * 128,
            transcendentals=0,
        ),
        name="update",
    )(weight, grad, left, right, left_root, right_root)


def norm_back(values, inverse, gain, grad):
    scaled = gain * grad
    mean = jnp.mean(values * scaled, axis=-1, keepdims=True)
    return inverse * scaled - values * (inverse * inverse * inverse * mean)


def inverse_norm(values):
    return lax.rsqrt(jnp.mean(values * values, axis=-1, keepdims=True) + norm_eps)


def forward_steps(tokens, cotangent, attn_gain, ffn_gain, stacks, token_order, sequence_ids):
    qkv_stack, out_stack, gateup_stack, down_stack = stacks
    row_count = tokens.shape[0]
    head_count = lax.axis_size("head")
    seq_count = lax.axis_size("seq")
    group = row_count * head_count
    head_index = lax.axis_index("head")
    local_width = QW // head_count
    seq_index = lax.axis_index("seq")
    gains = jnp.concatenate([attn_gain, ffn_gain]).astype(low).astype(full)[None]
    gains = lax.all_to_all(
        jnp.broadcast_to(gains, (head_count * seq_count, gains.shape[1])),
        ("head", "seq"),
        split_axis=0,
        concat_axis=0,
        tiled=True,
    )
    own_gains = attn_gain.shape[0]
    gain_one = gains[:, :own_gains].reshape(1, D)
    gain_two = gains[:, own_gains:].reshape(1, D)


    ids_own = lax.dynamic_slice_in_dim(sequence_ids, seq_index * group, group, 0)
    ids_before = lax.dynamic_slice_in_dim(
        sequence_ids, jnp.maximum(seq_index - 1, 0) * group, group, 0
    )
    ids_before = jnp.where(seq_index > 0, ids_before, -1)
    key_ids = jnp.concatenate([ids_before, ids_own])[:, None]
    query_ids = ids_own[None, :]
    qkv_rows = joined_halves(gather_rows(qkv_stack, 8, to_columns))
    out_rows = joined_halves(gather_rows(out_stack, 8, to_columns))
    gateup = gather_rows(gateup_stack, 16, to_units)
    down = gather_rows(down_stack, 8, to_columns)
    tokens_float = tokens.astype(full)
    normed_one = (tokens_float * inverse_norm(tokens_float) * gain_one).astype(low)
    normed_one_group = jnp.concatenate(head_gather(normed_one))
    feature_start = head_index * local_width
    features = lax.dynamic_slice_in_dim(normed_one_group, feature_start, local_width, 1)
    weights = in_order(head_gather(qkv_rows), 0)
    weights = jnp.concatenate(
        [lax.dynamic_slice_in_dim(weights, feature_start, local_width, 1), weights[:, QW:]], axis=1
    )
    projected = mul(normed_one_group, weights, NN, low)
    buffer_rows = ((token_order // row_count) ^ head_index) * row_count + token_order % row_count
    shuffle = (
        buffer_rows[:, None] == lax.broadcasted_iota(jnp.int32, (group, group), 1)
    ).astype(low)
    stream = mul(shuffle, projected, NN, low)
    kv_stream = stream[:, local_width:]
    kv_before = lax.ppermute(kv_stream, "seq", [(i, i + 1) for i in range(seq_count - 1)])
    kv_both = jnp.concatenate([kv_before, kv_stream], axis=0)
    kv_turned = kv_both.T
    mixed_stream, lse = attend(stream[:, :local_width], kv_both, kv_turned, key_ids, query_ids)
    mixed_group = mul(shuffle, mixed_stream, TN, low)
    part = mul(mixed_group, out_rows, NN, low)
    resid = tokens_float + head_sum([part[i * row_count :][:row_count] for i in range(4)])
    normed_two = (resid * inverse_norm(resid) * gain_two).astype(low)
    normed_group = jnp.concatenate(head_gather(normed_two))
    grad_group = jnp.concatenate(head_gather(cotangent))
    section = (
        jnp.concatenate([gain_one, gain_two]),
        resid,
        normed_group,
        grad_group,
        gateup,
        down,
        features,
        qkv_rows,
        out_rows,
        stream,
        kv_both,
        kv_turned,
        lse,
        mixed_group,
        shuffle,
        key_ids,
        query_ids,
    )
    return section


def backward_steps(
    tokens,
    cotangent,
    gains,
    resid,
    normed_part,
    ffn_part,
    gateup_wgrad,
    down_wgrad,
    features,
    qkv_rows,
    out_rows,
    stream,
    kv_both,
    kv_turned,
    lse,
    mixed_group,
    shuffle,
    key_ids,
    query_ids,
    counts,
):
    row_count = tokens.shape[0]
    group = row_count * lax.axis_size("head")
    seq_count = lax.axis_size("seq")
    local_width = features.shape[1]
    query_stream = stream[:, :local_width]
    gain_one, gain_two = gains[0], gains[1]
    tokens_float = tokens.astype(full)
    inverse_one = inverse_norm(tokens_float)
    inverse_two = inverse_norm(resid)
    normed_two_grad = head_sum([normed_part[i * row_count :][:row_count] for i in range(4)])
    gateup_grad_own = sum_rows(gateup_wgrad, counts[2], 16, from_units)
    down_grad_own = sum_rows(down_wgrad, counts[3], 8, from_columns)
    ffn_out = head_sum([ffn_part[i * row_count :][:row_count] for i in range(4)])
    block_out = (resid + ffn_out).astype(low)

    resid_grad = cotangent.astype(full) + norm_back(resid, inverse_two, gain_two, normed_two_grad)
    gain_two_grad = jnp.sum(normed_two_grad * resid * inverse_two, axis=0)
    proj_grad = resid_grad.astype(low)
    proj_grad_group = jnp.concatenate(head_gather(proj_grad))
    mixed_grad_group = mul(proj_grad_group, out_rows, NT, low)
    mixed_grad_stream = mul(shuffle, mixed_grad_group, NN, low)
    out_wgrad = split_halves(mul(mixed_group, proj_grad_group, TN, low), BLK)
    out_grad_own = sum_rows(out_wgrad, counts[1], 8, from_columns)

    query_grad, kv_grad = attend_back(
        query_stream, mixed_grad_stream, kv_both, kv_turned, key_ids, query_ids, lse
    )
    kv_later = lax.ppermute(
        kv_grad[:group].astype(low), "seq", [(i, i - 1) for i in range(1, seq_count)]
    )
    kv_grad = (kv_grad[group:] + kv_later.astype(full)).astype(low)
    grad_local = mul(shuffle, jnp.concatenate([query_grad, kv_grad], axis=1), TN, low)
    gathered = head_gather(grad_local)

    def own_order(value, j):
        quarters = [value[i * row_count :][:row_count] for i in range(4)]
        return jnp.concatenate([quarters[i ^ j] for i in range(4)])

    gathered = [own_order(value, j) for j, value in enumerate(gathered)]
    kv_total = sum(value[:, local_width:].astype(full) for value in gathered).astype(low)
    qkv_grad = jnp.concatenate(
        [in_order([value[:, :local_width] for value in gathered], 1), kv_total], axis=1
    )
    qkv_wgrad = split_halves(mul(features, qkv_grad, TN, low), BLK)
    qkv_grad_own = sum_rows(qkv_wgrad, counts[0], 8, from_columns)
    feature_grad = mul(qkv_grad, qkv_rows, NT, low)
    order = (0, 2, 1, 3)
    feature_parts = head_exchange([feature_grad[i * row_count :][:row_count] for i in range(4)])
    normed_one_grad = in_order([feature_parts[order.index(j)] for j in range(4)], 1).astype(full)
    input_grad = resid_grad + norm_back(tokens_float, inverse_one, gain_one, normed_one_grad)
    gain_one_grad = jnp.sum(normed_one_grad * tokens_float * inverse_one, axis=0)
    return (
        block_out,
        input_grad,
        jnp.stack([gain_one_grad, gain_two_grad]),
        gateup_grad_own,
        down_grad_own,
        qkv_grad_own,
        out_grad_own,
    )


def on_device(
    tokens,
    cotangent,
    attn_gain,
    ffn_gain,
    qkv_stack,
    out_stack,
    gateup_stack,
    down_stack,
    qkv_left,
    qkv_right,
    out_left,
    out_right,
    gateup_left,
    gateup_right,
    down_left,
    down_right,
    qkv_left_root,
    qkv_right_root,
    out_left_root,
    out_right_root,
    gateup_left_root,
    gateup_right_root,
    down_left_root,
    down_right_root,
    sequence_ids,
    token_order,
):
    row_count = tokens.shape[0]
    head_count = lax.axis_size("head")
    seq_count = lax.axis_size("seq")
    device_count = head_count * seq_count
    group = row_count * head_count
    seq_index = lax.axis_index("seq")
    local_width = QW // head_count

    own_gains = attn_gain.shape[0]
    stacks = (qkv_stack, out_stack, gateup_stack, down_stack)
    whole_rows = all(s.shape[0] % u == 0 for s, u in zip(stacks, (8, 8, 16, 8)))
    if whole_rows:
        tile = jnp.concatenate([attn_gain[None], ffn_gain[None]])
        section = forward_section(
            tokens,
            cotangent,
            jnp.pad(tile, ((0, 6), (0, 128 - own_gains))),
            stacks,
            token_order[None, :],
            sequence_ids[None, :],
            seq_count,
        )
    else:
        section = forward_steps(
            tokens, cotangent, attn_gain, ffn_gain, stacks, token_order, sequence_ids
        )
    (
        gains_both,
        resid,
        normed_group,
        grad_group,
        gateup,
        down,
        features,
        qkv_rows,
        out_all,
        stream,
        kv_both,
        kv_turned,
        lse,
        mixed_group,
        shuffle,
        key_ids,
        query_ids,
    ) = section
    gateup = gateup.reshape(-1, D)
    down = down.reshape(-1, 2, BLK, D // 2)
    unit_count = down.shape[0]
    hidden, gate_up_grad, normed_part, ffn_part = feed_forward(
        normed_group, grad_group, gateup, down
    )
    gateup_wgrad = mul(gate_up_grad, normed_group, NN, low)
    down_wgrad = split_halves(mul(hidden, grad_group, NN, low), BLK)
    kept = (features, qkv_rows, out_all, stream, kv_both, kv_turned, lse, mixed_group, shuffle)
    counts = [s.shape[0] for s in stacks]
    if not whole_rows:
        gateup_wgrad = gateup_wgrad.reshape(2 * unit_count, BLK, D)
    if whole_rows:
        (block_out, input_grad, gain_grads, gateup_own, down_own, qkv_own, out_own, *_) = (
            backward_section(
                seq_count,
                tokens,
                cotangent,
                gains_both,
                resid,
                normed_part,
                ffn_part,
                gateup_wgrad.reshape(seq_count, -1, D),
                down_wgrad.reshape(seq_count, -1, D // 2),
                *kept,
                key_ids,
                query_ids,
            )
        )
        gateup_grad_own, down_grad_own = gateup_own, down_own
        qkv_grad_own, out_grad_own = qkv_own, out_own
    else:
        section = backward_steps(
            tokens, cotangent, gains_both, resid, normed_part, ffn_part, gateup_wgrad, down_wgrad, *kept,
            key_ids, query_ids, counts,
        )
        (block_out, input_grad, gain_grads, gateup_grad_own, down_grad_own, qkv_grad_own, out_grad_own) = section
    gain_one_grad, gain_two_grad = gain_grads[0], gain_grads[1]
    gain_grads = jnp.concatenate(
        [gain_one_grad.reshape(device_count, -1), gain_two_grad.reshape(device_count, -1)], axis=1
    )
    gain_grads = lax.all_to_all(
        gain_grads, ("head", "seq"), split_axis=0, concat_axis=0, tiled=True
    )
    gain_grads = jnp.sum(gain_grads, axis=0)

    gateup_new = update(
        gateup_stack,
        gateup_grad_own,
        gateup_left,
        gateup_right,
        gateup_left_root,
        gateup_right_root,
        0.5 * D ** (-0.5),
        whole_rows,
    )
    down_new = update(
        down_stack,
        down_grad_own,
        down_left,
        down_right,
        down_left_root,
        down_right_root,
        0.5 * FF ** (-0.5),
    )
    out_new = update(
        out_stack,
        out_grad_own,
        out_left,
        out_right,
        out_left_root,
        out_right_root,
        0.5 * (QW // 64) ** (-0.5),
    )
    qkv_new = update(
        qkv_stack,
        qkv_grad_own,
        qkv_left,
        qkv_right,
        qkv_left_root,
        qkv_right_root,
        0.5 * D ** (-0.5),
    )
    return (
        (block_out, input_grad, gain_grads[:own_gains], gain_grads[own_gains:])
        + tuple(qkv_new)
        + tuple(out_new)
        + tuple(gateup_new)
        + tuple(down_new)
    )


def solution(mesh):
    rows = P(("seq", "head"), None)
    gain = P(("head", "seq"))
    blocks = P(("head", "seq"), None, None)
    return jax.shard_map(
        on_device,
        mesh=mesh,
        in_specs=(rows, rows, gain, gain) + (blocks,) * 20 + (P(), P("seq")),
        out_specs=(rows, rows, gain, gain) + (blocks,) * 12,
        check_vma=False,
    )
```

```python
import functools

import jax
import jax.numpy as jnp
from jax import lax
from jax.experimental import pallas as pl
from jax.experimental.pallas import tpu as pltpu
from jax.sharding import PartitionSpec as P

D = 1536
HEAD_DIM = 128
FF = 4608
WINDOW = 1024
GRID = 16
QW = 1536
QKV = 1792
BLK = 96
BQ = 112
BH = 96
NU = 48

norm_eps = 1e-06
stat_eps = 1e-06
neg_fill = -1e30

QUERY_TILE = 256
SPAN = WINDOW + QUERY_TILE

low = jnp.bfloat16
full = jnp.float32

NT = (((1,), (1,)), ((), ()))
NN = (((1,), (0,)), ((), ()))
TN = (((0,), (0,)), ((), ()))


def mul(a, b, dims, kind=full):
    return lax.dot_general(a, b, dims, preferred_element_type=kind)


def ring_place(index, count):
    return jnp.where(index % 2 == 0, index // 2, count - 1 - index // 2)


def ring_index(place, count):
    return jnp.where(place < count // 2, 2 * place, 2 * (count - 1 - place) + 1)


def ring_routes(count):
    order = [i for i in range(0, count, 2)] + [i for i in range(count - 1, 0, -2)]
    up = [(order[i], order[(i + 1) % count]) for i in range(count)]
    return up, [(b, a) for a, b in up]


def seq_gather(shard):
    count = lax.axis_size("seq")
    rows = shard.shape[0]
    half = rows // 2
    me = lax.axis_index("seq")
    place = ring_place(me, count)
    up, down = ring_routes(count)
    out = jnp.zeros((count,) + shard.shape, shard.dtype)
    out = lax.dynamic_update_slice(out, shard[None], (me, 0, 0))
    ahead = shard
    behind = shard
    for step in range(1, count // 2):
        ahead = lax.ppermute(ahead, "seq", up)
        behind = lax.ppermute(behind, "seq", down)
        out = lax.dynamic_update_slice(
            out, ahead[None], (ring_index((place - step + count) % count, count), 0, 0)
        )
        out = lax.dynamic_update_slice(
            out, behind[None], (ring_index((place + step) % count, count), 0, 0)
        )
    ahead = lax.ppermute(ahead[:half], "seq", up)
    behind = lax.ppermute(behind[half:], "seq", down)
    far = ring_index((place + count // 2) % count, count)
    out = lax.dynamic_update_slice(out, ahead[None], (far, 0, 0))
    return lax.dynamic_update_slice(out, behind[None], (far, half, 0))


def seq_sum(parts):
    count, rows = parts.shape[:2]
    half = rows // 2
    place = ring_place(lax.axis_index("seq"), count)
    up, down = ring_routes(count)

    def part(offset):
        index = ring_index((place + offset + count) % count, count)
        return lax.dynamic_slice_in_dim(parts, index, 1, 0)[0]

    far = part(count // 2)
    ahead = lax.ppermute(far[:half], "seq", up)
    behind = lax.ppermute(far[half:], "seq", down)
    for offset in range(count // 2 - 1, 0, -1):
        local = part(offset)
        if ahead.shape[0] == rows:
            local = (local.astype(full) + ahead.astype(full)).astype(low)
        else:
            local = jnp.concatenate(
                [(local[:half].astype(full) + ahead.astype(full)).astype(low), local[half:]]
            )
        ahead = lax.ppermute(local, "seq", up)
        local = part(-offset)
        if behind.shape[0] == rows:
            local = (local.astype(full) + behind.astype(full)).astype(low)
        else:
            local = jnp.concatenate(
                [local[:half], (local[half:].astype(full) + behind.astype(full)).astype(low)]
            )
        behind = lax.ppermute(local, "seq", down)
    return part(0).astype(full) + ahead.astype(full) + behind.astype(full)


def gather_rows(stack, unit, layout):
    short = stack.astype(low)
    if stack.shape[0] % unit == 0:
        shard = layout(short)
        rows = shard.reshape(-1, shard.shape[-1])
        out = seq_gather(rows)
        return out.reshape((-1,) + shard.shape[1:])
    return layout(lax.all_gather(short, "seq", axis=0, tiled=True))


def sum_rows(rows, local, unit, back):
    count = lax.axis_size("seq")
    if local % unit == 0:
        own = seq_sum(rows.reshape(count, -1, rows.shape[-1]))
        return back(own.reshape((-1,) + rows.shape[1:]))
    return lax.psum_scatter(back(rows), "seq", scatter_dimension=0, tiled=True).astype(full)


def to_columns(stack):
    n, i, j = stack.shape
    return stack.reshape(n // 8, 8, i, j).transpose(0, 2, 1, 3).reshape(n // 8, i, 8 * j)


def from_columns(rows):
    n, i, j = rows.shape
    return rows.reshape(n, i, 8, j // 8).transpose(0, 2, 1, 3).reshape(n * 8, i, j // 8)


def to_units(stack):
    n, i, j = stack.shape
    return stack.reshape(n // 16, 16, i, j).transpose(0, 3, 1, 2).reshape(n // 16, j, 16 * i)


def from_units(rows):
    n, j, i = rows.shape
    return rows.reshape(n, j, 16, i // 16).transpose(0, 2, 3, 1).reshape(n * 16, i // 16, j)


def joined_halves(rows):
    n, i, j = rows.shape
    return rows.reshape(n // 2, 2, i, j).transpose(0, 2, 1, 3).reshape(n // 2 * i, 2 * j)


def split_halves(matrix, i):
    rows, columns = matrix.shape
    half = columns // 2
    parts = [matrix[:, at : at + half].reshape(rows // i, i, half) for at in (0, half)]
    return jnp.stack(parts, axis=1).reshape(2 * rows // i, i, half)


def to_partner(value, which):
    count = lax.axis_size("head")
    return lax.ppermute(value, "head", [(i, i ^ which) for i in range(count)])


def head_gather(value):
    across = to_partner(value, 2)
    mate = to_partner(value, 1)
    return value, mate, across, to_partner(across, 1)


def head_exchange(parts):
    return (parts[0],) + tuple(to_partner(parts[j], j) for j in (2, 1, 3))


def head_sum(parts):
    across = (parts[2].astype(full) + to_partner(parts[3], 1).astype(full)).astype(low)
    across = to_partner(across, 2)
    mine = parts[0].astype(full) + to_partner(parts[1], 1).astype(full)
    return mine + across.astype(full)


def in_order(parts, axis):
    me = lax.axis_index("head")
    odd = me % 2 == 1
    lower = [jnp.where(odd, parts[1], parts[0]), jnp.where(odd, parts[0], parts[1])]
    upper = [jnp.where(odd, parts[3], parts[2]), jnp.where(odd, parts[2], parts[3])]
    second = me >= 2
    return jnp.concatenate(
        [jnp.where(second, b, a) for a, b in zip(lower, upper)]
        + [jnp.where(second, a, b) for a, b in zip(lower, upper)],
        axis=axis,
    )


def tile_bias(tile, key_ids, query_ids, bias_ref):
    start = pl.multiple_of(tile * QUERY_TILE, QUERY_TILE)
    shape = (SPAN, QUERY_TILE)
    key = lax.broadcasted_iota(jnp.int32, shape, 0)
    query = lax.broadcasted_iota(jnp.int32, shape, 1)
    same = key_ids[pl.ds(start, SPAN), :] == query_ids[...]
    allowed = same & (key > query) & (key <= query + WINDOW)
    bias_ref[...] = jnp.where(allowed, 0.0, neg_fill)


def attend_kernel(q_ref, kv_ref, kvt_ref, key_ids, query_ids, out_ref, lse_ref, bias_ref):
    tile = pl.program_id(0)
    start = pl.multiple_of(tile * QUERY_TILE, QUERY_TILE)

    @pl.when(pl.program_id(1) == 0)
    def _():
        tile_bias(tile, key_ids, query_ids, bias_ref)

    keys = kv_ref[pl.ds(start, SPAN), :HEAD_DIM]
    scores = mul(keys, q_ref[...], NT) * HEAD_DIM ** (-0.5) + bias_ref[...]
    top = jnp.max(scores, axis=0, keepdims=True)
    expo = jnp.exp(scores - top)
    total = jnp.sum(expo, axis=0, keepdims=True)
    values = kvt_ref[HEAD_DIM:, pl.ds(start, SPAN)]
    mixed = mul(values, expo.astype(low), NN) / total
    out_ref[...] = mixed.T.astype(low)
    lse_ref[0] = top + jnp.log(total)


def attend_back_kernel(
    q_ref, g_ref, kv_ref, kvt_ref, key_ids, query_ids, lse_ref, dq_ref, dkv_ref, bias_ref
):
    tile = pl.program_id(0)
    start = pl.multiple_of(tile * QUERY_TILE, QUERY_TILE)
    scale = HEAD_DIM ** (-0.5)

    @pl.when((tile == 0) & (pl.program_id(1) == 0))
    def _():
        dkv_ref[...] = jnp.zeros_like(dkv_ref)

    @pl.when(pl.program_id(1) == 0)
    def _():
        tile_bias(tile, key_ids, query_ids, bias_ref)

    here = pl.ds(start, SPAN)
    queries = q_ref[...]
    grads = g_ref[...]
    scores = mul(kv_ref[here, :HEAD_DIM], queries, NT) * scale + bias_ref[...]
    probs = jnp.exp(scores - lse_ref[0])
    prob_grad = mul(kv_ref[here, HEAD_DIM:], grads, NT)
    delta = jnp.sum(probs * prob_grad, axis=0, keepdims=True)
    score_grad = (probs * (prob_grad - delta)).astype(low)
    dq = mul(kvt_ref[:HEAD_DIM, here], score_grad, NN) * scale
    dq_ref[...] = dq.T.astype(low)
    dkv_ref[here, :HEAD_DIM] += mul(score_grad, queries, NN) * scale
    dkv_ref[here, HEAD_DIM:] += mul(probs.astype(low), grads, NN)


def attention_specs(group):
    whole = lambda *shape: pl.BlockSpec(shape, lambda t, h: (0,) * len(shape))
    head_rows = pl.BlockSpec((QUERY_TILE, HEAD_DIM), lambda t, h: (t, h))
    keys = whole(2 * group, 2 * HEAD_DIM)
    keys_turned = whole(2 * HEAD_DIM, 2 * group)
    key_ids = whole(2 * group, 1)
    query_ids = pl.BlockSpec((1, QUERY_TILE), lambda t, h: (0, t))
    lse = pl.BlockSpec((1, 1, QUERY_TILE), lambda t, h: (h, 0, t))
    return head_rows, keys, keys_turned, key_ids, query_ids, lse


attention_params = pltpu.CompilerParams(
    dimension_semantics=("arbitrary", "arbitrary"), vmem_limit_bytes=40 * 1024 * 1024
)


def attend(queries, kv, kv_turned, key_ids, query_ids):
    group, width = queries.shape
    heads = width // HEAD_DIM
    rows, keys, turned, kids, qids, lse = attention_specs(group)
    work = heads * (group // QUERY_TILE) * SPAN * QUERY_TILE
    return pl.pallas_call(
        attend_kernel,
        grid=(group // QUERY_TILE, heads),
        in_specs=[rows, keys, turned, kids, qids],
        out_specs=[rows, lse],
        out_shape=[
            jax.ShapeDtypeStruct((group, width), low),
            jax.ShapeDtypeStruct((heads, 1, group), full),
        ],
        scratch_shapes=[pltpu.VMEM((SPAN, QUERY_TILE), full)],
        compiler_params=attention_params,
        cost_estimate=pl.CostEstimate(
            flops=8 * work * HEAD_DIM, bytes_accessed=6 << 20, transcendentals=work
        ),
        name="attend",
    )(queries, kv, kv_turned, key_ids, query_ids)


def attend_back(queries, grads, kv, kv_turned, key_ids, query_ids, lse_rows):
    group, width = queries.shape
    heads = width // HEAD_DIM
    rows, keys, turned, kids, qids, lse = attention_specs(group)
    work = heads * (group // QUERY_TILE) * SPAN * QUERY_TILE
    return pl.pallas_call(
        attend_back_kernel,
        grid=(group // QUERY_TILE, heads),
        in_specs=[rows, rows, keys, turned, kids, qids, lse],
        out_specs=[rows, keys],
        out_shape=[
            jax.ShapeDtypeStruct((group, width), low),
            jax.ShapeDtypeStruct((2 * group, 2 * HEAD_DIM), full),
        ],
        scratch_shapes=[pltpu.VMEM((SPAN, QUERY_TILE), full)],
        compiler_params=attention_params,
        cost_estimate=pl.CostEstimate(
            flops=20 * work * HEAD_DIM, bytes_accessed=8 << 20, transcendentals=work
        ),
        name="attend_back",
    )(queries, grads, kv, kv_turned, key_ids, query_ids, lse_rows)


def remote(source, target, send, recv, where):
    return pltpu.make_async_remote_copy(
        src_ref=source,
        dst_ref=target,
        send_sem=send,
        recv_sem=recv,
        device_id=where,
        device_id_type=pl.DeviceIdType.MESH,
    )


class Ring:
    def __init__(self, count, view, send, recv, split=True):
        me = lax.axis_index("seq")
        self.split = split
        odd = lax.rem(me, 2)
        self.count = count
        self.view = view
        self.send = send
        self.recv = recv
        self.place = (1 - odd) * (me // 2) + odd * (count - 1 - me // 2)
        self.ahead = {"seq": self.shard(1)}
        self.behind = {"seq": self.shard(-1)}
        self.copies = []

    def shard(self, offset):
        place = lax.rem(self.place + offset + self.count, self.count)
        upper = place // (self.count // 2)
        return (1 - upper) * 2 * place + upper * (2 * (self.count - 1 - place) + 1)

    def pair(self, offset, step):
        last = step == self.count // 2
        halved = last and self.split
        views = [
            self.view(self.shard(-offset), 0 if halved else None),
            self.view(self.shard(offset), 1 if halved else None),
        ]
        if last and not self.split:
            views = views[:1]
        return [
            remote(view, view, self.send.at[i, step - 1], self.recv.at[i, step - 1], where)
            for i, (view, where) in enumerate(zip(views, (self.ahead, self.behind)))
        ]

    def start(self, step):
        for copy in self.pair(step - 1, step):
            copy.start()
            self.copies.append(copy)

    def arrive(self, step):
        for copy in self.pair(step, step):
            copy.wait_recv()

    def finish(self):
        for copy in self.copies:
            copy.wait_send()


def turned_row(row):
    size = row.shape[1]
    return jnp.broadcast_to(row.astype(full), (128, size)).T[:, :1]


def forward_kernel(
    count,
    tokens,
    cotangent,
    own_gains,
    qkv_stack,
    out_stack,
    gateup_stack,
    down_stack,
    order,
    ids,
    gains,
    resid,
    normed_group,
    grad_group,
    gateup,
    down,
    features_out,
    qkv_rows_out,
    out_all_out,
    stream_out,
    kv_both_out,
    kv_turned_out,
    lse,
    mixed_group_out,
    shuffle_out,
    key_ids,
    query_ids,
    tokens_group,
    normed,
    weights,
    projected,
    mixed,
    mixed_all,
    bias,
    wide,
    tall,
    gateup_own,
    down_own,
    gain_tiles,
    own_sem,
    ring_send,
    ring_recv,
    head_send,
    head_recv,
    kv_send,
    kv_recv,
    features,
    qkv_rows,
    out_all,
    stream,
    kv_both,
    kv_turned,
    mixed_group,
    shuffle,
    store_sem,
):
    rows = tokens.shape[0]
    group = 4 * rows
    width = features.shape[1]
    heads = width // HEAD_DIM
    head = lax.axis_index("head")
    me = lax.axis_index("seq")
    mate_head = head + 1 - 2 * lax.rem(head, 2)
    across_head = lax.rem(head + 2, 4)
    mate = {"head": mate_head}
    across = {"head": across_head}

    def band(of):
        return pl.ds(pl.multiple_of(of * width, 128), width)

    def chip_columns(of):
        return pl.ds(pl.multiple_of((of // 2) * 2 * width, 128), 2 * width)

    def quarter(ref, i):
        return ref.at[pl.ds(i * rows, rows)]

    copies = []

    def send(index, source, target, where):
        copy = remote(source, target, head_send.at[index], head_recv.at[index], where)
        copy.start()
        copies.append(copy)

    def arrived(index, target, where):
        remote(target, target, head_send.at[index], head_recv.at[index], where).wait_recv()

    def stack_view(ref, columns):
        def view(shard, part):
            first = pl.multiple_of(head * width + (shard // 2) * BLK, 32)
            at = pl.ds(pl.multiple_of(lax.rem(shard, 2) * columns, 128), columns)
            if part is None:
                return ref.at[pl.ds(first, BLK), at]
            return ref.at[pl.ds(pl.multiple_of(first + part * (BLK // 2), 16), BLK // 2), at]

        return view

    def gateup_view(shard, part):
        size = gateup.shape[1]
        if part is None:
            return gateup.at[shard]
        return gateup.at[shard, pl.ds(part * (size // 2), size // 2)]

    def down_view(shard, part):
        if part is None:
            return down.at[shard]
        return down.at[shard, :, pl.ds(part * (BLK // 2), BLK // 2)]

    qkv_view = stack_view(weights, QKV // 2)
    out_view = stack_view(out_all, D // 2)
    gain_view = lambda shard, part: gain_tiles.at[head, shard]
    qkv_ring, out_ring, gateup_ring, down_ring, gain_ring = rings = [
        Ring(count, view, ring_send.at[i], ring_recv.at[i], view is not gain_view)
        for i, view in enumerate((qkv_view, out_view, gateup_view, down_view, gain_view))
    ]

    barrier = pltpu.get_barrier_semaphore()
    for where in (qkv_ring.ahead, qkv_ring.behind, mate, across):
        pl.semaphore_signal(barrier, inc=1, device_id=where, device_id_type=pl.DeviceIdType.MESH)

    @pl.when(me > 0)
    def _():
        pl.semaphore_signal(
            barrier, inc=1, device_id={"seq": me - 1}, device_id_type=pl.DeviceIdType.MESH
        )

    def side_by_side(stack, first):
        size = stack.shape[2]
        blocks = 8
        for c in range(blocks):
            tall[c * size : (c + 1) * size, :] = stack[first + c].T
        return tall[: blocks * size, :].T.astype(low)

    qkv_view(me, None)[...] = side_by_side(qkv_stack, 0)
    gain_tiles[head, me] = own_gains[...]
    pl.semaphore_wait(barrier, 5 - me // (count - 1))
    send(0, tokens, quarter(tokens_group, 2), across)
    send(1, tokens, quarter(tokens_group, 1), mate)
    qkv_ring.start(1)
    gain_ring.start(1)
    for q in range(gateup_own.shape[0] // BLK):
        column = gateup_stack[q * GRID : (q + 1) * GRID].reshape(D, BLK)
        gateup_own[q * BLK : (q + 1) * BLK, :] = column.T.astype(low)
    for m in range(down_own.shape[0]):
        down_own[m] = side_by_side(down_stack, 8 * m)
    own = [
        pltpu.make_async_copy(gateup_own, gateup.at[me], own_sem.at[0]),
        pltpu.make_async_copy(down_own, down.at[me], own_sem.at[1]),
        pltpu.make_async_copy(cotangent, quarter(grad_group, 0), own_sem.at[2]),
    ]
    for copy in own:
        copy.start()
    out_view(me, None)[...] = side_by_side(out_stack, 0)
    for copy in own[:2]:
        copy.wait()

    def pump(step):
        if step > 1:
            gateup_ring.arrive(step - 1)
            down_ring.arrive(step - 1)
        if step <= count // 2:
            gateup_ring.start(step)
            down_ring.start(step)

    pump(1)
    tokens_group[:rows, :] = tokens[...]
    qkv_ring.arrive(1)
    qkv_ring.start(2)
    gain_ring.arrive(1)
    gain_ring.start(2)

    for i in range(4):
        at = turned_row(order[:, i * rows : (i + 1) * rows]).astype(jnp.int32)
        owner = at // rows
        flip = head - 4 * (owner // 2) * (head // 2) - 2 * lax.rem(owner, 2) * lax.rem(head, 2)
        place = (owner + flip) * rows + lax.rem(at, rows)
        shuffle[i * rows : (i + 1) * rows, :] = jnp.where(
            place == lax.broadcasted_iota(jnp.int32, (rows, group), 1), 1.0, 0.0
        ).astype(low)
    query_ids[...] = ids[:, pl.ds(pl.multiple_of(me * group, 128), group)].astype(full)
    before = (me - (me + count - 1) // count) * group
    for i in range(4):
        here = slice(i * rows, (i + 1) * rows)
        at = pl.multiple_of(before + i * rows, 128)
        key_ids[here, :] = jnp.where(me > 0, turned_row(ids[:, pl.ds(at, rows)]), -1.0)
        there = slice(group + i * rows, group + (i + 1) * rows)
        key_ids[there, :] = turned_row(query_ids[:, here])
    for step in range(2, count // 2):
        qkv_ring.arrive(step)
        qkv_ring.start(step + 1)
        gain_ring.arrive(step)
        gain_ring.start(step + 1)
    qkv_ring.arrive(count // 2)

    key_columns = pl.ds(QW, 2 * HEAD_DIM)

    def weight_parts(of, chip_of):
        return [weights.at[band(of), columns] for columns in (chip_columns(chip_of), key_columns)]

    gain_ring.arrive(count // 2)
    send(9, gain_tiles.at[head], gain_tiles.at[head], across)
    send(10, gain_tiles.at[head], gain_tiles.at[head], mate)
    for i, part in enumerate(weight_parts(head, across_head)):
        send(3 + i, part, part, across)
    for i, part in enumerate(weight_parts(head, head)):
        send(7 + i, part, part, mate)
    out_ring.start(1)
    pump(2)
    arrived(0, quarter(tokens_group, 2), across)
    send(2, quarter(tokens_group, 2), quarter(tokens_group, 3), mate)
    qkv_rows[...] = weights[band(head), :]
    arrived(9, gain_tiles.at[across_head], across)
    send(11, gain_tiles.at[across_head], gain_tiles.at[across_head], mate)
    arrived(10, gain_tiles.at[mate_head], mate)
    arrived(11, gain_tiles.at[3 - head], mate)
    size = D // (4 * count)
    for h in range(4):
        for i in range(count):
            at = (h * count + i) * size
            wide[:8, at : at + size] = gain_tiles[h, i][:, :size]
    gains[...] = wide[:2, :D].astype(low).astype(full)

    def norm_rows(i):
        here = pl.ds(i * rows, rows)
        values = tokens_group[here, :].astype(full)
        normed[here, :] = (values * inverse_norm(values) * gains[0:1, :]).astype(low)

    norm_rows(0)
    arrived(1, quarter(tokens_group, 1), mate)
    norm_rows(1)
    out_ring.arrive(1)
    out_ring.start(2)
    norm_rows(2)
    arrived(2, quarter(tokens_group, 3), mate)
    norm_rows(3)
    features[...] = normed[:, band(head)]
    for i, part in enumerate(weight_parts(across_head, head)):
        arrived(3 + i, part, across)
        send(5 + i, part, part, mate)
    out_ring.arrive(2)
    out_ring.start(3)
    for i, part in enumerate(weight_parts(mate_head, head)):
        arrived(7 + i, part, mate)
    send(27, cotangent, quarter(grad_group, 2), across)
    send(28, cotangent, quarter(grad_group, 1), mate)
    for i, part in enumerate(weight_parts(3 - head, head)):
        arrived(5 + i, part, mate)

    key_values = pl.ds(width, 2 * HEAD_DIM)

    def project(columns, target):
        def step(i, carry):
            here = pl.ds(pl.multiple_of(i * rows, rows), rows)
            projected[here, target] = mul(normed[here, :], weights[:, columns], NN).astype(low)
            return carry

        lax.fori_loop(0, 4, step, 0)

        def turn(i, carry):
            here = pl.ds(pl.multiple_of(i * rows, rows), rows)
            stream[here, target] = mul(shuffle[here, :], projected[:, target], NN).astype(low)
            return carry

        lax.fori_loop(0, 4, turn, 0)

    project(key_columns, key_values)
    kv_both[pl.ds(group, group), :] = stream[:, key_values]
    kv_copy = remote(
        kv_both.at[pl.ds(group, group)],
        kv_both.at[pl.ds(0, group)],
        kv_send,
        kv_recv,
        {"seq": lax.rem(me + 1, count)},
    )

    @pl.when(me < count - 1)
    def _():
        kv_copy.start()

    @pl.when(me == 0)
    def _():
        kv_both[pl.ds(0, group), :] = jnp.zeros((group, 2 * HEAD_DIM), low)

    out_ring.arrive(3)
    out_ring.start(4)
    project(band(head), pl.ds(0, width))
    pump(3)
    for i in range(4, 8):
        kv_turned[:, i * rows : (i + 1) * rows] = kv_both[i * rows : (i + 1) * rows, :].T
    out_ring.arrive(4)
    half = width // 2

    def out_part(of, i):
        return out_all.at[pl.ds(pl.multiple_of(of * width + i * half, 64), half)]

    for i in range(2):
        send(12 + i, out_part(head, i), out_part(head, i), across)
    send(16, out_all.at[band(head)], out_all.at[band(head)], mate)

    @pl.when(me > 0)
    def _():
        kv_copy.wait_recv()

    for i in range(4):
        kv_turned[:, i * rows : (i + 1) * rows] = kv_both[i * rows : (i + 1) * rows, :].T
    arrived(27, quarter(grad_group, 2), across)
    send(29, quarter(grad_group, 2), quarter(grad_group, 3), mate)

    def attend_tile(tile, carry):
        start = pl.multiple_of(tile * QUERY_TILE, QUERY_TILE)
        here = pl.ds(start, QUERY_TILE)
        span = pl.ds(start, SPAN)
        shape = (SPAN, QUERY_TILE)
        key = lax.broadcasted_iota(jnp.int32, shape, 0)
        query = lax.broadcasted_iota(jnp.int32, shape, 1)
        same = key_ids[span, :] == query_ids[:, here]
        allowed = same & (key > query) & (key <= query + WINDOW)
        bias[...] = jnp.where(allowed, 0.0, neg_fill)

        def attend_head(j, carry):
            lanes = pl.ds(pl.multiple_of(j * HEAD_DIM, HEAD_DIM), HEAD_DIM)
            scores = mul(kv_both[span, :HEAD_DIM], stream[here, lanes], NT)
            scores = scores * HEAD_DIM ** (-0.5) + bias[...]
            top = jnp.max(scores, axis=0, keepdims=True)
            expo = jnp.exp(scores - top)
            total = jnp.sum(expo, axis=0, keepdims=True)
            out = mul(kv_turned[HEAD_DIM:, span], expo.astype(low), NN) / total
            mixed[here, lanes] = out.T.astype(low)
            lse[j, :, here] = top + jnp.log(total)
            return carry

        return lax.fori_loop(0, heads, attend_head, carry)

    lax.fori_loop(0, group // QUERY_TILE, attend_tile, 0)

    def turn_back(i, carry):
        here = pl.ds(pl.multiple_of(i * rows, rows), rows)
        mixed_group[here, :] = mul(shuffle[:, here], mixed[...], TN).astype(low)
        return carry

    lax.fori_loop(0, 4, turn_back, 0)

    def mixed_part(of, i, size):
        return mixed_all.at[pl.ds(i * size, size), band(of)]

    for i in range(2):
        source = mixed_group.at[pl.ds(i * 2 * rows, 2 * rows)]
        send(17 + i, source, mixed_part(head, 1 - i, 2 * rows), across)
    for i in range(4):
        send(19 + i, quarter(mixed_group, i), mixed_part(head, i ^ 1, rows), mate)
    mixed_all[:, band(head)] = mixed_group[...]
    for i in range(2):
        arrived(12 + i, out_part(across_head, i), across)
        send(14 + i, out_part(across_head, i), out_part(across_head, i), mate)
    pump(4)
    arrived(16, out_all.at[band(mate_head)], mate)
    for i in range(2):
        arrived(14 + i, out_part(3 - head, i), mate)
    for i in range(4):
        arrived(19 + i, mixed_part(mate_head, i ^ 1, rows), mate)
    for i in range(2):
        arrived(17 + i, mixed_part(across_head, 1 - i, 2 * rows), across)
        for j in (2 - 2 * i, 3 - 2 * i):
            part = mixed_part(across_head, j, rows)
            send(23 + j, part, mixed_part(across_head, j ^ 1, rows), mate)
    for j in range(4):
        arrived(23 + j, mixed_part(3 - head, j ^ 1, rows), mate)

    stores = [
        pltpu.make_async_copy(source, target, store_sem.at[i])
        for i, (source, target) in enumerate(
            (
                (features, features_out),
                (qkv_rows, qkv_rows_out),
                (out_all, out_all_out),
                (stream, stream_out),
                (kv_both, kv_both_out),
                (kv_turned, kv_turned_out),
                (mixed_group, mixed_group_out),
                (shuffle, shuffle_out),
            )
        )
    ]
    for copy in stores:
        copy.start()

    def second(i, carry):
        here = pl.ds(pl.multiple_of((3 - i) * rows, rows), rows)
        resid[...] = tokens_group[here, :].astype(full) + mul(mixed_all[here, :], out_all[...], NN)
        values = resid[...]
        normed_group[here, :] = (values * inverse_norm(values) * gains[1:2, :]).astype(low)
        return carry

    lax.fori_loop(0, 4, second, 0)
    arrived(28, quarter(grad_group, 1), mate)
    arrived(29, quarter(grad_group, 3), mate)
    pump(5)
    own[2].wait()
    for copy in stores:
        copy.wait()
    for ring in rings:
        ring.finish()
    for copy in copies:
        copy.wait_send()

    @pl.when(me < count - 1)
    def _():
        kv_copy.wait_send()


def forward_section(tokens, cotangent, gains, stacks, order, ids, count):
    rows = tokens.shape[0]
    group = 4 * rows
    width = QW // 4
    steps = count // 2
    gateup_rows = stacks[2].shape[0] // GRID * BLK
    down_parts = stacks[3].shape[0] // 8
    vmem = pl.BlockSpec(memory_space=pltpu.VMEM)
    hbm = pl.BlockSpec(memory_space=pl.ANY)
    outs = [
        ((2, D), full, vmem),
        ((rows, D), full, vmem),
        ((group, D), low, vmem),
        ((group, D), low, hbm),
        ((count, gateup_rows, D), low, hbm),
        ((count, down_parts, BLK, D // 2), low, hbm),
        ((group, width), low, hbm),
        ((width, QKV), low, hbm),
        ((D, D), low, hbm),
        ((group, width + 2 * HEAD_DIM), low, hbm),
        ((2 * group, 2 * HEAD_DIM), low, hbm),
        ((2 * HEAD_DIM, 2 * group), low, hbm),
        ((width // HEAD_DIM, 1, group), full, vmem),
        ((group, width), low, hbm),
        ((group, group), low, hbm),
        ((2 * group, 1), full, vmem),
        ((1, group), full, vmem),
    ]
    dma = pltpu.SemaphoreType.DMA
    return pl.pallas_call(
        functools.partial(forward_kernel, count),
        in_specs=[vmem] * 9,
        out_specs=[spec for _, _, spec in outs],
        out_shape=[jax.ShapeDtypeStruct(shape, kind) for shape, kind, _ in outs],
        scratch_shapes=[
            pltpu.VMEM((group, D), low),
            pltpu.VMEM((group, D), low),
            pltpu.VMEM((D, QKV), low),
            pltpu.VMEM((group, width + 2 * HEAD_DIM), low),
            pltpu.VMEM((group, width), low),
            pltpu.VMEM((group, D), low),
            pltpu.VMEM((SPAN, QUERY_TILE), full),
            pltpu.VMEM((8, D), full),
            pltpu.VMEM((QKV // 2, BLK), full),
            pltpu.VMEM((gateup_rows, D), low),
            pltpu.VMEM((down_parts, BLK, D // 2), low),
            pltpu.VMEM((4, count, 8, 128), full),
            dma((3,)),
            dma((5, 2, steps)),
            dma((5, 2, steps)),
            dma((30,)),
            dma((30,)),
            dma,
            dma,
            *[pltpu.VMEM(outs[i][0], low) for i in (6, 7, 8, 9, 10, 11, 13, 14)],
            dma((8,)),
        ],
        compiler_params=pltpu.CompilerParams(
            collective_id=0, has_side_effects=True, vmem_limit_bytes=58 * 1024 * 1024
        ),
        name="forward_section",
    )(tokens, cotangent, gains, *stacks, order, ids)


class SumRing:
    def __init__(self, count, view, first, buffers, send, recv):
        self.ring = Ring(count, None, None, None)
        self.steps = count // 2
        self.view = view
        self.first = first
        self.buffers = buffers
        self.rows = buffers.shape[2]
        self.send = send
        self.recv = recv
        self.copies = []

    def where(self, way):
        return self.ring.behind if way else self.ring.ahead

    def half(self, way):
        return self.buffers.at[way, 0, pl.ds(way * (self.rows // 2), self.rows // 2)]

    def copy(self, way, step, source, target):
        return remote(source, target, self.send.at[way, step], self.recv.at[way, step], self.where(way))

    def start(self):
        shard = self.ring.shard(self.steps)
        for way in range(2):
            copy = self.copy(way, 0, self.first(shard, way), self.half(way))
            copy.start()
            self.copies.append(copy)

    def arrived(self, way, step):
        target = self.buffers.at[way, step] if step else self.half(way)
        self.copy(way, step, target, target).wait_recv()

    def step(self, step):
        block = 48
        for way in range(2):
            self.arrived(way, step - 1)
            offset = self.steps - step
            local = self.view(self.ring.shard(-offset if way else offset))
            buffer = self.buffers.at[way, step - 1]

            def add(i, carry):
                here = pl.ds(pl.multiple_of(i * block, 16), block)
                buffer[here, :] = (local[here, :].astype(full) + buffer[here, :].astype(full)).astype(low)
                return carry

            def keep(i, carry):
                here = pl.ds(pl.multiple_of(i * block, 16), block)
                buffer[here, :] = local[here, :]
                return carry

            blocks = self.rows // block
            if step > 1:
                lax.fori_loop(0, blocks, add, 0)
            else:
                lax.fori_loop(way * (blocks // 2), (way + 1) * (blocks // 2), add, 0)
                lax.fori_loop((1 - way) * (blocks // 2), (2 - way) * (blocks // 2), keep, 0)
            copy = self.copy(way, step, buffer, self.buffers.at[way, step])
            copy.start()
            self.copies.append(copy)

    def finish(self, out):
        block = 48
        last = self.steps - 1
        for way in range(2):
            self.arrived(way, last)
        local = self.view(self.ring.shard(0))

        def add(i, carry):
            here = pl.ds(pl.multiple_of(i * block, 16), block)
            out[here, :] = (
                local[here, :].astype(full)
                + self.buffers[0, last, here, :].astype(full)
                + self.buffers[1, last, here, :].astype(full)
            )
            return carry

        lax.fori_loop(0, self.rows // block, add, 0)
        for copy in self.copies:
            copy.wait_send()


class StagedSumRing(SumRing):
    def __init__(self, count, parts, buffers, held, terms, load, send, recv):
        size = parts.shape[1] // 2
        first = lambda shard, part: parts.at[shard, pl.ds(part * size, size)]
        super().__init__(count, None, first, buffers, send, recv)
        self.parts = parts
        self.held = held
        self.terms = terms
        self.load = load
        self.last = [None, None]

    def fetch(self, way, offset):
        shard = self.ring.shard(-offset if way else offset)
        copy = pltpu.make_async_copy(
            self.parts.at[shard], self.terms.at[way], self.load.at[1, way]
        )
        copy.start()
        return copy

    def start(self):
        super().start()
        self.fetched = [self.fetch(way, self.steps - 1) for way in range(2)]

    def take(self, way, step):
        self.arrived(way, step)
        if self.last[way] is not None:
            self.last[way].wait_send()
        source, target = self.buffers.at[way, step], self.held.at[way]
        if step == 0:
            half = pl.ds(way * (self.rows // 2), self.rows // 2)
            source, target = self.half(way), self.held.at[way, half]
        copy = pltpu.make_async_copy(source, target, self.load.at[0, way])
        copy.start()
        return copy

    def step(self, step):
        block = 48
        taken = [self.take(way, step - 1) for way in range(2)]
        for way in range(2):
            taken[way].wait()
            self.fetched[way].wait()
            held, terms = self.held.at[way], self.terms.at[way]

            def add(i, carry):
                here = pl.ds(pl.multiple_of(i * block, 16), block)
                held[here, :] = (terms[here, :].astype(full) + held[here, :].astype(full)).astype(low)
                return carry

            def keep(i, carry):
                here = pl.ds(pl.multiple_of(i * block, 16), block)
                held[here, :] = terms[here, :]
                return carry

            blocks = self.rows // block
            if step > 1:
                lax.fori_loop(0, blocks, add, 0)
            else:
                lax.fori_loop(way * (blocks // 2), (way + 1) * (blocks // 2), add, 0)
                lax.fori_loop((1 - way) * (blocks // 2), (2 - way) * (blocks // 2), keep, 0)
            self.last[way] = self.copy(way, step, held, self.buffers.at[way, step])
            self.last[way].start()
            if step < self.steps - 1 or way == 0:
                self.fetched[way] = self.fetch(way, self.steps - 1 - step)

    def finish(self, out):
        block = 48
        taken = [self.take(way, self.steps - 1) for way in range(2)]
        for copy in taken:
            copy.wait()
        self.fetched[0].wait()

        def add(i, carry):
            here = pl.ds(pl.multiple_of(i * block, 16), block)
            out[here, :] = (
                self.terms[0, here, :].astype(full)
                + self.held[0, here, :].astype(full)
                + self.held[1, here, :].astype(full)
            )
            return carry

        lax.fori_loop(0, self.rows // block, add, 0)
        for copy in self.copies:
            copy.wait_send()


def backward_kernel(
    count,
    tokens,
    cotangent,
    gains,
    resid,
    normed_part,
    ffn_part,
    gateup_parts,
    down_parts,
    features_in,
    qkv_rows_in,
    out_all_in,
    stream_in,
    kv_both_in,
    kv_turned_in,
    lse,
    mixed_group_in,
    shuffle_in,
    key_ids,
    query_ids,
    block_out,
    input_grad,
    gain_grads,
    gateup_grad,
    down_grad,
    qkv_grad,
    out_grad,
    gateup_sums,
    down_sums,
    gateup_held,
    gateup_terms,
    down_held,
    down_terms,
    part_quarter,
    qkv_local,
    out_local,
    qkv_sums,
    out_sums,
    sum_out,
    sum_in,
    proj_group,
    turned_out,
    turned_grad,
    grad_stream,
    kv_total,
    kv_out,
    kv_in,
    stream_grad,
    kv_mate,
    all_grad,
    normed_grad,
    bias,
    load_sem,
    part_sem,
    ring_send,
    ring_recv,
    head_send,
    head_recv,
    kv_send,
    kv_recv,
    features,
    qkv_rows,
    out_all,
    stream,
    kv_both,
    kv_turned,
    mixed_group,
    shuffle,
    take_sem,
):
    rows = tokens.shape[0]
    group = 4 * rows
    width = features.shape[1]
    heads = width // HEAD_DIM
    scale = HEAD_DIM ** (-0.5)
    query_grad = turned_grad
    feature_grad = grad_stream
    head = lax.axis_index("head")
    me = lax.axis_index("seq")
    mate_head = head + 1 - 2 * lax.rem(head, 2)
    across_head = lax.rem(head + 2, 4)
    mate = {"head": mate_head}
    across = {"head": across_head}
    corner = {"head": 3 - head}

    def lanes(of):
        return pl.ds(pl.multiple_of(of * width, 128), width)

    def quarter(i):
        return pl.ds(i * rows, rows)

    copies = []

    def send(index, source, target, where):
        copy = remote(source, target, head_send.at[index], head_recv.at[index], where)
        copy.start()
        copies.append(copy)

    def arrived(index, target, where):
        remote(target, target, head_send.at[index], head_recv.at[index], where).wait_recv()

    def shard_view(ref, columns):
        def view(shard, part=None):
            first = pl.multiple_of((shard // 2) * BLK, 32)
            at = pl.ds(pl.multiple_of(lax.rem(shard, 2) * columns, 128), columns)
            if part is None:
                return ref.at[pl.ds(first, BLK), at]
            return ref.at[pl.ds(pl.multiple_of(first + part * (BLK // 2), 16), BLK // 2), at]

        return view

    qkv_view = shard_view(qkv_local, QKV // 2)
    out_view = shard_view(out_local, D // 2)
    gateup_ring = StagedSumRing(
        count,
        gateup_parts,
        gateup_sums,
        gateup_held,
        gateup_terms,
        load_sem.at[0],
        ring_send.at[0],
        ring_recv.at[0],
    )
    down_ring = StagedSumRing(
        count,
        down_parts,
        down_sums,
        down_held,
        down_terms,
        load_sem.at[1],
        ring_send.at[1],
        ring_recv.at[1],
    )
    qkv_ring = SumRing(count, qkv_view, qkv_view, qkv_sums, ring_send.at[2], ring_recv.at[2])
    out_ring = SumRing(count, out_view, out_view, out_sums, ring_send.at[3], ring_recv.at[3])

    barrier = pltpu.get_barrier_semaphore()
    for where in (gateup_ring.where(0), gateup_ring.where(1), mate, across, corner):
        pl.semaphore_signal(barrier, inc=1, device_id=where, device_id_type=pl.DeviceIdType.MESH)

    @pl.when(me < count - 1)
    def _():
        pl.semaphore_signal(
            barrier, inc=1, device_id={"seq": me + 1}, device_id_type=pl.DeviceIdType.MESH
        )

    pl.semaphore_wait(barrier, 5 + (me + count - 1) // count)

    def fetch(value, i):
        copy = pltpu.make_async_copy(value.at[quarter(i)], part_quarter, part_sem)
        copy.start()
        copy.wait()
        return part_quarter[...].astype(full)

    def sum_first(base, slot, value):
        send(base, value.at[quarter(3)], sum_in.at[slot], mate)
        send(base + 1, value.at[quarter(1)], sum_in.at[slot + 1], mate)

    def sum_across(base, slot, value):
        own = fetch(value, 2)
        arrived(base, sum_in.at[slot], mate)
        sum_out[slot // 3] = (own + sum_in[slot].astype(full)).astype(low)
        send(base + 2, sum_out.at[slot // 3], sum_in.at[slot + 2], across)

    def sum_last(base, slot, value):
        own = fetch(value, 0)
        arrived(base + 1, sum_in.at[slot + 1], mate)
        own = own + sum_in[slot + 1].astype(full)
        arrived(base + 2, sum_in.at[slot + 2], across)
        return own + sum_in[slot + 2].astype(full)

    takes = [
        pltpu.make_async_copy(source, target, take_sem.at[i])
        for i, (source, target) in enumerate(
            (
                (features_in, features),
                (qkv_rows_in, qkv_rows),
                (out_all_in, out_all),
                (stream_in, stream),
                (kv_both_in, kv_both),
                (kv_turned_in, kv_turned),
                (mixed_group_in, mixed_group),
                (shuffle_in, shuffle),
            )
        )
    ]
    sum_first(0, 0, normed_part)
    for copy in takes:
        copy.start()
    gateup_ring.start()
    down_ring.start()
    sum_across(0, 0, normed_part)
    sum_first(3, 3, ffn_part)

    normed_two_grad = sum_last(0, 0, normed_part)
    values = resid[...]
    inverse = inverse_norm(values)
    gain_grads[1:2, :] = jnp.sum(normed_two_grad * values * inverse, axis=0, keepdims=True)
    input_grad[...] = cotangent[...].astype(full) + norm_back(
        values, inverse, gains[1:2, :], normed_two_grad
    )
    proj_group[quarter(0), :] = input_grad[...].astype(low)

    for copy in takes:
        copy.wait()

    def back_projection(of):
        weights = out_all[pl.ds(pl.multiple_of(of * width, 128), width), :]
        return mul(proj_group[quarter(0), :], weights, NT).astype(low)

    for j, of, where in ((2, across_head, across), (3, 3 - head, corner), (1, mate_head, mate)):
        turned_out[j - 1] = back_projection(of)
        send(31 + j, turned_out.at[j - 1], turned_grad.at[quarter(j)], where)
    send(6, proj_group.at[quarter(0)], proj_group.at[quarter(2)], across)
    send(7, proj_group.at[quarter(0)], proj_group.at[quarter(1)], mate)
    turned_grad[quarter(0), :] = back_projection(head)
    gateup_ring.step(1)
    down_ring.step(1)
    for j, where in ((1, mate), (2, across), (3, corner)):
        arrived(31 + j, turned_grad.at[quarter(j)], where)

    def turn(i, carry):
        here = pl.ds(pl.multiple_of(i * rows, rows), rows)
        grad_stream[here, :] = mul(shuffle[here, :], turned_grad[...], NN).astype(low)
        return carry

    lax.fori_loop(0, 4, turn, 0)

    kv_total[...] = jnp.zeros_like(kv_total)

    def back_tile(tile, carry):
        start = pl.multiple_of(tile * QUERY_TILE, QUERY_TILE)
        here = pl.ds(start, QUERY_TILE)
        span = pl.ds(start, SPAN)
        shape = (SPAN, QUERY_TILE)
        key = lax.broadcasted_iota(jnp.int32, shape, 0)
        query = lax.broadcasted_iota(jnp.int32, shape, 1)
        same = key_ids[span, :] == query_ids[:, here]
        allowed = same & (key > query) & (key <= query + WINDOW)
        bias[...] = jnp.where(allowed, 0.0, neg_fill)

        def back_head(j, carry):
            at = pl.ds(pl.multiple_of(j * HEAD_DIM, HEAD_DIM), HEAD_DIM)
            queries = stream[here, at]
            grads = grad_stream[here, at]
            scores = mul(kv_both[span, :HEAD_DIM], queries, NT) * scale + bias[...]
            probs = jnp.exp(scores - lse[j, :, here])
            prob_grad = mul(kv_both[span, HEAD_DIM:], grads, NT)
            delta = jnp.sum(probs * prob_grad, axis=0, keepdims=True)
            score_grad = (probs * (prob_grad - delta)).astype(low)
            turned = mul(kv_turned[:HEAD_DIM, span], score_grad, NN) * scale
            query_grad[here, at] = turned.T.astype(low)
            kv_total[span, :HEAD_DIM] += mul(score_grad, queries, NN) * scale
            kv_total[span, HEAD_DIM:] += mul(probs.astype(low), grads, NN)
            return carry

        return lax.fori_loop(0, heads, back_head, carry)

    lax.fori_loop(0, group // QUERY_TILE, back_tile, 0)
    kv_out[...] = kv_total[:group, :].astype(low)
    kv_copy = remote(kv_out, kv_in, kv_send, kv_recv, {"seq": lax.rem(me + count - 1, count)})

    @pl.when(me > 0)
    def _():
        kv_copy.start()

    def turn_back(i, carry):
        here = pl.ds(pl.multiple_of(i * rows, rows), rows)
        all_grad[here, lanes(head)] = mul(shuffle[:, here], query_grad[...], TN).astype(low)
        return carry

    lax.fori_loop(0, 4, turn_back, 0)

    def swapped(index, ref, columns, distance, where):
        for i in range(4):
            send(
                index + i,
                ref.at[quarter(i), columns],
                ref.at[quarter(i ^ distance), columns],
                where,
            )

    def swapped_arrived(index, ref, columns, distance, where):
        for i in range(4):
            arrived(index + i, ref.at[quarter(i ^ distance), columns], where)

    swapped(9, all_grad, lanes(head), 2, across)
    swapped(13, all_grad, lanes(head), 1, mate)
    arrived(6, proj_group.at[quarter(2)], across)
    send(8, proj_group.at[quarter(2)], proj_group.at[quarter(3)], mate)
    gateup_ring.step(2)
    down_ring.step(2)
    sum_across(3, 3, ffn_part)
    arrived(7, proj_group.at[quarter(1)], mate)
    arrived(8, proj_group.at[quarter(3)], mate)
    for i in range(3):
        at = slice(i * (D // 3), (i + 1) * (D // 3))
        out_local[:, at] = mul(mixed_group[...], proj_group[:, at], TN).astype(low)
    out_ring.start()

    @pl.when(me < count - 1)
    def _():
        kv_copy.wait_recv()
        kv_total[pl.ds(group, group), :] += kv_in[...].astype(full)

    stream_grad[...] = kv_total[pl.ds(group, group), :].astype(low)

    def turn_keys(i, carry):
        here = pl.ds(pl.multiple_of(i * rows, rows), rows)
        kv_mate[0, here, :] = mul(shuffle[:, here], stream_grad[...], TN).astype(low)
        return carry

    lax.fori_loop(0, 4, turn_keys, 0)
    for i in range(4):
        send(17 + i, kv_mate.at[0, quarter(i)], kv_mate.at[1, quarter(i ^ 1)], mate)
    for i in range(4):
        arrived(17 + i, kv_mate.at[1, quarter(i ^ 1)], mate)
    kv_total[pl.ds(0, group), :] = kv_mate[0].astype(full) + kv_mate[1].astype(full)
    kv_mate[2] = kv_total[pl.ds(0, group), :].astype(low)
    mine = pl.ds(pl.multiple_of(lax.rem(head, 2) * HEAD_DIM, HEAD_DIM), HEAD_DIM)
    of_mine = pl.ds(pl.multiple_of(QW + lax.rem(head, 2) * HEAD_DIM, HEAD_DIM), HEAD_DIM)
    of_mate = pl.ds(pl.multiple_of(QW + lax.rem(mate_head, 2) * HEAD_DIM, HEAD_DIM), HEAD_DIM)
    for i in range(4):
        send(21 + i, kv_mate.at[2, quarter(i), mine], kv_mate.at[3, quarter(i ^ 2), mine], across)
    out_ring.step(1)
    gateup_ring.step(3)
    down_ring.step(3)
    swapped_arrived(9, all_grad, lanes(across_head), 2, across)
    swapped(25, all_grad, lanes(across_head), 1, mate)
    swapped_arrived(13, all_grad, lanes(mate_head), 1, mate)
    for i in range(4):
        arrived(21 + i, kv_mate.at[3, quarter(i ^ 2), mine], across)
    all_grad[:, of_mine] = (
        kv_total[pl.ds(0, group), mine] + kv_mate[3, :, mine].astype(full)
    ).astype(low)
    swapped(35, all_grad, of_mine, 1, mate)
    swapped_arrived(35, all_grad, of_mate, 1, mate)
    swapped_arrived(25, all_grad, lanes(3 - head), 1, mate)

    for i in range(2):
        at = slice(i * (QKV // 2), (i + 1) * (QKV // 2))
        qkv_local[:, at] = mul(features[...], all_grad[:, at], TN).astype(low)
    qkv_ring.start()
    for i, where in ((2, across), (3, corner), (1, mate)):
        feature_grad[quarter(i), :] = mul(all_grad[quarter(i), :], qkv_rows[...], NT).astype(low)
        send(28 + i, feature_grad.at[quarter(i)], normed_grad.at[:, lanes(head)], where)
    normed_grad[:, lanes(head)] = mul(all_grad[quarter(0), :], qkv_rows[...], NT).astype(low)
    qkv_ring.step(1)
    out_ring.step(2)
    block_out[...] = (resid[...] + sum_last(3, 3, ffn_part)).astype(low)
    for i, where, of in ((2, across, across_head), (3, corner, 3 - head), (1, mate, mate_head)):
        arrived(28 + i, normed_grad.at[:, lanes(of)], where)
    qkv_ring.step(2)
    normed_one_grad = normed_grad[...].astype(full)
    values = tokens[...].astype(full)
    inverse = inverse_norm(values)
    gain_grads[0:1, :] = jnp.sum(normed_one_grad * values * inverse, axis=0, keepdims=True)
    input_grad[...] += norm_back(values, inverse, gains[0:1, :], normed_one_grad)
    qkv_ring.step(3)
    out_ring.step(3)
    gateup_ring.finish(gateup_grad)
    down_ring.finish(down_grad)
    out_ring.finish(out_grad)
    qkv_ring.finish(qkv_grad)
    for copy in copies:
        copy.wait_send()

    @pl.when(me > 0)
    def _():
        kv_copy.wait_send()


def backward_section(count, *values):
    (tokens, cotangent, gains, resid, normed_part, ffn_part, gateup_parts, down_parts) = values[:8]
    rows = tokens.shape[0]
    group = 4 * rows
    width = QW // 4
    steps = count // 2
    vmem = pl.BlockSpec(memory_space=pltpu.VMEM)
    hbm = pl.BlockSpec(memory_space=pl.ANY)
    shard = gateup_parts.shape[1:]
    down_shard = down_parts.shape[1:]
    outs = [
        ((rows, D), low),
        ((rows, D), full),
        ((2, D), full),
        (shard, full),
        (down_shard, full),
        ((BLK, QKV // 2), full),
        ((BLK, D // 2), full),
        ((2, steps) + shard, low),
        ((2, steps) + down_shard, low),
    ]
    dma = pltpu.SemaphoreType.DMA
    return pl.pallas_call(
        functools.partial(backward_kernel, count),
        in_specs=[vmem] * 4 + [hbm] * 10 + [vmem] + [hbm] * 2 + [vmem] * 2,
        out_specs=[vmem] * 7 + [hbm] * 2,
        out_shape=[jax.ShapeDtypeStruct(shape, kind) for shape, kind in outs],
        scratch_shapes=[
            pltpu.VMEM((2,) + shard, low),
            pltpu.VMEM((2,) + shard, low),
            pltpu.VMEM((2,) + down_shard, low),
            pltpu.VMEM((2,) + down_shard, low),
            pltpu.VMEM((rows, D), low),
            pltpu.VMEM((width, QKV), low),
            pltpu.VMEM((width, D), low),
            pltpu.VMEM((2, steps, BLK, QKV // 2), low),
            pltpu.VMEM((2, steps, BLK, D // 2), low),
            pltpu.VMEM((2, rows, D), low),
            pltpu.VMEM((6, rows, D), low),
            pltpu.VMEM((group, D), low),
            pltpu.VMEM((3, rows, width), low),
            pltpu.VMEM((group, width), low),
            pltpu.VMEM((group, width), low),
            pltpu.VMEM((2 * group, 2 * HEAD_DIM), full),
            pltpu.VMEM((group, 2 * HEAD_DIM), low),
            pltpu.VMEM((group, 2 * HEAD_DIM), low),
            pltpu.VMEM((group, 2 * HEAD_DIM), low),
            pltpu.VMEM((4, group, 2 * HEAD_DIM), low),
            pltpu.VMEM((group, QKV), low),
            pltpu.VMEM((rows, D), low),
            pltpu.VMEM((SPAN, QUERY_TILE), full),
            dma((2, 2, 2)),
            dma,
            dma((4, 2, steps)),
            dma((4, 2, steps)),
            dma((39,)),
            dma((39,)),
            dma,
            dma,
            *[pltpu.VMEM(values[i].shape, low) for i in (8, 9, 10, 11, 12, 13, 15, 16)],
            dma((8,)),
        ],
        compiler_params=pltpu.CompilerParams(
            collective_id=1, has_side_effects=True, vmem_limit_bytes=63 * 1024 * 1024
        ),
        name="backward_section",
    )(*values)


def ffn_kernel(
    normed, cotangent, gateup, down, hidden, gate_up_grad, normed_part, ffn_part, normed_sum, ffn_sum
):
    units = down.shape[0]
    tile = next(u for u in (6, 4, 3, 2, 1) if units % u == 0)
    size = normed.shape[0]
    half = D // 2
    root = (2.0 / 3.141592653589793) ** 0.5

    def step(c, carry):
        here = pl.ds(pl.multiple_of(c * tile * BLK, 32), tile * BLK)
        pair = pl.ds(pl.multiple_of(c * tile * 2 * BLK, 64), 2 * tile * BLK)
        weights = gateup[pair, :]
        parts = [down[pl.ds(c * tile, tile), i].reshape(tile * BLK, half) for i in range(2)]
        both = mul(weights, normed[...], NT).reshape(tile, 2, BLK, size)
        gate = both[:, 0].reshape(tile * BLK, size)
        upper = both[:, 1].reshape(tile * BLK, size)
        grad = mul(parts[0], cotangent[:, :half], NT) + mul(parts[1], cotangent[:, half:], NT)
        square = gate * gate
        bent = jnp.tanh(root * gate * (1.0 + 0.044715 * square))
        share = 0.5 * (1.0 + bent)
        active = gate * share
        slope = share + 0.5 * gate * (1.0 - bent * bent) * (root * (1.0 + 0.134145 * square))
        units_out = (active * upper).astype(low)
        grads = [(grad * upper * slope).astype(low), (grad * active).astype(low)]
        grads = [g.reshape(tile, 1, BLK, size) for g in grads]
        grads = jnp.concatenate(grads, axis=1).reshape(2 * tile * BLK, size)
        hidden[here, :] = units_out
        gate_up_grad[pair, :] = grads
        first = c == 0
        term = mul(grads, weights, TN)
        terms = [mul(units_out, part, TN) for part in parts]

        @pl.when(first)
        def _():
            normed_sum[...] = term
            ffn_sum[:, :half] = terms[0]
            ffn_sum[:, half:] = terms[1]

        @pl.when(jnp.logical_not(first))
        def _():
            normed_sum[...] += term
            ffn_sum[:, :half] += terms[0]
            ffn_sum[:, half:] += terms[1]

        return carry

    lax.fori_loop(0, units // tile, step, 0)
    normed_part[...] = normed_sum[...].astype(low)
    ffn_part[...] = ffn_sum[...].astype(low)


def feed_forward(normed, cotangent, gateup, down):
    group = normed.shape[0]
    units = down.shape[0]
    size = min(512, group)
    rows = pl.BlockSpec((size, D), lambda t: (t, 0))
    once = pl.Buffered(1)
    return pl.pallas_call(
        ffn_kernel,
        grid=(group // size,),
        in_specs=[
            rows,
            rows,
            pl.BlockSpec(gateup.shape, lambda t: (0, 0), pipeline_mode=once),
            pl.BlockSpec(down.shape, lambda t: (0, 0, 0, 0), pipeline_mode=once),
        ],
        out_specs=[
            pl.BlockSpec((units * BLK, size), lambda t: (0, t)),
            pl.BlockSpec((2 * units * BLK, size), lambda t: (0, t)),
            rows,
            rows,
        ],
        out_shape=[
            jax.ShapeDtypeStruct((units * BLK, group), low),
            jax.ShapeDtypeStruct((2 * units * BLK, group), low),
            jax.ShapeDtypeStruct((group, D), low),
            jax.ShapeDtypeStruct((group, D), low),
        ],
        scratch_shapes=[pltpu.VMEM((size, D), full), pltpu.VMEM((size, D), full)],
        compiler_params=pltpu.CompilerParams(vmem_limit_bytes=58 * 1024 * 1024),
        cost_estimate=pl.CostEstimate(
            flops=12 * units * BLK * group * D,
            bytes_accessed=40 << 20,
            transcendentals=units * BLK * group,
        ),
        name="feed_forward",
    )(normed, cotangent, gateup, down)


def update_kernel(
    rate, turned, w_ref, g_ref, l_ref, r_ref, lr_ref, rr_ref, ln_ref, rn_ref, wn_ref
):
    count, rows, columns = w_ref.shape
    blocks = g_ref[...].T.reshape(count, g_ref.shape[1] // count, g_ref.shape[0])
    for b in range(count):
        grad = blocks[b]
        other = grad.T
        if not turned:
            grad, other = other, grad
        square = jnp.sum(jnp.sum(grad * grad, axis=1, keepdims=True), axis=0, keepdims=True)
        square = square * (1.0 / (rows * columns)) + stat_eps
        grad = grad.astype(low)
        other = other.astype(low)
        ln_ref[b] = 0.5 * l_ref[b] + mul(grad, other, NN) * (0.5 / (columns * square))
        rn_ref[b] = 0.5 * r_ref[b] + mul(other, grad, NN) * (0.5 / (rows * square))
        step = mul(lr_ref[b].astype(low), grad, NN).astype(low)
        step = mul(step, rr_ref[b].astype(low), NN)
        wn_ref[b] = w_ref[b] - step * (rate * lax.rsqrt(square))


def update(weight, grad, left, right, left_root, right_root, rate, turned=False):
    count, rows, columns = weight.shape
    if grad.ndim == 3:
        grad = grad.transpose(1, 0, 2).reshape(rows, count * columns)
    height = columns if turned else rows
    batch = count // (grad.shape[0] // height)
    spec = lambda i, j: pl.BlockSpec((batch, i, j), lambda b: (b, 0, 0))
    return pl.pallas_call(
        functools.partial(update_kernel, rate, turned),
        grid=(count // batch,),
        in_specs=[
            spec(rows, columns),
            pl.BlockSpec((height, grad.shape[1]), lambda b: (b, 0)),
            spec(rows, rows),
            spec(columns, columns),
            spec(rows, rows),
            spec(columns, columns),
        ],
        out_specs=[spec(rows, rows), spec(columns, columns), spec(rows, columns)],
        out_shape=[
            jax.ShapeDtypeStruct(left.shape, full),
            jax.ShapeDtypeStruct(right.shape, full),
            jax.ShapeDtypeStruct(weight.shape, full),
        ],
        compiler_params=pltpu.CompilerParams(vmem_limit_bytes=58 * 1024 * 1024),
        cost_estimate=pl.CostEstimate(
            flops=16 * count * 256 * 256 * 128,
            bytes_accessed=36 * count * rows * 128,
            transcendentals=0,
        ),
        name="update",
    )(weight, grad, left, right, left_root, right_root)


def norm_back(values, inverse, gain, grad):
    scaled = gain * grad
    mean = jnp.mean(values * scaled, axis=-1, keepdims=True)
    return inverse * scaled - values * (inverse * inverse * inverse * mean)


def inverse_norm(values):
    return lax.rsqrt(jnp.mean(values * values, axis=-1, keepdims=True) + norm_eps)


def forward_steps(tokens, cotangent, attn_gain, ffn_gain, stacks, token_order, sequence_ids):
    qkv_stack, out_stack, gateup_stack, down_stack = stacks
    row_count = tokens.shape[0]
    head_count = lax.axis_size("head")
    seq_count = lax.axis_size("seq")
    group = row_count * head_count
    head_index = lax.axis_index("head")
    local_width = QW // head_count
    seq_index = lax.axis_index("seq")
    gains = jnp.concatenate([attn_gain, ffn_gain]).astype(low).astype(full)[None]
    gains = lax.all_to_all(
        jnp.broadcast_to(gains, (head_count * seq_count, gains.shape[1])),
        ("head", "seq"),
        split_axis=0,
        concat_axis=0,
        tiled=True,
    )
    own_gains = attn_gain.shape[0]
    gain_one = gains[:, :own_gains].reshape(1, D)
    gain_two = gains[:, own_gains:].reshape(1, D)


    ids_own = lax.dynamic_slice_in_dim(sequence_ids, seq_index * group, group, 0)
    ids_before = lax.dynamic_slice_in_dim(
        sequence_ids, jnp.maximum(seq_index - 1, 0) * group, group, 0
    )
    ids_before = jnp.where(seq_index > 0, ids_before, -1)
    key_ids = jnp.concatenate([ids_before, ids_own])[:, None]
    query_ids = ids_own[None, :]
    qkv_rows = joined_halves(gather_rows(qkv_stack, 8, to_columns))
    out_rows = joined_halves(gather_rows(out_stack, 8, to_columns))
    gateup = gather_rows(gateup_stack, 16, to_units)
    down = gather_rows(down_stack, 8, to_columns)
    tokens_float = tokens.astype(full)
    normed_one = (tokens_float * inverse_norm(tokens_float) * gain_one).astype(low)
    normed_one_group = jnp.concatenate(head_gather(normed_one))
    feature_start = head_index * local_width
    features = lax.dynamic_slice_in_dim(normed_one_group, feature_start, local_width, 1)
    weights = in_order(head_gather(qkv_rows), 0)
    weights = jnp.concatenate(
        [lax.dynamic_slice_in_dim(weights, feature_start, local_width, 1), weights[:, QW:]], axis=1
    )
    projected = mul(normed_one_group, weights, NN, low)
    buffer_rows = ((token_order // row_count) ^ head_index) * row_count + token_order % row_count
    shuffle = (
        buffer_rows[:, None] == lax.broadcasted_iota(jnp.int32, (group, group), 1)
    ).astype(low)
    stream = mul(shuffle, projected, NN, low)
    kv_stream = stream[:, local_width:]
    kv_before = lax.ppermute(kv_stream, "seq", [(i, i + 1) for i in range(seq_count - 1)])
    kv_both = jnp.concatenate([kv_before, kv_stream], axis=0)
    kv_turned = kv_both.T
    mixed_stream, lse = attend(stream[:, :local_width], kv_both, kv_turned, key_ids, query_ids)
    mixed_group = mul(shuffle, mixed_stream, TN, low)
    part = mul(mixed_group, out_rows, NN, low)
    resid = tokens_float + head_sum([part[i * row_count :][:row_count] for i in range(4)])
    normed_two = (resid * inverse_norm(resid) * gain_two).astype(low)
    normed_group = jnp.concatenate(head_gather(normed_two))
    grad_group = jnp.concatenate(head_gather(cotangent))
    section = (
        jnp.concatenate([gain_one, gain_two]),
        resid,
        normed_group,
        grad_group,
        gateup,
        down,
        features,
        qkv_rows,
        out_rows,
        stream,
        kv_both,
        kv_turned,
        lse,
        mixed_group,
        shuffle,
        key_ids,
        query_ids,
    )
    return section


def backward_steps(
    tokens,
    cotangent,
    gains,
    resid,
    normed_part,
    ffn_part,
    gateup_wgrad,
    down_wgrad,
    features,
    qkv_rows,
    out_rows,
    stream,
    kv_both,
    kv_turned,
    lse,
    mixed_group,
    shuffle,
    key_ids,
    query_ids,
    counts,
):
    row_count = tokens.shape[0]
    group = row_count * lax.axis_size("head")
    seq_count = lax.axis_size("seq")
    local_width = features.shape[1]
    query_stream = stream[:, :local_width]
    gain_one, gain_two = gains[0], gains[1]
    tokens_float = tokens.astype(full)
    inverse_one = inverse_norm(tokens_float)
    inverse_two = inverse_norm(resid)
    normed_two_grad = head_sum([normed_part[i * row_count :][:row_count] for i in range(4)])
    gateup_grad_own = sum_rows(gateup_wgrad, counts[2], 16, from_units)
    down_grad_own = sum_rows(down_wgrad, counts[3], 8, from_columns)
    ffn_out = head_sum([ffn_part[i * row_count :][:row_count] for i in range(4)])
    block_out = (resid + ffn_out).astype(low)

    resid_grad = cotangent.astype(full) + norm_back(resid, inverse_two, gain_two, normed_two_grad)
    gain_two_grad = jnp.sum(normed_two_grad * resid * inverse_two, axis=0)
    proj_grad = resid_grad.astype(low)
    proj_grad_group = jnp.concatenate(head_gather(proj_grad))
    mixed_grad_group = mul(proj_grad_group, out_rows, NT, low)
    mixed_grad_stream = mul(shuffle, mixed_grad_group, NN, low)
    out_wgrad = split_halves(mul(mixed_group, proj_grad_group, TN, low), BLK)
    out_grad_own = sum_rows(out_wgrad, counts[1], 8, from_columns)

    query_grad, kv_grad = attend_back(
        query_stream, mixed_grad_stream, kv_both, kv_turned, key_ids, query_ids, lse
    )
    kv_later = lax.ppermute(
        kv_grad[:group].astype(low), "seq", [(i, i - 1) for i in range(1, seq_count)]
    )
    kv_grad = (kv_grad[group:] + kv_later.astype(full)).astype(low)
    grad_local = mul(shuffle, jnp.concatenate([query_grad, kv_grad], axis=1), TN, low)
    gathered = head_gather(grad_local)

    def own_order(value, j):
        quarters = [value[i * row_count :][:row_count] for i in range(4)]
        return jnp.concatenate([quarters[i ^ j] for i in range(4)])

    gathered = [own_order(value, j) for j, value in enumerate(gathered)]
    kv_total = sum(value[:, local_width:].astype(full) for value in gathered).astype(low)
    qkv_grad = jnp.concatenate(
        [in_order([value[:, :local_width] for value in gathered], 1), kv_total], axis=1
    )
    qkv_wgrad = split_halves(mul(features, qkv_grad, TN, low), BLK)
    qkv_grad_own = sum_rows(qkv_wgrad, counts[0], 8, from_columns)
    feature_grad = mul(qkv_grad, qkv_rows, NT, low)
    order = (0, 2, 1, 3)
    feature_parts = head_exchange([feature_grad[i * row_count :][:row_count] for i in range(4)])
    normed_one_grad = in_order([feature_parts[order.index(j)] for j in range(4)], 1).astype(full)
    input_grad = resid_grad + norm_back(tokens_float, inverse_one, gain_one, normed_one_grad)
    gain_one_grad = jnp.sum(normed_one_grad * tokens_float * inverse_one, axis=0)
    return (
        block_out,
        input_grad,
        jnp.stack([gain_one_grad, gain_two_grad]),
        gateup_grad_own,
        down_grad_own,
        qkv_grad_own,
        out_grad_own,
    )


def on_device(
    tokens,
    cotangent,
    attn_gain,
    ffn_gain,
    qkv_stack,
    out_stack,
    gateup_stack,
    down_stack,
    qkv_left,
    qkv_right,
    out_left,
    out_right,
    gateup_left,
    gateup_right,
    down_left,
    down_right,
    qkv_left_root,
    qkv_right_root,
    out_left_root,
    out_right_root,
    gateup_left_root,
    gateup_right_root,
    down_left_root,
    down_right_root,
    sequence_ids,
    token_order,
):
    row_count = tokens.shape[0]
    head_count = lax.axis_size("head")
    seq_count = lax.axis_size("seq")
    device_count = head_count * seq_count
    group = row_count * head_count
    seq_index = lax.axis_index("seq")
    local_width = QW // head_count

    own_gains = attn_gain.shape[0]
    stacks = (qkv_stack, out_stack, gateup_stack, down_stack)
    whole_rows = all(s.shape[0] % u == 0 for s, u in zip(stacks, (8, 8, 16, 8)))
    if whole_rows:
        tile = jnp.concatenate([attn_gain[None], ffn_gain[None]])
        section = forward_section(
            tokens,
            cotangent,
            jnp.pad(tile, ((0, 6), (0, 128 - own_gains))),
            stacks,
            token_order[None, :],
            sequence_ids[None, :],
            seq_count,
        )
    else:
        section = forward_steps(
            tokens, cotangent, attn_gain, ffn_gain, stacks, token_order, sequence_ids
        )
    (
        gains_both,
        resid,
        normed_group,
        grad_group,
        gateup,
        down,
        features,
        qkv_rows,
        out_all,
        stream,
        kv_both,
        kv_turned,
        lse,
        mixed_group,
        shuffle,
        key_ids,
        query_ids,
    ) = section
    gateup = gateup.reshape(-1, D)
    down = down.reshape(-1, 2, BLK, D // 2)
    unit_count = down.shape[0]
    hidden, gate_up_grad, normed_part, ffn_part = feed_forward(
        normed_group, grad_group, gateup, down
    )
    gateup_wgrad = mul(gate_up_grad, normed_group, NN, low)
    down_wgrad = split_halves(mul(hidden, grad_group, NN, low), BLK)
    kept = (features, qkv_rows, out_all, stream, kv_both, kv_turned, lse, mixed_group, shuffle)
    counts = [s.shape[0] for s in stacks]
    if not whole_rows:
        gateup_wgrad = gateup_wgrad.reshape(2 * unit_count, BLK, D)
    if whole_rows:
        (block_out, input_grad, gain_grads, gateup_own, down_own, qkv_own, out_own, *_) = (
            backward_section(
                seq_count,
                tokens,
                cotangent,
                gains_both,
                resid,
                normed_part,
                ffn_part,
                gateup_wgrad.reshape(seq_count, -1, D),
                down_wgrad.reshape(seq_count, -1, D // 2),
                *kept,
                key_ids,
                query_ids,
            )
        )
        gateup_grad_own, down_grad_own = gateup_own, down_own
        qkv_grad_own, out_grad_own = qkv_own, out_own
    else:
        section = backward_steps(
            tokens, cotangent, gains_both, resid, normed_part, ffn_part, gateup_wgrad, down_wgrad, *kept,
            key_ids, query_ids, counts,
        )
        (block_out, input_grad, gain_grads, gateup_grad_own, down_grad_own, qkv_grad_own, out_grad_own) = section
    gain_one_grad, gain_two_grad = gain_grads[0], gain_grads[1]
    gain_grads = jnp.concatenate(
        [gain_one_grad.reshape(device_count, -1), gain_two_grad.reshape(device_count, -1)], axis=1
    )
    gain_grads = lax.all_to_all(
        gain_grads, ("head", "seq"), split_axis=0, concat_axis=0, tiled=True
    )
    gain_grads = jnp.sum(gain_grads, axis=0)

    gateup_new = update(
        gateup_stack,
        gateup_grad_own,
        gateup_left,
        gateup_right,
        gateup_left_root,
        gateup_right_root,
        0.5 * D ** (-0.5),
        whole_rows,
    )
    down_new = update(
        down_stack,
        down_grad_own,
        down_left,
        down_right,
        down_left_root,
        down_right_root,
        0.5 * FF ** (-0.5),
    )
    out_new = update(
        out_stack,
        out_grad_own,
        out_left,
        out_right,
        out_left_root,
        out_right_root,
        0.5 * (QW // 64) ** (-0.5),
    )
    qkv_new = update(
        qkv_stack,
        qkv_grad_own,
        qkv_left,
        qkv_right,
        qkv_left_root,
        qkv_right_root,
        0.5 * D ** (-0.5),
    )
    return (
        (block_out, input_grad, gain_grads[:own_gains], gain_grads[own_gains:])
        + tuple(qkv_new)
        + tuple(out_new)
        + tuple(gateup_new)
        + tuple(down_new)
    )


def solution(mesh):
    rows = P(("seq", "head"), None)
    gain = P(("head", "seq"))
    blocks = P(("head", "seq"), None, None)
    return jax.shard_map(
        on_device,
        mesh=mesh,
        in_specs=(rows, rows, gain, gain) + (blocks,) * 20 + (P(), P("seq")),
        out_specs=(rows, rows, gain, gain) + (blocks,) * 12,
        check_vma=False,
    )
```

```python
import functools

import jax
import jax.numpy as jnp
from jax import lax
from jax.experimental import pallas as pl
from jax.experimental.pallas import tpu as pltpu
from jax.sharding import PartitionSpec as P

D = 1536
HEAD_DIM = 128
FF = 4608
WINDOW = 1024
GRID = 16
QW = 1536
QKV = 1792
BLK = 96
BQ = 112
BH = 96
NU = 48

norm_eps = 1e-06
stat_eps = 1e-06
neg_fill = -1e30

QUERY_TILE = 256
SPAN = WINDOW + QUERY_TILE

low = jnp.bfloat16
full = jnp.float32

NT = (((1,), (1,)), ((), ()))
NN = (((1,), (0,)), ((), ()))
TN = (((0,), (0,)), ((), ()))


def mul(a, b, dims, kind=full):
    return lax.dot_general(a, b, dims, preferred_element_type=kind)


def ring_place(index, count):
    return jnp.where(index % 2 == 0, index // 2, count - 1 - index // 2)


def ring_index(place, count):
    return jnp.where(place < count // 2, 2 * place, 2 * (count - 1 - place) + 1)


def ring_routes(count):
    order = [i for i in range(0, count, 2)] + [i for i in range(count - 1, 0, -2)]
    up = [(order[i], order[(i + 1) % count]) for i in range(count)]
    return up, [(b, a) for a, b in up]


def seq_gather(shard):
    count = lax.axis_size("seq")
    rows = shard.shape[0]
    half = rows // 2
    me = lax.axis_index("seq")
    place = ring_place(me, count)
    up, down = ring_routes(count)
    out = jnp.zeros((count,) + shard.shape, shard.dtype)
    out = lax.dynamic_update_slice(out, shard[None], (me, 0, 0))
    ahead = shard
    behind = shard
    for step in range(1, count // 2):
        ahead = lax.ppermute(ahead, "seq", up)
        behind = lax.ppermute(behind, "seq", down)
        out = lax.dynamic_update_slice(
            out, ahead[None], (ring_index((place - step + count) % count, count), 0, 0)
        )
        out = lax.dynamic_update_slice(
            out, behind[None], (ring_index((place + step) % count, count), 0, 0)
        )
    ahead = lax.ppermute(ahead[:half], "seq", up)
    behind = lax.ppermute(behind[half:], "seq", down)
    far = ring_index((place + count // 2) % count, count)
    out = lax.dynamic_update_slice(out, ahead[None], (far, 0, 0))
    return lax.dynamic_update_slice(out, behind[None], (far, half, 0))


def seq_sum(parts):
    count, rows = parts.shape[:2]
    half = rows // 2
    place = ring_place(lax.axis_index("seq"), count)
    up, down = ring_routes(count)

    def part(offset):
        index = ring_index((place + offset + count) % count, count)
        return lax.dynamic_slice_in_dim(parts, index, 1, 0)[0]

    far = part(count // 2)
    ahead = lax.ppermute(far[:half], "seq", up)
    behind = lax.ppermute(far[half:], "seq", down)
    for offset in range(count // 2 - 1, 0, -1):
        local = part(offset)
        if ahead.shape[0] == rows:
            local = (local.astype(full) + ahead.astype(full)).astype(low)
        else:
            local = jnp.concatenate(
                [(local[:half].astype(full) + ahead.astype(full)).astype(low), local[half:]]
            )
        ahead = lax.ppermute(local, "seq", up)
        local = part(-offset)
        if behind.shape[0] == rows:
            local = (local.astype(full) + behind.astype(full)).astype(low)
        else:
            local = jnp.concatenate(
                [local[:half], (local[half:].astype(full) + behind.astype(full)).astype(low)]
            )
        behind = lax.ppermute(local, "seq", down)
    return part(0).astype(full) + ahead.astype(full) + behind.astype(full)


def gather_rows(stack, unit, layout):
    short = stack.astype(low)
    if stack.shape[0] % unit == 0:
        shard = layout(short)
        rows = shard.reshape(-1, shard.shape[-1])
        out = seq_gather(rows)
        return out.reshape((-1,) + shard.shape[1:])
    return layout(lax.all_gather(short, "seq", axis=0, tiled=True))


def sum_rows(rows, local, unit, back):
    count = lax.axis_size("seq")
    if local % unit == 0:
        own = seq_sum(rows.reshape(count, -1, rows.shape[-1]))
        return back(own.reshape((-1,) + rows.shape[1:]))
    return lax.psum_scatter(back(rows), "seq", scatter_dimension=0, tiled=True).astype(full)


def to_columns(stack):
    n, i, j = stack.shape
    return stack.reshape(n // 8, 8, i, j).transpose(0, 2, 1, 3).reshape(n // 8, i, 8 * j)


def from_columns(rows):
    n, i, j = rows.shape
    return rows.reshape(n, i, 8, j // 8).transpose(0, 2, 1, 3).reshape(n * 8, i, j // 8)


def to_units(stack):
    n, i, j = stack.shape
    return stack.reshape(n // 16, 16, i, j).transpose(0, 3, 1, 2).reshape(n // 16, j, 16 * i)


def from_units(rows):
    n, j, i = rows.shape
    return rows.reshape(n, j, 16, i // 16).transpose(0, 2, 3, 1).reshape(n * 16, i // 16, j)


def joined_halves(rows):
    n, i, j = rows.shape
    return rows.reshape(n // 2, 2, i, j).transpose(0, 2, 1, 3).reshape(n // 2 * i, 2 * j)


def split_halves(matrix, i):
    rows, columns = matrix.shape
    half = columns // 2
    parts = [matrix[:, at : at + half].reshape(rows // i, i, half) for at in (0, half)]
    return jnp.stack(parts, axis=1).reshape(2 * rows // i, i, half)


def to_partner(value, which):
    count = lax.axis_size("head")
    return lax.ppermute(value, "head", [(i, i ^ which) for i in range(count)])


def head_gather(value):
    across = to_partner(value, 2)
    mate = to_partner(value, 1)
    return value, mate, across, to_partner(across, 1)


def head_exchange(parts):
    return (parts[0],) + tuple(to_partner(parts[j], j) for j in (2, 1, 3))


def head_sum(parts):
    across = (parts[2].astype(full) + to_partner(parts[3], 1).astype(full)).astype(low)
    across = to_partner(across, 2)
    mine = parts[0].astype(full) + to_partner(parts[1], 1).astype(full)
    return mine + across.astype(full)


def in_order(parts, axis):
    me = lax.axis_index("head")
    odd = me % 2 == 1
    lower = [jnp.where(odd, parts[1], parts[0]), jnp.where(odd, parts[0], parts[1])]
    upper = [jnp.where(odd, parts[3], parts[2]), jnp.where(odd, parts[2], parts[3])]
    second = me >= 2
    return jnp.concatenate(
        [jnp.where(second, b, a) for a, b in zip(lower, upper)]
        + [jnp.where(second, a, b) for a, b in zip(lower, upper)],
        axis=axis,
    )


def tile_bias(tile, key_ids, query_ids, bias_ref):
    start = pl.multiple_of(tile * QUERY_TILE, QUERY_TILE)
    shape = (SPAN, QUERY_TILE)
    key = lax.broadcasted_iota(jnp.int32, shape, 0)
    query = lax.broadcasted_iota(jnp.int32, shape, 1)
    same = key_ids[pl.ds(start, SPAN), :] == query_ids[...]
    allowed = same & (key > query) & (key <= query + WINDOW)
    bias_ref[...] = jnp.where(allowed, 0.0, neg_fill)


def attend_kernel(q_ref, kv_ref, kvt_ref, key_ids, query_ids, out_ref, lse_ref, bias_ref):
    tile = pl.program_id(0)
    start = pl.multiple_of(tile * QUERY_TILE, QUERY_TILE)

    @pl.when(pl.program_id(1) == 0)
    def _():
        tile_bias(tile, key_ids, query_ids, bias_ref)

    keys = kv_ref[pl.ds(start, SPAN), :HEAD_DIM]
    scores = mul(keys, q_ref[...], NT) * HEAD_DIM ** (-0.5) + bias_ref[...]
    top = jnp.max(scores, axis=0, keepdims=True)
    expo = jnp.exp(scores - top)
    total = jnp.sum(expo, axis=0, keepdims=True)
    values = kvt_ref[HEAD_DIM:, pl.ds(start, SPAN)]
    mixed = mul(values, expo.astype(low), NN) / total
    out_ref[...] = mixed.T.astype(low)
    lse_ref[0] = top + jnp.log(total)


def attend_back_kernel(
    q_ref, g_ref, kv_ref, kvt_ref, key_ids, query_ids, lse_ref, dq_ref, dkv_ref, bias_ref
):
    tile = pl.program_id(0)
    start = pl.multiple_of(tile * QUERY_TILE, QUERY_TILE)
    scale = HEAD_DIM ** (-0.5)

    @pl.when((tile == 0) & (pl.program_id(1) == 0))
    def _():
        dkv_ref[...] = jnp.zeros_like(dkv_ref)

    @pl.when(pl.program_id(1) == 0)
    def _():
        tile_bias(tile, key_ids, query_ids, bias_ref)

    here = pl.ds(start, SPAN)
    queries = q_ref[...]
    grads = g_ref[...]
    scores = mul(kv_ref[here, :HEAD_DIM], queries, NT) * scale + bias_ref[...]
    probs = jnp.exp(scores - lse_ref[0])
    prob_grad = mul(kv_ref[here, HEAD_DIM:], grads, NT)
    delta = jnp.sum(probs * prob_grad, axis=0, keepdims=True)
    score_grad = (probs * (prob_grad - delta)).astype(low)
    dq = mul(kvt_ref[:HEAD_DIM, here], score_grad, NN) * scale
    dq_ref[...] = dq.T.astype(low)
    dkv_ref[here, :HEAD_DIM] += mul(score_grad, queries, NN) * scale
    dkv_ref[here, HEAD_DIM:] += mul(probs.astype(low), grads, NN)


def attention_specs(group):
    whole = lambda *shape: pl.BlockSpec(shape, lambda t, h: (0,) * len(shape))
    head_rows = pl.BlockSpec((QUERY_TILE, HEAD_DIM), lambda t, h: (t, h))
    keys = whole(2 * group, 2 * HEAD_DIM)
    keys_turned = whole(2 * HEAD_DIM, 2 * group)
    key_ids = whole(2 * group, 1)
    query_ids = pl.BlockSpec((1, QUERY_TILE), lambda t, h: (0, t))
    lse = pl.BlockSpec((1, 1, QUERY_TILE), lambda t, h: (h, 0, t))
    return head_rows, keys, keys_turned, key_ids, query_ids, lse


attention_params = pltpu.CompilerParams(
    dimension_semantics=("arbitrary", "arbitrary"), vmem_limit_bytes=40 * 1024 * 1024
)


def attend(queries, kv, kv_turned, key_ids, query_ids):
    group, width = queries.shape
    heads = width // HEAD_DIM
    rows, keys, turned, kids, qids, lse = attention_specs(group)
    work = heads * (group // QUERY_TILE) * SPAN * QUERY_TILE
    return pl.pallas_call(
        attend_kernel,
        grid=(group // QUERY_TILE, heads),
        in_specs=[rows, keys, turned, kids, qids],
        out_specs=[rows, lse],
        out_shape=[
            jax.ShapeDtypeStruct((group, width), low),
            jax.ShapeDtypeStruct((heads, 1, group), full),
        ],
        scratch_shapes=[pltpu.VMEM((SPAN, QUERY_TILE), full)],
        compiler_params=attention_params,
        cost_estimate=pl.CostEstimate(
            flops=8 * work * HEAD_DIM, bytes_accessed=6 << 20, transcendentals=work
        ),
        name="attend",
    )(queries, kv, kv_turned, key_ids, query_ids)


def attend_back(queries, grads, kv, kv_turned, key_ids, query_ids, lse_rows):
    group, width = queries.shape
    heads = width // HEAD_DIM
    rows, keys, turned, kids, qids, lse = attention_specs(group)
    work = heads * (group // QUERY_TILE) * SPAN * QUERY_TILE
    return pl.pallas_call(
        attend_back_kernel,
        grid=(group // QUERY_TILE, heads),
        in_specs=[rows, rows, keys, turned, kids, qids, lse],
        out_specs=[rows, keys],
        out_shape=[
            jax.ShapeDtypeStruct((group, width), low),
            jax.ShapeDtypeStruct((2 * group, 2 * HEAD_DIM), full),
        ],
        scratch_shapes=[pltpu.VMEM((SPAN, QUERY_TILE), full)],
        compiler_params=attention_params,
        cost_estimate=pl.CostEstimate(
            flops=20 * work * HEAD_DIM, bytes_accessed=8 << 20, transcendentals=work
        ),
        name="attend_back",
    )(queries, grads, kv, kv_turned, key_ids, query_ids, lse_rows)


def remote(source, target, send, recv, where):
    return pltpu.make_async_remote_copy(
        src_ref=source,
        dst_ref=target,
        send_sem=send,
        recv_sem=recv,
        device_id=where,
        device_id_type=pl.DeviceIdType.MESH,
    )


class Ring:
    def __init__(self, count, view, send, recv, split=True):
        me = lax.axis_index("seq")
        self.split = split
        odd = lax.rem(me, 2)
        self.count = count
        self.view = view
        self.send = send
        self.recv = recv
        self.place = (1 - odd) * (me // 2) + odd * (count - 1 - me // 2)
        self.ahead = {"seq": self.shard(1)}
        self.behind = {"seq": self.shard(-1)}
        self.copies = []

    def shard(self, offset):
        place = lax.rem(self.place + offset + self.count, self.count)
        upper = place // (self.count // 2)
        return (1 - upper) * 2 * place + upper * (2 * (self.count - 1 - place) + 1)

    def pair(self, offset, step):
        last = step == self.count // 2
        halved = last and self.split
        views = [
            self.view(self.shard(-offset), 0 if halved else None),
            self.view(self.shard(offset), 1 if halved else None),
        ]
        if last and not self.split:
            views = views[:1]
        return [
            remote(view, view, self.send.at[i, step - 1], self.recv.at[i, step - 1], where)
            for i, (view, where) in enumerate(zip(views, (self.ahead, self.behind)))
        ]

    def start(self, step):
        for copy in self.pair(step - 1, step):
            copy.start()
            self.copies.append(copy)

    def arrive(self, step):
        for copy in self.pair(step, step):
            copy.wait_recv()

    def finish(self):
        for copy in self.copies:
            copy.wait_send()


def turned_row(row):
    size = row.shape[1]
    return jnp.broadcast_to(row.astype(full), (128, size)).T[:, :1]


def forward_kernel(
    count,
    tokens,
    cotangent,
    own_gains,
    qkv_stack,
    out_stack,
    gateup_stack,
    down_stack,
    order,
    ids,
    gains,
    resid,
    normed_group,
    grad_group,
    gateup,
    down,
    features_out,
    qkv_rows_out,
    out_all_out,
    stream_out,
    kv_both_out,
    kv_turned_out,
    lse,
    mixed_group_out,
    shuffle_out,
    key_ids,
    query_ids,
    tokens_group,
    normed,
    weights,
    projected,
    mixed,
    mixed_all,
    bias,
    wide,
    tall,
    gateup_own,
    down_own,
    gain_tiles,
    own_sem,
    ring_send,
    ring_recv,
    head_send,
    head_recv,
    kv_send,
    kv_recv,
    features,
    qkv_rows,
    out_all,
    stream,
    kv_both,
    kv_turned,
    mixed_group,
    shuffle,
    store_sem,
):
    rows = tokens.shape[0]
    group = 4 * rows
    width = features.shape[1]
    heads = width // HEAD_DIM
    head = lax.axis_index("head")
    me = lax.axis_index("seq")
    mate_head = head + 1 - 2 * lax.rem(head, 2)
    across_head = lax.rem(head + 2, 4)
    mate = {"head": mate_head}
    across = {"head": across_head}

    def band(of):
        return pl.ds(pl.multiple_of(of * width, 128), width)

    def chip_columns(of):
        return pl.ds(pl.multiple_of((of // 2) * 2 * width, 128), 2 * width)

    def quarter(ref, i):
        return ref.at[pl.ds(i * rows, rows)]

    copies = []

    def send(index, source, target, where):
        copy = remote(source, target, head_send.at[index], head_recv.at[index], where)
        copy.start()
        copies.append(copy)

    def arrived(index, target, where):
        remote(target, target, head_send.at[index], head_recv.at[index], where).wait_recv()

    def stack_view(ref, columns):
        def view(shard, part):
            first = pl.multiple_of(head * width + (shard // 2) * BLK, 32)
            at = pl.ds(pl.multiple_of(lax.rem(shard, 2) * columns, 128), columns)
            if part is None:
                return ref.at[pl.ds(first, BLK), at]
            return ref.at[pl.ds(pl.multiple_of(first + part * (BLK // 2), 16), BLK // 2), at]

        return view

    def gateup_view(shard, part):
        size = gateup.shape[1]
        if part is None:
            return gateup.at[shard]
        return gateup.at[shard, pl.ds(part * (size // 2), size // 2)]

    def down_view(shard, part):
        if part is None:
            return down.at[shard]
        return down.at[shard, :, pl.ds(part * (BLK // 2), BLK // 2)]

    qkv_view = stack_view(weights, QKV // 2)
    out_view = stack_view(out_all, D // 2)
    gain_view = lambda shard, part: gain_tiles.at[head, shard]
    qkv_ring, out_ring, gateup_ring, down_ring, gain_ring = rings = [
        Ring(count, view, ring_send.at[i], ring_recv.at[i], view is not gain_view)
        for i, view in enumerate((qkv_view, out_view, gateup_view, down_view, gain_view))
    ]

    barrier = pltpu.get_barrier_semaphore()
    for where in (qkv_ring.ahead, qkv_ring.behind, mate, across):
        pl.semaphore_signal(barrier, inc=1, device_id=where, device_id_type=pl.DeviceIdType.MESH)

    @pl.when(me > 0)
    def _():
        pl.semaphore_signal(
            barrier, inc=1, device_id={"seq": me - 1}, device_id_type=pl.DeviceIdType.MESH
        )

    def side_by_side(stack, first):
        size = stack.shape[2]
        blocks = 8
        for c in range(blocks):
            tall[c * size : (c + 1) * size, :] = stack[first + c].T
        return tall[: blocks * size, :].T.astype(low)

    qkv_view(me, None)[...] = side_by_side(qkv_stack, 0)
    gain_tiles[head, me] = own_gains[...]
    pl.semaphore_wait(barrier, 5 - me // (count - 1))
    send(0, tokens, quarter(tokens_group, 2), across)
    send(1, tokens, quarter(tokens_group, 1), mate)
    qkv_ring.start(1)
    gain_ring.start(1)
    for q in range(gateup_own.shape[0] // BLK):
        column = gateup_stack[q * GRID : (q + 1) * GRID].reshape(D, BLK)
        gateup_own[q * BLK : (q + 1) * BLK, :] = column.T.astype(low)
    for m in range(down_own.shape[0]):
        down_own[m] = side_by_side(down_stack, 8 * m)
    own = [
        pltpu.make_async_copy(gateup_own, gateup.at[me], own_sem.at[0]),
        pltpu.make_async_copy(down_own, down.at[me], own_sem.at[1]),
        pltpu.make_async_copy(cotangent, quarter(grad_group, 0), own_sem.at[2]),
    ]
    for copy in own:
        copy.start()
    out_view(me, None)[...] = side_by_side(out_stack, 0)
    for copy in own[:2]:
        copy.wait()

    def pump(step):
        if step > 1:
            gateup_ring.arrive(step - 1)
            down_ring.arrive(step - 1)
        if step <= count // 2:
            gateup_ring.start(step)
            down_ring.start(step)

    pump(1)
    tokens_group[:rows, :] = tokens[...]
    qkv_ring.arrive(1)
    qkv_ring.start(2)
    gain_ring.arrive(1)
    gain_ring.start(2)

    for i in range(4):
        at = turned_row(order[:, i * rows : (i + 1) * rows]).astype(jnp.int32)
        owner = at // rows
        flip = head - 4 * (owner // 2) * (head // 2) - 2 * lax.rem(owner, 2) * lax.rem(head, 2)
        place = (owner + flip) * rows + lax.rem(at, rows)
        shuffle[i * rows : (i + 1) * rows, :] = jnp.where(
            place == lax.broadcasted_iota(jnp.int32, (rows, group), 1), 1.0, 0.0
        ).astype(low)
    query_ids[...] = ids[:, pl.ds(pl.multiple_of(me * group, 128), group)].astype(full)
    before = (me - (me + count - 1) // count) * group
    for i in range(4):
        here = slice(i * rows, (i + 1) * rows)
        at = pl.multiple_of(before + i * rows, 128)
        key_ids[here, :] = jnp.where(me > 0, turned_row(ids[:, pl.ds(at, rows)]), -1.0)
        there = slice(group + i * rows, group + (i + 1) * rows)
        key_ids[there, :] = turned_row(query_ids[:, here])
    for step in range(2, count // 2):
        qkv_ring.arrive(step)
        qkv_ring.start(step + 1)
        gain_ring.arrive(step)
        gain_ring.start(step + 1)
    qkv_ring.arrive(count // 2)

    key_columns = pl.ds(QW, 2 * HEAD_DIM)

    def weight_parts(of, chip_of):
        return [weights.at[band(of), columns] for columns in (chip_columns(chip_of), key_columns)]

    gain_ring.arrive(count // 2)
    send(9, gain_tiles.at[head], gain_tiles.at[head], across)
    send(10, gain_tiles.at[head], gain_tiles.at[head], mate)
    for i, part in enumerate(weight_parts(head, across_head)):
        send(3 + i, part, part, across)
    for i, part in enumerate(weight_parts(head, head)):
        send(7 + i, part, part, mate)
    out_ring.start(1)
    pump(2)
    arrived(0, quarter(tokens_group, 2), across)
    send(2, quarter(tokens_group, 2), quarter(tokens_group, 3), mate)
    qkv_rows[...] = weights[band(head), :]
    arrived(9, gain_tiles.at[across_head], across)
    send(11, gain_tiles.at[across_head], gain_tiles.at[across_head], mate)
    arrived(10, gain_tiles.at[mate_head], mate)
    arrived(11, gain_tiles.at[3 - head], mate)
    size = D // (4 * count)
    for h in range(4):
        for i in range(count):
            at = (h * count + i) * size
            wide[:8, at : at + size] = gain_tiles[h, i][:, :size]
    gains[...] = wide[:2, :D].astype(low).astype(full)

    def norm_rows(i):
        here = pl.ds(i * rows, rows)
        values = tokens_group[here, :].astype(full)
        normed[here, :] = (values * inverse_norm(values) * gains[0:1, :]).astype(low)

    norm_rows(0)
    arrived(1, quarter(tokens_group, 1), mate)
    norm_rows(1)
    out_ring.arrive(1)
    out_ring.start(2)
    norm_rows(2)
    arrived(2, quarter(tokens_group, 3), mate)
    norm_rows(3)
    features[...] = normed[:, band(head)]
    for i, part in enumerate(weight_parts(across_head, head)):
        arrived(3 + i, part, across)
        send(5 + i, part, part, mate)
    out_ring.arrive(2)
    out_ring.start(3)
    for i, part in enumerate(weight_parts(mate_head, head)):
        arrived(7 + i, part, mate)
    send(27, cotangent, quarter(grad_group, 2), across)
    send(28, cotangent, quarter(grad_group, 1), mate)
    for i, part in enumerate(weight_parts(3 - head, head)):
        arrived(5 + i, part, mate)

    key_values = pl.ds(width, 2 * HEAD_DIM)

    def project(columns, target):
        def step(i, carry):
            here = pl.ds(pl.multiple_of(i * rows, rows), rows)
            projected[here, target] = mul(normed[here, :], weights[:, columns], NN).astype(low)
            return carry

        lax.fori_loop(0, 4, step, 0)

        def turn(i, carry):
            here = pl.ds(pl.multiple_of(i * rows, rows), rows)
            stream[here, target] = mul(shuffle[here, :], projected[:, target], NN).astype(low)
            return carry

        lax.fori_loop(0, 4, turn, 0)

    project(key_columns, key_values)
    kv_both[pl.ds(group, group), :] = stream[:, key_values]
    kv_copy = remote(
        kv_both.at[pl.ds(group, group)],
        kv_both.at[pl.ds(0, group)],
        kv_send,
        kv_recv,
        {"seq": lax.rem(me + 1, count)},
    )

    @pl.when(me < count - 1)
    def _():
        kv_copy.start()

    @pl.when(me == 0)
    def _():
        kv_both[pl.ds(0, group), :] = jnp.zeros((group, 2 * HEAD_DIM), low)

    out_ring.arrive(3)
    out_ring.start(4)
    project(band(head), pl.ds(0, width))
    pump(3)
    for i in range(4, 8):
        kv_turned[:, i * rows : (i + 1) * rows] = kv_both[i * rows : (i + 1) * rows, :].T
    out_ring.arrive(4)
    half = width // 2

    def out_part(of, i):
        return out_all.at[pl.ds(pl.multiple_of(of * width + i * half, 64), half)]

    for i in range(2):
        send(12 + i, out_part(head, i), out_part(head, i), across)
    send(16, out_all.at[band(head)], out_all.at[band(head)], mate)

    @pl.when(me > 0)
    def _():
        kv_copy.wait_recv()

    for i in range(4):
        kv_turned[:, i * rows : (i + 1) * rows] = kv_both[i * rows : (i + 1) * rows, :].T
    arrived(27, quarter(grad_group, 2), across)
    send(29, quarter(grad_group, 2), quarter(grad_group, 3), mate)

    def attend_tile(tile, carry):
        start = pl.multiple_of(tile * QUERY_TILE, QUERY_TILE)
        here = pl.ds(start, QUERY_TILE)
        span = pl.ds(start, SPAN)
        shape = (SPAN, QUERY_TILE)
        key = lax.broadcasted_iota(jnp.int32, shape, 0)
        query = lax.broadcasted_iota(jnp.int32, shape, 1)
        same = key_ids[span, :] == query_ids[:, here]
        allowed = same & (key > query) & (key <= query + WINDOW)
        bias[...] = jnp.where(allowed, 0.0, neg_fill)

        def attend_head(j, carry):
            lanes = pl.ds(pl.multiple_of(j * HEAD_DIM, HEAD_DIM), HEAD_DIM)
            scores = mul(kv_both[span, :HEAD_DIM], stream[here, lanes], NT)
            scores = scores * HEAD_DIM ** (-0.5) + bias[...]
            top = jnp.max(scores, axis=0, keepdims=True)
            expo = jnp.exp(scores - top)
            total = jnp.sum(expo, axis=0, keepdims=True)
            out = mul(kv_turned[HEAD_DIM:, span], expo.astype(low), NN) / total
            mixed[here, lanes] = out.T.astype(low)
            lse[j, :, here] = top + jnp.log(total)
            return carry

        return lax.fori_loop(0, heads, attend_head, carry)

    lax.fori_loop(0, group // QUERY_TILE, attend_tile, 0)

    def turn_back(i, carry):
        here = pl.ds(pl.multiple_of(i * rows, rows), rows)
        mixed_group[here, :] = mul(shuffle[:, here], mixed[...], TN).astype(low)
        return carry

    lax.fori_loop(0, 4, turn_back, 0)

    def mixed_part(of, i, size):
        return mixed_all.at[pl.ds(i * size, size), band(of)]

    for i in range(2):
        source = mixed_group.at[pl.ds(i * 2 * rows, 2 * rows)]
        send(17 + i, source, mixed_part(head, 1 - i, 2 * rows), across)
    for i in range(4):
        send(19 + i, quarter(mixed_group, i), mixed_part(head, i ^ 1, rows), mate)
    mixed_all[:, band(head)] = mixed_group[...]
    for i in range(2):
        arrived(12 + i, out_part(across_head, i), across)
        send(14 + i, out_part(across_head, i), out_part(across_head, i), mate)
    pump(4)
    arrived(16, out_all.at[band(mate_head)], mate)
    for i in range(2):
        arrived(14 + i, out_part(3 - head, i), mate)
    for i in range(4):
        arrived(19 + i, mixed_part(mate_head, i ^ 1, rows), mate)
    for i in range(2):
        arrived(17 + i, mixed_part(across_head, 1 - i, 2 * rows), across)
        for j in (2 - 2 * i, 3 - 2 * i):
            part = mixed_part(across_head, j, rows)
            send(23 + j, part, mixed_part(across_head, j ^ 1, rows), mate)
    for j in range(4):
        arrived(23 + j, mixed_part(3 - head, j ^ 1, rows), mate)

    stores = [
        pltpu.make_async_copy(source, target, store_sem.at[i])
        for i, (source, target) in enumerate(
            (
                (features, features_out),
                (qkv_rows, qkv_rows_out),
                (out_all, out_all_out),
                (stream, stream_out),
                (kv_both, kv_both_out),
                (kv_turned, kv_turned_out),
                (mixed_group, mixed_group_out),
                (shuffle, shuffle_out),
            )
        )
    ]
    for copy in stores:
        copy.start()

    def second(i, carry):
        here = pl.ds(pl.multiple_of((3 - i) * rows, rows), rows)
        resid[...] = tokens_group[here, :].astype(full) + mul(mixed_all[here, :], out_all[...], NN)
        values = resid[...]
        normed_group[here, :] = (values * inverse_norm(values) * gains[1:2, :]).astype(low)
        return carry

    lax.fori_loop(0, 4, second, 0)
    arrived(28, quarter(grad_group, 1), mate)
    arrived(29, quarter(grad_group, 3), mate)
    pump(5)
    own[2].wait()
    for copy in stores:
        copy.wait()
    for ring in rings:
        ring.finish()
    for copy in copies:
        copy.wait_send()

    @pl.when(me < count - 1)
    def _():
        kv_copy.wait_send()


def forward_section(tokens, cotangent, gains, stacks, order, ids, count):
    rows = tokens.shape[0]
    group = 4 * rows
    width = QW // 4
    steps = count // 2
    gateup_rows = stacks[2].shape[0] // GRID * BLK
    down_parts = stacks[3].shape[0] // 8
    vmem = pl.BlockSpec(memory_space=pltpu.VMEM)
    hbm = pl.BlockSpec(memory_space=pl.ANY)
    outs = [
        ((2, D), full, vmem),
        ((rows, D), full, vmem),
        ((group, D), low, vmem),
        ((group, D), low, hbm),
        ((count, gateup_rows, D), low, hbm),
        ((count, down_parts, BLK, D // 2), low, hbm),
        ((group, width), low, hbm),
        ((width, QKV), low, hbm),
        ((D, D), low, hbm),
        ((group, width + 2 * HEAD_DIM), low, hbm),
        ((2 * group, 2 * HEAD_DIM), low, hbm),
        ((2 * HEAD_DIM, 2 * group), low, hbm),
        ((width // HEAD_DIM, 1, group), full, vmem),
        ((group, width), low, hbm),
        ((group, group), low, hbm),
        ((2 * group, 1), full, vmem),
        ((1, group), full, vmem),
    ]
    dma = pltpu.SemaphoreType.DMA
    return pl.pallas_call(
        functools.partial(forward_kernel, count),
        in_specs=[vmem] * 9,
        out_specs=[spec for _, _, spec in outs],
        out_shape=[jax.ShapeDtypeStruct(shape, kind) for shape, kind, _ in outs],
        scratch_shapes=[
            pltpu.VMEM((group, D), low),
            pltpu.VMEM((group, D), low),
            pltpu.VMEM((D, QKV), low),
            pltpu.VMEM((group, width + 2 * HEAD_DIM), low),
            pltpu.VMEM((group, width), low),
            pltpu.VMEM((group, D), low),
            pltpu.VMEM((SPAN, QUERY_TILE), full),
            pltpu.VMEM((8, D), full),
            pltpu.VMEM((QKV // 2, BLK), full),
            pltpu.VMEM((gateup_rows, D), low),
            pltpu.VMEM((down_parts, BLK, D // 2), low),
            pltpu.VMEM((4, count, 8, 128), full),
            dma((3,)),
            dma((5, 2, steps)),
            dma((5, 2, steps)),
            dma((30,)),
            dma((30,)),
            dma,
            dma,
            *[pltpu.VMEM(outs[i][0], low) for i in (6, 7, 8, 9, 10, 11, 13, 14)],
            dma((8,)),
        ],
        compiler_params=pltpu.CompilerParams(
            collective_id=0, has_side_effects=True, vmem_limit_bytes=58 * 1024 * 1024
        ),
        name="forward_section",
    )(tokens, cotangent, gains, *stacks, order, ids)


class SumRing:
    def __init__(self, count, view, first, buffers, send, recv):
        self.ring = Ring(count, None, None, None)
        self.steps = count // 2
        self.view = view
        self.first = first
        self.buffers = buffers
        self.rows = buffers.shape[2]
        self.send = send
        self.recv = recv
        self.copies = []

    def where(self, way):
        return self.ring.behind if way else self.ring.ahead

    def half(self, way):
        return self.buffers.at[way, 0, pl.ds(way * (self.rows // 2), self.rows // 2)]

    def copy(self, way, step, source, target):
        return remote(source, target, self.send.at[way, step], self.recv.at[way, step], self.where(way))

    def start(self):
        shard = self.ring.shard(self.steps)
        for way in range(2):
            copy = self.copy(way, 0, self.first(shard, way), self.half(way))
            copy.start()
            self.copies.append(copy)

    def arrived(self, way, step):
        target = self.buffers.at[way, step] if step else self.half(way)
        self.copy(way, step, target, target).wait_recv()

    def step(self, step):
        block = 48
        for way in range(2):
            self.arrived(way, step - 1)
            offset = self.steps - step
            local = self.view(self.ring.shard(-offset if way else offset))
            buffer = self.buffers.at[way, step - 1]

            def add(i, carry):
                here = pl.ds(pl.multiple_of(i * block, 16), block)
                buffer[here, :] = (local[here, :].astype(full) + buffer[here, :].astype(full)).astype(low)
                return carry

            def keep(i, carry):
                here = pl.ds(pl.multiple_of(i * block, 16), block)
                buffer[here, :] = local[here, :]
                return carry

            blocks = self.rows // block
            if step > 1:
                lax.fori_loop(0, blocks, add, 0)
            else:
                lax.fori_loop(way * (blocks // 2), (way + 1) * (blocks // 2), add, 0)
                lax.fori_loop((1 - way) * (blocks // 2), (2 - way) * (blocks // 2), keep, 0)
            copy = self.copy(way, step, buffer, self.buffers.at[way, step])
            copy.start()
            self.copies.append(copy)

    def finish(self, out):
        block = 48
        last = self.steps - 1
        for way in range(2):
            self.arrived(way, last)
        local = self.view(self.ring.shard(0))

        def add(i, carry):
            here = pl.ds(pl.multiple_of(i * block, 16), block)
            out[here, :] = (
                local[here, :].astype(full)
                + self.buffers[0, last, here, :].astype(full)
                + self.buffers[1, last, here, :].astype(full)
            )
            return carry

        lax.fori_loop(0, self.rows // block, add, 0)
        for copy in self.copies:
            copy.wait_send()


class StagedSumRing(SumRing):
    def __init__(self, count, parts, buffers, held, terms, load, send, recv):
        size = parts.shape[1] // 2
        first = lambda shard, part: parts.at[shard, pl.ds(part * size, size)]
        super().__init__(count, None, first, buffers, send, recv)
        self.parts = parts
        self.held = held
        self.terms = terms
        self.load = load
        self.last = [None, None]

    def fetch(self, way, offset):
        shard = self.ring.shard(-offset if way else offset)
        copy = pltpu.make_async_copy(
            self.parts.at[shard], self.terms.at[way], self.load.at[1, way]
        )
        copy.start()
        return copy

    def start(self):
        super().start()
        self.fetched = [self.fetch(way, self.steps - 1) for way in range(2)]

    def take(self, way, step):
        self.arrived(way, step)
        if self.last[way] is not None:
            self.last[way].wait_send()
        source, target = self.buffers.at[way, step], self.held.at[way]
        if step == 0:
            half = pl.ds(way * (self.rows // 2), self.rows // 2)
            source, target = self.half(way), self.held.at[way, half]
        copy = pltpu.make_async_copy(source, target, self.load.at[0, way])
        copy.start()
        return copy

    def step(self, step):
        block = 48
        taken = [self.take(way, step - 1) for way in range(2)]
        for way in range(2):
            taken[way].wait()
            self.fetched[way].wait()
            held, terms = self.held.at[way], self.terms.at[way]

            def add(i, carry):
                here = pl.ds(pl.multiple_of(i * block, 16), block)
                held[here, :] = (terms[here, :].astype(full) + held[here, :].astype(full)).astype(low)
                return carry

            def keep(i, carry):
                here = pl.ds(pl.multiple_of(i * block, 16), block)
                held[here, :] = terms[here, :]
                return carry

            blocks = self.rows // block
            if step > 1:
                lax.fori_loop(0, blocks, add, 0)
            else:
                lax.fori_loop(way * (blocks // 2), (way + 1) * (blocks // 2), add, 0)
                lax.fori_loop((1 - way) * (blocks // 2), (2 - way) * (blocks // 2), keep, 0)
            self.last[way] = self.copy(way, step, held, self.buffers.at[way, step])
            self.last[way].start()
            if step < self.steps - 1 or way == 0:
                self.fetched[way] = self.fetch(way, self.steps - 1 - step)

    def finish(self, out):
        block = 48
        taken = [self.take(way, self.steps - 1) for way in range(2)]
        for copy in taken:
            copy.wait()
        self.fetched[0].wait()

        def add(i, carry):
            here = pl.ds(pl.multiple_of(i * block, 16), block)
            out[here, :] = (
                self.terms[0, here, :].astype(full)
                + self.held[0, here, :].astype(full)
                + self.held[1, here, :].astype(full)
            )
            return carry

        lax.fori_loop(0, self.rows // block, add, 0)
        for copy in self.copies:
            copy.wait_send()


def backward_kernel(
    count,
    tokens,
    cotangent,
    gains,
    resid,
    normed_part,
    ffn_part,
    gateup_parts,
    down_parts,
    features_in,
    qkv_rows_in,
    out_all_in,
    stream_in,
    kv_both_in,
    kv_turned_in,
    lse,
    mixed_group_in,
    shuffle_in,
    key_ids,
    query_ids,
    block_out,
    input_grad,
    gain_grads,
    gateup_grad,
    down_grad,
    qkv_grad,
    out_grad,
    gateup_sums,
    down_sums,
    gateup_held,
    gateup_terms,
    down_held,
    down_terms,
    part_quarter,
    qkv_local,
    out_local,
    qkv_sums,
    out_sums,
    sum_out,
    sum_in,
    proj_group,
    turned_out,
    turned_grad,
    grad_stream,
    kv_total,
    kv_out,
    kv_in,
    stream_grad,
    kv_mate,
    all_grad,
    normed_grad,
    bias,
    load_sem,
    part_sem,
    ring_send,
    ring_recv,
    head_send,
    head_recv,
    kv_send,
    kv_recv,
    features,
    qkv_rows,
    out_all,
    stream,
    kv_both,
    kv_turned,
    mixed_group,
    shuffle,
    take_sem,
):
    rows = tokens.shape[0]
    group = 4 * rows
    width = features.shape[1]
    heads = width // HEAD_DIM
    scale = HEAD_DIM ** (-0.5)
    query_grad = turned_grad
    feature_grad = grad_stream
    head = lax.axis_index("head")
    me = lax.axis_index("seq")
    mate_head = head + 1 - 2 * lax.rem(head, 2)
    across_head = lax.rem(head + 2, 4)
    mate = {"head": mate_head}
    across = {"head": across_head}
    corner = {"head": 3 - head}

    def lanes(of):
        return pl.ds(pl.multiple_of(of * width, 128), width)

    def quarter(i):
        return pl.ds(i * rows, rows)

    copies = []

    def send(index, source, target, where):
        copy = remote(source, target, head_send.at[index], head_recv.at[index], where)
        copy.start()
        copies.append(copy)

    def arrived(index, target, where):
        remote(target, target, head_send.at[index], head_recv.at[index], where).wait_recv()

    def shard_view(ref, columns):
        def view(shard, part=None):
            first = pl.multiple_of((shard // 2) * BLK, 32)
            at = pl.ds(pl.multiple_of(lax.rem(shard, 2) * columns, 128), columns)
            if part is None:
                return ref.at[pl.ds(first, BLK), at]
            return ref.at[pl.ds(pl.multiple_of(first + part * (BLK // 2), 16), BLK // 2), at]

        return view

    qkv_view = shard_view(qkv_local, QKV // 2)
    out_view = shard_view(out_local, D // 2)
    gateup_ring = StagedSumRing(
        count,
        gateup_parts,
        gateup_sums,
        gateup_held,
        gateup_terms,
        load_sem.at[0],
        ring_send.at[0],
        ring_recv.at[0],
    )
    down_ring = StagedSumRing(
        count,
        down_parts,
        down_sums,
        down_held,
        down_terms,
        load_sem.at[1],
        ring_send.at[1],
        ring_recv.at[1],
    )
    qkv_ring = SumRing(count, qkv_view, qkv_view, qkv_sums, ring_send.at[2], ring_recv.at[2])
    out_ring = SumRing(count, out_view, out_view, out_sums, ring_send.at[3], ring_recv.at[3])

    barrier = pltpu.get_barrier_semaphore()
    for where in (gateup_ring.where(0), gateup_ring.where(1), mate, across, corner):
        pl.semaphore_signal(barrier, inc=1, device_id=where, device_id_type=pl.DeviceIdType.MESH)

    @pl.when(me < count - 1)
    def _():
        pl.semaphore_signal(
            barrier, inc=1, device_id={"seq": me + 1}, device_id_type=pl.DeviceIdType.MESH
        )

    pl.semaphore_wait(barrier, 5 + (me + count - 1) // count)

    def fetch(value, i):
        copy = pltpu.make_async_copy(value.at[quarter(i)], part_quarter, part_sem)
        copy.start()
        copy.wait()
        return part_quarter[...].astype(full)

    def sum_first(base, slot, value):
        send(base, value.at[quarter(3)], sum_in.at[slot], mate)
        send(base + 1, value.at[quarter(1)], sum_in.at[slot + 1], mate)

    def sum_across(base, slot, value):
        own = fetch(value, 2)
        arrived(base, sum_in.at[slot], mate)
        sum_out[slot // 3] = (own + sum_in[slot].astype(full)).astype(low)
        send(base + 2, sum_out.at[slot // 3], sum_in.at[slot + 2], across)

    def sum_last(base, slot, value):
        own = fetch(value, 0)
        arrived(base + 1, sum_in.at[slot + 1], mate)
        own = own + sum_in[slot + 1].astype(full)
        arrived(base + 2, sum_in.at[slot + 2], across)
        return own + sum_in[slot + 2].astype(full)

    takes = [
        pltpu.make_async_copy(source, target, take_sem.at[i])
        for i, (source, target) in enumerate(
            (
                (features_in, features),
                (qkv_rows_in, qkv_rows),
                (out_all_in, out_all),
                (stream_in, stream),
                (kv_both_in, kv_both),
                (kv_turned_in, kv_turned),
                (mixed_group_in, mixed_group),
                (shuffle_in, shuffle),
            )
        )
    ]
    sum_first(0, 0, normed_part)
    for copy in takes:
        copy.start()
    gateup_ring.start()
    down_ring.start()
    sum_across(0, 0, normed_part)
    sum_first(3, 3, ffn_part)

    normed_two_grad = sum_last(0, 0, normed_part)
    values = resid[...]
    inverse = inverse_norm(values)
    gain_grads[1:2, :] = jnp.sum(normed_two_grad * values * inverse, axis=0, keepdims=True)
    input_grad[...] = cotangent[...].astype(full) + norm_back(
        values, inverse, gains[1:2, :], normed_two_grad
    )
    proj_group[quarter(0), :] = input_grad[...].astype(low)

    for copy in takes:
        copy.wait()

    def back_projection(of):
        weights = out_all[pl.ds(pl.multiple_of(of * width, 128), width), :]
        return mul(proj_group[quarter(0), :], weights, NT).astype(low)

    for j, of, where in ((2, across_head, across), (3, 3 - head, corner), (1, mate_head, mate)):
        turned_out[j - 1] = back_projection(of)
        send(31 + j, turned_out.at[j - 1], turned_grad.at[quarter(j)], where)
    send(6, proj_group.at[quarter(0)], proj_group.at[quarter(2)], across)
    send(7, proj_group.at[quarter(0)], proj_group.at[quarter(1)], mate)
    turned_grad[quarter(0), :] = back_projection(head)
    gateup_ring.step(1)
    down_ring.step(1)
    for j, where in ((1, mate), (2, across), (3, corner)):
        arrived(31 + j, turned_grad.at[quarter(j)], where)

    def turn(i, carry):
        here = pl.ds(pl.multiple_of(i * rows, rows), rows)
        grad_stream[here, :] = mul(shuffle[here, :], turned_grad[...], NN).astype(low)
        return carry

    lax.fori_loop(0, 4, turn, 0)

    kv_total[...] = jnp.zeros_like(kv_total)

    def back_tile(tile, carry):
        start = pl.multiple_of(tile * QUERY_TILE, QUERY_TILE)
        here = pl.ds(start, QUERY_TILE)
        span = pl.ds(start, SPAN)
        shape = (SPAN, QUERY_TILE)
        key = lax.broadcasted_iota(jnp.int32, shape, 0)
        query = lax.broadcasted_iota(jnp.int32, shape, 1)
        same = key_ids[span, :] == query_ids[:, here]
        allowed = same & (key > query) & (key <= query + WINDOW)
        bias[...] = jnp.where(allowed, 0.0, neg_fill)

        def back_head(j, carry):
            at = pl.ds(pl.multiple_of(j * HEAD_DIM, HEAD_DIM), HEAD_DIM)
            queries = stream[here, at]
            grads = grad_stream[here, at]
            scores = mul(kv_both[span, :HEAD_DIM], queries, NT) * scale + bias[...]
            probs = jnp.exp(scores - lse[j, :, here])
            prob_grad = mul(kv_both[span, HEAD_DIM:], grads, NT)
            delta = jnp.sum(probs * prob_grad, axis=0, keepdims=True)
            score_grad = (probs * (prob_grad - delta)).astype(low)
            turned = mul(kv_turned[:HEAD_DIM, span], score_grad, NN) * scale
            query_grad[here, at] = turned.T.astype(low)
            kv_total[span, :HEAD_DIM] += mul(score_grad, queries, NN) * scale
            kv_total[span, HEAD_DIM:] += mul(probs.astype(low), grads, NN)
            return carry

        return lax.fori_loop(0, heads, back_head, carry)

    lax.fori_loop(0, group // QUERY_TILE, back_tile, 0)
    kv_out[...] = kv_total[:group, :].astype(low)
    kv_copy = remote(kv_out, kv_in, kv_send, kv_recv, {"seq": lax.rem(me + count - 1, count)})

    @pl.when(me > 0)
    def _():
        kv_copy.start()

    def turn_back(i, carry):
        here = pl.ds(pl.multiple_of(i * rows, rows), rows)
        all_grad[here, lanes(head)] = mul(shuffle[:, here], query_grad[...], TN).astype(low)
        return carry

    lax.fori_loop(0, 4, turn_back, 0)

    def swapped(index, ref, columns, distance, where):
        for i in range(4):
            send(
                index + i,
                ref.at[quarter(i), columns],
                ref.at[quarter(i ^ distance), columns],
                where,
            )

    def swapped_arrived(index, ref, columns, distance, where):
        for i in range(4):
            arrived(index + i, ref.at[quarter(i ^ distance), columns], where)

    swapped(9, all_grad, lanes(head), 2, across)
    swapped(13, all_grad, lanes(head), 1, mate)
    arrived(6, proj_group.at[quarter(2)], across)
    send(8, proj_group.at[quarter(2)], proj_group.at[quarter(3)], mate)
    gateup_ring.step(2)
    down_ring.step(2)
    sum_across(3, 3, ffn_part)
    arrived(7, proj_group.at[quarter(1)], mate)
    arrived(8, proj_group.at[quarter(3)], mate)
    for i in range(3):
        at = slice(i * (D // 3), (i + 1) * (D // 3))
        out_local[:, at] = mul(mixed_group[...], proj_group[:, at], TN).astype(low)
    out_ring.start()

    @pl.when(me < count - 1)
    def _():
        kv_copy.wait_recv()
        kv_total[pl.ds(group, group), :] += kv_in[...].astype(full)

    stream_grad[...] = kv_total[pl.ds(group, group), :].astype(low)

    def turn_keys(i, carry):
        here = pl.ds(pl.multiple_of(i * rows, rows), rows)
        kv_mate[0, here, :] = mul(shuffle[:, here], stream_grad[...], TN).astype(low)
        return carry

    lax.fori_loop(0, 4, turn_keys, 0)
    for i in range(4):
        send(17 + i, kv_mate.at[0, quarter(i)], kv_mate.at[1, quarter(i ^ 1)], mate)
    for i in range(4):
        arrived(17 + i, kv_mate.at[1, quarter(i ^ 1)], mate)
    kv_total[pl.ds(0, group), :] = kv_mate[0].astype(full) + kv_mate[1].astype(full)
    kv_mate[2] = kv_total[pl.ds(0, group), :].astype(low)
    mine = pl.ds(pl.multiple_of(lax.rem(head, 2) * HEAD_DIM, HEAD_DIM), HEAD_DIM)
    of_mine = pl.ds(pl.multiple_of(QW + lax.rem(head, 2) * HEAD_DIM, HEAD_DIM), HEAD_DIM)
    of_mate = pl.ds(pl.multiple_of(QW + lax.rem(mate_head, 2) * HEAD_DIM, HEAD_DIM), HEAD_DIM)
    for i in range(4):
        send(21 + i, kv_mate.at[2, quarter(i), mine], kv_mate.at[3, quarter(i ^ 2), mine], across)
    out_ring.step(1)
    gateup_ring.step(3)
    down_ring.step(3)
    swapped_arrived(9, all_grad, lanes(across_head), 2, across)
    swapped(25, all_grad, lanes(across_head), 1, mate)
    swapped_arrived(13, all_grad, lanes(mate_head), 1, mate)
    for i in range(4):
        arrived(21 + i, kv_mate.at[3, quarter(i ^ 2), mine], across)
    all_grad[:, of_mine] = (
        kv_total[pl.ds(0, group), mine] + kv_mate[3, :, mine].astype(full)
    ).astype(low)
    swapped(35, all_grad, of_mine, 1, mate)
    swapped_arrived(35, all_grad, of_mate, 1, mate)
    swapped_arrived(25, all_grad, lanes(3 - head), 1, mate)

    for i in range(2):
        at = slice(i * (QKV // 2), (i + 1) * (QKV // 2))
        qkv_local[:, at] = mul(features[...], all_grad[:, at], TN).astype(low)
    qkv_ring.start()
    for i, where in ((2, across), (3, corner), (1, mate)):
        feature_grad[quarter(i), :] = mul(all_grad[quarter(i), :], qkv_rows[...], NT).astype(low)
        send(28 + i, feature_grad.at[quarter(i)], normed_grad.at[:, lanes(head)], where)
    normed_grad[:, lanes(head)] = mul(all_grad[quarter(0), :], qkv_rows[...], NT).astype(low)
    qkv_ring.step(1)
    out_ring.step(2)
    block_out[...] = (resid[...] + sum_last(3, 3, ffn_part)).astype(low)
    for i, where, of in ((2, across, across_head), (3, corner, 3 - head), (1, mate, mate_head)):
        arrived(28 + i, normed_grad.at[:, lanes(of)], where)
    qkv_ring.step(2)
    normed_one_grad = normed_grad[...].astype(full)
    values = tokens[...].astype(full)
    inverse = inverse_norm(values)
    gain_grads[0:1, :] = jnp.sum(normed_one_grad * values * inverse, axis=0, keepdims=True)
    input_grad[...] += norm_back(values, inverse, gains[0:1, :], normed_one_grad)
    qkv_ring.step(3)
    out_ring.step(3)
    gateup_ring.finish(gateup_grad)
    down_ring.finish(down_grad)
    out_ring.finish(out_grad)
    qkv_ring.finish(qkv_grad)
    for copy in copies:
        copy.wait_send()

    @pl.when(me > 0)
    def _():
        kv_copy.wait_send()


def backward_section(count, *values):
    (tokens, cotangent, gains, resid, normed_part, ffn_part, gateup_parts, down_parts) = values[:8]
    rows = tokens.shape[0]
    group = 4 * rows
    width = QW // 4
    steps = count // 2
    vmem = pl.BlockSpec(memory_space=pltpu.VMEM)
    hbm = pl.BlockSpec(memory_space=pl.ANY)
    shard = gateup_parts.shape[1:]
    down_shard = down_parts.shape[1:]
    outs = [
        ((rows, D), low),
        ((rows, D), full),
        ((2, D), full),
        (shard, full),
        (down_shard, full),
        ((BLK, QKV // 2), full),
        ((BLK, D // 2), full),
        ((2, steps) + shard, low),
        ((2, steps) + down_shard, low),
    ]
    dma = pltpu.SemaphoreType.DMA
    return pl.pallas_call(
        functools.partial(backward_kernel, count),
        in_specs=[vmem] * 4 + [hbm] * 10 + [vmem] + [hbm] * 2 + [vmem] * 2,
        out_specs=[vmem] * 7 + [hbm] * 2,
        out_shape=[jax.ShapeDtypeStruct(shape, kind) for shape, kind in outs],
        scratch_shapes=[
            pltpu.VMEM((2,) + shard, low),
            pltpu.VMEM((2,) + shard, low),
            pltpu.VMEM((2,) + down_shard, low),
            pltpu.VMEM((2,) + down_shard, low),
            pltpu.VMEM((rows, D), low),
            pltpu.VMEM((width, QKV), low),
            pltpu.VMEM((width, D), low),
            pltpu.VMEM((2, steps, BLK, QKV // 2), low),
            pltpu.VMEM((2, steps, BLK, D // 2), low),
            pltpu.VMEM((2, rows, D), low),
            pltpu.VMEM((6, rows, D), low),
            pltpu.VMEM((group, D), low),
            pltpu.VMEM((3, rows, width), low),
            pltpu.VMEM((group, width), low),
            pltpu.VMEM((group, width), low),
            pltpu.VMEM((2 * group, 2 * HEAD_DIM), full),
            pltpu.VMEM((group, 2 * HEAD_DIM), low),
            pltpu.VMEM((group, 2 * HEAD_DIM), low),
            pltpu.VMEM((group, 2 * HEAD_DIM), low),
            pltpu.VMEM((4, group, 2 * HEAD_DIM), low),
            pltpu.VMEM((group, QKV), low),
            pltpu.VMEM((rows, D), low),
            pltpu.VMEM((SPAN, QUERY_TILE), full),
            dma((2, 2, 2)),
            dma,
            dma((4, 2, steps)),
            dma((4, 2, steps)),
            dma((39,)),
            dma((39,)),
            dma,
            dma,
            *[pltpu.VMEM(values[i].shape, low) for i in (8, 9, 10, 11, 12, 13, 15, 16)],
            dma((8,)),
        ],
        compiler_params=pltpu.CompilerParams(
            collective_id=1, has_side_effects=True, vmem_limit_bytes=63 * 1024 * 1024
        ),
        name="backward_section",
    )(*values)


def ffn_kernel(
    normed, cotangent, gateup, down, hidden, gate_up_grad, normed_part, ffn_part, normed_sum, ffn_sum
):
    units = down.shape[0]
    tile = next(u for u in (6, 4, 3, 2, 1) if units % u == 0)
    size = normed.shape[0]
    half = D // 2
    root = (2.0 / 3.141592653589793) ** 0.5

    def step(c, carry):
        here = pl.ds(pl.multiple_of(c * tile * BLK, 32), tile * BLK)
        pair = pl.ds(pl.multiple_of(c * tile * 2 * BLK, 64), 2 * tile * BLK)
        weights = gateup[pair, :]
        parts = [down[pl.ds(c * tile, tile), i].reshape(tile * BLK, half) for i in range(2)]
        both = mul(weights, normed[...], NT).reshape(tile, 2, BLK, size)
        gate = both[:, 0].reshape(tile * BLK, size)
        upper = both[:, 1].reshape(tile * BLK, size)
        grad = mul(parts[0], cotangent[:, :half], NT) + mul(parts[1], cotangent[:, half:], NT)
        square = gate * gate
        bent = jnp.tanh(root * gate * (1.0 + 0.044715 * square))
        share = 0.5 * (1.0 + bent)
        active = gate * share
        slope = share + 0.5 * gate * (1.0 - bent * bent) * (root * (1.0 + 0.134145 * square))
        units_out = (active * upper).astype(low)
        grads = [(grad * upper * slope).astype(low), (grad * active).astype(low)]
        grads = [g.reshape(tile, 1, BLK, size) for g in grads]
        grads = jnp.concatenate(grads, axis=1).reshape(2 * tile * BLK, size)
        hidden[here, :] = units_out
        gate_up_grad[pair, :] = grads
        first = c == 0
        term = mul(grads, weights, TN)
        terms = [mul(units_out, part, TN) for part in parts]

        @pl.when(first)
        def _():
            normed_sum[...] = term
            ffn_sum[:, :half] = terms[0]
            ffn_sum[:, half:] = terms[1]

        @pl.when(jnp.logical_not(first))
        def _():
            normed_sum[...] += term
            ffn_sum[:, :half] += terms[0]
            ffn_sum[:, half:] += terms[1]

        return carry

    lax.fori_loop(0, units // tile, step, 0, unroll=True)
    normed_part[...] = normed_sum[...].astype(low)
    ffn_part[...] = ffn_sum[...].astype(low)


def feed_forward(normed, cotangent, gateup, down):
    group = normed.shape[0]
    units = down.shape[0]
    size = min(512, group)
    rows = pl.BlockSpec((size, D), lambda t: (t, 0))
    once = pl.Buffered(1)
    return pl.pallas_call(
        ffn_kernel,
        grid=(group // size,),
        in_specs=[
            rows,
            rows,
            pl.BlockSpec(gateup.shape, lambda t: (0, 0), pipeline_mode=once),
            pl.BlockSpec(down.shape, lambda t: (0, 0, 0, 0), pipeline_mode=once),
        ],
        out_specs=[
            pl.BlockSpec((units * BLK, size), lambda t: (0, t)),
            pl.BlockSpec((2 * units * BLK, size), lambda t: (0, t)),
            rows,
            rows,
        ],
        out_shape=[
            jax.ShapeDtypeStruct((units * BLK, group), low),
            jax.ShapeDtypeStruct((2 * units * BLK, group), low),
            jax.ShapeDtypeStruct((group, D), low),
            jax.ShapeDtypeStruct((group, D), low),
        ],
        scratch_shapes=[pltpu.VMEM((size, D), full), pltpu.VMEM((size, D), full)],
        compiler_params=pltpu.CompilerParams(vmem_limit_bytes=58 * 1024 * 1024),
        cost_estimate=pl.CostEstimate(
            flops=12 * units * BLK * group * D,
            bytes_accessed=40 << 20,
            transcendentals=units * BLK * group,
        ),
        name="feed_forward",
    )(normed, cotangent, gateup, down)


def update_kernel(
    rate, turned, w_ref, g_ref, l_ref, r_ref, lr_ref, rr_ref, ln_ref, rn_ref, wn_ref
):
    count, rows, columns = w_ref.shape
    blocks = g_ref[...].T.reshape(count, g_ref.shape[1] // count, g_ref.shape[0])
    for b in range(count):
        grad = blocks[b]
        other = grad.T
        if not turned:
            grad, other = other, grad
        square = jnp.sum(jnp.sum(grad * grad, axis=1, keepdims=True), axis=0, keepdims=True)
        square = square * (1.0 / (rows * columns)) + stat_eps
        grad = grad.astype(low)
        other = other.astype(low)
        ln_ref[b] = 0.5 * l_ref[b] + mul(grad, other, NN) * (0.5 / (columns * square))
        rn_ref[b] = 0.5 * r_ref[b] + mul(other, grad, NN) * (0.5 / (rows * square))
        step = mul(lr_ref[b].astype(low), grad, NN).astype(low)
        step = mul(step, rr_ref[b].astype(low), NN)
        wn_ref[b] = w_ref[b] - step * (rate * lax.rsqrt(square))


def update(weight, grad, left, right, left_root, right_root, rate, turned=False):
    count, rows, columns = weight.shape
    if grad.ndim == 3:
        grad = grad.transpose(1, 0, 2).reshape(rows, count * columns)
    height = columns if turned else rows
    batch = count // (grad.shape[0] // height)
    spec = lambda i, j: pl.BlockSpec((batch, i, j), lambda b: (b, 0, 0))
    return pl.pallas_call(
        functools.partial(update_kernel, rate, turned),
        grid=(count // batch,),
        in_specs=[
            spec(rows, columns),
            pl.BlockSpec((height, grad.shape[1]), lambda b: (b, 0)),
            spec(rows, rows),
            spec(columns, columns),
            spec(rows, rows),
            spec(columns, columns),
        ],
        out_specs=[spec(rows, rows), spec(columns, columns), spec(rows, columns)],
        out_shape=[
            jax.ShapeDtypeStruct(left.shape, full),
            jax.ShapeDtypeStruct(right.shape, full),
            jax.ShapeDtypeStruct(weight.shape, full),
        ],
        compiler_params=pltpu.CompilerParams(vmem_limit_bytes=58 * 1024 * 1024),
        cost_estimate=pl.CostEstimate(
            flops=16 * count * 256 * 256 * 128,
            bytes_accessed=36 * count * rows * 128,
            transcendentals=0,
        ),
        name="update",
    )(weight, grad, left, right, left_root, right_root)


def norm_back(values, inverse, gain, grad):
    scaled = gain * grad
    mean = jnp.mean(values * scaled, axis=-1, keepdims=True)
    return inverse * scaled - values * (inverse * inverse * inverse * mean)


def inverse_norm(values):
    return lax.rsqrt(jnp.mean(values * values, axis=-1, keepdims=True) + norm_eps)


def forward_steps(tokens, cotangent, attn_gain, ffn_gain, stacks, token_order, sequence_ids):
    qkv_stack, out_stack, gateup_stack, down_stack = stacks
    row_count = tokens.shape[0]
    head_count = lax.axis_size("head")
    seq_count = lax.axis_size("seq")
    group = row_count * head_count
    head_index = lax.axis_index("head")
    local_width = QW // head_count
    seq_index = lax.axis_index("seq")
    gains = jnp.concatenate([attn_gain, ffn_gain]).astype(low).astype(full)[None]
    gains = lax.all_to_all(
        jnp.broadcast_to(gains, (head_count * seq_count, gains.shape[1])),
        ("head", "seq"),
        split_axis=0,
        concat_axis=0,
        tiled=True,
    )
    own_gains = attn_gain.shape[0]
    gain_one = gains[:, :own_gains].reshape(1, D)
    gain_two = gains[:, own_gains:].reshape(1, D)


    ids_own = lax.dynamic_slice_in_dim(sequence_ids, seq_index * group, group, 0)
    ids_before = lax.dynamic_slice_in_dim(
        sequence_ids, jnp.maximum(seq_index - 1, 0) * group, group, 0
    )
    ids_before = jnp.where(seq_index > 0, ids_before, -1)
    key_ids = jnp.concatenate([ids_before, ids_own])[:, None]
    query_ids = ids_own[None, :]
    qkv_rows = joined_halves(gather_rows(qkv_stack, 8, to_columns))
    out_rows = joined_halves(gather_rows(out_stack, 8, to_columns))
    gateup = gather_rows(gateup_stack, 16, to_units)
    down = gather_rows(down_stack, 8, to_columns)
    tokens_float = tokens.astype(full)
    normed_one = (tokens_float * inverse_norm(tokens_float) * gain_one).astype(low)
    normed_one_group = jnp.concatenate(head_gather(normed_one))
    feature_start = head_index * local_width
    features = lax.dynamic_slice_in_dim(normed_one_group, feature_start, local_width, 1)
    weights = in_order(head_gather(qkv_rows), 0)
    weights = jnp.concatenate(
        [lax.dynamic_slice_in_dim(weights, feature_start, local_width, 1), weights[:, QW:]], axis=1
    )
    projected = mul(normed_one_group, weights, NN, low)
    buffer_rows = ((token_order // row_count) ^ head_index) * row_count + token_order % row_count
    shuffle = (
        buffer_rows[:, None] == lax.broadcasted_iota(jnp.int32, (group, group), 1)
    ).astype(low)
    stream = mul(shuffle, projected, NN, low)
    kv_stream = stream[:, local_width:]
    kv_before = lax.ppermute(kv_stream, "seq", [(i, i + 1) for i in range(seq_count - 1)])
    kv_both = jnp.concatenate([kv_before, kv_stream], axis=0)
    kv_turned = kv_both.T
    mixed_stream, lse = attend(stream[:, :local_width], kv_both, kv_turned, key_ids, query_ids)
    mixed_group = mul(shuffle, mixed_stream, TN, low)
    part = mul(mixed_group, out_rows, NN, low)
    resid = tokens_float + head_sum([part[i * row_count :][:row_count] for i in range(4)])
    normed_two = (resid * inverse_norm(resid) * gain_two).astype(low)
    normed_group = jnp.concatenate(head_gather(normed_two))
    grad_group = jnp.concatenate(head_gather(cotangent))
    section = (
        jnp.concatenate([gain_one, gain_two]),
        resid,
        normed_group,
        grad_group,
        gateup,
        down,
        features,
        qkv_rows,
        out_rows,
        stream,
        kv_both,
        kv_turned,
        lse,
        mixed_group,
        shuffle,
        key_ids,
        query_ids,
    )
    return section


def backward_steps(
    tokens,
    cotangent,
    gains,
    resid,
    normed_part,
    ffn_part,
    gateup_wgrad,
    down_wgrad,
    features,
    qkv_rows,
    out_rows,
    stream,
    kv_both,
    kv_turned,
    lse,
    mixed_group,
    shuffle,
    key_ids,
    query_ids,
    counts,
):
    row_count = tokens.shape[0]
    group = row_count * lax.axis_size("head")
    seq_count = lax.axis_size("seq")
    local_width = features.shape[1]
    query_stream = stream[:, :local_width]
    gain_one, gain_two = gains[0], gains[1]
    tokens_float = tokens.astype(full)
    inverse_one = inverse_norm(tokens_float)
    inverse_two = inverse_norm(resid)
    normed_two_grad = head_sum([normed_part[i * row_count :][:row_count] for i in range(4)])
    gateup_grad_own = sum_rows(gateup_wgrad, counts[2], 16, from_units)
    down_grad_own = sum_rows(down_wgrad, counts[3], 8, from_columns)
    ffn_out = head_sum([ffn_part[i * row_count :][:row_count] for i in range(4)])
    block_out = (resid + ffn_out).astype(low)

    resid_grad = cotangent.astype(full) + norm_back(resid, inverse_two, gain_two, normed_two_grad)
    gain_two_grad = jnp.sum(normed_two_grad * resid * inverse_two, axis=0)
    proj_grad = resid_grad.astype(low)
    proj_grad_group = jnp.concatenate(head_gather(proj_grad))
    mixed_grad_group = mul(proj_grad_group, out_rows, NT, low)
    mixed_grad_stream = mul(shuffle, mixed_grad_group, NN, low)
    out_wgrad = split_halves(mul(mixed_group, proj_grad_group, TN, low), BLK)
    out_grad_own = sum_rows(out_wgrad, counts[1], 8, from_columns)

    query_grad, kv_grad = attend_back(
        query_stream, mixed_grad_stream, kv_both, kv_turned, key_ids, query_ids, lse
    )
    kv_later = lax.ppermute(
        kv_grad[:group].astype(low), "seq", [(i, i - 1) for i in range(1, seq_count)]
    )
    kv_grad = (kv_grad[group:] + kv_later.astype(full)).astype(low)
    grad_local = mul(shuffle, jnp.concatenate([query_grad, kv_grad], axis=1), TN, low)
    gathered = head_gather(grad_local)

    def own_order(value, j):
        quarters = [value[i * row_count :][:row_count] for i in range(4)]
        return jnp.concatenate([quarters[i ^ j] for i in range(4)])

    gathered = [own_order(value, j) for j, value in enumerate(gathered)]
    kv_total = sum(value[:, local_width:].astype(full) for value in gathered).astype(low)
    qkv_grad = jnp.concatenate(
        [in_order([value[:, :local_width] for value in gathered], 1), kv_total], axis=1
    )
    qkv_wgrad = split_halves(mul(features, qkv_grad, TN, low), BLK)
    qkv_grad_own = sum_rows(qkv_wgrad, counts[0], 8, from_columns)
    feature_grad = mul(qkv_grad, qkv_rows, NT, low)
    order = (0, 2, 1, 3)
    feature_parts = head_exchange([feature_grad[i * row_count :][:row_count] for i in range(4)])
    normed_one_grad = in_order([feature_parts[order.index(j)] for j in range(4)], 1).astype(full)
    input_grad = resid_grad + norm_back(tokens_float, inverse_one, gain_one, normed_one_grad)
    gain_one_grad = jnp.sum(normed_one_grad * tokens_float * inverse_one, axis=0)
    return (
        block_out,
        input_grad,
        jnp.stack([gain_one_grad, gain_two_grad]),
        gateup_grad_own,
        down_grad_own,
        qkv_grad_own,
        out_grad_own,
    )


def on_device(
    tokens,
    cotangent,
    attn_gain,
    ffn_gain,
    qkv_stack,
    out_stack,
    gateup_stack,
    down_stack,
    qkv_left,
    qkv_right,
    out_left,
    out_right,
    gateup_left,
    gateup_right,
    down_left,
    down_right,
    qkv_left_root,
    qkv_right_root,
    out_left_root,
    out_right_root,
    gateup_left_root,
    gateup_right_root,
    down_left_root,
    down_right_root,
    sequence_ids,
    token_order,
):
    row_count = tokens.shape[0]
    head_count = lax.axis_size("head")
    seq_count = lax.axis_size("seq")
    device_count = head_count * seq_count
    group = row_count * head_count
    seq_index = lax.axis_index("seq")
    local_width = QW // head_count

    own_gains = attn_gain.shape[0]
    stacks = (qkv_stack, out_stack, gateup_stack, down_stack)
    whole_rows = all(s.shape[0] % u == 0 for s, u in zip(stacks, (8, 8, 16, 8)))
    if whole_rows:
        tile = jnp.concatenate([attn_gain[None], ffn_gain[None]])
        section = forward_section(
            tokens,
            cotangent,
            jnp.pad(tile, ((0, 6), (0, 128 - own_gains))),
            stacks,
            token_order[None, :],
            sequence_ids[None, :],
            seq_count,
        )
    else:
        section = forward_steps(
            tokens, cotangent, attn_gain, ffn_gain, stacks, token_order, sequence_ids
        )
    (
        gains_both,
        resid,
        normed_group,
        grad_group,
        gateup,
        down,
        features,
        qkv_rows,
        out_all,
        stream,
        kv_both,
        kv_turned,
        lse,
        mixed_group,
        shuffle,
        key_ids,
        query_ids,
    ) = section
    gateup = gateup.reshape(-1, D)
    down = down.reshape(-1, 2, BLK, D // 2)
    unit_count = down.shape[0]
    hidden, gate_up_grad, normed_part, ffn_part = feed_forward(
        normed_group, grad_group, gateup, down
    )
    gateup_wgrad = mul(gate_up_grad, normed_group, NN, low)
    down_wgrad = split_halves(mul(hidden, grad_group, NN, low), BLK)
    kept = (features, qkv_rows, out_all, stream, kv_both, kv_turned, lse, mixed_group, shuffle)
    counts = [s.shape[0] for s in stacks]
    if not whole_rows:
        gateup_wgrad = gateup_wgrad.reshape(2 * unit_count, BLK, D)
    if whole_rows:
        (block_out, input_grad, gain_grads, gateup_own, down_own, qkv_own, out_own, *_) = (
            backward_section(
                seq_count,
                tokens,
                cotangent,
                gains_both,
                resid,
                normed_part,
                ffn_part,
                gateup_wgrad.reshape(seq_count, -1, D),
                down_wgrad.reshape(seq_count, -1, D // 2),
                *kept,
                key_ids,
                query_ids,
            )
        )
        gateup_grad_own, down_grad_own = gateup_own, down_own
        qkv_grad_own, out_grad_own = qkv_own, out_own
    else:
        section = backward_steps(
            tokens, cotangent, gains_both, resid, normed_part, ffn_part, gateup_wgrad, down_wgrad, *kept,
            key_ids, query_ids, counts,
        )
        (block_out, input_grad, gain_grads, gateup_grad_own, down_grad_own, qkv_grad_own, out_grad_own) = section
    gain_one_grad, gain_two_grad = gain_grads[0], gain_grads[1]
    gain_grads = jnp.concatenate(
        [gain_one_grad.reshape(device_count, -1), gain_two_grad.reshape(device_count, -1)], axis=1
    )
    gain_grads = lax.all_to_all(
        gain_grads, ("head", "seq"), split_axis=0, concat_axis=0, tiled=True
    )
    gain_grads = jnp.sum(gain_grads, axis=0)

    gateup_new = update(
        gateup_stack,
        gateup_grad_own,
        gateup_left,
        gateup_right,
        gateup_left_root,
        gateup_right_root,
        0.5 * D ** (-0.5),
        whole_rows,
    )
    down_new = update(
        down_stack,
        down_grad_own,
        down_left,
        down_right,
        down_left_root,
        down_right_root,
        0.5 * FF ** (-0.5),
    )
    out_new = update(
        out_stack,
        out_grad_own,
        out_left,
        out_right,
        out_left_root,
        out_right_root,
        0.5 * (QW // 64) ** (-0.5),
    )
    qkv_new = update(
        qkv_stack,
        qkv_grad_own,
        qkv_left,
        qkv_right,
        qkv_left_root,
        qkv_right_root,
        0.5 * D ** (-0.5),
    )
    return (
        (block_out, input_grad, gain_grads[:own_gains], gain_grads[own_gains:])
        + tuple(qkv_new)
        + tuple(out_new)
        + tuple(gateup_new)
        + tuple(down_new)
    )


def solution(mesh):
    rows = P(("seq", "head"), None)
    gain = P(("head", "seq"))
    blocks = P(("head", "seq"), None, None)
    return jax.shard_map(
        on_device,
        mesh=mesh,
        in_specs=(rows, rows, gain, gain) + (blocks,) * 20 + (P(), P("seq")),
        out_specs=(rows, rows, gain, gain) + (blocks,) * 12,
        check_vma=False,
    )
```

```python
import functools

import jax
import jax.numpy as jnp
from jax import lax
from jax.experimental import pallas as pl
from jax.experimental.pallas import tpu as pltpu
from jax.sharding import PartitionSpec as P

D = 1536
HEAD_DIM = 128
FF = 4608
WINDOW = 1024
GRID = 16
QW = 1536
QKV = 1792
BLK = 96
BQ = 112
BH = 96
NU = 48

norm_eps = 1e-06
stat_eps = 1e-06
neg_fill = -1e30

QUERY_TILE = 256
SPAN = WINDOW + QUERY_TILE

low = jnp.bfloat16
full = jnp.float32

NT = (((1,), (1,)), ((), ()))
NN = (((1,), (0,)), ((), ()))
TN = (((0,), (0,)), ((), ()))


def mul(a, b, dims, kind=full):
    return lax.dot_general(a, b, dims, preferred_element_type=kind)


def ring_place(index, count):
    return jnp.where(index % 2 == 0, index // 2, count - 1 - index // 2)


def ring_index(place, count):
    return jnp.where(place < count // 2, 2 * place, 2 * (count - 1 - place) + 1)


def ring_routes(count):
    order = [i for i in range(0, count, 2)] + [i for i in range(count - 1, 0, -2)]
    up = [(order[i], order[(i + 1) % count]) for i in range(count)]
    return up, [(b, a) for a, b in up]


def seq_gather(shard):
    count = lax.axis_size("seq")
    rows = shard.shape[0]
    half = rows // 2
    me = lax.axis_index("seq")
    place = ring_place(me, count)
    up, down = ring_routes(count)
    out = jnp.zeros((count,) + shard.shape, shard.dtype)
    out = lax.dynamic_update_slice(out, shard[None], (me, 0, 0))
    ahead = shard
    behind = shard
    for step in range(1, count // 2):
        ahead = lax.ppermute(ahead, "seq", up)
        behind = lax.ppermute(behind, "seq", down)
        out = lax.dynamic_update_slice(
            out, ahead[None], (ring_index((place - step + count) % count, count), 0, 0)
        )
        out = lax.dynamic_update_slice(
            out, behind[None], (ring_index((place + step) % count, count), 0, 0)
        )
    ahead = lax.ppermute(ahead[:half], "seq", up)
    behind = lax.ppermute(behind[half:], "seq", down)
    far = ring_index((place + count // 2) % count, count)
    out = lax.dynamic_update_slice(out, ahead[None], (far, 0, 0))
    return lax.dynamic_update_slice(out, behind[None], (far, half, 0))


def seq_sum(parts):
    count, rows = parts.shape[:2]
    half = rows // 2
    place = ring_place(lax.axis_index("seq"), count)
    up, down = ring_routes(count)

    def part(offset):
        index = ring_index((place + offset + count) % count, count)
        return lax.dynamic_slice_in_dim(parts, index, 1, 0)[0]

    far = part(count // 2)
    ahead = lax.ppermute(far[:half], "seq", up)
    behind = lax.ppermute(far[half:], "seq", down)
    for offset in range(count // 2 - 1, 0, -1):
        local = part(offset)
        if ahead.shape[0] == rows:
            local = (local.astype(full) + ahead.astype(full)).astype(low)
        else:
            local = jnp.concatenate(
                [(local[:half].astype(full) + ahead.astype(full)).astype(low), local[half:]]
            )
        ahead = lax.ppermute(local, "seq", up)
        local = part(-offset)
        if behind.shape[0] == rows:
            local = (local.astype(full) + behind.astype(full)).astype(low)
        else:
            local = jnp.concatenate(
                [local[:half], (local[half:].astype(full) + behind.astype(full)).astype(low)]
            )
        behind = lax.ppermute(local, "seq", down)
    return part(0).astype(full) + ahead.astype(full) + behind.astype(full)


def gather_rows(stack, unit, layout):
    short = stack.astype(low)
    if stack.shape[0] % unit == 0:
        shard = layout(short)
        rows = shard.reshape(-1, shard.shape[-1])
        out = seq_gather(rows)
        return out.reshape((-1,) + shard.shape[1:])
    return layout(lax.all_gather(short, "seq", axis=0, tiled=True))


def sum_rows(rows, local, unit, back):
    count = lax.axis_size("seq")
    if local % unit == 0:
        own = seq_sum(rows.reshape(count, -1, rows.shape[-1]))
        return back(own.reshape((-1,) + rows.shape[1:]))
    return lax.psum_scatter(back(rows), "seq", scatter_dimension=0, tiled=True).astype(full)


def to_columns(stack):
    n, i, j = stack.shape
    return stack.reshape(n // 8, 8, i, j).transpose(0, 2, 1, 3).reshape(n // 8, i, 8 * j)


def from_columns(rows):
    n, i, j = rows.shape
    return rows.reshape(n, i, 8, j // 8).transpose(0, 2, 1, 3).reshape(n * 8, i, j // 8)


def to_units(stack):
    n, i, j = stack.shape
    return stack.reshape(n // 16, 16, i, j).transpose(0, 3, 1, 2).reshape(n // 16, j, 16 * i)


def from_units(rows):
    n, j, i = rows.shape
    return rows.reshape(n, j, 16, i // 16).transpose(0, 2, 3, 1).reshape(n * 16, i // 16, j)


def joined_halves(rows):
    n, i, j = rows.shape
    return rows.reshape(n // 2, 2, i, j).transpose(0, 2, 1, 3).reshape(n // 2 * i, 2 * j)


def split_halves(matrix, i):
    rows, columns = matrix.shape
    half = columns // 2
    parts = [matrix[:, at : at + half].reshape(rows // i, i, half) for at in (0, half)]
    return jnp.stack(parts, axis=1).reshape(2 * rows // i, i, half)


def to_partner(value, which):
    count = lax.axis_size("head")
    return lax.ppermute(value, "head", [(i, i ^ which) for i in range(count)])


def head_gather(value):
    across = to_partner(value, 2)
    mate = to_partner(value, 1)
    return value, mate, across, to_partner(across, 1)


def head_exchange(parts):
    return (parts[0],) + tuple(to_partner(parts[j], j) for j in (2, 1, 3))


def head_sum(parts):
    across = (parts[2].astype(full) + to_partner(parts[3], 1).astype(full)).astype(low)
    across = to_partner(across, 2)
    mine = parts[0].astype(full) + to_partner(parts[1], 1).astype(full)
    return mine + across.astype(full)


def in_order(parts, axis):
    me = lax.axis_index("head")
    odd = me % 2 == 1
    lower = [jnp.where(odd, parts[1], parts[0]), jnp.where(odd, parts[0], parts[1])]
    upper = [jnp.where(odd, parts[3], parts[2]), jnp.where(odd, parts[2], parts[3])]
    second = me >= 2
    return jnp.concatenate(
        [jnp.where(second, b, a) for a, b in zip(lower, upper)]
        + [jnp.where(second, a, b) for a, b in zip(lower, upper)],
        axis=axis,
    )


def tile_bias(tile, key_ids, query_ids, bias_ref):
    start = pl.multiple_of(tile * QUERY_TILE, QUERY_TILE)
    shape = (SPAN, QUERY_TILE)
    key = lax.broadcasted_iota(jnp.int32, shape, 0)
    query = lax.broadcasted_iota(jnp.int32, shape, 1)
    same = key_ids[pl.ds(start, SPAN), :] == query_ids[...]
    allowed = same & (key > query) & (key <= query + WINDOW)
    bias_ref[...] = jnp.where(allowed, 0.0, neg_fill)


def attend_kernel(q_ref, kv_ref, kvt_ref, key_ids, query_ids, out_ref, lse_ref, bias_ref):
    tile = pl.program_id(0)
    start = pl.multiple_of(tile * QUERY_TILE, QUERY_TILE)

    @pl.when(pl.program_id(1) == 0)
    def _():
        tile_bias(tile, key_ids, query_ids, bias_ref)

    keys = kv_ref[pl.ds(start, SPAN), :HEAD_DIM]
    scores = mul(keys, q_ref[...], NT) * HEAD_DIM ** (-0.5) + bias_ref[...]
    top = jnp.max(scores, axis=0, keepdims=True)
    expo = jnp.exp(scores - top)
    total = jnp.sum(expo, axis=0, keepdims=True)
    values = kvt_ref[HEAD_DIM:, pl.ds(start, SPAN)]
    mixed = mul(values, expo.astype(low), NN) / total
    out_ref[...] = mixed.T.astype(low)
    lse_ref[0] = top + jnp.log(total)


def attend_back_kernel(
    q_ref, g_ref, kv_ref, kvt_ref, key_ids, query_ids, lse_ref, dq_ref, dkv_ref, bias_ref
):
    tile = pl.program_id(0)
    start = pl.multiple_of(tile * QUERY_TILE, QUERY_TILE)
    scale = HEAD_DIM ** (-0.5)

    @pl.when((tile == 0) & (pl.program_id(1) == 0))
    def _():
        dkv_ref[...] = jnp.zeros_like(dkv_ref)

    @pl.when(pl.program_id(1) == 0)
    def _():
        tile_bias(tile, key_ids, query_ids, bias_ref)

    here = pl.ds(start, SPAN)
    queries = q_ref[...]
    grads = g_ref[...]
    scores = mul(kv_ref[here, :HEAD_DIM], queries, NT) * scale + bias_ref[...]
    probs = jnp.exp(scores - lse_ref[0])
    prob_grad = mul(kv_ref[here, HEAD_DIM:], grads, NT)
    delta = jnp.sum(probs * prob_grad, axis=0, keepdims=True)
    score_grad = (probs * (prob_grad - delta)).astype(low)
    dq = mul(kvt_ref[:HEAD_DIM, here], score_grad, NN) * scale
    dq_ref[...] = dq.T.astype(low)
    dkv_ref[here, :HEAD_DIM] += mul(score_grad, queries, NN) * scale
    dkv_ref[here, HEAD_DIM:] += mul(probs.astype(low), grads, NN)


def attention_specs(group):
    whole = lambda *shape: pl.BlockSpec(shape, lambda t, h: (0,) * len(shape))
    head_rows = pl.BlockSpec((QUERY_TILE, HEAD_DIM), lambda t, h: (t, h))
    keys = whole(2 * group, 2 * HEAD_DIM)
    keys_turned = whole(2 * HEAD_DIM, 2 * group)
    key_ids = whole(2 * group, 1)
    query_ids = pl.BlockSpec((1, QUERY_TILE), lambda t, h: (0, t))
    lse = pl.BlockSpec((1, 1, QUERY_TILE), lambda t, h: (h, 0, t))
    return head_rows, keys, keys_turned, key_ids, query_ids, lse


attention_params = pltpu.CompilerParams(
    dimension_semantics=("arbitrary", "arbitrary"), vmem_limit_bytes=40 * 1024 * 1024
)


def attend(queries, kv, kv_turned, key_ids, query_ids):
    group, width = queries.shape
    heads = width // HEAD_DIM
    rows, keys, turned, kids, qids, lse = attention_specs(group)
    work = heads * (group // QUERY_TILE) * SPAN * QUERY_TILE
    return pl.pallas_call(
        attend_kernel,
        grid=(group // QUERY_TILE, heads),
        in_specs=[rows, keys, turned, kids, qids],
        out_specs=[rows, lse],
        out_shape=[
            jax.ShapeDtypeStruct((group, width), low),
            jax.ShapeDtypeStruct((heads, 1, group), full),
        ],
        scratch_shapes=[pltpu.VMEM((SPAN, QUERY_TILE), full)],
        compiler_params=attention_params,
        cost_estimate=pl.CostEstimate(
            flops=8 * work * HEAD_DIM, bytes_accessed=6 << 20, transcendentals=work
        ),
        name="attend",
    )(queries, kv, kv_turned, key_ids, query_ids)


def attend_back(queries, grads, kv, kv_turned, key_ids, query_ids, lse_rows):
    group, width = queries.shape
    heads = width // HEAD_DIM
    rows, keys, turned, kids, qids, lse = attention_specs(group)
    work = heads * (group // QUERY_TILE) * SPAN * QUERY_TILE
    return pl.pallas_call(
        attend_back_kernel,
        grid=(group // QUERY_TILE, heads),
        in_specs=[rows, rows, keys, turned, kids, qids, lse],
        out_specs=[rows, keys],
        out_shape=[
            jax.ShapeDtypeStruct((group, width), low),
            jax.ShapeDtypeStruct((2 * group, 2 * HEAD_DIM), full),
        ],
        scratch_shapes=[pltpu.VMEM((SPAN, QUERY_TILE), full)],
        compiler_params=attention_params,
        cost_estimate=pl.CostEstimate(
            flops=20 * work * HEAD_DIM, bytes_accessed=8 << 20, transcendentals=work
        ),
        name="attend_back",
    )(queries, grads, kv, kv_turned, key_ids, query_ids, lse_rows)


def remote(source, target, send, recv, where):
    return pltpu.make_async_remote_copy(
        src_ref=source,
        dst_ref=target,
        send_sem=send,
        recv_sem=recv,
        device_id=where,
        device_id_type=pl.DeviceIdType.MESH,
    )


class Ring:
    def __init__(self, count, view, send, recv, split=True):
        me = lax.axis_index("seq")
        self.split = split
        odd = lax.rem(me, 2)
        self.count = count
        self.view = view
        self.send = send
        self.recv = recv
        self.place = (1 - odd) * (me // 2) + odd * (count - 1 - me // 2)
        self.ahead = {"seq": self.shard(1)}
        self.behind = {"seq": self.shard(-1)}
        self.copies = []

    def shard(self, offset):
        place = lax.rem(self.place + offset + self.count, self.count)
        upper = place // (self.count // 2)
        return (1 - upper) * 2 * place + upper * (2 * (self.count - 1 - place) + 1)

    def pair(self, offset, step):
        last = step == self.count // 2
        halved = last and self.split
        views = [
            self.view(self.shard(-offset), 0 if halved else None),
            self.view(self.shard(offset), 1 if halved else None),
        ]
        if last and not self.split:
            views = views[:1]
        return [
            remote(view, view, self.send.at[i, step - 1], self.recv.at[i, step - 1], where)
            for i, (view, where) in enumerate(zip(views, (self.ahead, self.behind)))
        ]

    def start(self, step):
        for copy in self.pair(step - 1, step):
            copy.start()
            self.copies.append(copy)

    def arrive(self, step):
        for copy in self.pair(step, step):
            copy.wait_recv()

    def finish(self):
        for copy in self.copies:
            copy.wait_send()


def turned_row(row):
    size = row.shape[1]
    return jnp.broadcast_to(row.astype(full), (128, size)).T[:, :1]


def forward_kernel(
    count,
    tokens,
    cotangent,
    own_gains,
    qkv_stack,
    out_stack,
    gateup_stack,
    down_stack,
    order,
    ids,
    gains,
    resid,
    normed_group,
    grad_group,
    gateup,
    down,
    features_out,
    qkv_rows_out,
    out_all_out,
    stream_out,
    kv_both_out,
    kv_turned_out,
    lse,
    mixed_group_out,
    shuffle_out,
    key_ids,
    query_ids,
    tokens_group,
    normed,
    weights,
    projected,
    mixed,
    mixed_all,
    bias,
    wide,
    tall,
    gateup_own,
    down_own,
    gain_tiles,
    own_sem,
    ring_send,
    ring_recv,
    head_send,
    head_recv,
    kv_send,
    kv_recv,
    features,
    qkv_rows,
    out_all,
    stream,
    kv_both,
    kv_turned,
    mixed_group,
    shuffle,
    store_sem,
):
    rows = tokens.shape[0]
    group = 4 * rows
    width = features.shape[1]
    heads = width // HEAD_DIM
    head = lax.axis_index("head")
    me = lax.axis_index("seq")
    mate_head = head + 1 - 2 * lax.rem(head, 2)
    across_head = lax.rem(head + 2, 4)
    mate = {"head": mate_head}
    across = {"head": across_head}

    def band(of):
        return pl.ds(pl.multiple_of(of * width, 128), width)

    def chip_columns(of):
        return pl.ds(pl.multiple_of((of // 2) * 2 * width, 128), 2 * width)

    def quarter(ref, i):
        return ref.at[pl.ds(i * rows, rows)]

    copies = []

    def send(index, source, target, where):
        copy = remote(source, target, head_send.at[index], head_recv.at[index], where)
        copy.start()
        copies.append(copy)

    def arrived(index, target, where):
        remote(target, target, head_send.at[index], head_recv.at[index], where).wait_recv()

    def stack_view(ref, columns):
        def view(shard, part):
            first = pl.multiple_of(head * width + (shard // 2) * BLK, 32)
            at = pl.ds(pl.multiple_of(lax.rem(shard, 2) * columns, 128), columns)
            if part is None:
                return ref.at[pl.ds(first, BLK), at]
            return ref.at[pl.ds(pl.multiple_of(first + part * (BLK // 2), 16), BLK // 2), at]

        return view

    def gateup_view(shard, part):
        size = gateup.shape[1]
        if part is None:
            return gateup.at[shard]
        return gateup.at[shard, pl.ds(part * (size // 2), size // 2)]

    def down_view(shard, part):
        if part is None:
            return down.at[shard]
        return down.at[shard, :, pl.ds(part * (BLK // 2), BLK // 2)]

    qkv_view = stack_view(weights, QKV // 2)
    out_view = stack_view(out_all, D // 2)
    gain_view = lambda shard, part: gain_tiles.at[head, shard]
    qkv_ring, out_ring, gateup_ring, down_ring, gain_ring = rings = [
        Ring(count, view, ring_send.at[i], ring_recv.at[i], view is not gain_view)
        for i, view in enumerate((qkv_view, out_view, gateup_view, down_view, gain_view))
    ]

    barrier = pltpu.get_barrier_semaphore()
    for where in (qkv_ring.ahead, qkv_ring.behind, mate, across):
        pl.semaphore_signal(barrier, inc=1, device_id=where, device_id_type=pl.DeviceIdType.MESH)

    @pl.when(me > 0)
    def _():
        pl.semaphore_signal(
            barrier, inc=1, device_id={"seq": me - 1}, device_id_type=pl.DeviceIdType.MESH
        )

    def side_by_side(stack, first):
        size = stack.shape[2]
        blocks = 8
        for c in range(blocks):
            tall[c * size : (c + 1) * size, :] = stack[first + c].T
        return tall[: blocks * size, :].T.astype(low)

    qkv_view(me, None)[...] = side_by_side(qkv_stack, 0)
    gain_tiles[head, me] = own_gains[...]
    pl.semaphore_wait(barrier, 5 - me // (count - 1))
    send(0, tokens, quarter(tokens_group, 2), across)
    send(1, tokens, quarter(tokens_group, 1), mate)
    qkv_ring.start(1)
    gain_ring.start(1)
    for q in range(gateup_own.shape[0] // BLK):
        column = gateup_stack[q * GRID : (q + 1) * GRID].reshape(D, BLK)
        gateup_own[q * BLK : (q + 1) * BLK, :] = column.T.astype(low)
    for m in range(down_own.shape[0]):
        down_own[m] = side_by_side(down_stack, 8 * m)
    own = [
        pltpu.make_async_copy(gateup_own, gateup.at[me], own_sem.at[0]),
        pltpu.make_async_copy(down_own, down.at[me], own_sem.at[1]),
        pltpu.make_async_copy(cotangent, quarter(grad_group, 0), own_sem.at[2]),
    ]
    for copy in own:
        copy.start()
    out_view(me, None)[...] = side_by_side(out_stack, 0)
    for copy in own[:2]:
        copy.wait()

    def pump(step):
        if step > 1:
            gateup_ring.arrive(step - 1)
            down_ring.arrive(step - 1)
        if step <= count // 2:
            gateup_ring.start(step)
            down_ring.start(step)

    pump(1)
    tokens_group[:rows, :] = tokens[...]
    qkv_ring.arrive(1)
    qkv_ring.start(2)
    gain_ring.arrive(1)
    gain_ring.start(2)

    for i in range(4):
        at = turned_row(order[:, i * rows : (i + 1) * rows]).astype(jnp.int32)
        owner = at // rows
        flip = head - 4 * (owner // 2) * (head // 2) - 2 * lax.rem(owner, 2) * lax.rem(head, 2)
        place = (owner + flip) * rows + lax.rem(at, rows)
        shuffle[i * rows : (i + 1) * rows, :] = jnp.where(
            place == lax.broadcasted_iota(jnp.int32, (rows, group), 1), 1.0, 0.0
        ).astype(low)
    query_ids[...] = ids[:, pl.ds(pl.multiple_of(me * group, 128), group)].astype(full)
    before = (me - (me + count - 1) // count) * group
    for i in range(4):
        here = slice(i * rows, (i + 1) * rows)
        at = pl.multiple_of(before + i * rows, 128)
        key_ids[here, :] = jnp.where(me > 0, turned_row(ids[:, pl.ds(at, rows)]), -1.0)
        there = slice(group + i * rows, group + (i + 1) * rows)
        key_ids[there, :] = turned_row(query_ids[:, here])
    for step in range(2, count // 2):
        qkv_ring.arrive(step)
        qkv_ring.start(step + 1)
        gain_ring.arrive(step)
        gain_ring.start(step + 1)
    qkv_ring.arrive(count // 2)

    key_columns = pl.ds(QW, 2 * HEAD_DIM)

    def weight_parts(of, chip_of):
        return [weights.at[band(of), columns] for columns in (chip_columns(chip_of), key_columns)]

    gain_ring.arrive(count // 2)
    send(9, gain_tiles.at[head], gain_tiles.at[head], across)
    send(10, gain_tiles.at[head], gain_tiles.at[head], mate)
    for i, part in enumerate(weight_parts(head, across_head)):
        send(3 + i, part, part, across)
    for i, part in enumerate(weight_parts(head, head)):
        send(7 + i, part, part, mate)
    out_ring.start(1)
    pump(2)
    arrived(0, quarter(tokens_group, 2), across)
    send(2, quarter(tokens_group, 2), quarter(tokens_group, 3), mate)
    qkv_rows[...] = weights[band(head), :]
    arrived(9, gain_tiles.at[across_head], across)
    send(11, gain_tiles.at[across_head], gain_tiles.at[across_head], mate)
    arrived(10, gain_tiles.at[mate_head], mate)
    arrived(11, gain_tiles.at[3 - head], mate)
    size = D // (4 * count)
    for h in range(4):
        for i in range(count):
            at = (h * count + i) * size
            wide[:8, at : at + size] = gain_tiles[h, i][:, :size]
    gains[...] = wide[:2, :D].astype(low).astype(full)

    def norm_rows(i):
        here = pl.ds(i * rows, rows)
        values = tokens_group[here, :].astype(full)
        normed[here, :] = (values * inverse_norm(values) * gains[0:1, :]).astype(low)

    norm_rows(0)
    arrived(1, quarter(tokens_group, 1), mate)
    norm_rows(1)
    out_ring.arrive(1)
    out_ring.start(2)
    norm_rows(2)
    arrived(2, quarter(tokens_group, 3), mate)
    norm_rows(3)
    features[...] = normed[:, band(head)]
    for i, part in enumerate(weight_parts(across_head, head)):
        arrived(3 + i, part, across)
        send(5 + i, part, part, mate)
    out_ring.arrive(2)
    out_ring.start(3)
    for i, part in enumerate(weight_parts(mate_head, head)):
        arrived(7 + i, part, mate)
    send(27, cotangent, quarter(grad_group, 2), across)
    send(28, cotangent, quarter(grad_group, 1), mate)
    for i, part in enumerate(weight_parts(3 - head, head)):
        arrived(5 + i, part, mate)

    key_values = pl.ds(width, 2 * HEAD_DIM)

    def project(columns, target):
        def step(i, carry):
            here = pl.ds(pl.multiple_of(i * rows, rows), rows)
            projected[here, target] = mul(normed[here, :], weights[:, columns], NN).astype(low)
            return carry

        lax.fori_loop(0, 4, step, 0)

        def turn(i, carry):
            here = pl.ds(pl.multiple_of(i * rows, rows), rows)
            stream[here, target] = mul(shuffle[here, :], projected[:, target], NN).astype(low)
            return carry

        lax.fori_loop(0, 4, turn, 0)

    project(key_columns, key_values)
    kv_both[pl.ds(group, group), :] = stream[:, key_values]
    kv_copy = remote(
        kv_both.at[pl.ds(group, group)],
        kv_both.at[pl.ds(0, group)],
        kv_send,
        kv_recv,
        {"seq": lax.rem(me + 1, count)},
    )

    @pl.when(me < count - 1)
    def _():
        kv_copy.start()

    @pl.when(me == 0)
    def _():
        kv_both[pl.ds(0, group), :] = jnp.zeros((group, 2 * HEAD_DIM), low)

    out_ring.arrive(3)
    out_ring.start(4)
    project(band(head), pl.ds(0, width))
    pump(3)
    for i in range(4, 8):
        kv_turned[:, i * rows : (i + 1) * rows] = kv_both[i * rows : (i + 1) * rows, :].T
    out_ring.arrive(4)
    half = width // 2

    def out_part(of, i):
        return out_all.at[pl.ds(pl.multiple_of(of * width + i * half, 64), half)]

    for i in range(2):
        send(12 + i, out_part(head, i), out_part(head, i), across)
    send(16, out_all.at[band(head)], out_all.at[band(head)], mate)

    @pl.when(me > 0)
    def _():
        kv_copy.wait_recv()

    for i in range(4):
        kv_turned[:, i * rows : (i + 1) * rows] = kv_both[i * rows : (i + 1) * rows, :].T
    arrived(27, quarter(grad_group, 2), across)
    send(29, quarter(grad_group, 2), quarter(grad_group, 3), mate)

    def attend_tile(tile, carry):
        start = pl.multiple_of(tile * QUERY_TILE, QUERY_TILE)
        here = pl.ds(start, QUERY_TILE)
        span = pl.ds(start, SPAN)
        shape = (SPAN, QUERY_TILE)
        key = lax.broadcasted_iota(jnp.int32, shape, 0)
        query = lax.broadcasted_iota(jnp.int32, shape, 1)
        same = key_ids[span, :] == query_ids[:, here]
        allowed = same & (key > query) & (key <= query + WINDOW)
        bias[...] = jnp.where(allowed, 0.0, neg_fill)

        def attend_head(j, carry):
            lanes = pl.ds(pl.multiple_of(j * HEAD_DIM, HEAD_DIM), HEAD_DIM)
            scores = mul(kv_both[span, :HEAD_DIM], stream[here, lanes], NT)
            scores = scores * HEAD_DIM ** (-0.5) + bias[...]
            top = jnp.max(scores, axis=0, keepdims=True)
            expo = jnp.exp(scores - top)
            total = jnp.sum(expo, axis=0, keepdims=True)
            out = mul(kv_turned[HEAD_DIM:, span], expo.astype(low), NN) / total
            mixed[here, lanes] = out.T.astype(low)
            lse[j, :, here] = top + jnp.log(total)
            return carry

        return lax.fori_loop(0, heads, attend_head, carry)

    lax.fori_loop(0, group // QUERY_TILE, attend_tile, 0)

    def turn_back(i, carry):
        here = pl.ds(pl.multiple_of(i * rows, rows), rows)
        mixed_group[here, :] = mul(shuffle[:, here], mixed[...], TN).astype(low)
        return carry

    lax.fori_loop(0, 4, turn_back, 0)

    def mixed_part(of, i, size):
        return mixed_all.at[pl.ds(i * size, size), band(of)]

    for i in range(2):
        source = mixed_group.at[pl.ds(i * 2 * rows, 2 * rows)]
        send(17 + i, source, mixed_part(head, 1 - i, 2 * rows), across)
    for i in range(4):
        send(19 + i, quarter(mixed_group, i), mixed_part(head, i ^ 1, rows), mate)
    mixed_all[:, band(head)] = mixed_group[...]
    for i in range(2):
        arrived(12 + i, out_part(across_head, i), across)
        send(14 + i, out_part(across_head, i), out_part(across_head, i), mate)
    pump(4)
    arrived(16, out_all.at[band(mate_head)], mate)
    for i in range(2):
        arrived(14 + i, out_part(3 - head, i), mate)
    for i in range(4):
        arrived(19 + i, mixed_part(mate_head, i ^ 1, rows), mate)
    for i in range(2):
        arrived(17 + i, mixed_part(across_head, 1 - i, 2 * rows), across)
        for j in (2 - 2 * i, 3 - 2 * i):
            part = mixed_part(across_head, j, rows)
            send(23 + j, part, mixed_part(across_head, j ^ 1, rows), mate)
    for j in range(4):
        arrived(23 + j, mixed_part(3 - head, j ^ 1, rows), mate)

    stores = [
        pltpu.make_async_copy(source, target, store_sem.at[i])
        for i, (source, target) in enumerate(
            (
                (features, features_out),
                (qkv_rows, qkv_rows_out),
                (out_all, out_all_out),
                (stream, stream_out),
                (kv_both, kv_both_out),
                (kv_turned, kv_turned_out),
                (mixed_group, mixed_group_out),
                (shuffle, shuffle_out),
            )
        )
    ]
    for copy in stores:
        copy.start()

    def second(i, carry):
        here = pl.ds(pl.multiple_of((3 - i) * rows, rows), rows)
        resid[...] = tokens_group[here, :].astype(full) + mul(mixed_all[here, :], out_all[...], NN)
        values = resid[...]
        normed_group[here, :] = (values * inverse_norm(values) * gains[1:2, :]).astype(low)
        return carry

    lax.fori_loop(0, 4, second, 0)
    arrived(28, quarter(grad_group, 1), mate)
    arrived(29, quarter(grad_group, 3), mate)
    pump(5)
    own[2].wait()
    for copy in stores:
        copy.wait()
    for ring in rings:
        ring.finish()
    for copy in copies:
        copy.wait_send()

    @pl.when(me < count - 1)
    def _():
        kv_copy.wait_send()


def forward_section(tokens, cotangent, gains, stacks, order, ids, count):
    rows = tokens.shape[0]
    group = 4 * rows
    width = QW // 4
    steps = count // 2
    gateup_rows = stacks[2].shape[0] // GRID * BLK
    down_parts = stacks[3].shape[0] // 8
    vmem = pl.BlockSpec(memory_space=pltpu.VMEM)
    hbm = pl.BlockSpec(memory_space=pl.ANY)
    outs = [
        ((2, D), full, vmem),
        ((rows, D), full, vmem),
        ((group, D), low, vmem),
        ((group, D), low, hbm),
        ((count, gateup_rows, D), low, hbm),
        ((count, down_parts, BLK, D // 2), low, hbm),
        ((group, width), low, hbm),
        ((width, QKV), low, hbm),
        ((D, D), low, hbm),
        ((group, width + 2 * HEAD_DIM), low, hbm),
        ((2 * group, 2 * HEAD_DIM), low, hbm),
        ((2 * HEAD_DIM, 2 * group), low, hbm),
        ((width // HEAD_DIM, 1, group), full, vmem),
        ((group, width), low, hbm),
        ((group, group), low, hbm),
        ((2 * group, 1), full, vmem),
        ((1, group), full, vmem),
    ]
    dma = pltpu.SemaphoreType.DMA
    return pl.pallas_call(
        functools.partial(forward_kernel, count),
        in_specs=[vmem] * 9,
        out_specs=[spec for _, _, spec in outs],
        out_shape=[jax.ShapeDtypeStruct(shape, kind) for shape, kind, _ in outs],
        scratch_shapes=[
            pltpu.VMEM((group, D), low),
            pltpu.VMEM((group, D), low),
            pltpu.VMEM((D, QKV), low),
            pltpu.VMEM((group, width + 2 * HEAD_DIM), low),
            pltpu.VMEM((group, width), low),
            pltpu.VMEM((group, D), low),
            pltpu.VMEM((SPAN, QUERY_TILE), full),
            pltpu.VMEM((8, D), full),
            pltpu.VMEM((QKV // 2, BLK), full),
            pltpu.VMEM((gateup_rows, D), low),
            pltpu.VMEM((down_parts, BLK, D // 2), low),
            pltpu.VMEM((4, count, 8, 128), full),
            dma((3,)),
            dma((5, 2, steps)),
            dma((5, 2, steps)),
            dma((30,)),
            dma((30,)),
            dma,
            dma,
            *[pltpu.VMEM(outs[i][0], low) for i in (6, 7, 8, 9, 10, 11, 13, 14)],
            dma((8,)),
        ],
        compiler_params=pltpu.CompilerParams(
            collective_id=0, has_side_effects=True, vmem_limit_bytes=58 * 1024 * 1024
        ),
        name="forward_section",
    )(tokens, cotangent, gains, *stacks, order, ids)


class SumRing:
    def __init__(self, count, view, first, buffers, send, recv):
        self.ring = Ring(count, None, None, None)
        self.steps = count // 2
        self.view = view
        self.first = first
        self.buffers = buffers
        self.rows = buffers.shape[2]
        self.send = send
        self.recv = recv
        self.copies = []

    def where(self, way):
        return self.ring.behind if way else self.ring.ahead

    def half(self, way):
        return self.buffers.at[way, 0, pl.ds(way * (self.rows // 2), self.rows // 2)]

    def copy(self, way, step, source, target):
        return remote(source, target, self.send.at[way, step], self.recv.at[way, step], self.where(way))

    def start(self):
        shard = self.ring.shard(self.steps)
        for way in range(2):
            copy = self.copy(way, 0, self.first(shard, way), self.half(way))
            copy.start()
            self.copies.append(copy)

    def arrived(self, way, step):
        target = self.buffers.at[way, step] if step else self.half(way)
        self.copy(way, step, target, target).wait_recv()

    def step(self, step):
        block = 48
        for way in range(2):
            self.arrived(way, step - 1)
            offset = self.steps - step
            local = self.view(self.ring.shard(-offset if way else offset))
            buffer = self.buffers.at[way, step - 1]

            def add(i, carry):
                here = pl.ds(pl.multiple_of(i * block, 16), block)
                buffer[here, :] = (local[here, :].astype(full) + buffer[here, :].astype(full)).astype(low)
                return carry

            def keep(i, carry):
                here = pl.ds(pl.multiple_of(i * block, 16), block)
                buffer[here, :] = local[here, :]
                return carry

            blocks = self.rows // block
            if step > 1:
                lax.fori_loop(0, blocks, add, 0)
            else:
                lax.fori_loop(way * (blocks // 2), (way + 1) * (blocks // 2), add, 0)
                lax.fori_loop((1 - way) * (blocks // 2), (2 - way) * (blocks // 2), keep, 0)
            copy = self.copy(way, step, buffer, self.buffers.at[way, step])
            copy.start()
            self.copies.append(copy)

    def finish(self, out):
        block = 48
        last = self.steps - 1
        for way in range(2):
            self.arrived(way, last)
        local = self.view(self.ring.shard(0))

        def add(i, carry):
            here = pl.ds(pl.multiple_of(i * block, 16), block)
            out[here, :] = (
                local[here, :].astype(full)
                + self.buffers[0, last, here, :].astype(full)
                + self.buffers[1, last, here, :].astype(full)
            )
            return carry

        lax.fori_loop(0, self.rows // block, add, 0)
        for copy in self.copies:
            copy.wait_send()


class StagedSumRing(SumRing):
    def __init__(self, count, parts, buffers, held, terms, load, send, recv):
        size = parts.shape[1] // 2
        first = lambda shard, part: parts.at[shard, pl.ds(part * size, size)]
        super().__init__(count, None, first, buffers, send, recv)
        self.parts = parts
        self.held = held
        self.terms = terms
        self.load = load
        self.last = [None, None]

    def fetch(self, way, offset):
        shard = self.ring.shard(-offset if way else offset)
        copy = pltpu.make_async_copy(
            self.parts.at[shard], self.terms.at[way], self.load.at[1, way]
        )
        copy.start()
        return copy

    def start(self):
        super().start()
        self.fetched = [self.fetch(way, self.steps - 1) for way in range(2)]

    def take(self, way, step):
        self.arrived(way, step)
        if self.last[way] is not None:
            self.last[way].wait_send()
        source, target = self.buffers.at[way, step], self.held.at[way]
        if step == 0:
            half = pl.ds(way * (self.rows // 2), self.rows // 2)
            source, target = self.half(way), self.held.at[way, half]
        copy = pltpu.make_async_copy(source, target, self.load.at[0, way])
        copy.start()
        return copy

    def step(self, step):
        block = 48
        taken = [self.take(way, step - 1) for way in range(2)]
        for way in range(2):
            taken[way].wait()
            self.fetched[way].wait()
            held, terms = self.held.at[way], self.terms.at[way]

            def add(i, carry):
                here = pl.ds(pl.multiple_of(i * block, 16), block)
                held[here, :] = (terms[here, :].astype(full) + held[here, :].astype(full)).astype(low)
                return carry

            def keep(i, carry):
                here = pl.ds(pl.multiple_of(i * block, 16), block)
                held[here, :] = terms[here, :]
                return carry

            blocks = self.rows // block
            if step > 1:
                lax.fori_loop(0, blocks, add, 0)
            else:
                lax.fori_loop(way * (blocks // 2), (way + 1) * (blocks // 2), add, 0)
                lax.fori_loop((1 - way) * (blocks // 2), (2 - way) * (blocks // 2), keep, 0)
            self.last[way] = self.copy(way, step, held, self.buffers.at[way, step])
            self.last[way].start()
            if step < self.steps - 1 or way == 0:
                self.fetched[way] = self.fetch(way, self.steps - 1 - step)

    def finish(self, out):
        block = 48
        taken = [self.take(way, self.steps - 1) for way in range(2)]
        for copy in taken:
            copy.wait()
        self.fetched[0].wait()

        def add(i, carry):
            here = pl.ds(pl.multiple_of(i * block, 16), block)
            out[here, :] = (
                self.terms[0, here, :].astype(full)
                + self.held[0, here, :].astype(full)
                + self.held[1, here, :].astype(full)
            )
            return carry

        lax.fori_loop(0, self.rows // block, add, 0)
        for copy in self.copies:
            copy.wait_send()


def backward_kernel(
    count,
    tokens,
    cotangent,
    gains,
    resid,
    normed_part,
    ffn_part,
    gateup_parts,
    down_parts,
    features_in,
    qkv_rows_in,
    out_all_in,
    stream_in,
    kv_both_in,
    kv_turned_in,
    lse,
    mixed_group_in,
    shuffle_in,
    key_ids,
    query_ids,
    block_out,
    input_grad,
    gain_grads,
    gateup_grad,
    down_grad,
    qkv_grad,
    out_grad,
    gateup_sums,
    down_sums,
    gateup_held,
    gateup_terms,
    down_held,
    down_terms,
    part_quarter,
    qkv_local,
    out_local,
    qkv_sums,
    out_sums,
    sum_out,
    sum_in,
    proj_group,
    turned_out,
    turned_grad,
    grad_stream,
    kv_total,
    kv_out,
    kv_in,
    stream_grad,
    kv_mate,
    all_grad,
    normed_grad,
    bias,
    load_sem,
    part_sem,
    ring_send,
    ring_recv,
    head_send,
    head_recv,
    kv_send,
    kv_recv,
    features,
    qkv_rows,
    out_all,
    stream,
    kv_both,
    kv_turned,
    mixed_group,
    shuffle,
    take_sem,
):
    rows = tokens.shape[0]
    group = 4 * rows
    width = features.shape[1]
    heads = width // HEAD_DIM
    scale = HEAD_DIM ** (-0.5)
    query_grad = turned_grad
    feature_grad = grad_stream
    head = lax.axis_index("head")
    me = lax.axis_index("seq")
    mate_head = head + 1 - 2 * lax.rem(head, 2)
    across_head = lax.rem(head + 2, 4)
    mate = {"head": mate_head}
    across = {"head": across_head}
    corner = {"head": 3 - head}

    def lanes(of):
        return pl.ds(pl.multiple_of(of * width, 128), width)

    def quarter(i):
        return pl.ds(i * rows, rows)

    copies = []

    def send(index, source, target, where):
        copy = remote(source, target, head_send.at[index], head_recv.at[index], where)
        copy.start()
        copies.append(copy)

    def arrived(index, target, where):
        remote(target, target, head_send.at[index], head_recv.at[index], where).wait_recv()

    def shard_view(ref, columns):
        def view(shard, part=None):
            first = pl.multiple_of((shard // 2) * BLK, 32)
            at = pl.ds(pl.multiple_of(lax.rem(shard, 2) * columns, 128), columns)
            if part is None:
                return ref.at[pl.ds(first, BLK), at]
            return ref.at[pl.ds(pl.multiple_of(first + part * (BLK // 2), 16), BLK // 2), at]

        return view

    qkv_view = shard_view(qkv_local, QKV // 2)
    out_view = shard_view(out_local, D // 2)
    gateup_ring = StagedSumRing(
        count,
        gateup_parts,
        gateup_sums,
        gateup_held,
        gateup_terms,
        load_sem.at[0],
        ring_send.at[0],
        ring_recv.at[0],
    )
    down_ring = StagedSumRing(
        count,
        down_parts,
        down_sums,
        down_held,
        down_terms,
        load_sem.at[1],
        ring_send.at[1],
        ring_recv.at[1],
    )
    qkv_ring = SumRing(count, qkv_view, qkv_view, qkv_sums, ring_send.at[2], ring_recv.at[2])
    out_ring = SumRing(count, out_view, out_view, out_sums, ring_send.at[3], ring_recv.at[3])

    barrier = pltpu.get_barrier_semaphore()
    for where in (gateup_ring.where(0), gateup_ring.where(1), mate, across, corner):
        pl.semaphore_signal(barrier, inc=1, device_id=where, device_id_type=pl.DeviceIdType.MESH)

    @pl.when(me < count - 1)
    def _():
        pl.semaphore_signal(
            barrier, inc=1, device_id={"seq": me + 1}, device_id_type=pl.DeviceIdType.MESH
        )

    pl.semaphore_wait(barrier, 5 + (me + count - 1) // count)

    def fetch(value, i):
        copy = pltpu.make_async_copy(value.at[quarter(i)], part_quarter, part_sem)
        copy.start()
        copy.wait()
        return part_quarter[...].astype(full)

    def sum_first(base, slot, value):
        send(base, value.at[quarter(3)], sum_in.at[slot], mate)
        send(base + 1, value.at[quarter(1)], sum_in.at[slot + 1], mate)

    def sum_across(base, slot, value):
        own = fetch(value, 2)
        arrived(base, sum_in.at[slot], mate)
        sum_out[slot // 3] = (own + sum_in[slot].astype(full)).astype(low)
        send(base + 2, sum_out.at[slot // 3], sum_in.at[slot + 2], across)

    def sum_last(base, slot, value):
        own = fetch(value, 0)
        arrived(base + 1, sum_in.at[slot + 1], mate)
        own = own + sum_in[slot + 1].astype(full)
        arrived(base + 2, sum_in.at[slot + 2], across)
        return own + sum_in[slot + 2].astype(full)

    takes = [
        pltpu.make_async_copy(source, target, take_sem.at[i])
        for i, (source, target) in enumerate(
            (
                (features_in, features),
                (qkv_rows_in, qkv_rows),
                (out_all_in, out_all),
                (stream_in, stream),
                (kv_both_in, kv_both),
                (kv_turned_in, kv_turned),
                (mixed_group_in, mixed_group),
                (shuffle_in, shuffle),
            )
        )
    ]
    sum_first(0, 0, normed_part)
    for copy in takes:
        copy.start()
    gateup_ring.start()
    down_ring.start()
    sum_across(0, 0, normed_part)
    sum_first(3, 3, ffn_part)

    normed_two_grad = sum_last(0, 0, normed_part)
    values = resid[...]
    inverse = inverse_norm(values)
    gain_grads[1:2, :] = jnp.sum(normed_two_grad * values * inverse, axis=0, keepdims=True)
    input_grad[...] = cotangent[...].astype(full) + norm_back(
        values, inverse, gains[1:2, :], normed_two_grad
    )
    proj_group[quarter(0), :] = input_grad[...].astype(low)

    for copy in takes:
        copy.wait()

    def back_projection(of):
        weights = out_all[pl.ds(pl.multiple_of(of * width, 128), width), :]
        return mul(proj_group[quarter(0), :], weights, NT).astype(low)

    for j, of, where in ((2, across_head, across), (3, 3 - head, corner), (1, mate_head, mate)):
        turned_out[j - 1] = back_projection(of)
        send(31 + j, turned_out.at[j - 1], turned_grad.at[quarter(j)], where)
    send(6, proj_group.at[quarter(0)], proj_group.at[quarter(2)], across)
    send(7, proj_group.at[quarter(0)], proj_group.at[quarter(1)], mate)
    turned_grad[quarter(0), :] = back_projection(head)
    gateup_ring.step(1)
    down_ring.step(1)
    for j, where in ((1, mate), (2, across), (3, corner)):
        arrived(31 + j, turned_grad.at[quarter(j)], where)

    def turn(i, carry):
        here = pl.ds(pl.multiple_of(i * rows, rows), rows)
        grad_stream[here, :] = mul(shuffle[here, :], turned_grad[...], NN).astype(low)
        return carry

    lax.fori_loop(0, 4, turn, 0)

    kv_total[...] = jnp.zeros_like(kv_total)

    def back_tile(tile, carry):
        start = pl.multiple_of(tile * QUERY_TILE, QUERY_TILE)
        here = pl.ds(start, QUERY_TILE)
        span = pl.ds(start, SPAN)
        shape = (SPAN, QUERY_TILE)
        key = lax.broadcasted_iota(jnp.int32, shape, 0)
        query = lax.broadcasted_iota(jnp.int32, shape, 1)
        same = key_ids[span, :] == query_ids[:, here]
        allowed = same & (key > query) & (key <= query + WINDOW)
        bias[...] = jnp.where(allowed, 0.0, neg_fill)

        def back_head(j, carry):
            at = pl.ds(pl.multiple_of(j * HEAD_DIM, HEAD_DIM), HEAD_DIM)
            queries = stream[here, at]
            grads = grad_stream[here, at]
            scores = mul(kv_both[span, :HEAD_DIM], queries, NT) * scale + bias[...]
            probs = jnp.exp(scores - lse[j, :, here])
            prob_grad = mul(kv_both[span, HEAD_DIM:], grads, NT)
            delta = jnp.sum(probs * prob_grad, axis=0, keepdims=True)
            score_grad = (probs * (prob_grad - delta)).astype(low)
            turned = mul(kv_turned[:HEAD_DIM, span], score_grad, NN) * scale
            query_grad[here, at] = turned.T.astype(low)
            kv_total[span, :HEAD_DIM] += mul(score_grad, queries, NN) * scale
            kv_total[span, HEAD_DIM:] += mul(probs.astype(low), grads, NN)
            return carry

        return lax.fori_loop(0, heads, back_head, carry)

    lax.fori_loop(0, group // QUERY_TILE, back_tile, 0)
    kv_out[...] = kv_total[:group, :].astype(low)
    kv_copy = remote(kv_out, kv_in, kv_send, kv_recv, {"seq": lax.rem(me + count - 1, count)})

    @pl.when(me > 0)
    def _():
        kv_copy.start()

    def turn_back(i, carry):
        here = pl.ds(pl.multiple_of(i * rows, rows), rows)
        all_grad[here, lanes(head)] = mul(shuffle[:, here], query_grad[...], TN).astype(low)
        return carry

    lax.fori_loop(0, 4, turn_back, 0)

    def swapped(index, ref, columns, distance, where):
        for i in range(4):
            send(
                index + i,
                ref.at[quarter(i), columns],
                ref.at[quarter(i ^ distance), columns],
                where,
            )

    def swapped_arrived(index, ref, columns, distance, where):
        for i in range(4):
            arrived(index + i, ref.at[quarter(i ^ distance), columns], where)

    swapped(9, all_grad, lanes(head), 2, across)
    swapped(13, all_grad, lanes(head), 1, mate)
    arrived(6, proj_group.at[quarter(2)], across)
    send(8, proj_group.at[quarter(2)], proj_group.at[quarter(3)], mate)
    gateup_ring.step(2)
    down_ring.step(2)
    sum_across(3, 3, ffn_part)
    arrived(7, proj_group.at[quarter(1)], mate)
    arrived(8, proj_group.at[quarter(3)], mate)
    for i in range(3):
        at = slice(i * (D // 3), (i + 1) * (D // 3))
        out_local[:, at] = mul(mixed_group[...], proj_group[:, at], TN).astype(low)
    out_ring.start()

    @pl.when(me < count - 1)
    def _():
        kv_copy.wait_recv()
        kv_total[pl.ds(group, group), :] += kv_in[...].astype(full)

    stream_grad[...] = kv_total[pl.ds(group, group), :].astype(low)

    def turn_keys(i, carry):
        here = pl.ds(pl.multiple_of(i * rows, rows), rows)
        kv_mate[0, here, :] = mul(shuffle[:, here], stream_grad[...], TN).astype(low)
        return carry

    lax.fori_loop(0, 4, turn_keys, 0)
    for i in range(4):
        send(17 + i, kv_mate.at[0, quarter(i)], kv_mate.at[1, quarter(i ^ 1)], mate)
    for i in range(4):
        arrived(17 + i, kv_mate.at[1, quarter(i ^ 1)], mate)
    kv_total[pl.ds(0, group), :] = kv_mate[0].astype(full) + kv_mate[1].astype(full)
    kv_mate[2] = kv_total[pl.ds(0, group), :].astype(low)
    mine = pl.ds(pl.multiple_of(lax.rem(head, 2) * HEAD_DIM, HEAD_DIM), HEAD_DIM)
    of_mine = pl.ds(pl.multiple_of(QW + lax.rem(head, 2) * HEAD_DIM, HEAD_DIM), HEAD_DIM)
    of_mate = pl.ds(pl.multiple_of(QW + lax.rem(mate_head, 2) * HEAD_DIM, HEAD_DIM), HEAD_DIM)
    for i in range(4):
        send(21 + i, kv_mate.at[2, quarter(i), mine], kv_mate.at[3, quarter(i ^ 2), mine], across)
    out_ring.step(1)
    gateup_ring.step(3)
    swapped_arrived(9, all_grad, lanes(across_head), 2, across)
    swapped(25, all_grad, lanes(across_head), 1, mate)
    swapped_arrived(13, all_grad, lanes(mate_head), 1, mate)
    for i in range(4):
        arrived(21 + i, kv_mate.at[3, quarter(i ^ 2), mine], across)
    all_grad[:, of_mine] = (
        kv_total[pl.ds(0, group), mine] + kv_mate[3, :, mine].astype(full)
    ).astype(low)
    swapped(35, all_grad, of_mine, 1, mate)
    swapped_arrived(35, all_grad, of_mate, 1, mate)
    swapped_arrived(25, all_grad, lanes(3 - head), 1, mate)

    for i in range(2):
        at = slice(i * (QKV // 2), (i + 1) * (QKV // 2))
        qkv_local[:, at] = mul(features[...], all_grad[:, at], TN).astype(low)
    qkv_ring.start()
    down_ring.step(3)
    for i, where in ((2, across), (3, corner), (1, mate)):
        feature_grad[quarter(i), :] = mul(all_grad[quarter(i), :], qkv_rows[...], NT).astype(low)
        send(28 + i, feature_grad.at[quarter(i)], normed_grad.at[:, lanes(head)], where)
    normed_grad[:, lanes(head)] = mul(all_grad[quarter(0), :], qkv_rows[...], NT).astype(low)
    qkv_ring.step(1)
    out_ring.step(2)
    block_out[...] = (resid[...] + sum_last(3, 3, ffn_part)).astype(low)
    for i, where, of in ((2, across, across_head), (3, corner, 3 - head), (1, mate, mate_head)):
        arrived(28 + i, normed_grad.at[:, lanes(of)], where)
    qkv_ring.step(2)
    normed_one_grad = normed_grad[...].astype(full)
    values = tokens[...].astype(full)
    inverse = inverse_norm(values)
    gain_grads[0:1, :] = jnp.sum(normed_one_grad * values * inverse, axis=0, keepdims=True)
    input_grad[...] += norm_back(values, inverse, gains[0:1, :], normed_one_grad)
    qkv_ring.step(3)
    out_ring.step(3)
    gateup_ring.finish(gateup_grad)
    down_ring.finish(down_grad)
    out_ring.finish(out_grad)
    qkv_ring.finish(qkv_grad)
    for copy in copies:
        copy.wait_send()

    @pl.when(me > 0)
    def _():
        kv_copy.wait_send()


def backward_section(count, *values):
    (tokens, cotangent, gains, resid, normed_part, ffn_part, gateup_parts, down_parts) = values[:8]
    rows = tokens.shape[0]
    group = 4 * rows
    width = QW // 4
    steps = count // 2
    vmem = pl.BlockSpec(memory_space=pltpu.VMEM)
    hbm = pl.BlockSpec(memory_space=pl.ANY)
    shard = gateup_parts.shape[1:]
    down_shard = down_parts.shape[1:]
    outs = [
        ((rows, D), low),
        ((rows, D), full),
        ((2, D), full),
        (shard, full),
        (down_shard, full),
        ((BLK, QKV // 2), full),
        ((BLK, D // 2), full),
        ((2, steps) + shard, low),
        ((2, steps) + down_shard, low),
    ]
    dma = pltpu.SemaphoreType.DMA
    return pl.pallas_call(
        functools.partial(backward_kernel, count),
        in_specs=[vmem] * 4 + [hbm] * 10 + [vmem] + [hbm] * 2 + [vmem] * 2,
        out_specs=[vmem] * 7 + [hbm] * 2,
        out_shape=[jax.ShapeDtypeStruct(shape, kind) for shape, kind in outs],
        scratch_shapes=[
            pltpu.VMEM((2,) + shard, low),
            pltpu.VMEM((2,) + shard, low),
            pltpu.VMEM((2,) + down_shard, low),
            pltpu.VMEM((2,) + down_shard, low),
            pltpu.VMEM((rows, D), low),
            pltpu.VMEM((width, QKV), low),
            pltpu.VMEM((width, D), low),
            pltpu.VMEM((2, steps, BLK, QKV // 2), low),
            pltpu.VMEM((2, steps, BLK, D // 2), low),
            pltpu.VMEM((2, rows, D), low),
            pltpu.VMEM((6, rows, D), low),
            pltpu.VMEM((group, D), low),
            pltpu.VMEM((3, rows, width), low),
            pltpu.VMEM((group, width), low),
            pltpu.VMEM((group, width), low),
            pltpu.VMEM((2 * group, 2 * HEAD_DIM), full),
            pltpu.VMEM((group, 2 * HEAD_DIM), low),
            pltpu.VMEM((group, 2 * HEAD_DIM), low),
            pltpu.VMEM((group, 2 * HEAD_DIM), low),
            pltpu.VMEM((4, group, 2 * HEAD_DIM), low),
            pltpu.VMEM((group, QKV), low),
            pltpu.VMEM((rows, D), low),
            pltpu.VMEM((SPAN, QUERY_TILE), full),
            dma((2, 2, 2)),
            dma,
            dma((4, 2, steps)),
            dma((4, 2, steps)),
            dma((39,)),
            dma((39,)),
            dma,
            dma,
            *[pltpu.VMEM(values[i].shape, low) for i in (8, 9, 10, 11, 12, 13, 15, 16)],
            dma((8,)),
        ],
        compiler_params=pltpu.CompilerParams(
            collective_id=1, has_side_effects=True, vmem_limit_bytes=63 * 1024 * 1024
        ),
        name="backward_section",
    )(*values)


def ffn_kernel(
    normed, cotangent, gateup, down, hidden, gate_up_grad, normed_part, ffn_part, normed_sum, ffn_sum
):
    units = down.shape[0]
    tile = next(u for u in (6, 4, 3, 2, 1) if units % u == 0)
    size = normed.shape[0]
    half = D // 2
    root = (2.0 / 3.141592653589793) ** 0.5

    def step(c, carry):
        here = pl.ds(pl.multiple_of(c * tile * BLK, 32), tile * BLK)
        pair = pl.ds(pl.multiple_of(c * tile * 2 * BLK, 64), 2 * tile * BLK)
        weights = gateup[pair, :]
        parts = [down[pl.ds(c * tile, tile), i].reshape(tile * BLK, half) for i in range(2)]
        both = mul(weights, normed[...], NT).reshape(tile, 2, BLK, size)
        gate = both[:, 0].reshape(tile * BLK, size)
        upper = both[:, 1].reshape(tile * BLK, size)
        grad = mul(parts[0], cotangent[:, :half], NT) + mul(parts[1], cotangent[:, half:], NT)
        square = gate * gate
        bent = jnp.tanh(root * gate * (1.0 + 0.044715 * square))
        share = 0.5 * (1.0 + bent)
        active = gate * share
        slope = share + 0.5 * gate * (1.0 - bent * bent) * (root * (1.0 + 0.134145 * square))
        units_out = (active * upper).astype(low)
        grads = [(grad * upper * slope).astype(low), (grad * active).astype(low)]
        grads = [g.reshape(tile, 1, BLK, size) for g in grads]
        grads = jnp.concatenate(grads, axis=1).reshape(2 * tile * BLK, size)
        hidden[here, :] = units_out
        gate_up_grad[pair, :] = grads
        first = c == 0
        term = mul(grads, weights, TN)
        terms = [mul(units_out, part, TN) for part in parts]

        @pl.when(first)
        def _():
            normed_sum[...] = term
            ffn_sum[:, :half] = terms[0]
            ffn_sum[:, half:] = terms[1]

        @pl.when(jnp.logical_not(first))
        def _():
            normed_sum[...] += term
            ffn_sum[:, :half] += terms[0]
            ffn_sum[:, half:] += terms[1]

        return carry

    lax.fori_loop(0, units // tile, step, 0, unroll=True)
    normed_part[...] = normed_sum[...].astype(low)
    ffn_part[...] = ffn_sum[...].astype(low)


def feed_forward(normed, cotangent, gateup, down):
    group = normed.shape[0]
    units = down.shape[0]
    size = min(512, group)
    rows = pl.BlockSpec((size, D), lambda t: (t, 0))
    once = pl.Buffered(1)
    return pl.pallas_call(
        ffn_kernel,
        grid=(group // size,),
        in_specs=[
            rows,
            rows,
            pl.BlockSpec(gateup.shape, lambda t: (0, 0), pipeline_mode=once),
            pl.BlockSpec(down.shape, lambda t: (0, 0, 0, 0), pipeline_mode=once),
        ],
        out_specs=[
            pl.BlockSpec((units * BLK, size), lambda t: (0, t)),
            pl.BlockSpec((2 * units * BLK, size), lambda t: (0, t)),
            rows,
            rows,
        ],
        out_shape=[
            jax.ShapeDtypeStruct((units * BLK, group), low),
            jax.ShapeDtypeStruct((2 * units * BLK, group), low),
            jax.ShapeDtypeStruct((group, D), low),
            jax.ShapeDtypeStruct((group, D), low),
        ],
        scratch_shapes=[pltpu.VMEM((size, D), full), pltpu.VMEM((size, D), full)],
        compiler_params=pltpu.CompilerParams(vmem_limit_bytes=58 * 1024 * 1024),
        cost_estimate=pl.CostEstimate(
            flops=12 * units * BLK * group * D,
            bytes_accessed=40 << 20,
            transcendentals=units * BLK * group,
        ),
        name="feed_forward",
    )(normed, cotangent, gateup, down)


def update_kernel(
    rate, turned, w_ref, g_ref, l_ref, r_ref, lr_ref, rr_ref, ln_ref, rn_ref, wn_ref
):
    count, rows, columns = w_ref.shape
    blocks = g_ref[...].T.reshape(count, g_ref.shape[1] // count, g_ref.shape[0])
    for b in range(count):
        grad = blocks[b]
        other = grad.T
        if not turned:
            grad, other = other, grad
        square = jnp.sum(jnp.sum(grad * grad, axis=1, keepdims=True), axis=0, keepdims=True)
        square = square * (1.0 / (rows * columns)) + stat_eps
        grad = grad.astype(low)
        other = other.astype(low)
        ln_ref[b] = 0.5 * l_ref[b] + mul(grad, other, NN) * (0.5 / (columns * square))
        rn_ref[b] = 0.5 * r_ref[b] + mul(other, grad, NN) * (0.5 / (rows * square))
        step = mul(lr_ref[b].astype(low), grad, NN).astype(low)
        step = mul(step, rr_ref[b].astype(low), NN)
        wn_ref[b] = w_ref[b] - step * (rate * lax.rsqrt(square))


def update(weight, grad, left, right, left_root, right_root, rate, turned=False):
    count, rows, columns = weight.shape
    if grad.ndim == 3:
        grad = grad.transpose(1, 0, 2).reshape(rows, count * columns)
    height = columns if turned else rows
    batch = count // (grad.shape[0] // height)
    spec = lambda i, j: pl.BlockSpec((batch, i, j), lambda b: (b, 0, 0))
    return pl.pallas_call(
        functools.partial(update_kernel, rate, turned),
        grid=(count // batch,),
        in_specs=[
            spec(rows, columns),
            pl.BlockSpec((height, grad.shape[1]), lambda b: (b, 0)),
            spec(rows, rows),
            spec(columns, columns),
            spec(rows, rows),
            spec(columns, columns),
        ],
        out_specs=[spec(rows, rows), spec(columns, columns), spec(rows, columns)],
        out_shape=[
            jax.ShapeDtypeStruct(left.shape, full),
            jax.ShapeDtypeStruct(right.shape, full),
            jax.ShapeDtypeStruct(weight.shape, full),
        ],
        compiler_params=pltpu.CompilerParams(vmem_limit_bytes=58 * 1024 * 1024),
        cost_estimate=pl.CostEstimate(
            flops=16 * count * 256 * 256 * 128,
            bytes_accessed=36 * count * rows * 128,
            transcendentals=0,
        ),
        name="update",
    )(weight, grad, left, right, left_root, right_root)


def norm_back(values, inverse, gain, grad):
    scaled = gain * grad
    mean = jnp.mean(values * scaled, axis=-1, keepdims=True)
    return inverse * scaled - values * (inverse * inverse * inverse * mean)


def inverse_norm(values):
    return lax.rsqrt(jnp.mean(values * values, axis=-1, keepdims=True) + norm_eps)


def forward_steps(tokens, cotangent, attn_gain, ffn_gain, stacks, token_order, sequence_ids):
    qkv_stack, out_stack, gateup_stack, down_stack = stacks
    row_count = tokens.shape[0]
    head_count = lax.axis_size("head")
    seq_count = lax.axis_size("seq")
    group = row_count * head_count
    head_index = lax.axis_index("head")
    local_width = QW // head_count
    seq_index = lax.axis_index("seq")
    gains = jnp.concatenate([attn_gain, ffn_gain]).astype(low).astype(full)[None]
    gains = lax.all_to_all(
        jnp.broadcast_to(gains, (head_count * seq_count, gains.shape[1])),
        ("head", "seq"),
        split_axis=0,
        concat_axis=0,
        tiled=True,
    )
    own_gains = attn_gain.shape[0]
    gain_one = gains[:, :own_gains].reshape(1, D)
    gain_two = gains[:, own_gains:].reshape(1, D)


    ids_own = lax.dynamic_slice_in_dim(sequence_ids, seq_index * group, group, 0)
    ids_before = lax.dynamic_slice_in_dim(
        sequence_ids, jnp.maximum(seq_index - 1, 0) * group, group, 0
    )
    ids_before = jnp.where(seq_index > 0, ids_before, -1)
    key_ids = jnp.concatenate([ids_before, ids_own])[:, None]
    query_ids = ids_own[None, :]
    qkv_rows = joined_halves(gather_rows(qkv_stack, 8, to_columns))
    out_rows = joined_halves(gather_rows(out_stack, 8, to_columns))
    gateup = gather_rows(gateup_stack, 16, to_units)
    down = gather_rows(down_stack, 8, to_columns)
    tokens_float = tokens.astype(full)
    normed_one = (tokens_float * inverse_norm(tokens_float) * gain_one).astype(low)
    normed_one_group = jnp.concatenate(head_gather(normed_one))
    feature_start = head_index * local_width
    features = lax.dynamic_slice_in_dim(normed_one_group, feature_start, local_width, 1)
    weights = in_order(head_gather(qkv_rows), 0)
    weights = jnp.concatenate(
        [lax.dynamic_slice_in_dim(weights, feature_start, local_width, 1), weights[:, QW:]], axis=1
    )
    projected = mul(normed_one_group, weights, NN, low)
    buffer_rows = ((token_order // row_count) ^ head_index) * row_count + token_order % row_count
    shuffle = (
        buffer_rows[:, None] == lax.broadcasted_iota(jnp.int32, (group, group), 1)
    ).astype(low)
    stream = mul(shuffle, projected, NN, low)
    kv_stream = stream[:, local_width:]
    kv_before = lax.ppermute(kv_stream, "seq", [(i, i + 1) for i in range(seq_count - 1)])
    kv_both = jnp.concatenate([kv_before, kv_stream], axis=0)
    kv_turned = kv_both.T
    mixed_stream, lse = attend(stream[:, :local_width], kv_both, kv_turned, key_ids, query_ids)
    mixed_group = mul(shuffle, mixed_stream, TN, low)
    part = mul(mixed_group, out_rows, NN, low)
    resid = tokens_float + head_sum([part[i * row_count :][:row_count] for i in range(4)])
    normed_two = (resid * inverse_norm(resid) * gain_two).astype(low)
    normed_group = jnp.concatenate(head_gather(normed_two))
    grad_group = jnp.concatenate(head_gather(cotangent))
    section = (
        jnp.concatenate([gain_one, gain_two]),
        resid,
        normed_group,
        grad_group,
        gateup,
        down,
        features,
        qkv_rows,
        out_rows,
        stream,
        kv_both,
        kv_turned,
        lse,
        mixed_group,
        shuffle,
        key_ids,
        query_ids,
    )
    return section


def backward_steps(
    tokens,
    cotangent,
    gains,
    resid,
    normed_part,
    ffn_part,
    gateup_wgrad,
    down_wgrad,
    features,
    qkv_rows,
    out_rows,
    stream,
    kv_both,
    kv_turned,
    lse,
    mixed_group,
    shuffle,
    key_ids,
    query_ids,
    counts,
):
    row_count = tokens.shape[0]
    group = row_count * lax.axis_size("head")
    seq_count = lax.axis_size("seq")
    local_width = features.shape[1]
    query_stream = stream[:, :local_width]
    gain_one, gain_two = gains[0], gains[1]
    tokens_float = tokens.astype(full)
    inverse_one = inverse_norm(tokens_float)
    inverse_two = inverse_norm(resid)
    normed_two_grad = head_sum([normed_part[i * row_count :][:row_count] for i in range(4)])
    gateup_grad_own = sum_rows(gateup_wgrad, counts[2], 16, from_units)
    down_grad_own = sum_rows(down_wgrad, counts[3], 8, from_columns)
    ffn_out = head_sum([ffn_part[i * row_count :][:row_count] for i in range(4)])
    block_out = (resid + ffn_out).astype(low)

    resid_grad = cotangent.astype(full) + norm_back(resid, inverse_two, gain_two, normed_two_grad)
    gain_two_grad = jnp.sum(normed_two_grad * resid * inverse_two, axis=0)
    proj_grad = resid_grad.astype(low)
    proj_grad_group = jnp.concatenate(head_gather(proj_grad))
    mixed_grad_group = mul(proj_grad_group, out_rows, NT, low)
    mixed_grad_stream = mul(shuffle, mixed_grad_group, NN, low)
    out_wgrad = split_halves(mul(mixed_group, proj_grad_group, TN, low), BLK)
    out_grad_own = sum_rows(out_wgrad, counts[1], 8, from_columns)

    query_grad, kv_grad = attend_back(
        query_stream, mixed_grad_stream, kv_both, kv_turned, key_ids, query_ids, lse
    )
    kv_later = lax.ppermute(
        kv_grad[:group].astype(low), "seq", [(i, i - 1) for i in range(1, seq_count)]
    )
    kv_grad = (kv_grad[group:] + kv_later.astype(full)).astype(low)
    grad_local = mul(shuffle, jnp.concatenate([query_grad, kv_grad], axis=1), TN, low)
    gathered = head_gather(grad_local)

    def own_order(value, j):
        quarters = [value[i * row_count :][:row_count] for i in range(4)]
        return jnp.concatenate([quarters[i ^ j] for i in range(4)])

    gathered = [own_order(value, j) for j, value in enumerate(gathered)]
    kv_total = sum(value[:, local_width:].astype(full) for value in gathered).astype(low)
    qkv_grad = jnp.concatenate(
        [in_order([value[:, :local_width] for value in gathered], 1), kv_total], axis=1
    )
    qkv_wgrad = split_halves(mul(features, qkv_grad, TN, low), BLK)
    qkv_grad_own = sum_rows(qkv_wgrad, counts[0], 8, from_columns)
    feature_grad = mul(qkv_grad, qkv_rows, NT, low)
    order = (0, 2, 1, 3)
    feature_parts = head_exchange([feature_grad[i * row_count :][:row_count] for i in range(4)])
    normed_one_grad = in_order([feature_parts[order.index(j)] for j in range(4)], 1).astype(full)
    input_grad = resid_grad + norm_back(tokens_float, inverse_one, gain_one, normed_one_grad)
    gain_one_grad = jnp.sum(normed_one_grad * tokens_float * inverse_one, axis=0)
    return (
        block_out,
        input_grad,
        jnp.stack([gain_one_grad, gain_two_grad]),
        gateup_grad_own,
        down_grad_own,
        qkv_grad_own,
        out_grad_own,
    )


def on_device(
    tokens,
    cotangent,
    attn_gain,
    ffn_gain,
    qkv_stack,
    out_stack,
    gateup_stack,
    down_stack,
    qkv_left,
    qkv_right,
    out_left,
    out_right,
    gateup_left,
    gateup_right,
    down_left,
    down_right,
    qkv_left_root,
    qkv_right_root,
    out_left_root,
    out_right_root,
    gateup_left_root,
    gateup_right_root,
    down_left_root,
    down_right_root,
    sequence_ids,
    token_order,
):
    row_count = tokens.shape[0]
    head_count = lax.axis_size("head")
    seq_count = lax.axis_size("seq")
    device_count = head_count * seq_count
    group = row_count * head_count
    seq_index = lax.axis_index("seq")
    local_width = QW // head_count

    own_gains = attn_gain.shape[0]
    stacks = (qkv_stack, out_stack, gateup_stack, down_stack)
    whole_rows = all(s.shape[0] % u == 0 for s, u in zip(stacks, (8, 8, 16, 8)))
    if whole_rows:
        tile = jnp.concatenate([attn_gain[None], ffn_gain[None]])
        section = forward_section(
            tokens,
            cotangent,
            jnp.pad(tile, ((0, 6), (0, 128 - own_gains))),
            stacks,
            token_order[None, :],
            sequence_ids[None, :],
            seq_count,
        )
    else:
        section = forward_steps(
            tokens, cotangent, attn_gain, ffn_gain, stacks, token_order, sequence_ids
        )
    (
        gains_both,
        resid,
        normed_group,
        grad_group,
        gateup,
        down,
        features,
        qkv_rows,
        out_all,
        stream,
        kv_both,
        kv_turned,
        lse,
        mixed_group,
        shuffle,
        key_ids,
        query_ids,
    ) = section
    gateup = gateup.reshape(-1, D)
    down = down.reshape(-1, 2, BLK, D // 2)
    unit_count = down.shape[0]
    hidden, gate_up_grad, normed_part, ffn_part = feed_forward(
        normed_group, grad_group, gateup, down
    )
    gateup_wgrad = mul(gate_up_grad, normed_group, NN, low)
    down_wgrad = split_halves(mul(hidden, grad_group, NN, low), BLK)
    kept = (features, qkv_rows, out_all, stream, kv_both, kv_turned, lse, mixed_group, shuffle)
    counts = [s.shape[0] for s in stacks]
    if not whole_rows:
        gateup_wgrad = gateup_wgrad.reshape(2 * unit_count, BLK, D)
    if whole_rows:
        (block_out, input_grad, gain_grads, gateup_own, down_own, qkv_own, out_own, *_) = (
            backward_section(
                seq_count,
                tokens,
                cotangent,
                gains_both,
                resid,
                normed_part,
                ffn_part,
                gateup_wgrad.reshape(seq_count, -1, D),
                down_wgrad.reshape(seq_count, -1, D // 2),
                *kept,
                key_ids,
                query_ids,
            )
        )
        gateup_grad_own, down_grad_own = gateup_own, down_own
        qkv_grad_own, out_grad_own = qkv_own, out_own
    else:
        section = backward_steps(
            tokens, cotangent, gains_both, resid, normed_part, ffn_part, gateup_wgrad, down_wgrad, *kept,
            key_ids, query_ids, counts,
        )
        (block_out, input_grad, gain_grads, gateup_grad_own, down_grad_own, qkv_grad_own, out_grad_own) = section
    gain_one_grad, gain_two_grad = gain_grads[0], gain_grads[1]
    gain_grads = jnp.concatenate(
        [gain_one_grad.reshape(device_count, -1), gain_two_grad.reshape(device_count, -1)], axis=1
    )
    gain_grads = lax.all_to_all(
        gain_grads, ("head", "seq"), split_axis=0, concat_axis=0, tiled=True
    )
    gain_grads = jnp.sum(gain_grads, axis=0)

    gateup_new = update(
        gateup_stack,
        gateup_grad_own,
        gateup_left,
        gateup_right,
        gateup_left_root,
        gateup_right_root,
        0.5 * D ** (-0.5),
        whole_rows,
    )
    down_new = update(
        down_stack,
        down_grad_own,
        down_left,
        down_right,
        down_left_root,
        down_right_root,
        0.5 * FF ** (-0.5),
    )
    out_new = update(
        out_stack,
        out_grad_own,
        out_left,
        out_right,
        out_left_root,
        out_right_root,
        0.5 * (QW // 64) ** (-0.5),
    )
    qkv_new = update(
        qkv_stack,
        qkv_grad_own,
        qkv_left,
        qkv_right,
        qkv_left_root,
        qkv_right_root,
        0.5 * D ** (-0.5),
    )
    return (
        (block_out, input_grad, gain_grads[:own_gains], gain_grads[own_gains:])
        + tuple(qkv_new)
        + tuple(out_new)
        + tuple(gateup_new)
        + tuple(down_new)
    )


def solution(mesh):
    rows = P(("seq", "head"), None)
    gain = P(("head", "seq"))
    blocks = P(("head", "seq"), None, None)
    return jax.shard_map(
        on_device,
        mesh=mesh,
        in_specs=(rows, rows, gain, gain) + (blocks,) * 20 + (P(), P("seq")),
        out_specs=(rows, rows, gain, gain) + (blocks,) * 12,
        check_vma=False,
    )
```
